32 devices in a mesh: dp: 16 (over z, x, core), head: 2 (over y).
Axes of the slice: x: 2, y: 2, z: 4, core: 2. Of those that a mesh axis runs over, the one named last changes fastest.
Arguments:
- tokens: bfloat16 [16384, 768], P('dp'), may hold values from -6 to 6
- cotangent: bfloat16 [16384, 768], P(('dp', 'head')), may hold values from -6 to 6
- form_number: int32 [16, 1024], P('dp'), may hold values from 0 to 2, never falling along the last dimension, each value on 1 to 709 neighbouring positions
- sequence_bucket: int32 [16384, 1024], P('dp'), may hold values from 0 to 31
- horizontal_bucket: int32 [16384, 1024], P('dp'), may hold values from 0 to 63
- vertical_bucket: int32 [16384, 1024], P('dp'), may hold values from 0 to 63
- project_weight: bfloat16 [768, 3, 768], P(None, None, 'head'), may hold values from -0.21875 to 0.21875
- query_bias: bfloat16 [768], P('head'), may hold values from -3 to 3
- value_bias: bfloat16 [768], P('head'), may hold values from -3 to 3
- output_weight: bfloat16 [768, 768], P('head'), may hold values from -1.75 to 1.75
- output_bias: bfloat16 [768], replicated, may hold values from -3 to 3
- first_gain: bfloat16 [768], replicated, may hold values from 0.5 to 1.5
- first_shift: bfloat16 [768], replicated, may hold values from -2 to 2
- up_weight: bfloat16 [768, 3072], P(None, 'head'), may hold values from -0.21875 to 0.21875
- up_bias: bfloat16 [3072], P('head'), may hold values from -3 to 3
- down_weight: bfloat16 [3072, 768], P('head'), may hold values from -0.109375 to 0.109375
- down_bias: bfloat16 [768], replicated, may hold values from -3 to 3
- second_gain: bfloat16 [768], replicated, may hold values from 0.5 to 1.5
- second_shift: bfloat16 [768], replicated, may hold values from -2 to 2
- sequence_table: bfloat16 [32, 12], P(None, 'head'), may hold values from -4 to 4
- horizontal_table: bfloat16 [64, 12], P(None, 'head'), may hold values from -4 to 4
- vertical_table: bfloat16 [64, 12], P(None, 'head'), may hold values from -4 to 4
- project_weight_average: float32 [768, 3, 768], P('dp', None, 'head'), may hold values from -0.21875 to 0.21875
- query_bias_average: float32 [768], P('head'), may hold values from -3 to 3
- value_bias_average: float32 [768], P('head'), may hold values from -3 to 3
- output_weight_average: float32 [768, 768], P('head', 'dp'), may hold values from -1.75 to 1.75
- output_bias_average: float32 [768], replicated, may hold values from -3 to 3
- first_gain_average: float32 [768], replicated, may hold values from 0.5 to 1.5
- first_shift_average: float32 [768], replicated, may hold values from -2 to 2
- up_weight_average: float32 [768, 3072], P('dp', 'head'), may hold values from -0.21875 to 0.21875
- up_bias_average: float32 [3072], P('head'), may hold values from -3 to 3
- down_weight_average: float32 [3072, 768], P(('head', 'dp')), may hold values from -0.109375 to 0.109375
- down_bias_average: float32 [768], replicated, may hold values from -3 to 3
- second_gain_average: float32 [768], replicated, may hold values from 0.5 to 1.5
- second_shift_average: float32 [768], replicated, may hold values from -2 to 2
- sequence_table_average: float32 [32, 12], P(None, 'head'), may hold values from -4 to 4
- horizontal_table_average: float32 [64, 12], P(None, 'head'), may hold values from -4 to 4
- vertical_table_average: float32 [64, 12], P(None, 'head'), may hold values from -4 to 4
Outputs:
- layer_output: float32 [16384, 768], P(('dp', 'head'))
- tokens_gradient: float32 [16384, 768], P(('dp', 'head'))
- project_weight_gradient: float32 [768, 3, 768], P(None, None, 'head')
- query_bias_gradient: float32 [768], P('head')
- value_bias_gradient: float32 [768], P('head')
- output_weight_gradient: float32 [768, 768], P('head')
- output_bias_gradient: float32 [768], replicated
- first_gain_gradient: float32 [768], replicated
- first_shift_gradient: float32 [768], replicated
- up_weight_gradient: float32 [768, 3072], P(None, 'head')
- up_bias_gradient: float32 [3072], P('head')
- down_weight_gradient: float32 [3072, 768], P('head')
- down_bias_gradient: float32 [768], replicated
- second_gain_gradient: float32 [768], replicated
- second_shift_gradient: float32 [768], replicated
- sequence_table_gradient: float32 [32, 12], P(None, 'head')
- horizontal_table_gradient: float32 [64, 12], P(None, 'head')
- vertical_table_gradient: float32 [64, 12], P(None, 'head')
- project_weight_renewed: float32 [768, 3, 768], P('dp', None, 'head')
- query_bias_renewed: float32 [768], P('head')
- value_bias_renewed: float32 [768], P('head')
- output_weight_renewed: float32 [768, 768], P('head', 'dp')
- output_bias_renewed: float32 [768], replicated
- first_gain_renewed: float32 [768], replicated
- first_shift_renewed: float32 [768], replicated
- up_weight_renewed: float32 [768, 3072], P('dp', 'head')
- up_bias_renewed: float32 [3072], P('head')
- down_weight_renewed: float32 [3072, 768], P(('head', 'dp'))
- down_bias_renewed: float32 [768], replicated
- second_gain_renewed: float32 [768], replicated
- second_shift_renewed: float32 [768], replicated
- sequence_table_renewed: float32 [32, 12], P(None, 'head')
- horizontal_table_renewed: float32 [64, 12], P(None, 'head')
- vertical_table_renewed: float32 [64, 12], P(None, 'head')
The draws below stay inside these ranges and needn't reach their ends.
Inputs may be any that keep to these rules, and one draw needn't show every extreme that they name: `form_number`: along each pack of 1024 positions the form numbers never fall; a form has at most min(709, 1024) positions, and some form has exactly that many.
All inputs are finite; a program needn't handle non-finite values.
Results may differ from the reference program's by a relative error of at most 0.014.
Values may be sent and summed in bfloat16 or wider, within the bound.
A program may use at most 256 MiB of HBM per device.

```python
import math
import jax
import jax.numpy as jnp
import numpy as np
from jax import lax

D = 768
H = 12
DH = 64
FF = 3072
B1 = 32
B2 = 64
FORM = 709
ROWS = 1024
PACKS = 16
TOKENS = 16384
N_DP = 16


def place_ends(drawn, stream_key, least, top_value):
    extent = drawn.shape
    place = [jax.random.randint(jax.random.fold_in(stream_key, axis), (), 0, extent[axis]) for axis in range(len(extent))]
    drawn = drawn.at[tuple(place)].set(least)
    longest = extent.index(max(extent))
    place[longest] = (place[longest] + 1) % extent[longest]
    return drawn.at[tuple(place)].set(top_value)


def block_levels(rng, dims, cuts, low, top_value):
    level = 1.0
    for axis_at, shards_of in cuts:
        draws = jax.random.uniform(jax.random.fold_in(jax.random.fold_in(rng, 6), axis_at), (shards_of,), jnp.float32, low / len(cuts), top_value / len(cuts))
        level = level * jnp.repeat(jnp.exp(draws), dims[axis_at] // shards_of).reshape((-1,) + (1,) * (len(dims) - 1 - axis_at))
    return level


def profile(amount, total, most, lean):
    portions = [(1 << 20) // math.isqrt(grade ** lean) + 1 for grade in range(2, amount + 1)]
    surplus, given = total - most - (amount - 1), [1] * (amount - 1)
    while surplus > 0:
        candidates = [i for i in range(amount - 1) if given[i] < most]
        mass, left = sum([portions[i] for i in candidates]), surplus
        for i in candidates:
            more = min(most - given[i], max(1, left * portions[i] // mass), surplus)
            given[i] = given[i] + more
            surplus = surplus - more
    return np.array([most] + given)


def ragged(rng, number_of, total, limit, lean):
    if number_of == 2:
        one = jax.random.randint(rng, (), max(1, total - limit), min(limit, total - 1) + 1)
        return jnp.stack([one, total - one])
    lengths = jnp.asarray(profile(number_of, total, limit, lean), jnp.int32)
    couples = (number_of - 1) // 2
    source_of, taker = lengths[1:1 + 2 * couples:2], lengths[2:2 + 2 * couples:2]
    room = jnp.minimum(source_of - 1, limit - taker)
    passed = jax.random.randint(jax.random.fold_in(rng, 1), (couples,), 0, 1 << 20) % (room + 1)
    lengths = lengths.at[1:1 + 2 * couples:2].set(source_of - passed).at[2:2 + 2 * couples:2].set(taker + passed)
    return lengths[jax.random.permutation(jax.random.fold_in(rng, 2), number_of)]


def bell_draw(rng, dims, scale, reach, cuts=(), kind=jnp.bfloat16):
    level = block_levels(rng, dims, cuts, -0.22, 0.18) if cuts else 1.0
    values = jax.random.normal(rng, dims, jnp.float32) * scale * level
    return jnp.minimum(jnp.maximum(values, -reach), reach).astype(kind)


def setup_inputs(seed: int = 0) -> dict:
    key_list = jax.random.split(jax.random.key(seed), 39)
    return {
        "tokens": bell_draw(key_list[0], (TOKENS, D), 1.0, 6.0, ((0, 16),)),
        "cotangent": bell_draw(key_list[1], (TOKENS, D), 1.0, 6.0, ((0, 32),)),
        "form_number": jax.vmap(lambda own: jnp.searchsorted(jnp.cumsum(ragged(own, 3, ROWS, min(FORM, ROWS), 0)), jnp.arange(ROWS), side="right"))(jax.random.split(key_list[2], PACKS)).reshape((PACKS, ROWS)).astype(jnp.int32),
        "sequence_bucket": place_ends(jax.random.randint(key_list[3], (TOKENS, ROWS), 0, B1), jax.random.fold_in(key_list[3], 1), 0, B1 - 1).astype(jnp.int32),
        "horizontal_bucket": place_ends(jax.random.randint(key_list[4], (TOKENS, ROWS), 0, B2), jax.random.fold_in(key_list[4], 1), 0, B2 - 1).astype(jnp.int32),
        "vertical_bucket": place_ends(jax.random.randint(key_list[5], (TOKENS, ROWS), 0, B2), jax.random.fold_in(key_list[5], 1), 0, B2 - 1).astype(jnp.int32),
        "project_weight": bell_draw(key_list[6], (D, 3, D), D ** -0.5, 0.21875, ((2, 2),)),
        "query_bias": bell_draw(key_list[7], (D,), 0.5, 3.0, ((0, 2),)),
        "value_bias": bell_draw(key_list[8], (D,), 0.5, 3.0, ((0, 2),)),
        "output_weight": bell_draw(key_list[9], (D, D), (D // 64) ** -0.5, 1.75, ((0, 2),)),
        "output_bias": bell_draw(key_list[10], (D,), 0.5, 3.0),
        "first_gain": jnp.clip(1.0 + 0.1 * jax.random.normal(key_list[11], (D,), jnp.float32), 0.5, 1.5).astype(jnp.bfloat16),
        "first_shift": bell_draw(key_list[12], (D,), 0.3, 2.0),
        "up_weight": bell_draw(key_list[13], (D, FF), D ** -0.5, 0.21875, ((1, 2),)),
        "up_bias": bell_draw(key_list[14], (FF,), 0.5, 3.0, ((0, 2),)),
        "down_weight": bell_draw(key_list[15], (FF, D), FF ** -0.5, 0.109375, ((0, 2),)),
        "down_bias": bell_draw(key_list[16], (D,), 0.5, 3.0),
        "second_gain": jnp.clip(1.0 + 0.1 * jax.random.normal(key_list[17], (D,), jnp.float32), 0.5, 1.5).astype(jnp.bfloat16),
        "second_shift": bell_draw(key_list[18], (D,), 0.3, 2.0),
        "sequence_table": bell_draw(key_list[19], (B1, H), 0.7, 4.0, ((1, 2),)),
        "horizontal_table": bell_draw(key_list[20], (B2, H), 0.7, 4.0, ((1, 2),)),
        "vertical_table": bell_draw(key_list[21], (B2, H), 0.7, 4.0, ((1, 2),)),
        "project_weight_average": bell_draw(key_list[22], (D, 3, D), D ** -0.5, 0.21875, ((0, 16), (2, 2)), jnp.float32),
        "query_bias_average": bell_draw(key_list[23], (D,), 0.5, 3.0, ((0, 2),), jnp.float32),
        "value_bias_average": bell_draw(key_list[24], (D,), 0.5, 3.0, ((0, 2),), jnp.float32),
        "output_weight_average": bell_draw(key_list[25], (D, D), (D // 64) ** -0.5, 1.75, ((0, 2), (1, 16)), jnp.float32),
        "output_bias_average": bell_draw(key_list[26], (D,), 0.5, 3.0, (), jnp.float32),
        "first_gain_average": jnp.clip(1.0 + 0.1 * jax.random.normal(key_list[27], (D,), jnp.float32), 0.5, 1.5),
        "first_shift_average": bell_draw(key_list[28], (D,), 0.3, 2.0, (), jnp.float32),
        "up_weight_average": bell_draw(key_list[29], (D, FF), D ** -0.5, 0.21875, ((0, 16), (1, 2)), jnp.float32),
        "up_bias_average": bell_draw(key_list[30], (FF,), 0.5, 3.0, ((0, 2),), jnp.float32),
        "down_weight_average": bell_draw(key_list[31], (FF, D), FF ** -0.5, 0.109375, ((0, 32),), jnp.float32),
        "down_bias_average": bell_draw(key_list[32], (D,), 0.5, 3.0, (), jnp.float32),
        "second_gain_average": jnp.clip(1.0 + 0.1 * jax.random.normal(key_list[33], (D,), jnp.float32), 0.5, 1.5),
        "second_shift_average": bell_draw(key_list[34], (D,), 0.3, 2.0, (), jnp.float32),
        "sequence_table_average": bell_draw(key_list[35], (B1, H), 0.7, 4.0, ((1, 2),), jnp.float32),
        "horizontal_table_average": bell_draw(key_list[36], (B2, H), 0.7, 4.0, ((1, 2),), jnp.float32),
        "vertical_table_average": bell_draw(key_list[37], (B2, H), 0.7, 4.0, ((1, 2),), jnp.float32),
    }


@jax.custom_vjp
def low(v):
    return lax.optimization_barrier(v.astype(jnp.bfloat16)).astype(jnp.float32)

@jax.custom_vjp
def low_back(v):
    return v

def low_keep(v):
    return (low(v), None)

def low_pass(kept, grad):
    return (grad,)

def back_keep(v):
    return (v, None)

def back_low(kept, grad):
    return (low(grad),)
low.defvjp(low_keep, low_pass)
low_back.defvjp(back_keep, back_low)
norm_epsilon = 1e-05
highest = lax.Precision.HIGHEST
masked_score = -1e+30

def rounded_both(value):
    return low_back(low(value))

def layer_norm(value, gain, shift):
    center = value - lax.optimization_barrier(jnp.mean(value, axis=-1, keepdims=True))
    spread = lax.optimization_barrier(jnp.mean(center * center, axis=-1, keepdims=True))
    return center * lax.rsqrt(spread + norm_epsilon) * gain + shift

def pack_layer(weights, block):
    project_weight, query_bias, value_bias, output_weight, output_bias, first_gain, first_shift, up_weight, up_bias, down_weight, down_bias, second_gain, second_shift, sequence_table, horizontal_table, vertical_table = weights
    pack_rows, form_row, sequence_bucket, horizontal_bucket, vertical_bucket = block
    projected = jnp.einsum('rd,dcf->rcf', pack_rows, project_weight, precision=highest)
    query = rounded_both((projected[:, 0] + query_bias) * 0.125).reshape(ROWS, H, DH)
    key = rounded_both(projected[:, 1]).reshape(ROWS, H, DH)
    value = rounded_both(projected[:, 2] + value_bias).reshape(ROWS, H, DH)
    bias = low(sequence_table)[sequence_bucket] + low(horizontal_table)[horizontal_bucket] + low(vertical_table)[vertical_bucket]
    score = jnp.einsum('qhd,khd->hqk', query, key, precision=highest) + jnp.transpose(bias, (2, 0, 1))
    score = low_back(score)
    same_form = (form_row[:, None] == form_row[None, :])[None]
    score = jnp.where(same_form, score, masked_score)
    top = lax.optimization_barrier(jnp.max(score, axis=-1, keepdims=True))
    weight = jnp.exp(score - top)
    probs = weight / lax.optimization_barrier(jnp.sum(weight, axis=-1, keepdims=True))
    context = jnp.einsum('hqk,khd->qhd', low(probs), value, precision=highest)
    context = rounded_both(context.reshape(ROWS, D))
    attend = low_back(jnp.dot(context, output_weight, precision=highest) + output_bias)
    normed = layer_norm(pack_rows + attend, first_gain, first_shift)
    up = low_back(jnp.dot(low(normed), up_weight, precision=highest) + up_bias)
    act = low(jax.nn.gelu(up, approximate=False))
    feed = low_back(jnp.dot(act, down_weight, precision=highest) + down_bias)
    return layer_norm(normed + feed, second_gain, second_shift)

def reference(tokens, cotangent, form_number, sequence_bucket, horizontal_bucket, vertical_bucket, project_weight, query_bias, value_bias, output_weight, output_bias, first_gain, first_shift, up_weight, up_bias, down_weight, down_bias, second_gain, second_shift, sequence_table, horizontal_table, vertical_table, project_weight_average, query_bias_average, value_bias_average, output_weight_average, output_bias_average, first_gain_average, first_shift_average, up_weight_average, up_bias_average, down_weight_average, down_bias_average, second_gain_average, second_shift_average, sequence_table_average, horizontal_table_average, vertical_table_average):
    weights = (project_weight, query_bias, value_bias, output_weight, output_bias, first_gain, first_shift, up_weight, up_bias, down_weight, down_bias, second_gain, second_shift, sequence_table, horizontal_table, vertical_table)
    averages = (project_weight_average, query_bias_average, value_bias_average, output_weight_average, output_bias_average, first_gain_average, first_shift_average, up_weight_average, up_bias_average, down_weight_average, down_bias_average, second_gain_average, second_shift_average, sequence_table_average, horizontal_table_average, vertical_table_average)
    weights_wide = tuple((item.astype(jnp.float32) for item in weights))
    integer_blocks = (form_number, sequence_bucket.reshape(N_DP, ROWS, ROWS), horizontal_bucket.reshape(N_DP, ROWS, ROWS), vertical_bucket.reshape(N_DP, ROWS, ROWS))

    def forward(rows_in, *params):
        packs = rows_in.reshape(N_DP, ROWS, D)
        layer_fn = jax.checkpoint(lambda block: pack_layer(params, block))
        outputs = lax.map(layer_fn, (packs,) + integer_blocks)
        return outputs.reshape(TOKENS, D)
    layer_output, pullback = jax.vjp(forward, tokens.astype(jnp.float32), *weights_wide)
    grads = pullback(cotangent.astype(jnp.float32))
    renewed = tuple((0.5 * avg_item + 0.5 * (weight_item - grad_item / TOKENS) for avg_item, weight_item, grad_item in zip(averages, weights_wide, grads[1:])))
    return (layer_output, grads[0], grads[1], grads[2], grads[3], grads[4], grads[5], grads[6], grads[7], grads[8], grads[9], grads[10], grads[11], grads[12], grads[13], grads[14], grads[15], grads[16], renewed[0], renewed[1], renewed[2], renewed[3], renewed[4], renewed[5], renewed[6], renewed[7], renewed[8], renewed[9], renewed[10], renewed[11], renewed[12], renewed[13], renewed[14], renewed[15])
```

```python
import functools
import jax
import jax.numpy as jnp
from jax import lax
from jax.experimental import pallas as pl
from jax.sharding import PartitionSpec as P
from jax.experimental.pallas import tpu as pltpu

F32, BF16, I32 = jnp.float32, jnp.bfloat16, jnp.int32
SCALE_BITS = 27
STEP = 2.0**11
VM = 56 * 2**20


def dot_nt(a, b):
    return lax.dot_general(a, b, (((1,), (1,)), ((), ())), preferred_element_type=F32)


def dot_tn(a, b):
    return lax.dot_general(a, b, (((0,), (0,)), ((), ())), preferred_element_type=F32)


def dot_general_t(w, x):
    return lax.dot_general(w, x, (((0,), (1,)), ((), ())), preferred_element_type=F32)


def dot_tt(a, b):
    return lax.dot_general(a, b, (((0,), (1,)), ((), ())), preferred_element_type=F32)


def dot_nn(a, b):
    return lax.dot_general(a, b, (((1,), (0,)), ((), ())), preferred_element_type=F32)


def split_pair(x):
    lane = lax.broadcasted_iota(I32, x.shape, 1)
    zero = jnp.zeros_like(x)
    return jnp.concatenate([jnp.where(lane < 64, x, zero), jnp.where(lane < 64, zero, x)], axis=0)


def fwd_kernel(off, seq, hor, ver, formc, formr, tab, q, kt, v, p_out, c_out, b_ref, *, pairs, qb):
    keys = v.shape[0]
    chunk = 128
    tbs = [jnp.broadcast_to(tab[i : i + 1, :], (8, chunk)) for i in range(3 * pairs)]

    def gather(r, _):
        rs = pl.ds(pl.multiple_of(r * 8, 8), 8)
        for c in range(keys // chunk):
            ls = slice(c * chunk, (c + 1) * chunk)
            sums = [None] * pairs
            for t, b in enumerate((seq, hor, ver)):
                idx = b[rs, ls]
                for j in range(pairs):
                    g = jnp.take_along_axis(tbs[3 * j + t], idx, axis=1, mode="promise_in_bounds")
                    sums[j] = g if t == 0 else sums[j] + g
            for j in range(pairs):
                b_ref[j, rs, ls] = sums[j]
        return 0

    lax.fori_loop(0, qb // 8, gather, 0)
    same = formc[...] == formr[...]
    for j in range(pairs):
        lanes = slice(j * 128, (j + 1) * 128)
        q2 = split_pair(q[:, lanes])
        s2 = dot_nn(q2, kt[lanes, :])
        bias = b_ref[j]
        for g in range(2):
            x = s2[g * qb : (g + 1) * qb] + (bias << 16 if g else bias).astype(F32)
            x = jnp.where(same, x, -1e30)
            top = jnp.max(x, axis=1, keepdims=True)
            e = jnp.exp2((x - top) * (1.4426950408889634 * 2.0**-SCALE_BITS))
            inv = 1.0 / jnp.sum(e, axis=1, keepdims=True)
            p_out[2 * j + g] = (e * inv).astype(BF16)
        c0 = dot_nn(p_out[2 * j], v[:, lanes])
        c1 = dot_nn(p_out[2 * j + 1], v[:, lanes])
        lane = lax.broadcasted_iota(I32, c0.shape, 1)
        c_out[:, lanes] = jnp.where(lane < 64, c0, c1).astype(BF16)


def attend_fwd(off, buckets, formc, formr, tab, q, kt, v, qb=128):
    nq, width = q.shape
    keys = v.shape[0]
    pairs = width // 128
    bspec = pl.BlockSpec((qb, keys), lambda i, off: (i + off[0], 0))
    full = lambda a: pl.BlockSpec(a.shape, lambda i, off: (0,) * a.ndim)
    return pl.pallas_call(
        functools.partial(fwd_kernel, pairs=pairs, qb=qb),
        out_shape=(
            jax.ShapeDtypeStruct((2 * pairs, nq, keys), BF16),
            jax.ShapeDtypeStruct((nq, width), BF16),
        ),
        grid_spec=pltpu.PrefetchScalarGridSpec(
            num_scalar_prefetch=1,
            grid=(nq // qb,),
            in_specs=[bspec] * 3
            + [
                pl.BlockSpec((qb, 1), lambda i, off: (i + off[0], 0)),
                full(formr),
                full(tab),
                pl.BlockSpec((qb, width), lambda i, off: (i, 0)),
                full(kt),
                full(v),
            ],
            out_specs=(
                pl.BlockSpec((2 * pairs, qb, keys), lambda i, off: (0, i, 0)),
                pl.BlockSpec((qb, width), lambda i, off: (i, 0)),
            ),
            scratch_shapes=[pltpu.VMEM((pairs, qb, keys), I32)],
        ),
        compiler_params=pltpu.CompilerParams(vmem_limit_bytes=VM),
        cost_estimate=pl.CostEstimate(
            flops=4 * nq * keys * width, bytes_accessed=16 * 2**20, transcendentals=nq * keys * 2 * pairs
        ),
    )(off, *buckets, formc, formr, tab, q, kt, v)


def bwd_kernel(q, k, vt, do, p, ds_out, dq_out, dk_out, dv_out, *, pairs, qb):
    keys = k.shape[0]

    @pl.when(pl.program_id(0) == 0)
    def _():
        dk_out[...] = jnp.zeros_like(dk_out)
        dv_out[...] = jnp.zeros_like(dv_out)

    for j in range(pairs):
        lanes = slice(j * 128, (j + 1) * 128)
        q2 = split_pair(q[:, lanes])
        do2 = split_pair(do[:, lanes])
        dp2 = dot_nn(do2, vt[lanes, :])

        for g in range(2):
            ps = p[2 * j + g].astype(F32)
            ts = ps * dp2[g * qb : (g + 1) * qb]
            inner = jnp.sum(ts, axis=1, keepdims=True)
            ds_out[2 * j + g] = (ts - ps * inner).astype(BF16)
        d0 = dot_nn(ds_out[2 * j], k[:, lanes])
        d1 = dot_nn(ds_out[2 * j + 1], k[:, lanes])
        lane = lax.broadcasted_iota(I32, d0.shape, 1)
        dq_out[:, lanes] = jnp.where(lane < 64, d0, d1).astype(BF16) * jnp.array(0.125, BF16)
        ds2 = ds_out[2 * j : 2 * j + 2].reshape(2 * qb, keys)
        p2 = p[2 * j : 2 * j + 2].reshape(2 * qb, keys)
        dk_out[lanes, :] += dot_tn(q2, ds2)
        dv_out[lanes, :] += dot_tn(do2, p2)


def attend_bwd(q, k, vt, do, p, qb=128):
    nq, width = q.shape
    keys = k.shape[0]
    pairs = width // 128
    full = lambda a: pl.BlockSpec(a.shape, lambda i: (0,) * a.ndim)
    row = pl.BlockSpec((qb, width), lambda i: (i, 0))
    big = pl.BlockSpec((2 * pairs, qb, keys), lambda i: (0, i, 0))
    acc = pl.BlockSpec((width, keys), lambda i: (0, 0))
    return pl.pallas_call(
        functools.partial(bwd_kernel, pairs=pairs, qb=qb),
        out_shape=(
            jax.ShapeDtypeStruct((2 * pairs, nq, keys), BF16),
            jax.ShapeDtypeStruct((nq, width), BF16),
            jax.ShapeDtypeStruct((width, keys), F32),
            jax.ShapeDtypeStruct((width, keys), F32),
        ),
        grid=(nq // qb,),
        in_specs=[row, full(k), full(vt), row, big],
        out_specs=(big, row, acc, acc),
        compiler_params=pltpu.CompilerParams(vmem_limit_bytes=VM),
        cost_estimate=pl.CostEstimate(
            flops=8 * nq * keys * width, bytes_accessed=30 * 2**20, transcendentals=0
        ),
    )(q, k, vt, do, p)


def hist_kernel(off, seq, hor, ver, dsa, dsb, seq_out, hor_out, ver_out, rhs_ref, *, qb, bits):
    keys = seq.shape[1]
    heads = (dsa.shape[0], dsb.shape[0])
    nh = sum(heads)
    outs = (seq_out, hor_out, ver_out)

    @pl.when(pl.program_id(0) == 0)
    def _():
        for o in outs:
            o[...] = jnp.zeros_like(o)

    def rows(r, _):
        rs = pl.ds(pl.multiple_of(r * 16, 16), 16)
        dfull = [d[h, rs, :].astype(F32) for d, n in ((dsa, heads[0]), (dsb, heads[1])) for h in range(n)]
        for half in range(2):
            d8 = [d[half * 8 : half * 8 + 8] for d in dfull]
            for t, b in enumerate((seq, hor, ver)):
                idx = b[pl.ds(pl.multiple_of(r * 16 + half * 8, 8), 8), :]
                signs = [(((idx << (31 - i)) >> 31) | 1).astype(F32) for i in range(bits[t])]
                rhs = jnp.concatenate(
                    [jnp.concatenate([d, d * signs[0]], axis=0).astype(BF16) for d in d8], axis=0
                )
                first = jnp.concatenate([jnp.ones_like(signs[1]), signs[1]], axis=0).astype(BF16)
                tiles = [first]
                for i in range(2, bits[t]):
                    s2 = jnp.concatenate([signs[i], signs[i]], axis=0).astype(BF16)
                    tiles = tiles + [x * s2 for x in tiles]
                lhs = jnp.concatenate(tiles, axis=0)
                outs[t][...] += dot_nt(lhs, rhs)
        return 0

    lax.fori_loop(0, qb // 16, rows, 0)


def hist(off, buckets, dsa, dsb, bits, qb=128):
    nq, keys = dsa.shape[1], dsa.shape[2]
    nh = dsa.shape[0] + dsb.shape[0]
    bspec = pl.BlockSpec((qb, keys), lambda i, off: (i + off[0], 0))
    shapes = [(2 ** (b - 1) * 8, nh * 16) for b in bits]
    return pl.pallas_call(
        functools.partial(hist_kernel, qb=qb, bits=bits),
        out_shape=tuple(jax.ShapeDtypeStruct(s, F32) for s in shapes),
        grid_spec=pltpu.PrefetchScalarGridSpec(
            num_scalar_prefetch=1,
            grid=(nq // qb,),
            in_specs=[bspec] * 3
            + [pl.BlockSpec((d.shape[0], qb, keys), lambda i, off: (0, i, 0)) for d in (dsa, dsb)],
            out_specs=tuple(pl.BlockSpec(s, lambda i, off: (0, 0)) for s in shapes),
            scratch_shapes=[pltpu.VMEM((nh * 16, keys), BF16)],
        ),
        compiler_params=pltpu.CompilerParams(vmem_limit_bytes=VM),
        cost_estimate=pl.CostEstimate(
            flops=2 * nq * keys * 160 * nh * 8, bytes_accessed=20 * 2**20, transcendentals=0
        ),
    )(off, *buckets, dsa, dsb)


def unhist(acc, bits, nh):
    n = 2**bits
    a = acc.reshape(n // 2, 8, nh, 2, 8)
    m = jnp.einsum("fqhvq->fhv", a)
    b = jnp.arange(n)
    sign = lambda i: 1.0 - 2.0 * ((b >> i) & 1).astype(F32)
    tiles = [jnp.stack([jnp.ones((n,), F32), sign(1)])]
    for i in range(2, bits):
        tiles = tiles + [x * sign(i)[None] for x in tiles]
    lhs = jnp.concatenate(tiles)
    var = jnp.stack([jnp.ones((n,), F32), sign(0)])
    return jnp.einsum("fhv,fb,vb->bh", m, lhs, var, precision=lax.Precision.HIGHEST) / n


def pack_tables(tables):
    rows = [jnp.pad(t.astype(F32).T, ((0, 0), (0, 128 - t.shape[0]))) for t in tables]
    fixed = jnp.round(jnp.stack(rows, axis=1) * STEP).astype(I32)
    fixed = fixed.reshape(fixed.shape[0] // 2, 2, 3, 128)
    return (fixed[:, 0] * 65536 + fixed[:, 1]).reshape(-1, 128)


norm_epsilon = 1e-05


def mm(a, b):
    return jnp.dot(a, b, preferred_element_type=F32)


def normalize(value):
    center = value - jnp.mean(value, axis=-1, keepdims=True)
    spread = jnp.mean(center * center, axis=-1, keepdims=True)
    root = lax.rsqrt(spread + norm_epsilon)
    return center * root, root


def normalize_back(grad, normed, root):
    return root * (
        grad
        - jnp.mean(grad, axis=-1, keepdims=True)
        - normed * jnp.mean(grad * normed, axis=-1, keepdims=True)
    )


def gelu_parts(u):
    t = 1.0 / (1.0 + (0.3275911 * 0.7071067811865476) * jnp.abs(u))
    e = jnp.exp(-0.5 * u * u)
    poly = t * (
        0.254829592 + t * (-0.284496736 + t * (1.421413741 + t * (-1.453152027 + t * 1.061405429)))
    )
    tail = 0.5 * e * poly
    below = jnp.where(u >= 0, 1.0 - tail, tail)
    return u * below, below + u * (e * 0.3989422804014327)


def swap_dp(x, bit):
    n = lax.axis_size("dp")
    return lax.ppermute(x, "dp", [(i, i ^ bit) for i in range(n)])


def swap_head(x):
    return lax.ppermute(x, "head", [(0, 1), (1, 0)])


def dp_bits():
    n, bit, out = lax.axis_size("dp"), 1, []
    while bit < n:
        out.append(bit)
        bit *= 2
    return out


def bit_of(bit):
    return (lax.axis_index("dp") // bit) % 2


def in_order(first, mine, theirs):
    low = jnp.where(first == 0, mine, theirs)
    high = jnp.where(first == 0, theirs, mine)
    return jnp.concatenate([low, high], axis=0)


def rows_of(x, index, rows):
    return lax.dynamic_slice_in_dim(x, index * rows, rows, 0)


def fetch_other(w):
    rows = w.shape[0] // 4
    c, x = bit_of(1), bit_of(2)
    mine = swap_head(rows_of(w, 2 * c + x, rows))
    half = in_order(x, mine, swap_dp(mine, 2))
    return in_order(c, half, swap_dp(half, 1))


def halve(g, bit):
    rows = g.shape[0] // 2
    b = bit_of(bit)
    got = swap_dp(rows_of(g, 1 - b, rows), bit)
    return (rows_of(g, b, rows).astype(F32) + got.astype(F32)).astype(BF16)


def reduce_grad(own, other, head_first):
    bits = dp_bits()
    own, other = halve(own, 1), halve(other, 1)
    if not head_first:
        own, other = halve(own, 2), halve(other, 2)
    g = (own.astype(F32) + swap_head(other).astype(F32)).astype(BF16)
    for bit in bits[1 if head_first else 2 :]:
        g = halve(g, bit)
    for bit in reversed(bits):
        g = in_order(bit_of(bit), g, swap_dp(g, bit))
    return g.astype(F32)


def local(
    tokens,
    cotangent,
    form_number,
    sequence_bucket,
    horizontal_bucket,
    vertical_bucket,
    project_weight,
    query_bias,
    value_bias,
    output_weight,
    output_bias,
    first_gain,
    first_shift,
    up_weight,
    up_bias,
    down_weight,
    down_bias,
    second_gain,
    second_shift,
    sequence_table,
    horizontal_table,
    vertical_table,
    project_weight_average,
    query_bias_average,
    value_bias_average,
    output_weight_average,
    output_bias_average,
    first_gain_average,
    first_shift_average,
    up_weight_average,
    up_bias_average,
    down_weight_average,
    down_bias_average,
    second_gain_average,
    second_shift_average,
    sequence_table_average,
    horizontal_table_average,
    vertical_table_average,
):
    total_rows, model_width = tokens.shape
    local_width = project_weight.shape[2]
    local_heads = sequence_table.shape[1]
    hidden = up_weight.shape[1]
    share_rows = total_rows // lax.axis_size("head")
    head_index = lax.axis_index("head")
    share_start = head_index * share_rows
    block_rows = 128
    off = jnp.full((1,), head_index * (share_rows // block_rows), I32)
    buckets = (sequence_bucket, horizontal_bucket, vertical_bucket)
    tables = (sequence_table, horizontal_table, vertical_table)
    bits = tuple((t.shape[0] - 1).bit_length() for t in tables)
    flat_project = project_weight.reshape(model_width, 3 * local_width)

    small = jnp.concatenate(
        [query_bias, value_bias, up_bias] + [t.reshape(-1) for t in tables]
    ).reshape(1, -1)
    project_weights = (flat_project, fetch_other(flat_project))
    small_other = swap_head(small)[0]
    output_weights = (output_weight, fetch_other(output_weight))
    up_weights = (up_weight, fetch_other(up_weight))
    down_weights = (down_weight, fetch_other(down_weight))
    cuts = [local_width, 2 * local_width, 2 * local_width + hidden]
    ends = []
    for t in tables:
        ends.append(cuts[-1] + t.size)
        cuts.append(ends[-1])
    other_query_bias = small_other[: cuts[0]]
    other_value_bias = small_other[cuts[0] : cuts[1]]
    other_up_bias = small_other[cuts[1] : cuts[2]]
    other_tables = tuple(
        small_other[cuts[2 + i] : cuts[3 + i]].reshape(t.shape) for i, t in enumerate(tables)
    )
    query_biases = (query_bias, other_query_bias)
    value_biases = (value_bias, other_value_bias)
    up_biases = (up_bias, other_up_bias)
    packed_tables = (pack_tables(tables), pack_tables(other_tables))

    form_row = form_number.reshape(1, total_rows)
    form_column = form_number.reshape(total_rows, 1)
    own_tokens = rows_of(tokens, head_index, share_rows)

    scaled, keys, values_t, probs, contexts = [], [], [], [], []
    attend = output_bias.astype(F32)
    for s in range(2):
        wq = project_weights[s][:, :local_width]
        wk = project_weights[s][:, local_width : 2 * local_width]
        wv = project_weights[s][:, 2 * local_width :]
        bv = value_biases[s].astype(F32)
        q = ((mm(own_tokens, wq) + query_biases[s].astype(F32)) * 0.125).astype(BF16)
        q = q * jnp.array(2.0**SCALE_BITS, BF16)
        k = mm(tokens, wk).astype(BF16)
        kt = dot_general_t(wk, tokens).astype(BF16)
        v = (mm(tokens, wv) + bv).astype(BF16)
        vt = (dot_general_t(wv, tokens) + bv[:, None]).astype(BF16)
        p, context = attend_fwd(
            off, buckets, form_column, form_row, packed_tables[s], q, kt, v, qb=block_rows
        )
        attend = attend + mm(context, output_weights[s])
        scaled.append(q)
        keys.append(k)
        values_t.append(vt)
        probs.append(p)
        contexts.append(context)
    n1, root1 = normalize(own_tokens.astype(F32) + attend)
    normed = n1 * first_gain.astype(F32) + first_shift.astype(F32)
    normed_low = normed.astype(BF16)
    feed = down_bias.astype(F32)
    acts, slopes = [], []
    for s in range(2):
        up = mm(normed_low, up_weights[s]) + up_biases[s].astype(F32)
        act, slope = gelu_parts(up)
        act = act.astype(BF16)
        feed = feed + mm(act, down_weights[s])
        acts.append(act)
        slopes.append(slope.astype(BF16))
    n2, root2 = normalize(normed + feed)
    layer_output = n2 * second_gain.astype(F32) + second_shift.astype(F32)

    cot = cotangent.astype(F32)
    back_second = normalize_back(cot * second_gain.astype(F32), n2, root2)
    second_gain_part = jnp.sum(cot * n2, axis=0)
    second_shift_part = jnp.sum(cot, axis=0)
    back_feed = back_second.astype(BF16)
    down_bias_part = jnp.sum(back_feed.astype(F32), axis=0)
    back_normed = back_second
    up_bias_parts, down_grads, up_grads = [], [], []
    for s in range(2):
        down_grads.append(dot_tn(acts[s], back_feed).astype(BF16))
        back_up = (dot_nt(back_feed, down_weights[s]) * slopes[s].astype(F32)).astype(BF16)
        up_bias_parts.append(jnp.sum(back_up.astype(F32), axis=0))
        up_grads.append(dot_tn(normed_low, back_up).astype(BF16))
        back_normed = back_normed + dot_nt(back_up, up_weights[s])
    down_total = reduce_grad(down_grads[0], down_grads[1], True)
    up_total = reduce_grad(up_grads[0], up_grads[1], False)
    first_gain_part = jnp.sum(back_normed * n1, axis=0)
    first_shift_part = jnp.sum(back_normed, axis=0)
    back_first = normalize_back(back_normed * first_gain.astype(F32), n1, root1)
    back_attend = back_first.astype(BF16)
    output_bias_part = jnp.sum(back_attend.astype(F32), axis=0)
    output_grads = [dot_tn(contexts[s], back_attend).astype(BF16) for s in range(2)]
    output_total = reduce_grad(output_grads[0], output_grads[1], True)

    tokens_part = back_first
    other_part = jnp.zeros((share_rows, model_width), F32)
    back_scores, project_grads, query_bias_parts, value_bias_parts = [], [], [], []
    for s in range(2):
        wq = project_weights[s][:, :local_width]
        wk = project_weights[s][:, local_width : 2 * local_width]
        wv = project_weights[s][:, 2 * local_width :]
        back_context = dot_nt(back_attend, output_weights[s]).astype(BF16)
        ds, dq, dkt, dvt = attend_bwd(
            scaled[s], keys[s], values_t[s], back_context, probs[s], qb=block_rows
        )
        dkt = (dkt * 2.0**-SCALE_BITS).astype(BF16)
        dvt = dvt.astype(BF16)
        back_scores.append(ds)
        query_bias_parts.append(jnp.sum(dq.astype(F32), axis=0))
        value_bias_parts.append(jnp.sum(dvt.astype(F32), axis=1))
        project_grads.append(
            jnp.concatenate(
                [dot_tn(own_tokens, dq), dot_tt(tokens, dkt), dot_tt(tokens, dvt)], axis=1
            ).astype(BF16)
        )
        tokens_part = tokens_part + dot_nt(dq, wq)
        for grad, weight in ((dkt, wk), (dvt, wv)):
            own = lax.dynamic_slice_in_dim(grad, share_start, share_rows, 1)
            far = lax.dynamic_slice_in_dim(grad, (1 - head_index) * share_rows, share_rows, 1)
            tokens_part = tokens_part + dot_tt(own, weight)
            other_part = other_part + dot_tt(far, weight)
    tokens_gradient = tokens_part + swap_head(other_part.astype(BF16)).astype(F32)
    project_total = reduce_grad(project_grads[0], project_grads[1], True).reshape(
        model_width, 3, local_width
    )
    counts = hist(off, buckets, back_scores[0], back_scores[1], bits, qb=block_rows)
    table_parts = [unhist(a, b, 2 * local_heads) for a, b in zip(counts, bits)]

    common = [
        first_gain_part,
        first_shift_part,
        second_gain_part,
        second_shift_part,
        output_bias_part,
        down_bias_part,
    ]
    halves = [
        [query_bias_parts[s], value_bias_parts[s], up_bias_parts[s]]
        + [t[:, s * local_heads : (s + 1) * local_heads].reshape(-1) for t in table_parts]
        for s in range(2)
    ]
    sizes = [a.size for a in common + halves[0]]
    padding = -sum(sizes) % 1024
    mine = jnp.concatenate(common + halves[0] + [jnp.zeros((padding,), F32)]).reshape(-1, 128)
    theirs = jnp.concatenate(common + halves[1] + [jnp.zeros((padding,), F32)]).reshape(-1, 128)
    sums = mine + swap_head(theirs)
    for bit in dp_bits():
        sums = sums + swap_dp(sums, bit)
    sums = sums.reshape(-1)
    totals, at = [], 0
    for size in sizes:
        totals.append(sums[at : at + size])
        at += size
    (
        first_gain_total,
        first_shift_total,
        second_gain_total,
        second_shift_total,
        output_bias_total,
        down_bias_total,
        query_bias_total,
        value_bias_total,
        up_bias_total,
        sequence_total,
        horizontal_total,
        vertical_total,
    ) = totals
    sequence_total = sequence_total.reshape(sequence_table.shape)
    horizontal_total = horizontal_total.reshape(horizontal_table.shape)
    vertical_total = vertical_total.reshape(vertical_table.shape)
    up_weight_total, down_weight_total, output_weight_total = up_total, down_total, output_total
    token_count = total_rows * lax.axis_size("dp")
    group_count = lax.axis_size("dp")
    group_index = lax.axis_index("dp")

    def renew(average, weight, gradient):
        return 0.5 * average + 0.5 * (weight.astype(jnp.float32) - gradient / token_count)

    def part_of(array, along):
        width = array.shape[along] // group_count
        return lax.dynamic_slice_in_dim(array, group_index * width, width, along)

    return (
        layer_output,
        tokens_gradient,
        project_total,
        query_bias_total,
        value_bias_total,
        output_weight_total,
        output_bias_total,
        first_gain_total,
        first_shift_total,
        up_weight_total,
        up_bias_total,
        down_weight_total,
        down_bias_total,
        second_gain_total,
        second_shift_total,
        sequence_total,
        horizontal_total,
        vertical_total,
        renew(project_weight_average, part_of(project_weight, 0), part_of(project_total, 0)),
        renew(query_bias_average, query_bias, query_bias_total),
        renew(value_bias_average, value_bias, value_bias_total),
        renew(output_weight_average, part_of(output_weight, 1), part_of(output_weight_total, 1)),
        renew(output_bias_average, output_bias, output_bias_total),
        renew(first_gain_average, first_gain, first_gain_total),
        renew(first_shift_average, first_shift, first_shift_total),
        renew(up_weight_average, part_of(up_weight, 0), part_of(up_weight_total, 0)),
        renew(up_bias_average, up_bias, up_bias_total),
        renew(down_weight_average, part_of(down_weight, 0), part_of(down_weight_total, 0)),
        renew(down_bias_average, down_bias, down_bias_total),
        renew(second_gain_average, second_gain, second_gain_total),
        renew(second_shift_average, second_shift, second_shift_total),
        renew(sequence_table_average, sequence_table, sequence_total),
        renew(horizontal_table_average, horizontal_table, horizontal_total),
        renew(vertical_table_average, vertical_table, vertical_total),
    )


def solution(mesh):
    in_specs = (
        P("dp", None),
        P(("dp", "head"), None),
        P("dp", None),
        P("dp", None),
        P("dp", None),
        P("dp", None),
        P(None, None, "head"),
        P("head"),
        P("head"),
        P("head", None),
        P(),
        P(),
        P(),
        P(None, "head"),
        P("head"),
        P("head", None),
        P(),
        P(),
        P(),
        P(None, "head"),
        P(None, "head"),
        P(None, "head"),
        P("dp", None, "head"),
        P("head"),
        P("head"),
        P("head", "dp"),
        P(),
        P(),
        P(),
        P("dp", "head"),
        P("head"),
        P(("head", "dp"), None),
        P(),
        P(),
        P(),
        P(None, "head"),
        P(None, "head"),
        P(None, "head"),
    )
    out_specs = (
        P(("dp", "head"), None),
        P(("dp", "head"), None),
        P(None, None, "head"),
        P("head"),
        P("head"),
        P("head", None),
        P(),
        P(),
        P(),
        P(None, "head"),
        P("head"),
        P("head", None),
        P(),
        P(),
        P(),
        P(None, "head"),
        P(None, "head"),
        P(None, "head"),
        P("dp", None, "head"),
        P("head"),
        P("head"),
        P("head", "dp"),
        P(),
        P(),
        P(),
        P("dp", "head"),
        P("head"),
        P(("head", "dp"), None),
        P(),
        P(),
        P(),
        P(None, "head"),
        P(None, "head"),
        P(None, "head"),
    )
    return jax.shard_map(local, mesh=mesh, in_specs=in_specs, out_specs=out_specs, check_vma=False)
```

```python
import functools
import jax
import jax.numpy as jnp
from jax import lax
from jax.experimental import pallas as pl
from jax.sharding import PartitionSpec as P
from jax.experimental.pallas import tpu as pltpu

F32, BF16, I32 = jnp.float32, jnp.bfloat16, jnp.int32
SCALE_BITS = 27
STEP = 2.0**11
VM = 56 * 2**20
SAME = 2**17


def encode(buckets, same):
    seq, hor, ver = buckets
    return seq + 32 * hor + 2048 * ver + jnp.where(same, SAME, 0)


def buckets_of(code):
    return code & 31, (code >> 5) & 63, (code >> 11) & 63


def dot_nt(a, b):
    return lax.dot_general(a, b, (((1,), (1,)), ((), ())), preferred_element_type=F32)


def dot_tn(a, b):
    return lax.dot_general(a, b, (((0,), (0,)), ((), ())), preferred_element_type=F32)


def dot_general_t(w, x):
    return lax.dot_general(w, x, (((0,), (1,)), ((), ())), preferred_element_type=F32)


def dot_tt(a, b):
    return lax.dot_general(a, b, (((0,), (1,)), ((), ())), preferred_element_type=F32)


def dot_nn(a, b):
    return lax.dot_general(a, b, (((1,), (0,)), ((), ())), preferred_element_type=F32)


def split_pair(x):
    lane = lax.broadcasted_iota(I32, x.shape, 1)
    zero = jnp.zeros_like(x)
    return jnp.concatenate([jnp.where(lane < 64, x, zero), jnp.where(lane < 64, zero, x)], axis=0)


def partner(axis, bit):
    i = lax.axis_index(axis)
    low = lax.rem(lax.div(i, bit), 2)
    return {axis: i + bit * (1 - 2 * low)}


def dp_bit(bit):
    return lax.rem(lax.div(lax.axis_index("dp"), bit), 2)


def greet(partners):
    barrier = pltpu.get_barrier_semaphore()
    for p in partners:
        pl.semaphore_signal(barrier, inc=1, device_id=p, device_id_type=pl.DeviceIdType.MESH)
    pl.semaphore_wait(barrier, len(partners))


def remote(src, dst, send, recv, to):
    return pltpu.make_async_remote_copy(
        src_ref=src,
        dst_ref=dst,
        send_sem=send,
        recv_sem=recv,
        device_id=to,
        device_id_type=pl.DeviceIdType.MESH,
    )


def fetch_hops(weights, others, send, recv):
    hops = [[], [], []]
    for n, (w, o) in enumerate(zip(weights, others)):
        rows = w.shape[0] // 4
        quarter = 2 * dp_bit(1) + dp_bit(2)
        one = pl.ds(pl.multiple_of(quarter * rows, rows), rows)
        two = pl.ds(pl.multiple_of(dp_bit(1) * (2 * rows), 2 * rows), 2 * rows)
        hops[0].append(remote(w.at[one], o.at[one], send.at[n, 0], recv.at[n, 0], partner("head", 1)))
        hops[1].append(remote(o.at[one], o.at[one], send.at[n, 1], recv.at[n, 1], partner("dp", 2)))
        hops[2].append(remote(o.at[two], o.at[two], send.at[n, 2], recv.at[n, 2], partner("dp", 1)))
    return hops


def fwd_kernel(*refs, pairs, qb, n_fetch, steps):
    code, tab, q, kt, v = refs[:5]
    weights = refs[5 : 5 + n_fetch]
    p_out, c_out = refs[5 + n_fetch : 7 + n_fetch]
    others = refs[7 + n_fetch : 7 + 2 * n_fetch]
    b_ref, send, recv = refs[7 + 2 * n_fetch :]
    keys = v.shape[0]
    chunk = 128
    step = pl.program_id(0)
    hops = fetch_hops(weights, others, send, recv)
    at = [0, steps // 2, (3 * steps) // 4]

    @pl.when(step == 0)
    def _():
        greet([partner("head", 1), partner("dp", 2), partner("dp", 1)])
        for copy in hops[0]:
            copy.start()

    for hop in (1, 2):

        @pl.when(step == at[hop])
        def _():
            for before, copy in zip(hops[hop - 1], hops[hop]):
                before.wait_recv()
                copy.start()

    tbs = [jnp.broadcast_to(tab[i : i + 1, :], (8, chunk)) for i in range(3 * pairs)]

    def gather(r, _):
        rs = pl.ds(pl.multiple_of(r * 8, 8), 8)
        for c in range(keys // chunk):
            ls = slice(c * chunk, (c + 1) * chunk)
            sums = [None] * pairs
            for t, idx in enumerate(buckets_of(code[rs, ls])):
                for j in range(pairs):
                    g = jnp.take_along_axis(tbs[3 * j + t], idx, axis=1, mode="promise_in_bounds")
                    sums[j] = g if t == 0 else sums[j] + g
            for j in range(pairs):
                b_ref[j, rs, ls] = sums[j]
        return 0

    lax.fori_loop(0, qb // 8, gather, 0)
    same = code[...] >= SAME
    for j in range(pairs):
        lanes = slice(j * 128, (j + 1) * 128)
        q2 = split_pair(q[:, lanes])
        s2 = dot_nn(q2, kt[lanes, :])
        bias = b_ref[j]
        for g in range(2):
            x = s2[g * qb : (g + 1) * qb] + (bias << 16 if g else bias).astype(F32)
            x = jnp.where(same, x, -1e30)
            top = jnp.max(x, axis=1, keepdims=True)
            e = jnp.exp2((x - top) * (1.4426950408889634 * 2.0**-SCALE_BITS))
            inv = 1.0 / jnp.sum(e, axis=1, keepdims=True)
            p_out[2 * j + g] = (e * inv).astype(BF16)
        c0 = dot_nn(p_out[2 * j], v[:, lanes])
        c1 = dot_nn(p_out[2 * j + 1], v[:, lanes])
        lane = lax.broadcasted_iota(I32, c0.shape, 1)
        c_out[:, lanes] = jnp.where(lane < 64, c0, c1).astype(BF16)

    @pl.when(step == steps - 1)
    def _():
        for copy in hops[2]:
            copy.wait_recv()
        for hop in hops:
            for copy in hop:
                copy.wait_send()


def attend_fwd(code, tab, q, kt, v, weights, collective_id, qb=128):
    nq, width = q.shape
    keys = v.shape[0]
    pairs = width // 128
    n = len(weights)
    steps = nq // qb
    full = lambda a: pl.BlockSpec(a.shape, lambda i: (0,) * a.ndim)
    anywhere = pl.BlockSpec(memory_space=pl.ANY)
    return pl.pallas_call(
        functools.partial(fwd_kernel, pairs=pairs, qb=qb, n_fetch=n, steps=steps),
        out_shape=(
            jax.ShapeDtypeStruct((2 * pairs, nq, keys), BF16),
            jax.ShapeDtypeStruct((nq, width), BF16),
        )
        + tuple(jax.ShapeDtypeStruct(w.shape, w.dtype) for w in weights),
        grid=(steps,),
        in_specs=[
            pl.BlockSpec((qb, keys), lambda i: (i, 0)),
            full(tab),
            pl.BlockSpec((qb, width), lambda i: (i, 0)),
            full(kt),
            full(v),
        ]
        + [anywhere] * n,
        out_specs=(
            pl.BlockSpec((2 * pairs, qb, keys), lambda i: (0, i, 0)),
            pl.BlockSpec((qb, width), lambda i: (i, 0)),
        )
        + (anywhere,) * n,
        scratch_shapes=[
            pltpu.VMEM((pairs, qb, keys), I32),
            pltpu.SemaphoreType.DMA((n, 3)),
            pltpu.SemaphoreType.DMA((n, 3)),
        ],
        compiler_params=pltpu.CompilerParams(
            vmem_limit_bytes=VM, collective_id=collective_id, has_side_effects=True
        ),
        cost_estimate=pl.CostEstimate(
            flops=4 * nq * keys * width, bytes_accessed=90 * 2**20, transcendentals=nq * keys * 2 * pairs
        ),
    )(code, tab, q, kt, v, *weights)


def bwd_kernel(q, k, vt, do, p, ds_out, dq_out, dk_out, dv_out, *, pairs, qb):
    keys = k.shape[0]

    @pl.when(pl.program_id(0) == 0)
    def _():
        dk_out[...] = jnp.zeros_like(dk_out)
        dv_out[...] = jnp.zeros_like(dv_out)

    for j in range(pairs):
        lanes = slice(j * 128, (j + 1) * 128)
        q2 = split_pair(q[:, lanes])
        do2 = split_pair(do[:, lanes])
        dp2 = dot_nn(do2, vt[lanes, :])

        for g in range(2):
            ps = p[2 * j + g].astype(F32)
            ts = ps * dp2[g * qb : (g + 1) * qb]
            inner = jnp.sum(ts, axis=1, keepdims=True)
            ds_out[2 * j + g] = (ts - ps * inner).astype(BF16)
        d0 = dot_nn(ds_out[2 * j], k[:, lanes])
        d1 = dot_nn(ds_out[2 * j + 1], k[:, lanes])
        lane = lax.broadcasted_iota(I32, d0.shape, 1)
        dq_out[:, lanes] = jnp.where(lane < 64, d0, d1).astype(BF16) * jnp.array(0.125, BF16)
        ds2 = ds_out[2 * j : 2 * j + 2].reshape(2 * qb, keys)
        p2 = p[2 * j : 2 * j + 2].reshape(2 * qb, keys)
        dk_out[lanes, :] += dot_tn(q2, ds2)
        dv_out[lanes, :] += dot_tn(do2, p2)


def attend_bwd(q, k, vt, do, p, qb=128):
    nq, width = q.shape
    keys = k.shape[0]
    pairs = width // 128
    full = lambda a: pl.BlockSpec(a.shape, lambda i: (0,) * a.ndim)
    row = pl.BlockSpec((qb, width), lambda i: (i, 0))
    big = pl.BlockSpec((2 * pairs, qb, keys), lambda i: (0, i, 0))
    acc = pl.BlockSpec((width, keys), lambda i: (0, 0))
    return pl.pallas_call(
        functools.partial(bwd_kernel, pairs=pairs, qb=qb),
        out_shape=(
            jax.ShapeDtypeStruct((2 * pairs, nq, keys), BF16),
            jax.ShapeDtypeStruct((nq, width), BF16),
            jax.ShapeDtypeStruct((width, keys), F32),
            jax.ShapeDtypeStruct((width, keys), F32),
        ),
        grid=(nq // qb,),
        in_specs=[row, full(k), full(vt), row, big],
        out_specs=(big, row, acc, acc),
        compiler_params=pltpu.CompilerParams(vmem_limit_bytes=VM),
        cost_estimate=pl.CostEstimate(
            flops=8 * nq * keys * width, bytes_accessed=30 * 2**20, transcendentals=0
        ),
    )(q, k, vt, do, p)


def hist_kernel(code, dsa, dsb, seq_out, hor_out, ver_out, *, qb, bits):
    outs = (seq_out, hor_out, ver_out)
    heads = dsa.shape[0]

    @pl.when(pl.program_id(0) == 0)
    def _():
        for o in outs:
            o[...] = jnp.zeros_like(o)

    def rows(r, _):
        rs = pl.ds(pl.multiple_of(r * 16, 16), 16)
        dfull = [d[h, rs, :].astype(F32) for d in (dsa, dsb) for h in range(heads)]
        for half in range(2):
            d8 = [d[half * 8 : half * 8 + 8] for d in dfull]
            packed = code[pl.ds(pl.multiple_of(r * 16 + half * 8, 8), 8), :]
            low = 0
            for t in range(3):
                signs = [(((packed << (31 - low - i)) >> 31) | 1).astype(F32) for i in range(bits[t])]
                low += bits[t]
                rhs = jnp.concatenate(
                    [jnp.concatenate([d, d * signs[0]], axis=0).astype(BF16) for d in d8], axis=0
                )
                first = jnp.concatenate([jnp.ones_like(signs[1]), signs[1]], axis=0).astype(BF16)
                tiles = [first]
                for i in range(2, bits[t]):
                    s2 = jnp.concatenate([signs[i], signs[i]], axis=0).astype(BF16)
                    tiles = tiles + [x * s2 for x in tiles]
                lhs = jnp.concatenate(tiles, axis=0)
                outs[t][...] += dot_nt(lhs, rhs)
        return 0

    lax.fori_loop(0, qb // 16, rows, 0)


def hist(code, dsa, dsb, bits, qb=128):
    nq, keys = dsa.shape[1], dsa.shape[2]
    nh = dsa.shape[0] + dsb.shape[0]
    shapes = [(2 ** (b - 1) * 8, nh * 16) for b in bits]
    return pl.pallas_call(
        functools.partial(hist_kernel, qb=qb, bits=bits),
        out_shape=tuple(jax.ShapeDtypeStruct(s, F32) for s in shapes),
        grid=(nq // qb,),
        in_specs=[pl.BlockSpec((qb, keys), lambda i: (i, 0))]
        + [pl.BlockSpec((d.shape[0], qb, keys), lambda i: (0, i, 0)) for d in (dsa, dsb)],
        out_specs=tuple(pl.BlockSpec(s, lambda i: (0, 0)) for s in shapes),
        compiler_params=pltpu.CompilerParams(vmem_limit_bytes=VM),
        cost_estimate=pl.CostEstimate(
            flops=2 * nq * keys * 160 * nh * 8, bytes_accessed=110 * 2**20, transcendentals=0
        ),
    )(code, dsa, dsb)


def unhist(acc, bits, nh):
    n = 2**bits
    a = acc.reshape(n // 2, 8, nh, 2, 8)
    m = jnp.einsum("fqhvq->fhv", a)
    b = jnp.arange(n)
    sign = lambda i: 1.0 - 2.0 * ((b >> i) & 1).astype(F32)
    tiles = [jnp.stack([jnp.ones((n,), F32), sign(1)])]
    for i in range(2, bits):
        tiles = tiles + [x * sign(i)[None] for x in tiles]
    lhs = jnp.concatenate(tiles)
    var = jnp.stack([jnp.ones((n,), F32), sign(0)])
    return jnp.einsum("fhv,fb,vb->bh", m, lhs, var, precision=lax.Precision.HIGHEST) / n


def pack_tables(tables):
    rows = [jnp.pad(t.astype(F32).T, ((0, 0), (0, 128 - t.shape[0]))) for t in tables]
    fixed = jnp.round(jnp.stack(rows, axis=1) * STEP).astype(I32)
    fixed = fixed.reshape(fixed.shape[0] // 2, 2, 3, 128)
    return (fixed[:, 0] * 65536 + fixed[:, 1]).reshape(-1, 128)


norm_epsilon = 1e-05


def mm(a, b):
    return jnp.dot(a, b, preferred_element_type=F32)


def normalize(value):
    center = value - jnp.mean(value, axis=-1, keepdims=True)
    spread = jnp.mean(center * center, axis=-1, keepdims=True)
    root = lax.rsqrt(spread + norm_epsilon)
    return center * root, root


def normalize_back(grad, normed, root):
    return root * (
        grad
        - jnp.mean(grad, axis=-1, keepdims=True)
        - normed * jnp.mean(grad * normed, axis=-1, keepdims=True)
    )


def gelu_parts(u):
    t = 1.0 / (1.0 + (0.3275911 * 0.7071067811865476) * jnp.abs(u))
    e = jnp.exp(-0.5 * u * u)
    poly = t * (
        0.254829592 + t * (-0.284496736 + t * (1.421413741 + t * (-1.453152027 + t * 1.061405429)))
    )
    tail = 0.5 * e * poly
    below = jnp.where(u >= 0, 1.0 - tail, tail)
    return u * below, below + u * (e * 0.3989422804014327)


def swap_dp(x, bit):
    n = lax.axis_size("dp")
    return lax.ppermute(x, "dp", [(i, i ^ bit) for i in range(n)])


def swap_head(x):
    return lax.ppermute(x, "head", [(0, 1), (1, 0)])


def dp_bits():
    n, bit, out = lax.axis_size("dp"), 1, []
    while bit < n:
        out.append(bit)
        bit *= 2
    return out


def bit_of(bit):
    return (lax.axis_index("dp") // bit) % 2


def in_order(first, mine, theirs):
    low = jnp.where(first == 0, mine, theirs)
    high = jnp.where(first == 0, theirs, mine)
    return jnp.concatenate([low, high], axis=0)


def rows_of(x, index, rows):
    return lax.dynamic_slice_in_dim(x, index * rows, rows, 0)


def halve(g, bit):
    rows = g.shape[0] // 2
    b = bit_of(bit)
    got = swap_dp(rows_of(g, 1 - b, rows), bit)
    return (rows_of(g, b, rows).astype(F32) + got.astype(F32)).astype(BF16)


def reduce_grad(own, other, head_first):
    bits = dp_bits()
    own, other = halve(own, 1), halve(other, 1)
    if not head_first:
        own, other = halve(own, 2), halve(other, 2)
    g = (own.astype(F32) + swap_head(other).astype(F32)).astype(BF16)
    for bit in bits[1 if head_first else 2 :]:
        g = halve(g, bit)
    for bit in reversed(bits):
        g = in_order(bit_of(bit), g, swap_dp(g, bit))
    return g.astype(F32)


def local(
    tokens,
    cotangent,
    form_number,
    sequence_bucket,
    horizontal_bucket,
    vertical_bucket,
    project_weight,
    query_bias,
    value_bias,
    output_weight,
    output_bias,
    first_gain,
    first_shift,
    up_weight,
    up_bias,
    down_weight,
    down_bias,
    second_gain,
    second_shift,
    sequence_table,
    horizontal_table,
    vertical_table,
    project_weight_average,
    query_bias_average,
    value_bias_average,
    output_weight_average,
    output_bias_average,
    first_gain_average,
    first_shift_average,
    up_weight_average,
    up_bias_average,
    down_weight_average,
    down_bias_average,
    second_gain_average,
    second_shift_average,
    sequence_table_average,
    horizontal_table_average,
    vertical_table_average,
):
    total_rows, model_width = tokens.shape
    local_width = project_weight.shape[2]
    local_heads = sequence_table.shape[1]
    hidden = up_weight.shape[1]
    share_rows = total_rows // lax.axis_size("head")
    head_index = lax.axis_index("head")
    share_start = head_index * share_rows
    block_rows = 128
    buckets = (sequence_bucket, horizontal_bucket, vertical_bucket)
    tables = (sequence_table, horizontal_table, vertical_table)
    bits = tuple((t.shape[0] - 1).bit_length() for t in tables)
    flat_project = project_weight.reshape(model_width, 3 * local_width)

    small = jnp.concatenate(
        [query_bias, value_bias, up_bias] + [t.reshape(-1) for t in tables]
    ).reshape(1, -1)
    small_other = swap_head(small)[0]
    cuts = [local_width, 2 * local_width, 2 * local_width + hidden]
    for t in tables:
        cuts.append(cuts[-1] + t.size)
    other_tables = tuple(
        small_other[cuts[2 + i] : cuts[3 + i]].reshape(t.shape) for i, t in enumerate(tables)
    )
    query_biases = (query_bias, small_other[: cuts[0]])
    value_biases = (value_bias, small_other[cuts[0] : cuts[1]])
    up_biases = (up_bias, small_other[cuts[1] : cuts[2]])
    packed_tables = (pack_tables(tables), pack_tables(other_tables))
    project_weights = [flat_project]
    output_weights, up_weights, down_weights = [output_weight], [up_weight], [down_weight]

    form_row = form_number.reshape(total_rows)
    form_own = lax.dynamic_slice_in_dim(form_row, share_start, share_rows, 0)
    code = encode(
        [rows_of(b, head_index, share_rows) for b in buckets], form_own[:, None] == form_row[None, :]
    )
    own_tokens = rows_of(tokens, head_index, share_rows)

    scaled, keys, values_t, probs, contexts = [], [], [], [], []
    for s in range(2):
        wq = project_weights[s][:, :local_width]
        wk = project_weights[s][:, local_width : 2 * local_width]
        wv = project_weights[s][:, 2 * local_width :]
        bv = value_biases[s].astype(F32)
        q = ((mm(own_tokens, wq) + query_biases[s].astype(F32)) * 0.125).astype(BF16)
        q = q * jnp.array(2.0**SCALE_BITS, BF16)
        k = mm(tokens, wk).astype(BF16)
        kt = dot_general_t(wk, tokens).astype(BF16)
        v = (mm(tokens, wv) + bv).astype(BF16)
        vt = (dot_general_t(wv, tokens) + bv[:, None]).astype(BF16)
        fetch = (output_weight, up_weight, down_weight) if s else (flat_project,)
        p, context, *fetched = attend_fwd(
            code, packed_tables[s], q, kt, v, fetch, s, qb=block_rows
        )
        if s:
            output_weights.append(fetched[0])
            up_weights.append(fetched[1])
            down_weights.append(fetched[2])
        else:
            project_weights.append(fetched[0])
        scaled.append(q)
        keys.append(k)
        values_t.append(vt)
        probs.append(p)
        contexts.append(context)
    attend = output_bias.astype(F32) + sum(mm(contexts[s], output_weights[s]) for s in range(2))
    n1, root1 = normalize(own_tokens.astype(F32) + attend)
    normed = n1 * first_gain.astype(F32) + first_shift.astype(F32)
    normed_low = normed.astype(BF16)
    feed = down_bias.astype(F32)
    acts, slopes = [], []
    for s in range(2):
        up = mm(normed_low, up_weights[s]) + up_biases[s].astype(F32)
        act, slope = gelu_parts(up)
        act = act.astype(BF16)
        feed = feed + mm(act, down_weights[s])
        acts.append(act)
        slopes.append(slope.astype(BF16))
    n2, root2 = normalize(normed + feed)
    layer_output = n2 * second_gain.astype(F32) + second_shift.astype(F32)

    cot = cotangent.astype(F32)
    back_second = normalize_back(cot * second_gain.astype(F32), n2, root2)
    second_gain_part = jnp.sum(cot * n2, axis=0)
    second_shift_part = jnp.sum(cot, axis=0)
    back_feed = back_second.astype(BF16)
    down_bias_part = jnp.sum(back_feed.astype(F32), axis=0)
    back_normed = back_second
    up_bias_parts, down_grads, up_grads = [], [], []
    for s in range(2):
        down_grads.append(dot_tn(acts[s], back_feed).astype(BF16))
        back_up = (dot_nt(back_feed, down_weights[s]) * slopes[s].astype(F32)).astype(BF16)
        up_bias_parts.append(jnp.sum(back_up.astype(F32), axis=0))
        up_grads.append(dot_tn(normed_low, back_up).astype(BF16))
        back_normed = back_normed + dot_nt(back_up, up_weights[s])
    down_total = reduce_grad(down_grads[0], down_grads[1], True)
    up_total = reduce_grad(up_grads[0], up_grads[1], False)
    first_gain_part = jnp.sum(back_normed * n1, axis=0)
    first_shift_part = jnp.sum(back_normed, axis=0)
    back_first = normalize_back(back_normed * first_gain.astype(F32), n1, root1)
    back_attend = back_first.astype(BF16)
    output_bias_part = jnp.sum(back_attend.astype(F32), axis=0)
    output_grads = [dot_tn(contexts[s], back_attend).astype(BF16) for s in range(2)]
    output_total = reduce_grad(output_grads[0], output_grads[1], True)

    tokens_part = back_first
    other_part = jnp.zeros((share_rows, model_width), F32)
    back_scores, project_grads, query_bias_parts, value_bias_parts = [], [], [], []
    for s in range(2):
        wq = project_weights[s][:, :local_width]
        wk = project_weights[s][:, local_width : 2 * local_width]
        wv = project_weights[s][:, 2 * local_width :]
        back_context = dot_nt(back_attend, output_weights[s]).astype(BF16)
        ds, dq, dkt, dvt = attend_bwd(
            scaled[s], keys[s], values_t[s], back_context, probs[s], qb=block_rows
        )
        dkt = (dkt * 2.0**-SCALE_BITS).astype(BF16)
        dvt = dvt.astype(BF16)
        back_scores.append(ds)
        query_bias_parts.append(jnp.sum(dq.astype(F32), axis=0))
        value_bias_parts.append(jnp.sum(dvt.astype(F32), axis=1))
        project_grads.append(
            jnp.concatenate(
                [dot_tn(own_tokens, dq), dot_tt(tokens, dkt), dot_tt(tokens, dvt)], axis=1
            ).astype(BF16)
        )
        tokens_part = tokens_part + dot_nt(dq, wq)
        for grad, weight in ((dkt, wk), (dvt, wv)):
            own = lax.dynamic_slice_in_dim(grad, share_start, share_rows, 1)
            far = lax.dynamic_slice_in_dim(grad, (1 - head_index) * share_rows, share_rows, 1)
            tokens_part = tokens_part + dot_tt(own, weight)
            other_part = other_part + dot_tt(far, weight)
    tokens_gradient = tokens_part + swap_head(other_part.astype(BF16)).astype(F32)
    project_total = reduce_grad(project_grads[0], project_grads[1], True).reshape(
        model_width, 3, local_width
    )
    counts = hist(code, back_scores[0], back_scores[1], bits, qb=block_rows)
    table_parts = [unhist(a, b, 2 * local_heads) for a, b in zip(counts, bits)]

    common = [
        first_gain_part,
        first_shift_part,
        second_gain_part,
        second_shift_part,
        output_bias_part,
        down_bias_part,
    ]
    halves = [
        [query_bias_parts[s], value_bias_parts[s], up_bias_parts[s]]
        + [t[:, s * local_heads : (s + 1) * local_heads].reshape(-1) for t in table_parts]
        for s in range(2)
    ]
    sizes = [a.size for a in common + halves[0]]
    padding = -sum(sizes) % 1024
    mine = jnp.concatenate(common + halves[0] + [jnp.zeros((padding,), F32)]).reshape(-1, 128)
    theirs = jnp.concatenate(common + halves[1] + [jnp.zeros((padding,), F32)]).reshape(-1, 128)
    sums = mine + swap_head(theirs)
    for bit in dp_bits():
        sums = sums + swap_dp(sums, bit)
    sums = sums.reshape(-1)
    totals, at = [], 0
    for size in sizes:
        totals.append(sums[at : at + size])
        at += size
    (
        first_gain_total,
        first_shift_total,
        second_gain_total,
        second_shift_total,
        output_bias_total,
        down_bias_total,
        query_bias_total,
        value_bias_total,
        up_bias_total,
        sequence_total,
        horizontal_total,
        vertical_total,
    ) = totals
    sequence_total = sequence_total.reshape(sequence_table.shape)
    horizontal_total = horizontal_total.reshape(horizontal_table.shape)
    vertical_total = vertical_total.reshape(vertical_table.shape)
    up_weight_total, down_weight_total, output_weight_total = up_total, down_total, output_total
    token_count = total_rows * lax.axis_size("dp")
    group_count = lax.axis_size("dp")
    group_index = lax.axis_index("dp")

    def renew(average, weight, gradient):
        return 0.5 * average + 0.5 * (weight.astype(jnp.float32) - gradient / token_count)

    def part_of(array, along):
        width = array.shape[along] // group_count
        return lax.dynamic_slice_in_dim(array, group_index * width, width, along)

    return (
        layer_output,
        tokens_gradient,
        project_total,
        query_bias_total,
        value_bias_total,
        output_weight_total,
        output_bias_total,
        first_gain_total,
        first_shift_total,
        up_weight_total,
        up_bias_total,
        down_weight_total,
        down_bias_total,
        second_gain_total,
        second_shift_total,
        sequence_total,
        horizontal_total,
        vertical_total,
        renew(project_weight_average, part_of(project_weight, 0), part_of(project_total, 0)),
        renew(query_bias_average, query_bias, query_bias_total),
        renew(value_bias_average, value_bias, value_bias_total),
        renew(output_weight_average, part_of(output_weight, 1), part_of(output_weight_total, 1)),
        renew(output_bias_average, output_bias, output_bias_total),
        renew(first_gain_average, first_gain, first_gain_total),
        renew(first_shift_average, first_shift, first_shift_total),
        renew(up_weight_average, part_of(up_weight, 0), part_of(up_weight_total, 0)),
        renew(up_bias_average, up_bias, up_bias_total),
        renew(down_weight_average, part_of(down_weight, 0), part_of(down_weight_total, 0)),
        renew(down_bias_average, down_bias, down_bias_total),
        renew(second_gain_average, second_gain, second_gain_total),
        renew(second_shift_average, second_shift, second_shift_total),
        renew(sequence_table_average, sequence_table, sequence_total),
        renew(horizontal_table_average, horizontal_table, horizontal_total),
        renew(vertical_table_average, vertical_table, vertical_total),
    )


def solution(mesh):
    in_specs = (
        P("dp", None),
        P(("dp", "head"), None),
        P("dp", None),
        P("dp", None),
        P("dp", None),
        P("dp", None),
        P(None, None, "head"),
        P("head"),
        P("head"),
        P("head", None),
        P(),
        P(),
        P(),
        P(None, "head"),
        P("head"),
        P("head", None),
        P(),
        P(),
        P(),
        P(None, "head"),
        P(None, "head"),
        P(None, "head"),
        P("dp", None, "head"),
        P("head"),
        P("head"),
        P("head", "dp"),
        P(),
        P(),
        P(),
        P("dp", "head"),
        P("head"),
        P(("head", "dp"), None),
        P(),
        P(),
        P(),
        P(None, "head"),
        P(None, "head"),
        P(None, "head"),
    )
    out_specs = (
        P(("dp", "head"), None),
        P(("dp", "head"), None),
        P(None, None, "head"),
        P("head"),
        P("head"),
        P("head", None),
        P(),
        P(),
        P(),
        P(None, "head"),
        P("head"),
        P("head", None),
        P(),
        P(),
        P(),
        P(None, "head"),
        P(None, "head"),
        P(None, "head"),
        P("dp", None, "head"),
        P("head"),
        P("head"),
        P("head", "dp"),
        P(),
        P(),
        P(),
        P("dp", "head"),
        P("head"),
        P(("head", "dp"), None),
        P(),
        P(),
        P(),
        P(None, "head"),
        P(None, "head"),
        P(None, "head"),
    )
    return jax.shard_map(local, mesh=mesh, in_specs=in_specs, out_specs=out_specs, check_vma=False)
```

```python
import functools
import jax
import jax.numpy as jnp
from jax import lax
from jax.experimental import pallas as pl
from jax.sharding import PartitionSpec as P
from jax.experimental.pallas import tpu as pltpu

F32, BF16, I32 = jnp.float32, jnp.bfloat16, jnp.int32
SCALE_BITS = 27
STEP = 2.0**11
VM = 56 * 2**20
BACK_VM = 60 * 2**20
SAME = 2**17


def encode(buckets, same):
    seq, hor, ver = buckets
    return seq + 32 * hor + 2048 * ver + jnp.where(same, SAME, 0)


def buckets_of(code):
    return code & 31, (code >> 5) & 63, (code >> 11) & 63


def dot_nt(a, b):
    return lax.dot_general(a, b, (((1,), (1,)), ((), ())), preferred_element_type=F32)


def dot_tn(a, b):
    return lax.dot_general(a, b, (((0,), (0,)), ((), ())), preferred_element_type=F32)


def dot_general_t(w, x):
    return lax.dot_general(w, x, (((0,), (1,)), ((), ())), preferred_element_type=F32)


def dot_tt(a, b):
    return lax.dot_general(a, b, (((0,), (1,)), ((), ())), preferred_element_type=F32)


def dot_nn(a, b):
    return lax.dot_general(a, b, (((1,), (0,)), ((), ())), preferred_element_type=F32)


def split_pair(x):
    lane = lax.broadcasted_iota(I32, x.shape, 1)
    zero = jnp.zeros_like(x)
    return jnp.concatenate([jnp.where(lane < 64, x, zero), jnp.where(lane < 64, zero, x)], axis=0)


def partner(axis, bit):
    i = lax.axis_index(axis)
    low = lax.rem(lax.div(i, bit), 2)
    return {axis: i + bit * (1 - 2 * low)}


def dp_bit(bit):
    return lax.rem(lax.div(lax.axis_index("dp"), bit), 2)


def greet(partners):
    barrier = pltpu.get_barrier_semaphore()
    for p in partners:
        pl.semaphore_signal(barrier, inc=1, device_id=p, device_id_type=pl.DeviceIdType.MESH)
    pl.semaphore_wait(barrier, len(partners))


def remote(src, dst, send, recv, to):
    return pltpu.make_async_remote_copy(
        src_ref=src,
        dst_ref=dst,
        send_sem=send,
        recv_sem=recv,
        device_id=to,
        device_id_type=pl.DeviceIdType.MESH,
    )


def fetch_copies(mode, source, out, send, recv):
    if mode == "small":
        return [remote(source, out, send.at[0], recv.at[0], partner("head", 1)), None, None], []
    rows = source.shape[0] if mode == "rest" else source.shape[0] // 4
    quarter = 2 * dp_bit(1) + dp_bit(2)
    one = pl.ds(pl.multiple_of(quarter * rows, rows), rows)
    two = pl.ds(pl.multiple_of(dp_bit(1) * (2 * rows), 2 * rows), 2 * rows)
    hops, local = [None, None, None], []
    if mode == "first":
        hops[0] = remote(source.at[one], out, send.at[0], recv.at[0], partner("head", 1))
    else:
        if mode == "all":
            hops[0] = remote(source.at[one], out.at[one], send.at[0], recv.at[0], partner("head", 1))
            quarter_ref = out.at[one]
        else:
            quarter_ref = source
            local.append(pltpu.make_async_copy(source, out.at[one], send.at[0]))
        hops[1] = remote(quarter_ref, out.at[one], send.at[1], recv.at[1], partner("dp", 2))
        hops[2] = remote(out.at[two], out.at[two], send.at[2], recv.at[2], partner("dp", 1))
    return hops, local


def fetched_shape(mode, w):
    rows = {"all": 1, "small": 1, "first": 0.25, "rest": 4}[mode] * w.shape[0]
    return jax.ShapeDtypeStruct((int(rows), w.shape[1]), w.dtype)


def fwd_kernel(*refs, pairs, qb, modes, points, steps):
    n = len(modes)
    code, tab, q, kt, v = refs[:5]
    sources = refs[5 : 5 + n]
    p_out, c_out = refs[5 + n : 7 + n]
    outs = refs[7 + n : 7 + 2 * n]
    b_ref, t_ref, send, recv = refs[7 + 2 * n :]
    keys = v.shape[0]
    chunk = 128
    step = pl.program_id(0)
    hops, local = [], []
    for i in range(n):
        h, l = fetch_copies(modes[i], sources[i], outs[i], send.at[i], recv.at[i])
        hops.append(h)
        local += l

    def point(now):
        for i in range(n):
            for hop in range(3):
                if points[i][hop] == now:
                    if hop and hops[i][hop - 1] is not None:
                        hops[i][hop - 1].wait_recv()
                    hops[i][hop].start()

    @pl.when(step == 0)
    def _():
        greet([partner("head", 1), partner("dp", 2), partner("dp", 1)])
        for copy in local:
            copy.start()
        for j in range(pairs):
            for t in range(3):
                ls = slice(t * chunk, (t + 1) * chunk)
                fixed = [jnp.round(tab[2 * j + g : 2 * j + g + 1, ls] * STEP).astype(I32) for g in range(2)]
                t_ref[8 * (3 * j + t) : 8 * (3 * j + t) + 8, :] = jnp.broadcast_to(
                    fixed[0] * 65536 + fixed[1], (8, chunk)
                )
        point(0)

    for now in sorted(set(sum(points, ()))):
        if 0 < now < 2 * steps and now % 2 == 0:

            @pl.when(step == now // 2)
            def _():
                if local and now == min(p[2] for p, m in zip(points, modes) if m == "rest"):
                    for copy in local:
                        copy.wait()
                point(now)

    tbs = [t_ref[8 * i : 8 * i + 8, :] for i in range(3 * pairs)]

    def gather(r, _):
        rs = pl.ds(pl.multiple_of(r * 8, 8), 8)
        for c in range(keys // chunk):
            ls = slice(c * chunk, (c + 1) * chunk)
            sums = [None] * pairs
            for t, idx in enumerate(buckets_of(code[rs, ls])):
                for j in range(pairs):
                    g = jnp.take_along_axis(tbs[3 * j + t], idx, axis=1, mode="promise_in_bounds")
                    sums[j] = g if t == 0 else sums[j] + g
            for j in range(pairs):
                b_ref[j, rs, ls] = sums[j]
        return 0

    lax.fori_loop(0, qb // 8, gather, 0)
    for now in sorted(set(sum(points, ()))):
        if 0 < now < 2 * steps and now % 2 == 1:

            @pl.when(step == now // 2)
            def _():
                point(now)

    same = code[...] >= SAME
    for j in range(pairs):
        lanes = slice(j * 128, (j + 1) * 128)
        q2 = split_pair(q[:, lanes])
        s2 = dot_nn(q2, kt[lanes, :])
        bias = b_ref[j]
        for g in range(2):
            x = s2[g * qb : (g + 1) * qb] + (bias << 16 if g else bias).astype(F32)
            x = jnp.where(same, x, -1e30)
            top = jnp.max(x, axis=1, keepdims=True)
            e = jnp.exp2((x - top) * (1.4426950408889634 * 2.0**-SCALE_BITS))
            inv = 1.0 / jnp.sum(e, axis=1, keepdims=True)
            p_out[2 * j + g] = (e * inv).astype(BF16)
        c0 = dot_nn(p_out[2 * j], v[:, lanes])
        c1 = dot_nn(p_out[2 * j + 1], v[:, lanes])
        lane = lax.broadcasted_iota(I32, c0.shape, 1)
        c_out[:, lanes] = jnp.where(lane < 64, c0, c1).astype(BF16)

    @pl.when(step == steps - 1)
    def _():
        for now in range(2 * steps, max(sum(points, ())) + 1):
            point(now)
        for i in range(n):
            last = [copy for copy in hops[i] if copy is not None][-1]
            last.wait_recv()
        for i in range(n):
            for copy in hops[i]:
                if copy is not None:
                    copy.wait_send()


def attend_fwd(code, tab, q, kt, v, fetch, collective_id, qb=128):
    nq, width = q.shape
    keys = v.shape[0]
    pairs = width // 128
    modes = tuple(f[0] for f in fetch)
    points = tuple(f[1] for f in fetch)
    sources = [f[2] for f in fetch]
    n = len(fetch)
    steps = nq // qb
    full = lambda a: pl.BlockSpec(a.shape, lambda i: (0,) * a.ndim)
    anywhere = pl.BlockSpec(memory_space=pl.ANY)
    return pl.pallas_call(
        functools.partial(fwd_kernel, pairs=pairs, qb=qb, modes=modes, points=points, steps=steps),
        out_shape=(
            jax.ShapeDtypeStruct((2 * pairs, nq, keys), BF16),
            jax.ShapeDtypeStruct((nq, width), BF16),
        )
        + tuple(fetched_shape(m, w) for m, w in zip(modes, sources)),
        grid=(steps,),
        in_specs=[
            pl.BlockSpec((qb, keys), lambda i: (i, 0)),
            full(tab),
            pl.BlockSpec((qb, width), lambda i: (i, 0)),
            full(kt),
            full(v),
        ]
        + [anywhere] * n,
        out_specs=(
            pl.BlockSpec((2 * pairs, qb, keys), lambda i: (0, i, 0)),
            pl.BlockSpec((qb, width), lambda i: (i, 0)),
        )
        + (anywhere,) * n,
        scratch_shapes=[
            pltpu.VMEM((pairs, qb, keys), I32),
            pltpu.VMEM((pairs * 24, 128), I32),
            pltpu.SemaphoreType.DMA((n, 3)),
            pltpu.SemaphoreType.DMA((n, 3)),
        ],
        compiler_params=pltpu.CompilerParams(
            vmem_limit_bytes=VM, collective_id=collective_id, has_side_effects=True
        ),
        cost_estimate=pl.CostEstimate(
            flops=4 * nq * keys * width, bytes_accessed=90 * 2**20, transcendentals=nq * keys * 2 * pairs
        ),
    )(code, tab, q, kt, v, *sources)


def add_rows(dst, a, b, tile):
    rows = dst[2]

    def body(i, _):
        at = lambda x: pl.ds(pl.multiple_of(x[1] + i * tile, 16), tile)
        dst[0][at(dst), :] = a[0][at(a), :] + b[0][at(b), :]
        return 0

    lax.fori_loop(0, rows // tile, body, 0)


STREAM_SEMS = 14


def stream_phases(own, other, kept, piece, full, columns, bufs, send, recv, head_first):
    rows = own.shape[0]
    half, tile = rows // 2, rows // 16
    rc, r1, r2, r3, r4 = bufs
    c, x, z0, z1 = (dp_bit(b) for b in (1, 2, 4, 8))
    part = lambda ref, bit, n: ref.at[pl.ds(pl.multiple_of(bit * n, 16), n)]
    cut = lambda ref, start, n: ref.at[pl.ds(pl.multiple_of(start, 16), n), columns]
    to = [partner("dp", 1), partner("dp", 2), partner("dp", 4), partner("dp", 8), partner("head", 1)]
    hop0 = [
        remote(cut(own, (1 - c) * half, half), rc.at[0], send.at[0], recv.at[0], to[0]),
        remote(cut(other, (1 - c) * half, half), rc.at[1], send.at[1], recv.at[1], to[0]),
    ]
    if head_first:
        hop1 = [remote(rc.at[1], r1, send.at[2], recv.at[2], to[4])]
        hop2 = [remote(part(rc.at[0], 1 - x, half // 2), r2, send.at[4], recv.at[4], to[1])]
    else:
        hop1 = [
            remote(part(rc.at[n], 1 - x, half // 2), r1.at[n], send.at[2 + n], recv.at[2 + n], to[1])
            for n in range(2)
        ]
        hop2 = [remote(r1.at[1], r2, send.at[4], recv.at[4], to[4])]
    hop3 = [remote(part(r2, 1 - z0, half // 4), r3, send.at[5], recv.at[5], to[2])]
    hop4 = [remote(part(r3, 1 - z1, half // 8), r4, send.at[6], recv.at[6], to[3])]
    at_x = c * half + x * (half // 2)
    at_z = at_x + z0 * (half // 4)
    at_end = at_z + z1 * (half // 8)
    there = lambda start, n: full.at[pl.ds(pl.multiple_of(start, 16), n), columns]
    spans = [(at_end, half // 8, 3), (at_z, half // 4, 2), (at_x, half // 2, 1), (c * half, half, 0)]
    hop5 = [remote(piece, there(at_end, half // 8), send.at[7], recv.at[7], to[3])]
    back = [hop5]
    for i, (start, n, which) in enumerate(spans[1:]):
        ref = there(start, n)
        back.append([remote(ref, ref, send.at[8 + i], recv.at[8 + i], to[which])])
    local = [pltpu.make_async_copy(piece, there(at_end, half // 8), send.at[11])]
    keep = []
    if kept is not None:
        keep = [
            pltpu.make_async_copy(cut(g, c * half, half), kept[n], send.at[12 + n])
            for n, g in enumerate((own, other))
        ]

    def start(hop):
        for copy in hop:
            copy.start()

    def arrive(hop):
        for copy in hop:
            copy.wait_recv()

    def phase0():
        start(hop0)
        start(keep)

    def phase1():
        for copy in keep:
            copy.wait()
        arrive(hop0)
        for n, g in enumerate((own, other)):
            mine = (kept[n], 0) if keep else (g, c * half)
            add_rows((rc.at[n], 0, half), (rc.at[n], 0), mine, tile)
        start(hop1)

    def phase2():
        arrive(hop1)
        if head_first:
            add_rows((rc.at[0], 0, half), (rc.at[0], 0), (r1, 0), tile)
        else:
            for n in range(2):
                add_rows((r1.at[n], 0, half // 2), (r1.at[n], 0), (rc.at[n], x * (half // 2)), tile)
        start(hop2)

    def phase3():
        arrive(hop2)
        if head_first:
            add_rows((r2, 0, half // 2), (r2, 0), (rc.at[0], x * (half // 2)), tile)
        else:
            add_rows((r2, 0, half // 2), (r2, 0), (r1.at[0], 0), tile)
        start(hop3)

    def phase4():
        arrive(hop3)
        add_rows((r3, 0, half // 4), (r3, 0), (r2, z0 * (half // 4)), tile)
        start(hop4)

    def phase5():
        arrive(hop4)
        add_rows((piece, 0, half // 8), (r4, 0), (r3, z1 * (half // 8)), tile)
        start(local)
        start(back[0])

    def gather(i):
        def phase():
            if i == 1:
                for copy in local:
                    copy.wait()
            arrive(back[i - 1])
            start(back[i])

        return phase

    def finish():
        arrive(back[3])
        for hop in [hop0, hop1, hop2, hop3, hop4] + back:
            for copy in hop:
                copy.wait_send()

    return [phase0, phase1, phase2, phase3, phase4, phase5, gather(1), gather(2), gather(3), finish]


def stream_scratch(rows, columns, head_first, keep):
    half = rows // 2
    first = (half, columns) if head_first else (2, half // 2, columns)
    shapes = [(2, half, columns), first, (half // 2, columns), (half // 4, columns), (half // 8, columns)]
    shapes.append((half // 8, columns))
    if keep:
        shapes += [(half, columns)] * 2
    return [pltpu.VMEM(s, BF16) for s in shapes] + [pltpu.SemaphoreType.DMA((STREAM_SEMS,))] * 2


def sum_phases(own, other, bufs, send, recv):
    to = [partner("head", 1)] + [partner("dp", b) for b in (1, 2, 4, 8)]
    hops = [
        remote(other if i == 0 else own.at[i - 1], bufs.at[i], send.at[i], recv.at[i], to[i])
        for i in range(5)
    ]

    def phase(i):
        def run():
            if i:
                hops[i - 1].wait_recv()
                if i > 1:
                    own[i - 1] = own[i - 2] + bufs[i - 1]
                else:
                    own[0] = own[5] + bufs[0]
            if i < 5:
                hops[i].start()
            else:
                for copy in hops:
                    copy.wait_send()

        return run

    return [phase(i) for i in range(6)]


def attend_back(q, k, vt, do, p, ds, at, dq, dk, dv, pairs, qb):
    for j in range(pairs):
        lanes = slice(j * 128, (j + 1) * 128)
        q2 = split_pair(q[:, lanes])
        do2 = split_pair(do[:, lanes])
        dp2 = dot_nn(do2, vt[lanes, :])
        parts = []
        for g in range(2):
            ps = p[2 * j + g].astype(F32)
            ts = ps * dp2[g * qb : (g + 1) * qb]
            inner = jnp.sum(ts, axis=1, keepdims=True)
            parts.append((ts - ps * inner).astype(BF16))
            ds[2 * j + g, pl.ds(at, qb), :] = parts[g]
        d0 = dot_nn(parts[0], k[:, lanes])
        d1 = dot_nn(parts[1], k[:, lanes])
        lane = lax.broadcasted_iota(I32, d0.shape, 1)
        dq[pl.ds(at, qb), lanes] = jnp.where(lane < 64, d0, d1).astype(BF16) * jnp.array(0.125, BF16)
        dk[lanes, :] += dot_tn(q2, jnp.concatenate(parts, axis=0))
        dv[lanes, :] += dot_tn(do2, p[2 * j : 2 * j + 2].reshape(2 * qb, p.shape[2]))


def count_rows(code, ds, at, outs, bits, nq):
    heads = ds.shape[0]

    def rows(r, _):
        rs = pl.ds(pl.multiple_of(at + r * 16, 16), 16)
        dfull = [ds[h, rs, :].astype(F32) for h in range(heads)]
        for half in range(2):
            d8 = [d[half * 8 : half * 8 + 8] for d in dfull]
            packed = code[pl.ds(pl.multiple_of(r * 16 + half * 8, 8), 8), :]
            low = 0
            for t in range(3):
                signs = [(((packed << (31 - low - i)) >> 31) | 1).astype(F32) for i in range(bits[t])]
                low += bits[t]
                rhs = jnp.concatenate(
                    [jnp.concatenate([d, d * signs[0]], axis=0).astype(BF16) for d in d8], axis=0
                )
                first = jnp.concatenate([jnp.ones_like(signs[1]), signs[1]], axis=0).astype(BF16)
                tiles = [first]
                for i in range(2, bits[t]):
                    s2 = jnp.concatenate([signs[i], signs[i]], axis=0).astype(BF16)
                    tiles = tiles + [x * s2 for x in tiles]
                outs[t][...] += dot_nt(jnp.concatenate(tiles, axis=0), rhs)
        return 0

    lax.fori_loop(0, nq // 16, rows, 0)


def table_sums(acc, bits, first, heads):
    n = 2**bits
    high = lax.Precision.HIGHEST
    iota = lambda shape, d: lax.broadcasted_iota(I32, shape, d)
    row, col = iota(acc.shape, 0), iota(acc.shape, 1)
    kept = jnp.where((row & 7) == (col & 7), acc, 0.0)
    shape = (n, acc.shape[0])
    odd = (iota(shape, 1) >> 3) & (iota(shape, 0) >> 1)
    odd = odd ^ (odd >> 4)
    odd = odd ^ (odd >> 2)
    odd = odd ^ (odd >> 1)
    left = (1 - 2 * (odd & 1)).astype(F32)
    shape = (n, acc.shape[1])
    odd = iota(shape, 0) & (iota(shape, 1) >> 3) & 1
    mixed = jnp.dot(left, kept, precision=high, preferred_element_type=F32)
    mixed = mixed * (1 - 2 * odd).astype(F32) * (1.0 / n)
    shape = (8, acc.shape[1])
    head = iota(shape, 0)
    pick = ((iota(shape, 1) >> 4) == head + first) & (head < heads)
    return lax.dot_general(
        pick.astype(F32), mixed, (((1,), (1,)), ((), ())), precision=high, preferred_element_type=F32
    )


def back_kernel(*refs, pairs, qb, hb, steps, bits, fast, chunks, plan):
    refs = list(refs)
    take = lambda n: [refs.pop(0) for _ in range(n)]
    sides = [take(5), take(5)]
    code, xt, *weights = take(4)
    down_own, down_other, up_own, up_other, out_own, out_other, pre_own, pre_other = take(8)
    full_down, full_up, full_out, *full_project = take(6) if fast else [None] * 6
    token_out, sum_out = take(2)
    if fast:
        token_far = None
    else:
        token_far, sum_far = take(2)
        project = [take(3), take(3)]
    ds, dk, dv, dq, dkt, dvt = take(6)
    accs = take(3)
    if fast:
        project = [take(3), take(3)]
        token_far, token_near = take(2)
        sums, sum_other, sum_bufs = take(3)
        token_send, sum_send, sum_recv = take(3)
    step = pl.program_id(0)
    width = 2 * pairs * 64
    nq = qb * steps
    h = lax.axis_index("head")
    near = pl.ds(pl.multiple_of(h * nq, nq), nq)
    far = pl.ds(pl.multiple_of((1 - h) * nq, nq), nq)
    last = 2 * steps + 2 + (steps * qb) // hb

    if fast:
        phases = []
        sources = []
        for own, other, full, m in ((down_own, down_other, full_down, 0), (up_own, up_other, full_up, 1)):
            cols = own.shape[1] // chunks
            for i in range(chunks):
                sources.append((own, other, full, slice(i * cols, (i + 1) * cols), True))
        sources.append((out_own, out_other, full_out, slice(0, width), False))
        for i in range(3):
            sources.append((project[0][i], project[1][i], full_project[i], slice(0, width), False))
        spare = [project[0][:2], [project[0][2], project[1][0]]]
        assert all(slot <= steps for slot, stream, phase in plan[0] if stream < chunks and phase < 2)
        assert chunks == 2
        for n, (own, other, full, columns, keep) in enumerate(sources):
            bufs = take(5)
            (piece,) = take(1)
            kept = None
            if keep:
                kept = spare[n] if n < chunks else take(2)
            send, recv = take(2)
            phases.append(
                stream_phases(own, other, kept, piece, full, columns, bufs, send, recv, plan[1][n])
            )
        token_hop = remote(token_far, token_near, token_send.at[0], token_send.at[1], partner("head", 1))

        def token_end():
            token_hop.wait_recv()
            token_out[...] = token_out[...] + token_near[...].astype(F32)
            token_hop.wait_send()

        phases.append([token_hop.start, token_end])
        phases.append(sum_phases(sums, sum_other, sum_bufs, sum_send, sum_recv))

        @pl.when(step == 0)
        def _():
            greet([partner("head", 1)] + [partner("dp", b) for b in (1, 2, 4, 8)])

        for now in sorted(set(p[0] for p in plan[0])):
            if now < last:

                @pl.when(step == now)
                def _():
                    for slot, stream, phase in plan[0]:
                        if slot == now:
                            phases[stream][phase]()

    @pl.when(step == 0)
    def _():
        for o in accs:
            o[...] = jnp.zeros_like(o)

    for s in range(2):
        q, k, vt, do, p = sides[s]
        first = s * (steps + 1)

        @pl.when((step >= first) & (step < first + steps))
        def _():
            block = step - first

            @pl.when(block == 0)
            def _():
                dk[...] = jnp.zeros_like(dk)
                dv[...] = jnp.zeros_like(dv)

            at = pl.multiple_of(block * qb, qb)
            side_ds = ds.at[s * 2 * pairs : (s + 1) * 2 * pairs]
            attend_back(q, k, vt, do, p, side_ds, at, dq, dk, dv, pairs, qb)

        @pl.when(step == first + steps)
        def _():
            dkt[...] = (dk[...] * 2.0**-SCALE_BITS).astype(BF16)
            dvt[...] = dv[...].astype(BF16)
            w = weights[s]
            wq, wk, wv = (w[:, i * width : (i + 1) * width] for i in range(3))
            project[s][0][...] = dot_nn(xt[:, near], dq[...]).astype(BF16)
            project[s][1][...] = dot_nt(xt[...], dkt[...]).astype(BF16)
            project[s][2][...] = dot_nt(xt[...], dvt[...]).astype(BF16)
            mine = dot_nt(wq, dq[...]) + dot_nn(wk, dkt[:, near]) + dot_nn(wv, dvt[:, near])
            theirs = dot_nn(wk, dkt[:, far]) + dot_nn(wv, dvt[:, far])
            if s:
                token_out[...] += mine
                token_far[...] = (token_far[...].astype(F32) + theirs).astype(BF16)
            else:
                token_out[...] = mine
                token_far[...] = theirs.astype(BF16)
            bias = sum_other if fast and s else sums.at[5] if fast else sum_far if s else sum_out
            ones = jnp.ones((8, nq), BF16)
            bias[8:16, :] = dot_nn(ones, dq[...])
            ones = jnp.ones((8, xt.shape[1]), BF16)
            bias[16:24, :] = dot_nt(ones, dvt[...])

    @pl.when(step >= 2 * steps + 2)
    def _():
        count_rows(code, ds, (step - 2 * steps - 2) * hb, accs, bits, hb)

    @pl.when(step == last - 1)
    def _():
        if fast:
            outs = (sums.at[5], sum_other)
        else:
            outs = (sum_out, sum_far)
        heads = 2 * pairs
        for s, o in enumerate(outs):
            o[0:8, :] = jnp.zeros((8, width), F32)
            for t, (acc, b) in enumerate(zip(accs, bits)):
                o[0:8, t * 128 : t * 128 + 2**b] = table_sums(acc[...], b, s * heads, heads)
            o[24:, :] = (pre_other if s else pre_own)[...]
        if fast:
            for slot, stream, phase in plan[0]:
                if slot >= last:
                    phases[stream][phase]()
            sum_out[...] = sums[4]


def attend_backward(sides, code, xt, weights, bits, grads, pre, collective_id, fast, plan, chunks, qb=128, hb=64):
    nq, width = sides[0][0].shape
    keys = sides[0][1].shape[0]
    model = xt.shape[0]
    pairs = width // 128
    heads = 2 * pairs
    steps = nq // qb
    ratio = qb // hb
    full = lambda shape: pl.BlockSpec(shape, lambda i: (0,) * len(shape), pipeline_mode=pl.Buffered(1))
    anywhere = pl.BlockSpec(memory_space=pl.ANY)
    in_specs, operands = [], []
    for s in range(2):
        clip = lambda i, s=s: jnp.clip(i - s * (steps + 1), 0, steps - 1)
        row = pl.BlockSpec((qb, width), lambda i, clip=clip: (clip(i), 0))
        big = pl.BlockSpec((heads, qb, keys), lambda i, clip=clip: (0, clip(i), 0))
        in_specs += [row, full((keys, width)), full((width, keys)), row, big]
        operands += list(sides[s])
    in_specs.append(
        pl.BlockSpec((hb, keys), lambda i: (jnp.clip(i - 2 * steps - 2, 0, steps * ratio - 1), 0))
    )
    in_specs += [full(a.shape) for a in (xt, *weights)]
    in_specs += [anywhere] * 4 + [full(a.shape) for a in (*grads[4:], *pre)]
    operands += [code, xt, *weights, *grads, *pre]
    sum_shape = (24 + pre[0].shape[0], width)
    project_shape = (model, width)
    shapes, out_specs = [], []
    if fast:
        for g in (grads[0], grads[2], grads[4]):
            shapes.append((g.shape, BF16))
        shapes += [(project_shape, BF16)] * 3
        out_specs += [anywhere] * 6
    shapes += [((model, nq), F32), (sum_shape, F32)]
    if not fast:
        shapes += [((model, nq), BF16), (sum_shape, F32)] + [(project_shape, BF16)] * 6
    out_specs += [full(s) for s, _ in shapes[len(out_specs) :]]
    scratch = [
        pltpu.VMEM((2 * heads, nq, keys), BF16),
        pltpu.VMEM((width, keys), F32),
        pltpu.VMEM((width, keys), F32),
        pltpu.VMEM((nq, width), BF16),
        pltpu.VMEM((width, keys), BF16),
        pltpu.VMEM((width, keys), BF16),
    ] + [pltpu.VMEM((2 ** (b - 1) * 8, 2 * heads * 16), F32) for b in bits]
    params = dict(vmem_limit_bytes=BACK_VM)
    if fast:
        scratch += [pltpu.VMEM(project_shape, BF16)] * 6
        scratch += [pltpu.VMEM((model, nq), BF16)] * 2
        scratch += [pltpu.VMEM((6, *sum_shape), F32), pltpu.VMEM(sum_shape, F32)]
        scratch += [pltpu.VMEM((5, *sum_shape), F32)]
        scratch += [pltpu.SemaphoreType.DMA((2,)), pltpu.SemaphoreType.DMA((5,)), pltpu.SemaphoreType.DMA((5,))]
        n = 0
        for g in (grads[0], grads[2]):
            for _ in range(chunks):
                scratch += stream_scratch(g.shape[0], g.shape[1] // chunks, plan[1][n], n >= chunks)
                n += 1
        for _ in range(4):
            scratch += stream_scratch(model, width, plan[1][n], False)
            n += 1
        params.update(collective_id=collective_id, has_side_effects=True)
    return pl.pallas_call(
        functools.partial(
            back_kernel, pairs=pairs, qb=qb, hb=hb, steps=steps, bits=bits, fast=fast, chunks=chunks, plan=plan
        ),
        out_shape=tuple(jax.ShapeDtypeStruct(s, t) for s, t in shapes),
        grid=(2 * steps + 2 + steps * ratio,),
        in_specs=in_specs,
        out_specs=tuple(out_specs),
        scratch_shapes=scratch,
        compiler_params=pltpu.CompilerParams(**params),
        cost_estimate=pl.CostEstimate(
            flops=16 * nq * keys * width, bytes_accessed=300 * 2**20, transcendentals=0
        ),
    )(*operands)


norm_epsilon = 1e-05


def mm(a, b):
    return jnp.dot(a, b, preferred_element_type=F32)


def normalize(value):
    center = value - jnp.mean(value, axis=-1, keepdims=True)
    spread = jnp.mean(center * center, axis=-1, keepdims=True)
    root = lax.rsqrt(spread + norm_epsilon)
    return center * root, root


def normalize_back(grad, normed, root):
    return root * (
        grad
        - jnp.mean(grad, axis=-1, keepdims=True)
        - normed * jnp.mean(grad * normed, axis=-1, keepdims=True)
    )


def gelu_parts(u):
    t = 1.0 / (1.0 + (0.3275911 * 0.7071067811865476) * jnp.abs(u))
    e = jnp.exp(-0.5 * u * u)
    poly = t * (
        0.254829592 + t * (-0.284496736 + t * (1.421413741 + t * (-1.453152027 + t * 1.061405429)))
    )
    tail = 0.5 * e * poly
    below = jnp.where(u >= 0, 1.0 - tail, tail)
    return u * below, below + u * (e * 0.3989422804014327)


def swap_dp(x, bit):
    n = lax.axis_size("dp")
    return lax.ppermute(x, "dp", [(i, i ^ bit) for i in range(n)])


def swap_head(x):
    return lax.ppermute(x, "head", [(0, 1), (1, 0)])


def dp_bits():
    n, bit, out = lax.axis_size("dp"), 1, []
    while bit < n:
        out.append(bit)
        bit *= 2
    return out


def bit_of(bit):
    return (lax.axis_index("dp") // bit) % 2


def in_order(first, mine, theirs):
    low = jnp.where(first == 0, mine, theirs)
    high = jnp.where(first == 0, theirs, mine)
    return jnp.concatenate([low, high], axis=0)


def rows_of(x, index, rows):
    return lax.dynamic_slice_in_dim(x, index * rows, rows, 0)


def halve(g, bit):
    rows = g.shape[0] // 2
    b = bit_of(bit)
    got = swap_dp(rows_of(g, 1 - b, rows), bit)
    return (rows_of(g, b, rows).astype(F32) + got.astype(F32)).astype(BF16)


def reduce_grad(own, other, head_first):
    bits = dp_bits()
    own, other = halve(own, 1), halve(other, 1)
    if not head_first:
        own, other = halve(own, 2), halve(other, 2)
    g = (own.astype(F32) + swap_head(other).astype(F32)).astype(BF16)
    for bit in bits[1 if head_first else 2 :]:
        g = halve(g, bit)
    for bit in reversed(bits):
        g = in_order(bit_of(bit), g, swap_dp(g, bit))
    return g.astype(F32)


BACK_CHUNKS = 2
BACK_PLAN = (
    ((0, 0, 0), (0, 1, 0), (0, 2, 0), (0, 3, 0), (0, 4, 0), (2, 0, 1), (2, 1, 1), (3, 2, 1), (3, 3, 1), (4, 4, 1), (7, 0, 2), (7, 1, 2), (9, 4, 2), (10, 1, 3), (10, 2, 2), (10, 8, 0), (10, 5, 0), (10, 6, 0), (10, 7, 0), (11, 5, 1), (11, 6, 1), (12, 1, 4), (12, 2, 3), (12, 7, 1), (13, 3, 2), (14, 1, 5), (14, 2, 4), (14, 5, 2), (15, 0, 3), (15, 4, 3), (15, 6, 2), (16, 1, 6), (16, 2, 5), (17, 0, 4), (17, 4, 4), (17, 7, 2), (18, 2, 6), (18, 1, 7), (18, 9, 0), (18, 3, 3), (18, 0, 5), (18, 4, 5), (18, 8, 1), (18, 2, 7), (18, 0, 6), (18, 4, 6), (18, 5, 3), (18, 3, 4), (18, 1, 8), (18, 6, 3), (18, 1, 9), (18, 0, 7), (18, 4, 7), (18, 3, 5), (18, 7, 3), (18, 5, 4), (18, 2, 8), (18, 9, 1), (18, 6, 4), (18, 2, 9), (18, 9, 2), (18, 7, 4), (18, 3, 6), (18, 5, 5), (18, 0, 8), (18, 6, 5), (18, 7, 5), (18, 3, 7), (18, 0, 9), (18, 4, 8), (18, 5, 6), (18, 9, 3), (18, 6, 6), (18, 4, 9), (18, 7, 6), (18, 5, 7), (18, 9, 4), (18, 6, 7), (18, 3, 8), (18, 7, 7), (18, 9, 5), (18, 3, 9), (18, 5, 8), (18, 5, 9), (18, 6, 8), (18, 6, 9), (18, 7, 8), (18, 7, 9)),
    (False, True, True, True, False, False, False, False),
)


def local(
    tokens,
    cotangent,
    form_number,
    sequence_bucket,
    horizontal_bucket,
    vertical_bucket,
    project_weight,
    query_bias,
    value_bias,
    output_weight,
    output_bias,
    first_gain,
    first_shift,
    up_weight,
    up_bias,
    down_weight,
    down_bias,
    second_gain,
    second_shift,
    sequence_table,
    horizontal_table,
    vertical_table,
    project_weight_average,
    query_bias_average,
    value_bias_average,
    output_weight_average,
    output_bias_average,
    first_gain_average,
    first_shift_average,
    up_weight_average,
    up_bias_average,
    down_weight_average,
    down_bias_average,
    second_gain_average,
    second_shift_average,
    sequence_table_average,
    horizontal_table_average,
    vertical_table_average,
):
    total_rows, model_width = tokens.shape
    local_width = project_weight.shape[2]
    local_heads = sequence_table.shape[1]
    hidden = up_weight.shape[1]
    share_rows = total_rows // lax.axis_size("head")
    head_index = lax.axis_index("head")
    share_start = head_index * share_rows
    block_rows = 128
    buckets = (sequence_bucket, horizontal_bucket, vertical_bucket)
    tables = (sequence_table, horizontal_table, vertical_table)
    bits = tuple((t.shape[0] - 1).bit_length() for t in tables)
    flat_project = project_weight.reshape(model_width, 3 * local_width)

    params = jnp.concatenate(
        [first_gain, first_shift, second_gain, second_shift, output_bias, down_bias]
    ).reshape(6, 1, model_width)
    gain1, shift1, gain2, shift2, output_shift, down_shift = (params[i].astype(F32) for i in range(6))
    lanes = [jnp.pad(t.T, ((0, 0), (0, local_width // 3 - t.shape[0]))) for t in tables]
    small = jnp.concatenate(
        [
            jnp.concatenate(lanes, axis=1),
            jnp.concatenate([query_bias, value_bias, up_bias]).reshape(-1, local_width),
        ],
        axis=0,
    ).astype(F32)
    small = jnp.pad(small, ((0, 16 - small.shape[0]), (0, 0)))
    smalls, project_weights = [small], [flat_project]
    output_weights, up_weights, down_weights = [output_weight], [up_weight], [down_weight]

    form_row = form_number.reshape(total_rows)
    form_own = lax.dynamic_slice_in_dim(form_row, share_start, share_rows, 0)
    code = encode(
        [rows_of(b, head_index, share_rows) for b in buckets], form_own[:, None] == form_row[None, :]
    )
    own_tokens = rows_of(tokens, head_index, share_rows)

    scaled, keys, values_t, probs, contexts = [], [], [], [], []
    for s in range(2):
        wq = project_weights[s][:, :local_width]
        wk = project_weights[s][:, local_width : 2 * local_width]
        wv = project_weights[s][:, 2 * local_width :]
        bq = smalls[s][local_heads : local_heads + 1]
        bv = smalls[s][local_heads + 1 : local_heads + 2]
        q = ((mm(own_tokens, wq) + bq) * 0.125).astype(BF16)
        q = q * jnp.array(2.0**SCALE_BITS, BF16)
        k = mm(tokens, wk).astype(BF16)
        kt = dot_general_t(wk, tokens).astype(BF16)
        v = (mm(tokens, wv) + bv).astype(BF16)
        vt = (dot_general_t(wv, tokens) + bv.reshape(-1, 1)).astype(BF16)
        if s == 0:
            fetch = (
                ("small", (0, -1, -1), small),
                ("all", (0, 3, 7), flat_project),
                ("all", (0, 4, 7), output_weight),
                ("first", (0, -1, -1), up_weight),
            )
        else:
            fetch = (("rest", (-1, 0, 4), up_part), ("all", (0, 4, 8), down_weight))
        p, context, *fetched = attend_fwd(code, smalls[s], q, kt, v, fetch, s, qb=block_rows)
        if s == 0:
            smalls.append(fetched[0])
            project_weights.append(fetched[1])
            output_weights.append(fetched[2])
            up_part = fetched[3]
        else:
            up_weights.append(fetched[0])
            down_weights.append(fetched[1])
        scaled.append(q)
        keys.append(k)
        values_t.append(vt)
        probs.append(p)
        contexts.append(context)
    attend = output_shift + sum(mm(contexts[s], output_weights[s]) for s in range(2))
    n1, root1 = normalize(own_tokens.astype(F32) + attend)
    normed = n1 * gain1 + shift1
    normed_low = normed.astype(BF16)
    feed = down_shift
    acts, slopes = [], []
    for s in range(2):
        bu = smalls[s][local_heads + 2 : local_heads + 2 + hidden // local_width].reshape(1, hidden)
        act, slope = gelu_parts(mm(normed_low, up_weights[s]) + bu)
        act = act.astype(BF16)
        feed = feed + mm(act, down_weights[s])
        acts.append(act)
        slopes.append(slope.astype(BF16))
    n2, root2 = normalize(normed + feed)
    layer_output = n2 * gain2 + shift2

    cot = cotangent.astype(F32)
    back_second = normalize_back(cot * gain2, n2, root2)
    second_gain_part = jnp.sum(cot * n2, axis=0)
    second_shift_part = jnp.sum(cot, axis=0)
    back_feed = back_second.astype(BF16)
    down_bias_part = jnp.sum(back_feed.astype(F32), axis=0)
    back_normed = back_second
    up_bias_parts, down_grads, up_grads = [], [], []
    for s in range(2):
        down_grads.append(dot_tn(acts[s], back_feed).astype(BF16))
        back_up = (dot_nt(back_feed, down_weights[s]) * slopes[s].astype(F32)).astype(BF16)
        up_bias_parts.append(jnp.sum(back_up.astype(F32), axis=0))
        up_grads.append(dot_tn(normed_low, back_up).astype(BF16))
        back_normed = back_normed + dot_nt(back_up, up_weights[s])
    first_gain_part = jnp.sum(back_normed * n1, axis=0)
    first_shift_part = jnp.sum(back_normed, axis=0)
    back_first = normalize_back(back_normed * gain1, n1, root1)
    back_attend = back_first.astype(BF16)
    output_bias_part = jnp.sum(back_attend.astype(F32), axis=0)

    sides, output_grads = [], []
    for s in range(2):
        back_context = dot_nt(back_attend, output_weights[s]).astype(BF16)
        sides.append((scaled[s], keys[s], values_t[s], back_context, probs[s]))
        output_grads.append(dot_tn(back_attend, contexts[s]).astype(BF16))
    common = [
        first_gain_part,
        first_shift_part,
        second_gain_part,
        second_shift_part,
        output_bias_part,
        down_bias_part,
    ]
    pre = [jnp.concatenate(common + [up_bias_parts[s]]).reshape(-1, local_width) for s in range(2)]
    fast = lax.axis_size("dp") == 16
    results = attend_backward(
        sides,
        code,
        tokens.T,
        project_weights,
        bits,
        (*down_grads, *up_grads, *output_grads),
        pre,
        2,
        fast,
        BACK_PLAN,
        BACK_CHUNKS,
        qb=block_rows,
    )
    if fast:
        down_total, up_total, output_total = (r.astype(F32) for r in results[:3])
        project_total = [r.astype(F32) for r in results[3:6]]
        tokens_gradient, sums = results[6:]
    else:
        tokens_gradient, sums, far, sums_other = results[:4]
        tokens_gradient = tokens_gradient + swap_head(far).astype(F32)
        sums = sums + swap_head(sums_other)
        for bit in dp_bits():
            sums = sums + swap_dp(sums, bit)
        down_total, up_total = reduce_grad(*down_grads, True), reduce_grad(*up_grads, False)
        output_total = reduce_grad(*output_grads, True)
        project_total = [reduce_grad(results[4 + i], results[7 + i], False) for i in range(3)]
    tokens_gradient = back_first + tokens_gradient.T
    project_total = jnp.stack(project_total, axis=1)
    output_total = output_total.T
    query_bias_total, value_bias_total = sums[8], sums[16]
    tail = sums[24:].reshape(-1)
    (
        first_gain_total,
        first_shift_total,
        second_gain_total,
        second_shift_total,
        output_bias_total,
        down_bias_total,
    ) = (tail[i * model_width : (i + 1) * model_width] for i in range(6))
    up_bias_total = tail[6 * model_width :]
    sequence_total, horizontal_total, vertical_total = (
        sums[:local_heads, i * 128 : i * 128 + t.shape[0]].T for i, t in enumerate(tables)
    )
    up_weight_total, down_weight_total, output_weight_total = up_total, down_total, output_total
    token_count = total_rows * lax.axis_size("dp")
    group_count = lax.axis_size("dp")
    group_index = lax.axis_index("dp")

    def renew(average, weight, gradient):
        return 0.5 * average + 0.5 * (weight.astype(jnp.float32) - gradient / token_count)

    def part_of(array, along):
        width = array.shape[along] // group_count
        return lax.dynamic_slice_in_dim(array, group_index * width, width, along)

    return (
        layer_output,
        tokens_gradient,
        project_total,
        query_bias_total,
        value_bias_total,
        output_weight_total,
        output_bias_total,
        first_gain_total,
        first_shift_total,
        up_weight_total,
        up_bias_total,
        down_weight_total,
        down_bias_total,
        second_gain_total,
        second_shift_total,
        sequence_total,
        horizontal_total,
        vertical_total,
        renew(project_weight_average, part_of(project_weight, 0), part_of(project_total, 0)),
        renew(query_bias_average, query_bias, query_bias_total),
        renew(value_bias_average, value_bias, value_bias_total),
        renew(output_weight_average, part_of(output_weight, 1), part_of(output_weight_total, 1)),
        renew(output_bias_average, output_bias, output_bias_total),
        renew(first_gain_average, first_gain, first_gain_total),
        renew(first_shift_average, first_shift, first_shift_total),
        renew(up_weight_average, part_of(up_weight, 0), part_of(up_weight_total, 0)),
        renew(up_bias_average, up_bias, up_bias_total),
        renew(down_weight_average, part_of(down_weight, 0), part_of(down_weight_total, 0)),
        renew(down_bias_average, down_bias, down_bias_total),
        renew(second_gain_average, second_gain, second_gain_total),
        renew(second_shift_average, second_shift, second_shift_total),
        renew(sequence_table_average, sequence_table, sequence_total),
        renew(horizontal_table_average, horizontal_table, horizontal_total),
        renew(vertical_table_average, vertical_table, vertical_total),
    )


def solution(mesh):
    in_specs = (
        P("dp", None),
        P(("dp", "head"), None),
        P("dp", None),
        P("dp", None),
        P("dp", None),
        P("dp", None),
        P(None, None, "head"),
        P("head"),
        P("head"),
        P("head", None),
        P(),
        P(),
        P(),
        P(None, "head"),
        P("head"),
        P("head", None),
        P(),
        P(),
        P(),
        P(None, "head"),
        P(None, "head"),
        P(None, "head"),
        P("dp", None, "head"),
        P("head"),
        P("head"),
        P("head", "dp"),
        P(),
        P(),
        P(),
        P("dp", "head"),
        P("head"),
        P(("head", "dp"), None),
        P(),
        P(),
        P(),
        P(None, "head"),
        P(None, "head"),
        P(None, "head"),
    )
    out_specs = (
        P(("dp", "head"), None),
        P(("dp", "head"), None),
        P(None, None, "head"),
        P("head"),
        P("head"),
        P("head", None),
        P(),
        P(),
        P(),
        P(None, "head"),
        P("head"),
        P("head", None),
        P(),
        P(),
        P(),
        P(None, "head"),
        P(None, "head"),
        P(None, "head"),
        P("dp", None, "head"),
        P("head"),
        P("head"),
        P("head", "dp"),
        P(),
        P(),
        P(),
        P("dp", "head"),
        P("head"),
        P(("head", "dp"), None),
        P(),
        P(),
        P(),
        P(None, "head"),
        P(None, "head"),
        P(None, "head"),
    )
    return jax.shard_map(local, mesh=mesh, in_specs=in_specs, out_specs=out_specs, check_vma=False)
```

```python
import functools
import jax
import jax.numpy as jnp
from jax import lax
from jax.experimental import pallas as pl
from jax.sharding import PartitionSpec as P
from jax.experimental.pallas import tpu as pltpu

F32, BF16, I32 = jnp.float32, jnp.bfloat16, jnp.int32
SCALE_BITS = 27
STEP = 2.0**11
VM = 56 * 2**20
BACK_VM = 60 * 2**20
SAME = 2**17


def encode(buckets, same):
    seq, hor, ver = buckets
    return seq + 32 * hor + 2048 * ver + jnp.where(same, SAME, 0)


def buckets_of(code):
    return code & 31, (code >> 5) & 63, (code >> 11) & 63


def dot_nt(a, b):
    return lax.dot_general(a, b, (((1,), (1,)), ((), ())), preferred_element_type=F32)


def dot_tn(a, b):
    return lax.dot_general(a, b, (((0,), (0,)), ((), ())), preferred_element_type=F32)


def dot_general_t(w, x):
    return lax.dot_general(w, x, (((0,), (1,)), ((), ())), preferred_element_type=F32)


def dot_tt(a, b):
    return lax.dot_general(a, b, (((0,), (1,)), ((), ())), preferred_element_type=F32)


def dot_nn(a, b):
    return lax.dot_general(a, b, (((1,), (0,)), ((), ())), preferred_element_type=F32)


def split_pair(x):
    lane = lax.broadcasted_iota(I32, x.shape, 1)
    zero = jnp.zeros_like(x)
    return jnp.concatenate([jnp.where(lane < 64, x, zero), jnp.where(lane < 64, zero, x)], axis=0)


def partner(axis, bit):
    i = lax.axis_index(axis)
    low = lax.rem(lax.div(i, bit), 2)
    return {axis: i + bit * (1 - 2 * low)}


def dp_bit(bit):
    return lax.rem(lax.div(lax.axis_index("dp"), bit), 2)


def greet(partners):
    barrier = pltpu.get_barrier_semaphore()
    for p in partners:
        pl.semaphore_signal(barrier, inc=1, device_id=p, device_id_type=pl.DeviceIdType.MESH)
    pl.semaphore_wait(barrier, len(partners))


def remote(src, dst, send, recv, to):
    return pltpu.make_async_remote_copy(
        src_ref=src,
        dst_ref=dst,
        send_sem=send,
        recv_sem=recv,
        device_id=to,
        device_id_type=pl.DeviceIdType.MESH,
    )


def fetch_copies(mode, source, out, send, recv):
    if mode == "small":
        return [remote(source, out, send.at[0], recv.at[0], partner("head", 1)), None, None], []
    rows = source.shape[0] if mode == "rest" else source.shape[0] // 4
    quarter = 2 * dp_bit(1) + dp_bit(2)
    one = pl.ds(pl.multiple_of(quarter * rows, rows), rows)
    two = pl.ds(pl.multiple_of(dp_bit(1) * (2 * rows), 2 * rows), 2 * rows)
    hops, local = [None, None, None], []
    if mode == "first":
        hops[0] = remote(source.at[one], out, send.at[0], recv.at[0], partner("head", 1))
    else:
        if mode == "all":
            hops[0] = remote(source.at[one], out.at[one], send.at[0], recv.at[0], partner("head", 1))
            quarter_ref = out.at[one]
        else:
            quarter_ref = source
            local.append(pltpu.make_async_copy(source, out.at[one], send.at[0]))
        hops[1] = remote(quarter_ref, out.at[one], send.at[1], recv.at[1], partner("dp", 2))
        hops[2] = remote(out.at[two], out.at[two], send.at[2], recv.at[2], partner("dp", 1))
    return hops, local


def fetched_shape(mode, w):
    rows = {"all": 1, "small": 1, "first": 0.25, "rest": 4}[mode] * w.shape[0]
    return jax.ShapeDtypeStruct((int(rows), w.shape[1]), w.dtype)


def fwd_kernel(*refs, pairs, qb, modes, points, steps):
    n = len(modes)
    code, tab, q, kt, v = refs[:5]
    sources = refs[5 : 5 + n]
    p_out, c_out = refs[5 + n : 7 + n]
    outs = refs[7 + n : 7 + 2 * n]
    b_ref, t_ref, send, recv = refs[7 + 2 * n :]
    keys = v.shape[0]
    chunk = 128
    step = pl.program_id(0)
    hops, local = [], []
    for i in range(n):
        h, l = fetch_copies(modes[i], sources[i], outs[i], send.at[i], recv.at[i])
        hops.append(h)
        local += l

    def point(now):
        for i in range(n):
            for hop in range(3):
                if points[i][hop] == now:
                    if hop and hops[i][hop - 1] is not None:
                        hops[i][hop - 1].wait_recv()
                    hops[i][hop].start()

    @pl.when(step == 0)
    def _():
        greet([partner("head", 1), partner("dp", 2), partner("dp", 1)])
        for copy in local:
            copy.start()
        for j in range(pairs):
            for t in range(3):
                ls = slice(t * chunk, (t + 1) * chunk)
                fixed = [jnp.round(tab[2 * j + g : 2 * j + g + 1, ls] * STEP).astype(I32) for g in range(2)]
                t_ref[8 * (3 * j + t) : 8 * (3 * j + t) + 8, :] = jnp.broadcast_to(
                    fixed[0] * 65536 + fixed[1], (8, chunk)
                )
        point(0)

    for now in sorted(set(sum(points, ()))):
        if 0 < now < 2 * steps and now % 2 == 0:

            @pl.when(step == now // 2)
            def _():
                if local and now == min(p[2] for p, m in zip(points, modes) if m == "rest"):
                    for copy in local:
                        copy.wait()
                point(now)

    tbs = [t_ref[8 * i : 8 * i + 8, :] for i in range(3 * pairs)]

    def gather(r, _):
        rs = pl.ds(pl.multiple_of(r * 8, 8), 8)
        for c in range(keys // chunk):
            ls = slice(c * chunk, (c + 1) * chunk)
            sums = [None] * pairs
            for t, idx in enumerate(buckets_of(code[rs, ls])):
                for j in range(pairs):
                    g = jnp.take_along_axis(tbs[3 * j + t], idx, axis=1, mode="promise_in_bounds")
                    sums[j] = g if t == 0 else sums[j] + g
            for j in range(pairs):
                b_ref[j, rs, ls] = sums[j]
        return 0

    lax.fori_loop(0, qb // 8, gather, 0)
    for now in sorted(set(sum(points, ()))):
        if 0 < now < 2 * steps and now % 2 == 1:

            @pl.when(step == now // 2)
            def _():
                point(now)

    same = code[...] >= SAME
    for j in range(pairs):
        lanes = slice(j * 128, (j + 1) * 128)
        q2 = split_pair(q[:, lanes])
        s2 = dot_nn(q2, kt[lanes, :])
        bias = b_ref[j]
        for g in range(2):
            x = s2[g * qb : (g + 1) * qb] + (bias << 16 if g else bias).astype(F32)
            x = jnp.where(same, x, -1e30)
            top = jnp.max(x, axis=1, keepdims=True)
            e = jnp.exp2((x - top) * (1.4426950408889634 * 2.0**-SCALE_BITS))
            inv = 1.0 / jnp.sum(e, axis=1, keepdims=True)
            p_out[2 * j + g] = (e * inv).astype(BF16)
        c0 = dot_nn(p_out[2 * j], v[:, lanes])
        c1 = dot_nn(p_out[2 * j + 1], v[:, lanes])
        lane = lax.broadcasted_iota(I32, c0.shape, 1)
        c_out[:, lanes] = jnp.where(lane < 64, c0, c1).astype(BF16)

    @pl.when(step == steps - 1)
    def _():
        for now in range(2 * steps, max(sum(points, ())) + 1):
            point(now)
        for i in range(n):
            last = [copy for copy in hops[i] if copy is not None][-1]
            last.wait_recv()
        for i in range(n):
            for copy in hops[i]:
                if copy is not None:
                    copy.wait_send()


def attend_fwd(code, tab, q, kt, v, fetch, collective_id, qb=128):
    nq, width = q.shape
    keys = v.shape[0]
    pairs = width // 128
    modes = tuple(f[0] for f in fetch)
    points = tuple(f[1] for f in fetch)
    sources = [f[2] for f in fetch]
    n = len(fetch)
    steps = nq // qb
    full = lambda a: pl.BlockSpec(a.shape, lambda i: (0,) * a.ndim)
    anywhere = pl.BlockSpec(memory_space=pl.ANY)
    return pl.pallas_call(
        functools.partial(fwd_kernel, pairs=pairs, qb=qb, modes=modes, points=points, steps=steps),
        out_shape=(
            jax.ShapeDtypeStruct((2 * pairs, nq, keys), BF16),
            jax.ShapeDtypeStruct((nq, width), BF16),
        )
        + tuple(fetched_shape(m, w) for m, w in zip(modes, sources)),
        grid=(steps,),
        in_specs=[
            pl.BlockSpec((qb, keys), lambda i: (i, 0)),
            full(tab),
            pl.BlockSpec((qb, width), lambda i: (i, 0)),
            full(kt),
            full(v),
        ]
        + [anywhere] * n,
        out_specs=(
            pl.BlockSpec((2 * pairs, qb, keys), lambda i: (0, i, 0)),
            pl.BlockSpec((qb, width), lambda i: (i, 0)),
        )
        + (anywhere,) * n,
        scratch_shapes=[
            pltpu.VMEM((pairs, qb, keys), I32),
            pltpu.VMEM((pairs * 24, 128), I32),
            pltpu.SemaphoreType.DMA((n, 3)),
            pltpu.SemaphoreType.DMA((n, 3)),
        ],
        compiler_params=pltpu.CompilerParams(
            vmem_limit_bytes=VM, collective_id=collective_id, has_side_effects=True
        ),
        cost_estimate=pl.CostEstimate(
            flops=4 * nq * keys * width, bytes_accessed=90 * 2**20, transcendentals=nq * keys * 2 * pairs
        ),
    )(code, tab, q, kt, v, *sources)


def add_rows(dst, a, b, tile):
    rows = dst[2]

    def body(i, _):
        at = lambda x: pl.ds(pl.multiple_of(x[1] + i * tile, 16), tile)
        dst[0][at(dst), :] = a[0][at(a), :] + b[0][at(b), :]
        return 0

    lax.fori_loop(0, rows // tile, body, 0)


STREAM_SEMS = 14


def stream_phases(own, other, kept, piece, full, columns, bufs, send, recv, head_first):
    rows = own.shape[0]
    half, tile = rows // 2, rows // 16
    rc, r1, r2, r3, r4 = bufs
    c, x, z0, z1 = (dp_bit(b) for b in (1, 2, 4, 8))
    part = lambda ref, bit, n: ref.at[pl.ds(pl.multiple_of(bit * n, 16), n)]
    cut = lambda ref, start, n: ref.at[pl.ds(pl.multiple_of(start, 16), n), columns]
    to = [partner("dp", 1), partner("dp", 2), partner("dp", 4), partner("dp", 8), partner("head", 1)]
    hop0 = [
        remote(cut(own, (1 - c) * half, half), rc.at[0], send.at[0], recv.at[0], to[0]),
        remote(cut(other, (1 - c) * half, half), rc.at[1], send.at[1], recv.at[1], to[0]),
    ]
    if head_first:
        hop1 = [remote(rc.at[1], r1, send.at[2], recv.at[2], to[4])]
        hop2 = [remote(part(rc.at[0], 1 - x, half // 2), r2, send.at[4], recv.at[4], to[1])]
    else:
        hop1 = [
            remote(part(rc.at[n], 1 - x, half // 2), r1.at[n], send.at[2 + n], recv.at[2 + n], to[1])
            for n in range(2)
        ]
        hop2 = [remote(r1.at[1], r2, send.at[4], recv.at[4], to[4])]
    hop3 = [remote(part(r2, 1 - z0, half // 4), r3, send.at[5], recv.at[5], to[2])]
    hop4 = [remote(part(r3, 1 - z1, half // 8), r4, send.at[6], recv.at[6], to[3])]
    at_x = c * half + x * (half // 2)
    at_z = at_x + z0 * (half // 4)
    at_end = at_z + z1 * (half // 8)
    there = lambda start, n: full.at[pl.ds(pl.multiple_of(start, 16), n), columns]
    spans = [(at_end, half // 8, 3), (at_z, half // 4, 2), (at_x, half // 2, 1), (c * half, half, 0)]
    hop5 = [remote(piece, there(at_end, half // 8), send.at[7], recv.at[7], to[3])]
    back = [hop5]
    for i, (start, n, which) in enumerate(spans[1:]):
        ref = there(start, n)
        back.append([remote(ref, ref, send.at[8 + i], recv.at[8 + i], to[which])])
    local = [pltpu.make_async_copy(piece, there(at_end, half // 8), send.at[11])]
    keep = []
    if kept is not None:
        keep = [
            pltpu.make_async_copy(cut(g, c * half, half), kept[n], send.at[12 + n])
            for n, g in enumerate((own, other))
        ]

    def start(hop):
        for copy in hop:
            copy.start()

    def arrive(hop):
        for copy in hop:
            copy.wait_recv()

    def phase0():
        start(hop0)
        start(keep)

    def phase1():
        for copy in keep:
            copy.wait()
        arrive(hop0)
        for n, g in enumerate((own, other)):
            mine = (kept[n], 0) if keep else (g, c * half)
            add_rows((rc.at[n], 0, half), (rc.at[n], 0), mine, tile)
        start(hop1)

    def phase2():
        arrive(hop1)
        if head_first:
            add_rows((rc.at[0], 0, half), (rc.at[0], 0), (r1, 0), tile)
        else:
            for n in range(2):
                add_rows((r1.at[n], 0, half // 2), (r1.at[n], 0), (rc.at[n], x * (half // 2)), tile)
        start(hop2)

    def phase3():
        arrive(hop2)
        if head_first:
            add_rows((r2, 0, half // 2), (r2, 0), (rc.at[0], x * (half // 2)), tile)
        else:
            add_rows((r2, 0, half // 2), (r2, 0), (r1.at[0], 0), tile)
        start(hop3)

    def phase4():
        arrive(hop3)
        add_rows((r3, 0, half // 4), (r3, 0), (r2, z0 * (half // 4)), tile)
        start(hop4)

    def phase5():
        arrive(hop4)
        add_rows((piece, 0, half // 8), (r4, 0), (r3, z1 * (half // 8)), tile)
        start(local)
        start(back[0])

    def gather(i):
        def phase():
            if i == 1:
                for copy in local:
                    copy.wait()
            arrive(back[i - 1])
            start(back[i])

        return phase

    def finish():
        arrive(back[3])
        for hop in [hop0, hop1, hop2, hop3, hop4] + back:
            for copy in hop:
                copy.wait_send()

    return [phase0, phase1, phase2, phase3, phase4, phase5, gather(1), gather(2), gather(3), finish]


def stream_scratch(rows, columns, head_first, keep):
    half = rows // 2
    first = (half, columns) if head_first else (2, half // 2, columns)
    shapes = [(2, half, columns), first, (half // 2, columns), (half // 4, columns), (half // 8, columns)]
    shapes.append((half // 8, columns))
    if keep:
        shapes += [(half, columns)] * 2
    return [pltpu.VMEM(s, BF16) for s in shapes] + [pltpu.SemaphoreType.DMA((STREAM_SEMS,))] * 2


def sum_phases(own, other, bufs, send, recv):
    to = [partner("head", 1)] + [partner("dp", b) for b in (1, 2, 4, 8)]
    hops = [
        remote(other if i == 0 else own.at[i - 1], bufs.at[i], send.at[i], recv.at[i], to[i])
        for i in range(5)
    ]

    def phase(i):
        def run():
            if i:
                hops[i - 1].wait_recv()
                if i > 1:
                    own[i - 1] = own[i - 2] + bufs[i - 1]
                else:
                    own[0] = own[5] + bufs[0]
            if i < 5:
                hops[i].start()
            else:
                for copy in hops:
                    copy.wait_send()

        return run

    return [phase(i) for i in range(6)]


def attend_back(q, k, vt, do, p, ds, at, dq, dk, dv, pairs, qb):
    for j in range(pairs):
        lanes = slice(j * 128, (j + 1) * 128)
        q2 = split_pair(q[:, lanes])
        do2 = split_pair(do[:, lanes])
        dp2 = dot_nn(do2, vt[lanes, :])
        parts = []
        for g in range(2):
            ps = p[2 * j + g].astype(F32)
            ts = ps * dp2[g * qb : (g + 1) * qb]
            inner = jnp.sum(ts, axis=1, keepdims=True)
            parts.append((ts - ps * inner).astype(BF16))
            ds[2 * j + g, pl.ds(at, qb), :] = parts[g]
        d0 = dot_nn(parts[0], k[:, lanes])
        d1 = dot_nn(parts[1], k[:, lanes])
        lane = lax.broadcasted_iota(I32, d0.shape, 1)
        dq[pl.ds(at, qb), lanes] = jnp.where(lane < 64, d0, d1).astype(BF16) * jnp.array(0.125, BF16)
        dk[lanes, :] += dot_tn(q2, jnp.concatenate(parts, axis=0))
        dv[lanes, :] += dot_tn(do2, p[2 * j : 2 * j + 2].reshape(2 * qb, p.shape[2]))


def count_rows(code, ds, at, outs, bits, nq):
    heads = ds.shape[0]

    def rows(r, _):
        rs = pl.ds(pl.multiple_of(at + r * 16, 16), 16)
        dfull = [ds[h, rs, :].astype(F32) for h in range(heads)]
        for half in range(2):
            d8 = [d[half * 8 : half * 8 + 8] for d in dfull]
            packed = code[pl.ds(pl.multiple_of(r * 16 + half * 8, 8), 8), :]
            low = 0
            for t in range(3):
                signs = [(((packed << (31 - low - i)) >> 31) | 1).astype(F32) for i in range(bits[t])]
                low += bits[t]
                rhs = jnp.concatenate(
                    [jnp.concatenate([d, d * signs[0]], axis=0).astype(BF16) for d in d8], axis=0
                )
                first = jnp.concatenate([jnp.ones_like(signs[1]), signs[1]], axis=0).astype(BF16)
                tiles = [first]
                for i in range(2, bits[t]):
                    s2 = jnp.concatenate([signs[i], signs[i]], axis=0).astype(BF16)
                    tiles = tiles + [x * s2 for x in tiles]
                outs[t][...] += dot_nt(jnp.concatenate(tiles, axis=0), rhs)
        return 0

    lax.fori_loop(0, nq // 16, rows, 0)


def table_sums(acc, bits, first, heads):
    n = 2**bits
    high = lax.Precision.HIGHEST
    iota = lambda shape, d: lax.broadcasted_iota(I32, shape, d)
    row, col = iota(acc.shape, 0), iota(acc.shape, 1)
    kept = jnp.where((row & 7) == (col & 7), acc, 0.0)
    shape = (n, acc.shape[0])
    odd = (iota(shape, 1) >> 3) & (iota(shape, 0) >> 1)
    odd = odd ^ (odd >> 4)
    odd = odd ^ (odd >> 2)
    odd = odd ^ (odd >> 1)
    left = (1 - 2 * (odd & 1)).astype(F32)
    shape = (n, acc.shape[1])
    odd = iota(shape, 0) & (iota(shape, 1) >> 3) & 1
    mixed = jnp.dot(left, kept, precision=high, preferred_element_type=F32)
    mixed = mixed * (1 - 2 * odd).astype(F32) * (1.0 / n)
    shape = (8, acc.shape[1])
    head = iota(shape, 0)
    pick = ((iota(shape, 1) >> 4) == head + first) & (head < heads)
    return lax.dot_general(
        pick.astype(F32), mixed, (((1,), (1,)), ((), ())), precision=high, preferred_element_type=F32
    )


def back_kernel(*refs, pairs, qb, hb, steps, bits, fast, chunks, plan):
    refs = list(refs)
    take = lambda n: [refs.pop(0) for _ in range(n)]
    sides = [take(5), take(5)]
    code, xt, *weights = take(4)
    down_own, down_other, up_own, up_other, out_own, out_other, pre_own, pre_other = take(8)
    full_down, full_up, full_out, *full_project = take(6) if fast else [None] * 6
    token_out, sum_out = take(2)
    if fast:
        token_far = None
    else:
        token_far, sum_far = take(2)
        project = [take(3), take(3)]
    ds, dk, dv, dq, dkt, dvt = take(6)
    accs = take(3)
    if fast:
        project = [take(3), take(3)]
        token_far, token_near = take(2)
        sums, sum_other, sum_bufs = take(3)
        token_send, sum_send, sum_recv = take(3)
    step = pl.program_id(0)
    width = 2 * pairs * 64
    nq = qb * steps
    model = xt.shape[0]
    h = lax.axis_index("head")
    near = pl.ds(pl.multiple_of(h * nq, nq), nq)
    far = pl.ds(pl.multiple_of((1 - h) * nq, nq), nq)
    last = 2 * steps + 2 + (steps * qb) // hb

    if fast:
        phases = []
        sources = []
        for own, other, full, m in ((down_own, down_other, full_down, 0), (up_own, up_other, full_up, 1)):
            cols = own.shape[1] // chunks
            for i in range(chunks):
                sources.append((own, other, full, slice(i * cols, (i + 1) * cols), True))
        sources.append((out_own, out_other, full_out, slice(0, width), False))
        for i in range(3):
            sources.append((project[0][i], project[1][i], full_project[i], slice(0, width), False))
        spare = [project[0][:2], [project[0][2], project[1][0]]]
        assert all(slot <= steps for slot, stream, phase in plan[0] if stream < chunks and phase < 2)
        assert chunks == 2
        for n, (own, other, full, columns, keep) in enumerate(sources):
            bufs = take(5)
            (piece,) = take(1)
            kept = None
            if keep:
                kept = spare[n] if n < chunks else take(2)
            send, recv = take(2)
            phases.append(
                stream_phases(own, other, kept, piece, full, columns, bufs, send, recv, plan[1][n])
            )
        token_hop = remote(token_far, token_near, token_send.at[0], token_send.at[1], partner("head", 1))

        def token_end():
            token_hop.wait_recv()
            token_out[...] = token_out[...] + token_near[...].astype(F32)
            token_hop.wait_send()

        phases.append([token_hop.start, token_end])
        phases.append(sum_phases(sums, sum_other, sum_bufs, sum_send, sum_recv))

        @pl.when(step == 0)
        def _():
            greet([partner("head", 1)] + [partner("dp", b) for b in (1, 2, 4, 8)])

        for now in sorted(set(p[0] for p in plan[0])):
            if now < last:

                @pl.when(step == now)
                def _():
                    for slot, stream, phase in plan[0]:
                        if slot == now:
                            phases[stream][phase]()

    @pl.when(step == 0)
    def _():
        for o in accs:
            o[...] = jnp.zeros_like(o)

    for s in range(2):
        q, k, vt, do, p = sides[s]
        first = s * (steps + 1)

        @pl.when((step >= first) & (step < first + steps))
        def _():
            block = step - first

            @pl.when(block == 0)
            def _():
                dk[...] = jnp.zeros_like(dk)
                dv[...] = jnp.zeros_like(dv)

            at = pl.multiple_of(block * qb, qb)
            side_ds = ds.at[s * 2 * pairs : (s + 1) * 2 * pairs]
            attend_back(q, k, vt, do, p, side_ds, at, dq, dk, dv, pairs, qb)

        @pl.when(step == first + steps)
        def _():
            dkt[...] = (dk[...] * 2.0**-SCALE_BITS).astype(BF16)
            dvt[...] = dv[...].astype(BF16)
            w = weights[s]
            wq, wk, wv = (w[i * model : (i + 1) * model, :] for i in range(3))
            project[s][0][...] = dot_nn(xt[:, near], dq[...]).astype(BF16)
            project[s][1][...] = dot_nt(xt[...], dkt[...]).astype(BF16)
            project[s][2][...] = dot_nt(xt[...], dvt[...]).astype(BF16)
            mine = dot_nt(wq, dq[...]) + dot_nn(wk, dkt[:, near]) + dot_nn(wv, dvt[:, near])
            theirs = dot_nn(wk, dkt[:, far]) + dot_nn(wv, dvt[:, far])
            if s:
                token_out[...] += mine
                token_far[...] = (token_far[...].astype(F32) + theirs).astype(BF16)
            else:
                token_out[...] = mine
                token_far[...] = theirs.astype(BF16)
            bias = sum_other if fast and s else sums.at[5] if fast else sum_far if s else sum_out
            ones = jnp.ones((8, nq), BF16)
            bias[8:16, :] = dot_nn(ones, dq[...])
            ones = jnp.ones((8, xt.shape[1]), BF16)
            bias[16:24, :] = dot_nt(ones, dvt[...])

    @pl.when(step >= 2 * steps + 2)
    def _():
        count_rows(code, ds, (step - 2 * steps - 2) * hb, accs, bits, hb)

    @pl.when(step == last - 1)
    def _():
        if fast:
            outs = (sums.at[5], sum_other)
        else:
            outs = (sum_out, sum_far)
        heads = 2 * pairs
        for s, o in enumerate(outs):
            o[0:8, :] = jnp.zeros((8, width), F32)
            for t, (acc, b) in enumerate(zip(accs, bits)):
                o[0:8, t * 128 : t * 128 + 2**b] = table_sums(acc[...], b, s * heads, heads)
            o[24:, :] = (pre_other if s else pre_own)[...]
        if fast:
            for slot, stream, phase in plan[0]:
                if slot >= last:
                    phases[stream][phase]()
            sum_out[...] = sums[4]


def attend_backward(sides, code, xt, weights, bits, grads, pre, collective_id, fast, plan, chunks, qb=128, hb=64):
    nq, width = sides[0][0].shape
    keys = sides[0][1].shape[0]
    model = xt.shape[0]
    pairs = width // 128
    heads = 2 * pairs
    steps = nq // qb
    ratio = qb // hb
    full = lambda shape: pl.BlockSpec(shape, lambda i: (0,) * len(shape), pipeline_mode=pl.Buffered(1))
    anywhere = pl.BlockSpec(memory_space=pl.ANY)
    in_specs, operands = [], []
    for s in range(2):
        clip = lambda i, s=s: jnp.clip(i - s * (steps + 1), 0, steps - 1)
        row = pl.BlockSpec((qb, width), lambda i, clip=clip: (clip(i), 0))
        big = pl.BlockSpec((heads, qb, keys), lambda i, clip=clip: (0, clip(i), 0))
        in_specs += [row, full((keys, width)), full((width, keys)), row, big]
        operands += list(sides[s])
    in_specs.append(
        pl.BlockSpec((hb, keys), lambda i: (jnp.clip(i - 2 * steps - 2, 0, steps * ratio - 1), 0))
    )
    in_specs += [full(a.shape) for a in (xt, *weights)]
    in_specs += [anywhere] * 4 + [full(a.shape) for a in (*grads[4:], *pre)]
    operands += [code, xt, *weights, *grads, *pre]
    sum_shape = (24 + pre[0].shape[0], width)
    project_shape = (model, width)
    shapes, out_specs = [], []
    if fast:
        for g in (grads[0], grads[2], grads[4]):
            shapes.append((g.shape, BF16))
        shapes += [(project_shape, BF16)] * 3
        out_specs += [anywhere] * 6
    shapes += [((model, nq), F32), (sum_shape, F32)]
    if not fast:
        shapes += [((model, nq), BF16), (sum_shape, F32)] + [(project_shape, BF16)] * 6
    out_specs += [full(s) for s, _ in shapes[len(out_specs) :]]
    scratch = [
        pltpu.VMEM((2 * heads, nq, keys), BF16),
        pltpu.VMEM((width, keys), F32),
        pltpu.VMEM((width, keys), F32),
        pltpu.VMEM((nq, width), BF16),
        pltpu.VMEM((width, keys), BF16),
        pltpu.VMEM((width, keys), BF16),
    ] + [pltpu.VMEM((2 ** (b - 1) * 8, 2 * heads * 16), F32) for b in bits]
    params = dict(vmem_limit_bytes=BACK_VM)
    if fast:
        scratch += [pltpu.VMEM(project_shape, BF16)] * 6
        scratch += [pltpu.VMEM((model, nq), BF16)] * 2
        scratch += [pltpu.VMEM((6, *sum_shape), F32), pltpu.VMEM(sum_shape, F32)]
        scratch += [pltpu.VMEM((5, *sum_shape), F32)]
        scratch += [pltpu.SemaphoreType.DMA((2,)), pltpu.SemaphoreType.DMA((5,)), pltpu.SemaphoreType.DMA((5,))]
        n = 0
        for g in (grads[0], grads[2]):
            for _ in range(chunks):
                scratch += stream_scratch(g.shape[0], g.shape[1] // chunks, plan[1][n], n >= chunks)
                n += 1
        for _ in range(4):
            scratch += stream_scratch(model, width, plan[1][n], False)
            n += 1
        params.update(collective_id=collective_id, has_side_effects=True)
    return pl.pallas_call(
        functools.partial(
            back_kernel, pairs=pairs, qb=qb, hb=hb, steps=steps, bits=bits, fast=fast, chunks=chunks, plan=plan
        ),
        out_shape=tuple(jax.ShapeDtypeStruct(s, t) for s, t in shapes),
        grid=(2 * steps + 2 + steps * ratio,),
        in_specs=in_specs,
        out_specs=tuple(out_specs),
        scratch_shapes=scratch,
        compiler_params=pltpu.CompilerParams(**params),
        cost_estimate=pl.CostEstimate(
            flops=16 * nq * keys * width, bytes_accessed=300 * 2**20, transcendentals=0
        ),
    )(*operands)


norm_epsilon = 1e-05


def mm(a, b):
    return jnp.dot(a, b, preferred_element_type=F32)


def normalize(value):
    center = value - jnp.mean(value, axis=-1, keepdims=True)
    spread = jnp.mean(center * center, axis=-1, keepdims=True)
    root = lax.rsqrt(spread + norm_epsilon)
    return center * root, root


def normalize_back(grad, normed, root):
    return root * (
        grad
        - jnp.mean(grad, axis=-1, keepdims=True)
        - normed * jnp.mean(grad * normed, axis=-1, keepdims=True)
    )


def gelu_parts(u):
    t = 1.0 / (1.0 + (0.3275911 * 0.7071067811865476) * jnp.abs(u))
    e = jnp.exp(-0.5 * u * u)
    poly = t * (
        0.254829592 + t * (-0.284496736 + t * (1.421413741 + t * (-1.453152027 + t * 1.061405429)))
    )
    tail = 0.5 * e * poly
    below = jnp.where(u >= 0, 1.0 - tail, tail)
    return u * below, below + u * (e * 0.3989422804014327)


def swap_dp(x, bit):
    n = lax.axis_size("dp")
    return lax.ppermute(x, "dp", [(i, i ^ bit) for i in range(n)])


def swap_head(x):
    return lax.ppermute(x, "head", [(0, 1), (1, 0)])


def dp_bits():
    n, bit, out = lax.axis_size("dp"), 1, []
    while bit < n:
        out.append(bit)
        bit *= 2
    return out


def bit_of(bit):
    return (lax.axis_index("dp") // bit) % 2


def in_order(first, mine, theirs):
    low = jnp.where(first == 0, mine, theirs)
    high = jnp.where(first == 0, theirs, mine)
    return jnp.concatenate([low, high], axis=0)


def rows_of(x, index, rows):
    return lax.dynamic_slice_in_dim(x, index * rows, rows, 0)


def halve(g, bit):
    rows = g.shape[0] // 2
    b = bit_of(bit)
    got = swap_dp(rows_of(g, 1 - b, rows), bit)
    return (rows_of(g, b, rows).astype(F32) + got.astype(F32)).astype(BF16)


def reduce_grad(own, other, head_first):
    bits = dp_bits()
    own, other = halve(own, 1), halve(other, 1)
    if not head_first:
        own, other = halve(own, 2), halve(other, 2)
    g = (own.astype(F32) + swap_head(other).astype(F32)).astype(BF16)
    for bit in bits[1 if head_first else 2 :]:
        g = halve(g, bit)
    for bit in reversed(bits):
        g = in_order(bit_of(bit), g, swap_dp(g, bit))
    return g.astype(F32)


BACK_CHUNKS = 2
BACK_PLAN = (
    ((0, 0, 0), (0, 1, 0), (0, 2, 0), (0, 3, 0), (0, 4, 0), (2, 0, 1), (2, 1, 1), (3, 2, 1), (3, 3, 1), (4, 4, 1), (7, 0, 2), (7, 1, 2), (9, 4, 2), (10, 1, 3), (10, 2, 2), (10, 8, 0), (10, 5, 0), (10, 6, 0), (10, 7, 0), (11, 5, 1), (11, 6, 1), (12, 1, 4), (12, 2, 3), (12, 7, 1), (13, 3, 2), (14, 1, 5), (14, 2, 4), (14, 5, 2), (15, 0, 3), (15, 4, 3), (15, 6, 2), (16, 1, 6), (16, 2, 5), (17, 0, 4), (17, 4, 4), (17, 7, 2), (18, 2, 6), (18, 1, 7), (18, 9, 0), (18, 3, 3), (18, 0, 5), (18, 4, 5), (18, 8, 1), (18, 2, 7), (18, 0, 6), (18, 4, 6), (18, 5, 3), (18, 3, 4), (18, 1, 8), (18, 6, 3), (18, 1, 9), (18, 0, 7), (18, 4, 7), (18, 3, 5), (18, 7, 3), (18, 5, 4), (18, 2, 8), (18, 9, 1), (18, 6, 4), (18, 2, 9), (18, 9, 2), (18, 7, 4), (18, 3, 6), (18, 5, 5), (18, 0, 8), (18, 6, 5), (18, 7, 5), (18, 3, 7), (18, 0, 9), (18, 4, 8), (18, 5, 6), (18, 9, 3), (18, 6, 6), (18, 4, 9), (18, 7, 6), (18, 5, 7), (18, 9, 4), (18, 6, 7), (18, 3, 8), (18, 7, 7), (18, 9, 5), (18, 3, 9), (18, 5, 8), (18, 5, 9), (18, 6, 8), (18, 6, 9), (18, 7, 8), (18, 7, 9)),
    (False, True, True, True, False, False, False, False),
)


def row_sums(x):
    return jnp.sum(x, axis=0, keepdims=True)


def ffn_kernel(
    x, cot, ctx_a, ctx_b, ow_a, ow_b, params, small_a, small_b, uw_a, uw_b, dw_a, dw_b,
    out, first, do_a, do_b, go_a, go_b, pre_a, pre_b, gd_a, gd_b, gu_a, gu_b,
    uw, dw, act, slope, gd, gu, sem_in, sem_out,
    *, heads, chunk,
):
    width = ctx_a.shape[1]
    model = x.shape[1]
    hidden = uw_a.shape[1]
    per = hidden // chunk
    loads = []
    for s, (u, d) in enumerate(((uw_a, dw_a), (uw_b, dw_b))):
        for i in range(per):
            n = s * per + i
            cols = slice(i * chunk, (i + 1) * chunk)
            loads.append(
                (
                    pltpu.make_async_copy(u.at[:, cols], uw.at[n], sem_in.at[n]),
                    pltpu.make_async_copy(d.at[cols, :], dw.at[n], sem_in.at[2 * per + n]),
                )
            )
    for pair in loads:
        for copy in pair:
            copy.start()
    gain1, shift1, gain2, shift2, output_shift, down_shift = (params[i : i + 1, :] for i in range(6))

    def put(i, vector):
        for o in (pre_a, pre_b):
            for n in range(model // width):
                o[i * (model // width) + n : i * (model // width) + n + 1, :] = vector[
                    :, n * width : (n + 1) * width
                ]

    attend = dot_nn(ctx_a[...], ow_a[...]) + dot_nn(ctx_b[...], ow_b[...]) + output_shift
    n1, root1 = normalize(x[...].astype(F32) + attend)
    normed = n1 * gain1 + shift1
    low = normed.astype(BF16)
    feed = normed + down_shift
    for n in range(2 * per):
        small = (small_a, small_b)[n // per]
        at = heads + 2 + (n % per) * (chunk // width)
        bias = jnp.concatenate([small[at + i : at + i + 1, :] for i in range(chunk // width)], axis=1)
        loads[n][0].wait()
        a, slope_n = gelu_parts(dot_nn(low, uw[n]) + bias)
        act[n] = a.astype(BF16)
        slope[n] = slope_n.astype(BF16)
        loads[n][1].wait()
        feed = feed + dot_nn(act[n], dw[n])
    n2, root2 = normalize(feed)
    out[...] = n2 * gain2 + shift2
    g = cot[...].astype(F32)
    put(2, row_sums(g * n2))
    put(3, row_sums(g))
    back = normalize_back(g * gain2, n2, root2)
    back_feed = back.astype(BF16)
    put(5, row_sums(back_feed.astype(F32)))
    stores = []
    for n in range(2 * per):
        s, i = n // per, n % per
        cols = slice(i * chunk, (i + 1) * chunk)
        gd[n] = dot_tn(act[n], back_feed).astype(BF16)
        stores.append(pltpu.make_async_copy(gd.at[n], (gd_a, gd_b)[s].at[cols, :], sem_out.at[n]))
        stores[-1].start()
        back_up = (dot_nt(back_feed, dw[n]) * slope[n].astype(F32)).astype(BF16)
        total = row_sums(back_up.astype(F32))
        for j in range(chunk // width):
            at = 6 * (model // width) + i * (chunk // width) + j
            (pre_a, pre_b)[s][at : at + 1, :] = total[:, j * width : (j + 1) * width]
        gu[n] = dot_tn(low, back_up).astype(BF16)
        stores.append(
            pltpu.make_async_copy(gu.at[n], (gu_a, gu_b)[s].at[:, cols], sem_out.at[2 * per + n])
        )
        stores[-1].start()
        back = back + dot_nt(back_up, uw[n])
    put(0, row_sums(back * n1))
    put(1, row_sums(back))
    back = normalize_back(back * gain1, n1, root1)
    first[...] = back
    back_attend = back.astype(BF16)
    put(4, row_sums(back_attend.astype(F32)))
    for ctx, ow, do, go in ((ctx_a, ow_a, do_a, go_a), (ctx_b, ow_b, do_b, go_b)):
        do[...] = dot_nt(back_attend, ow[...]).astype(BF16)
        go[...] = dot_tn(back_attend, ctx[...]).astype(BF16)
    for copy in stores:
        copy.wait()


def feed_forward(x, cot, contexts, output_weights, params, smalls, up_weights, down_weights, heads, chunk=768):
    nq, model = x.shape
    width = contexts[0].shape[1]
    hidden = up_weights[0].shape[1]
    n = 2 * hidden // chunk
    here = pl.BlockSpec(memory_space=pltpu.VMEM)
    anywhere = pl.BlockSpec(memory_space=pl.ANY)
    pre_rows = 6 * (model // width) + hidden // width
    shape = jax.ShapeDtypeStruct
    return pl.pallas_call(
        functools.partial(ffn_kernel, heads=heads, chunk=chunk),
        out_shape=(
            shape((nq, model), F32),
            shape((nq, model), F32),
            shape((nq, width), BF16),
            shape((nq, width), BF16),
            shape((model, width), BF16),
            shape((model, width), BF16),
            shape((pre_rows, width), F32),
            shape((pre_rows, width), F32),
            shape((hidden, model), BF16),
            shape((hidden, model), BF16),
            shape((model, hidden), BF16),
            shape((model, hidden), BF16),
        ),
        in_specs=[here] * 9 + [anywhere] * 4,
        out_specs=(here,) * 8 + (anywhere,) * 4,
        scratch_shapes=[
            pltpu.VMEM((n, model, chunk), BF16),
            pltpu.VMEM((n, chunk, model), BF16),
            pltpu.VMEM((n, nq, chunk), BF16),
            pltpu.VMEM((n, nq, chunk), BF16),
            pltpu.VMEM((n, chunk, model), BF16),
            pltpu.VMEM((n, model, chunk), BF16),
            pltpu.SemaphoreType.DMA((2 * n,)),
            pltpu.SemaphoreType.DMA((2 * n,)),
        ],
        compiler_params=pltpu.CompilerParams(vmem_limit_bytes=VM),
        cost_estimate=pl.CostEstimate(
            flops=12 * nq * model * 2 * hidden, bytes_accessed=100 * 2**20, transcendentals=nq * 4 * hidden
        ),
    )(x, cot, *contexts, *output_weights, params, *smalls, *up_weights, *down_weights)


def finish_kernel(index, *refs, count, heads, scale):
    refs = list(refs)
    take = lambda n: [refs.pop(0) for _ in range(n)]
    down, up, out, *project = take(6)
    down_piece, up_piece, out_piece, *project_piece = take(6)
    tokens_t, first, sums, params, small = take(5)
    project_w, out_w, up_w, down_w = take(4)
    project_a, query_a, value_a, out_a, out_shift_a, gain1_a, shift1_a = take(7)
    up_a, up_bias_a, down_a, down_shift_a, gain2_a, shift2_a, *table_a = take(9)
    tokens_o, project_o, query_o, value_o, out_o, out_shift_o, gain1_o, shift1_o = take(8)
    up_o, up_bias_o, down_o, down_shift_o, gain2_o, shift2_o, *table_o = take(9)
    project_r, query_r, value_r, out_r, out_shift_r, gain1_r, shift1_r = take(7)
    up_r, up_bias_r, down_r, down_shift_r, gain2_r, shift2_r, *table_r = take(9)
    wide = lambda ref: ref[...].astype(F32)
    renew = lambda average, weight, grad: 0.5 * average + 0.5 * (weight - grad * scale)

    down_o[...] = wide(down)
    up_o[...] = wide(up)
    out_o[...] = jnp.transpose(wide(out))
    for i in range(3):
        project_o[i] = wide(project[i])
    tokens_o[...] = first[...] + jnp.transpose(tokens_t[...])

    @pl.when(pl.program_id(0) == 0)
    def _():
        up_r[...] = renew(up_a[...], wide(up_w), wide(up_piece))
        down_r[...] = renew(down_a[...], wide(down_w), wide(down_piece))
        out_r[...] = renew(out_a[...], jnp.transpose(wide(out_w)), wide(out_piece))
        for i in range(3):
            project_r[i] = renew(project_a[i], project_w[i].astype(F32), wide(project_piece[i]))
        width = sums.shape[1]

        def vector(ref, at, n):
            return jnp.concatenate([ref[at + i : at + i + 1, :] for i in range(n)], axis=1)

        def flat(o, r, a, weight, grad):
            n = a.shape[0]
            o[...] = grad.reshape(n)
            r[...] = renew(a[...], weight.reshape(n), grad.reshape(n))

        flat(query_o, query_r, query_a, small[heads : heads + 1, :], sums[8:9, :])
        flat(value_o, value_r, value_a, small[heads + 1 : heads + 2, :], sums[16:17, :])
        two = params.shape[1] // width
        commons = (
            (gain1_o, gain1_r, gain1_a),
            (shift1_o, shift1_r, shift1_a),
            (gain2_o, gain2_r, gain2_a),
            (shift2_o, shift2_r, shift2_a),
            (out_shift_o, out_shift_r, out_shift_a),
            (down_shift_o, down_shift_r, down_shift_a),
        )
        for i, (o, r, a) in enumerate(commons):
            flat(o, r, a, params[i : i + 1, :], vector(sums, 24 + two * i, two))
        many = up_bias_a.shape[0] // width
        flat(
            up_bias_o, up_bias_r, up_bias_a, vector(small, heads + 2, many), vector(sums, 24 + 6 * two, many)
        )
        for t, (o, r, a) in enumerate(zip(table_o, table_r, table_a)):
            n = a.shape[1]
            grad = sums[0:heads, t * 128 : t * 128 + n]
            o[...] = grad
            r[...] = renew(a[...], small[0:heads, t * 128 : t * 128 + n], grad)


def finish(index, totals, tokens_t, first, sums, params, small, weights, averages, count, tokens_count, heads):
    swap = lambda a: a.transpose(1, 0, 2) if a.ndim == 3 else a.T
    turned = (0, 3, 13, 14, 15)
    averages = [swap(a) if i in turned else a for i, a in enumerate(averages)]
    down, up, out, *project = totals
    model = first.shape[1]
    nq = first.shape[0]
    width = project[0].shape[1]
    steps = model // 128
    full = lambda a: pl.BlockSpec(a.shape, lambda i, d: (0,) * len(a.shape))
    rows = lambda a: pl.BlockSpec((a.shape[0] // steps, a.shape[1]), lambda i, d: (i, 0))
    piece = lambda a: pl.BlockSpec(
        (a.shape[0] // count, *a.shape[1:]), lambda i, d: (d[0],) + (0,) * (len(a.shape) - 1)
    )
    columns = lambda n: pl.BlockSpec((n, 128), lambda i, d: (0, i))
    shape = lambda s: jax.ShapeDtypeStruct(s, F32)
    project_w, out_w, up_w, down_w = weights
    in_specs = [rows(a) for a in totals] + [piece(a) for a in totals]
    in_specs += [rows(tokens_t), columns(nq), full(sums), full(params), full(small)]
    project_spec = pl.BlockSpec((3, model // count, width), lambda i, d: (0, d[0], 0))
    in_specs += [project_spec, full(out_w), piece(up_w), piece(down_w)] + [full(a) for a in averages]
    grads = [
        shape((3, model, width)), shape((width,)), shape((width,)), shape((width, model)), shape((model,)),
        shape((model,)), shape((model,)), shape(up.shape), shape((up.shape[1],)), shape(down.shape),
        shape((model,)), shape((model,)), shape((model,)), *(shape(a.shape) for a in averages[13:]),
    ]
    specs = [full(g) for g in grads]
    specs[0] = pl.BlockSpec((3, 128, width), lambda i, d: (0, i, 0))
    specs[3] = columns(width)
    specs[7] = rows(up)
    specs[9] = rows(down)
    tokens, *results = pl.pallas_call(
        functools.partial(finish_kernel, count=count, heads=heads, scale=1.0 / tokens_count),
        out_shape=(shape((nq, model)), *grads, *(shape(a.shape) for a in averages)),
        grid_spec=pltpu.PrefetchScalarGridSpec(
            num_scalar_prefetch=1,
            grid=(steps,),
            in_specs=in_specs,
            out_specs=(columns(nq), *specs, *(full(a) for a in averages)),
        ),
        compiler_params=pltpu.CompilerParams(vmem_limit_bytes=VM),
        cost_estimate=pl.CostEstimate(flops=2**24, bytes_accessed=40 * 2**20, transcendentals=0),
    )(index, *totals, *totals, tokens_t, first, sums, params, small, *weights, *averages)
    grads, renewed = results[:16], results[16:]
    grads = [swap(a) if i in turned and i != 3 else a for i, a in enumerate(grads)]
    return tokens, *grads, *(swap(a) if i in turned else a for i, a in enumerate(renewed))


def local(
    tokens,
    cotangent,
    form_number,
    sequence_bucket,
    horizontal_bucket,
    vertical_bucket,
    project_weight,
    query_bias,
    value_bias,
    output_weight,
    output_bias,
    first_gain,
    first_shift,
    up_weight,
    up_bias,
    down_weight,
    down_bias,
    second_gain,
    second_shift,
    sequence_table,
    horizontal_table,
    vertical_table,
    project_weight_average,
    query_bias_average,
    value_bias_average,
    output_weight_average,
    output_bias_average,
    first_gain_average,
    first_shift_average,
    up_weight_average,
    up_bias_average,
    down_weight_average,
    down_bias_average,
    second_gain_average,
    second_shift_average,
    sequence_table_average,
    horizontal_table_average,
    vertical_table_average,
):
    total_rows, model_width = tokens.shape
    local_width = project_weight.shape[2]
    local_heads = sequence_table.shape[1]
    hidden = up_weight.shape[1]
    share_rows = total_rows // lax.axis_size("head")
    head_index = lax.axis_index("head")
    share_start = head_index * share_rows
    block_rows = 128
    buckets = (sequence_bucket, horizontal_bucket, vertical_bucket)
    tables = (sequence_table, horizontal_table, vertical_table)
    bits = tuple((t.shape[0] - 1).bit_length() for t in tables)
    project_stack = project_weight.transpose(1, 0, 2)
    flat_project = project_stack.reshape(3 * model_width, local_width)

    params = jnp.concatenate(
        [first_gain, first_shift, second_gain, second_shift, output_bias, down_bias]
    ).reshape(6, model_width).astype(F32)
    lanes = [jnp.pad(t.T, ((0, 0), (0, local_width // 3 - t.shape[0]))) for t in tables]
    small = jnp.concatenate(
        [
            jnp.concatenate(lanes, axis=1),
            jnp.concatenate([query_bias, value_bias, up_bias]).reshape(-1, local_width),
        ],
        axis=0,
    ).astype(F32)
    small = jnp.pad(small, ((0, 16 - small.shape[0]), (0, 0)))
    smalls, project_weights = [small], [flat_project]
    output_weights, up_weights, down_weights = [output_weight], [up_weight], [down_weight]

    form_row = form_number.reshape(total_rows)
    form_own = lax.dynamic_slice_in_dim(form_row, share_start, share_rows, 0)
    code = encode(
        [rows_of(b, head_index, share_rows) for b in buckets], form_own[:, None] == form_row[None, :]
    )
    own_tokens = rows_of(tokens, head_index, share_rows)

    scaled, keys, values_t, probs, contexts = [], [], [], [], []
    for s in range(2):
        wq, wk, wv = (project_weights[s][i * model_width : (i + 1) * model_width] for i in range(3))
        bq = smalls[s][local_heads : local_heads + 1]
        bv = smalls[s][local_heads + 1 : local_heads + 2]
        q = ((mm(own_tokens, wq) + bq) * 0.125).astype(BF16)
        q = q * jnp.array(2.0**SCALE_BITS, BF16)
        k = mm(tokens, wk).astype(BF16)
        kt = dot_general_t(wk, tokens).astype(BF16)
        v = (mm(tokens, wv) + bv).astype(BF16)
        vt = (dot_general_t(wv, tokens) + bv.reshape(-1, 1)).astype(BF16)
        if s == 0:
            fetch = (
                ("small", (0, -1, -1), small),
                ("all", (0, 3, 7), flat_project),
                ("all", (0, 4, 7), output_weight),
                ("first", (0, -1, -1), up_weight),
            )
        else:
            fetch = (("rest", (-1, 0, 4), up_part), ("all", (0, 4, 8), down_weight))
        p, context, *fetched = attend_fwd(code, smalls[s], q, kt, v, fetch, s, qb=block_rows)
        if s == 0:
            smalls.append(fetched[0])
            project_weights.append(fetched[1])
            output_weights.append(fetched[2])
            up_part = fetched[3]
        else:
            up_weights.append(fetched[0])
            down_weights.append(fetched[1])
        scaled.append(q)
        keys.append(k)
        values_t.append(vt)
        probs.append(p)
        contexts.append(context)
    (
        layer_output, back_first, back_own, back_other, out_own, out_other, pre_own, pre_other, *grads
    ) = feed_forward(
        own_tokens, cotangent, contexts, output_weights, params, smalls, up_weights, down_weights, local_heads
    )

    sides = [
        (scaled[s], keys[s], values_t[s], (back_own, back_other)[s], probs[s]) for s in range(2)
    ]
    pre = (pre_own, pre_other)
    fast = lax.axis_size("dp") == 16
    results = attend_backward(
        sides,
        code,
        tokens.T,
        project_weights,
        bits,
        (*grads, out_own, out_other),
        pre,
        2,
        fast,
        BACK_PLAN,
        BACK_CHUNKS,
        qb=block_rows,
    )
    token_count = total_rows * lax.axis_size("dp")
    group_count = lax.axis_size("dp")
    group_index = lax.axis_index("dp")
    if fast:
        width = model_width // group_count
        output_piece = lax.dynamic_slice_in_dim(output_weight, group_index * width, width, 1)
        averages = (
            project_weight_average, query_bias_average, value_bias_average, output_weight_average,
            output_bias_average, first_gain_average, first_shift_average, up_weight_average, up_bias_average,
            down_weight_average, down_bias_average, second_gain_average, second_shift_average,
            sequence_table_average, horizontal_table_average, vertical_table_average,
        )
        return layer_output, *finish(
            jnp.full((1,), group_index, I32),
            results[:6],
            results[6],
            back_first,
            results[7],
            params,
            small,
            (project_stack, output_piece, up_weight, down_weight),
            averages,
            group_count,
            token_count,
            local_heads,
        )
    tokens_gradient, sums, far, sums_other = results[:4]
    tokens_gradient = tokens_gradient + swap_head(far).astype(F32)
    sums = sums + swap_head(sums_other)
    for bit in dp_bits():
        sums = sums + swap_dp(sums, bit)
    down_total, up_total = reduce_grad(*grads[:2], True), reduce_grad(*grads[2:], False)
    output_total = reduce_grad(out_own, out_other, True)
    project_total = [reduce_grad(results[4 + i], results[7 + i], False) for i in range(3)]
    tokens_gradient = back_first + tokens_gradient.T
    project_total = jnp.stack(project_total, axis=1)
    output_total = output_total.T
    query_bias_total, value_bias_total = sums[8], sums[16]
    tail = sums[24:].reshape(-1)
    (
        first_gain_total,
        first_shift_total,
        second_gain_total,
        second_shift_total,
        output_bias_total,
        down_bias_total,
    ) = (tail[i * model_width : (i + 1) * model_width] for i in range(6))
    up_bias_total = tail[6 * model_width :]
    sequence_total, horizontal_total, vertical_total = (
        sums[:local_heads, i * 128 : i * 128 + t.shape[0]].T for i, t in enumerate(tables)
    )
    up_weight_total, down_weight_total, output_weight_total = up_total, down_total, output_total

    def renew(average, weight, gradient):
        return 0.5 * average + 0.5 * (weight.astype(jnp.float32) - gradient / token_count)

    def part_of(array, along):
        width = array.shape[along] // group_count
        return lax.dynamic_slice_in_dim(array, group_index * width, width, along)

    return (
        layer_output,
        tokens_gradient,
        project_total,
        query_bias_total,
        value_bias_total,
        output_weight_total,
        output_bias_total,
        first_gain_total,
        first_shift_total,
        up_weight_total,
        up_bias_total,
        down_weight_total,
        down_bias_total,
        second_gain_total,
        second_shift_total,
        sequence_total,
        horizontal_total,
        vertical_total,
        renew(project_weight_average, part_of(project_weight, 0), part_of(project_total, 0)),
        renew(query_bias_average, query_bias, query_bias_total),
        renew(value_bias_average, value_bias, value_bias_total),
        renew(output_weight_average, part_of(output_weight, 1), part_of(output_weight_total, 1)),
        renew(output_bias_average, output_bias, output_bias_total),
        renew(first_gain_average, first_gain, first_gain_total),
        renew(first_shift_average, first_shift, first_shift_total),
        renew(up_weight_average, part_of(up_weight, 0), part_of(up_weight_total, 0)),
        renew(up_bias_average, up_bias, up_bias_total),
        renew(down_weight_average, part_of(down_weight, 0), part_of(down_weight_total, 0)),
        renew(down_bias_average, down_bias, down_bias_total),
        renew(second_gain_average, second_gain, second_gain_total),
        renew(second_shift_average, second_shift, second_shift_total),
        renew(sequence_table_average, sequence_table, sequence_total),
        renew(horizontal_table_average, horizontal_table, horizontal_total),
        renew(vertical_table_average, vertical_table, vertical_total),
    )


def solution(mesh):
    in_specs = (
        P("dp", None),
        P(("dp", "head"), None),
        P("dp", None),
        P("dp", None),
        P("dp", None),
        P("dp", None),
        P(None, None, "head"),
        P("head"),
        P("head"),
        P("head", None),
        P(),
        P(),
        P(),
        P(None, "head"),
        P("head"),
        P("head", None),
        P(),
        P(),
        P(),
        P(None, "head"),
        P(None, "head"),
        P(None, "head"),
        P("dp", None, "head"),
        P("head"),
        P("head"),
        P("head", "dp"),
        P(),
        P(),
        P(),
        P("dp", "head"),
        P("head"),
        P(("head", "dp"), None),
        P(),
        P(),
        P(),
        P(None, "head"),
        P(None, "head"),
        P(None, "head"),
    )
    out_specs = (
        P(("dp", "head"), None),
        P(("dp", "head"), None),
        P(None, None, "head"),
        P("head"),
        P("head"),
        P("head", None),
        P(),
        P(),
        P(),
        P(None, "head"),
        P("head"),
        P("head", None),
        P(),
        P(),
        P(),
        P(None, "head"),
        P(None, "head"),
        P(None, "head"),
        P("dp", None, "head"),
        P("head"),
        P("head"),
        P("head", "dp"),
        P(),
        P(),
        P(),
        P("dp", "head"),
        P("head"),
        P(("head", "dp"), None),
        P(),
        P(),
        P(),
        P(None, "head"),
        P(None, "head"),
        P(None, "head"),
    )
    return jax.shard_map(local, mesh=mesh, in_specs=in_specs, out_specs=out_specs, check_vma=False)
```

```python
import functools
import jax
import jax.numpy as jnp
from jax import lax
from jax.experimental import pallas as pl
from jax.sharding import PartitionSpec as P
from jax.experimental.pallas import tpu as pltpu

F32, BF16, I32 = jnp.float32, jnp.bfloat16, jnp.int32
SCALE_BITS = 27
STEP = 2.0**11
VM = 56 * 2**20
BACK_VM = 60 * 2**20
SAME = 2**17


def encode(buckets, same):
    seq, hor, ver = buckets
    return seq + 32 * hor + 2048 * ver + jnp.where(same, SAME, 0)


def buckets_of(code):
    return code & 31, (code >> 5) & 63, (code >> 11) & 63


def dot_nt(a, b):
    return lax.dot_general(a, b, (((1,), (1,)), ((), ())), preferred_element_type=F32)


def dot_tn(a, b):
    return lax.dot_general(a, b, (((0,), (0,)), ((), ())), preferred_element_type=F32)


def dot_general_t(w, x):
    return lax.dot_general(w, x, (((0,), (1,)), ((), ())), preferred_element_type=F32)


def dot_tt(a, b):
    return lax.dot_general(a, b, (((0,), (1,)), ((), ())), preferred_element_type=F32)


def dot_nn(a, b):
    return lax.dot_general(a, b, (((1,), (0,)), ((), ())), preferred_element_type=F32)


def split_pair(x):
    lane = lax.broadcasted_iota(I32, x.shape, 1)
    zero = jnp.zeros_like(x)
    return jnp.concatenate([jnp.where(lane < 64, x, zero), jnp.where(lane < 64, zero, x)], axis=0)


def partner(axis, bit):
    i = lax.axis_index(axis)
    low = lax.rem(lax.div(i, bit), 2)
    return {axis: i + bit * (1 - 2 * low)}


def dp_bit(bit):
    return lax.rem(lax.div(lax.axis_index("dp"), bit), 2)


def greet(partners):
    barrier = pltpu.get_barrier_semaphore()
    for p in partners:
        pl.semaphore_signal(barrier, inc=1, device_id=p, device_id_type=pl.DeviceIdType.MESH)
    pl.semaphore_wait(barrier, len(partners))


def remote(src, dst, send, recv, to):
    return pltpu.make_async_remote_copy(
        src_ref=src,
        dst_ref=dst,
        send_sem=send,
        recv_sem=recv,
        device_id=to,
        device_id_type=pl.DeviceIdType.MESH,
    )


def fetch_copies(mode, source, out, send, recv):
    if mode == "small":
        return [remote(source, out, send.at[0], recv.at[0], partner("head", 1)), None, None], []
    rows = source.shape[0] if mode == "rest" else source.shape[0] // 4
    quarter = 2 * dp_bit(1) + dp_bit(2)
    one = pl.ds(pl.multiple_of(quarter * rows, rows), rows)
    two = pl.ds(pl.multiple_of(dp_bit(1) * (2 * rows), 2 * rows), 2 * rows)
    hops, local = [None, None, None], []
    if mode == "first":
        hops[0] = remote(source.at[one], out, send.at[0], recv.at[0], partner("head", 1))
    else:
        if mode == "all":
            hops[0] = remote(source.at[one], out.at[one], send.at[0], recv.at[0], partner("head", 1))
            quarter_ref = out.at[one]
        else:
            quarter_ref = source
            local.append(pltpu.make_async_copy(source, out.at[one], send.at[0]))
        hops[1] = remote(quarter_ref, out.at[one], send.at[1], recv.at[1], partner("dp", 2))
        hops[2] = remote(out.at[two], out.at[two], send.at[2], recv.at[2], partner("dp", 1))
    return hops, local


def fetched_shape(mode, w):
    rows = {"all": 1, "small": 1, "first": 0.25, "rest": 4}[mode] * w.shape[0]
    return jax.ShapeDtypeStruct((int(rows), w.shape[1]), w.dtype)


def fwd_kernel(*refs, pairs, qb, modes, points, steps):
    n = len(modes)
    code, tab, q, kt, v = refs[:5]
    sources = refs[5 : 5 + n]
    p_out, c_out = refs[5 + n : 7 + n]
    outs = refs[7 + n : 7 + 2 * n]
    b_ref, t_ref, send, recv = refs[7 + 2 * n :]
    keys = v.shape[0]
    chunk = 128
    step = pl.program_id(0)
    hops, local = [], []
    for i in range(n):
        h, l = fetch_copies(modes[i], sources[i], outs[i], send.at[i], recv.at[i])
        hops.append(h)
        local += l

    def point(now):
        for i in range(n):
            for hop in range(3):
                if points[i][hop] == now:
                    if hop and hops[i][hop - 1] is not None:
                        hops[i][hop - 1].wait_recv()
                    hops[i][hop].start()

    @pl.when(step == 0)
    def _():
        greet([partner("head", 1), partner("dp", 2), partner("dp", 1)])
        for copy in local:
            copy.start()
        for j in range(pairs):
            for t in range(3):
                ls = slice(t * chunk, (t + 1) * chunk)
                fixed = [jnp.round(tab[2 * j + g : 2 * j + g + 1, ls] * STEP).astype(I32) for g in range(2)]
                t_ref[8 * (3 * j + t) : 8 * (3 * j + t) + 8, :] = jnp.broadcast_to(
                    fixed[0] * 65536 + fixed[1], (8, chunk)
                )
        point(0)

    for now in sorted(set(sum(points, ()))):
        if 0 < now < 2 * steps and now % 2 == 0:

            @pl.when(step == now // 2)
            def _():
                if local and now == min(p[2] for p, m in zip(points, modes) if m == "rest"):
                    for copy in local:
                        copy.wait()
                point(now)

    tbs = [t_ref[8 * i : 8 * i + 8, :] for i in range(3 * pairs)]

    def gather(r, _):
        rs = pl.ds(pl.multiple_of(r * 8, 8), 8)
        for c in range(keys // chunk):
            ls = slice(c * chunk, (c + 1) * chunk)
            sums = [None] * pairs
            for t, idx in enumerate(buckets_of(code[rs, ls])):
                for j in range(pairs):
                    g = jnp.take_along_axis(tbs[3 * j + t], idx, axis=1, mode="promise_in_bounds")
                    sums[j] = g if t == 0 else sums[j] + g
            for j in range(pairs):
                b_ref[j, rs, ls] = sums[j]
        return 0

    lax.fori_loop(0, qb // 8, gather, 0)
    for now in sorted(set(sum(points, ()))):
        if 0 < now < 2 * steps and now % 2 == 1:

            @pl.when(step == now // 2)
            def _():
                point(now)

    same = code[...] >= SAME
    def pair(j, _):
        lanes = pl.ds(pl.multiple_of(j * 128, 128), 128)
        q2 = split_pair(q[:, lanes])
        s2 = dot_nn(q2, kt[lanes, :])
        bias = b_ref[j]
        for g in range(2):
            x = s2[g * qb : (g + 1) * qb] + (bias << 16 if g else bias).astype(F32)
            x = jnp.where(same, x, -1e30)
            top = jnp.max(x, axis=1, keepdims=True)
            e = jnp.exp2((x - top) * (1.4426950408889634 * 2.0**-SCALE_BITS))
            inv = 1.0 / jnp.sum(e, axis=1, keepdims=True)
            p_out[2 * j + g] = (e * inv).astype(BF16)
        c0 = dot_nn(p_out[2 * j], v[:, lanes])
        c1 = dot_nn(p_out[2 * j + 1], v[:, lanes])
        lane = lax.broadcasted_iota(I32, c0.shape, 1)
        c_out[:, lanes] = jnp.where(lane < 64, c0, c1).astype(BF16)
        return 0

    lax.fori_loop(0, pairs, pair, 0)

    @pl.when(step == steps - 1)
    def _():
        for now in range(2 * steps, max(sum(points, ())) + 1):
            point(now)
        for i in range(n):
            last = [copy for copy in hops[i] if copy is not None][-1]
            last.wait_recv()
        for i in range(n):
            for copy in hops[i]:
                if copy is not None:
                    copy.wait_send()


def attend_fwd(code, tab, q, kt, v, fetch, collective_id, qb=128):
    nq, width = q.shape
    keys = v.shape[0]
    pairs = width // 128
    modes = tuple(f[0] for f in fetch)
    points = tuple(f[1] for f in fetch)
    sources = [f[2] for f in fetch]
    n = len(fetch)
    steps = nq // qb
    full = lambda a: pl.BlockSpec(a.shape, lambda i: (0,) * a.ndim)
    anywhere = pl.BlockSpec(memory_space=pl.ANY)
    return pl.pallas_call(
        functools.partial(fwd_kernel, pairs=pairs, qb=qb, modes=modes, points=points, steps=steps),
        out_shape=(
            jax.ShapeDtypeStruct((2 * pairs, nq, keys), BF16),
            jax.ShapeDtypeStruct((nq, width), BF16),
        )
        + tuple(fetched_shape(m, w) for m, w in zip(modes, sources)),
        grid=(steps,),
        in_specs=[
            pl.BlockSpec((qb, keys), lambda i: (i, 0)),
            full(tab),
            pl.BlockSpec((qb, width), lambda i: (i, 0)),
            full(kt),
            full(v),
        ]
        + [full(w) if m == "rest" else anywhere for m, w in zip(modes, sources)],
        out_specs=(
            pl.BlockSpec((2 * pairs, qb, keys), lambda i: (0, i, 0)),
            pl.BlockSpec((qb, width), lambda i: (i, 0)),
        )
        + (anywhere,) * n,
        scratch_shapes=[
            pltpu.VMEM((pairs, qb, keys), I32),
            pltpu.VMEM((pairs * 24, 128), I32),
            pltpu.SemaphoreType.DMA((n, 3)),
            pltpu.SemaphoreType.DMA((n, 3)),
        ],
        compiler_params=pltpu.CompilerParams(
            vmem_limit_bytes=VM, collective_id=collective_id, has_side_effects=True
        ),
        cost_estimate=pl.CostEstimate(
            flops=4 * nq * keys * width, bytes_accessed=90 * 2**20, transcendentals=nq * keys * 2 * pairs
        ),
    )(code, tab, q, kt, v, *sources)


def add_rows(dst, a, b, tile):
    rows = dst[2]

    def body(i, _):
        at = lambda x: pl.ds(pl.multiple_of(x[1] + i * tile, 16), tile)
        dst[0][at(dst), :] = a[0][at(a), :] + b[0][at(b), :]
        return 0

    lax.fori_loop(0, rows // tile, body, 0)


STREAM_SEMS = 17
ORDER_BITS = {"x": 2, "0": 4, "1": 8}


def stream_phases(own, other, kept, piece, full, columns, bufs, send, recv, order):
    half = own.shape[0] // 2
    tile = half // 8
    c = dp_bit(1)
    cut = lambda ref, start, n: ref.at[pl.ds(pl.multiple_of(start, 16), n), columns]
    part = lambda ref, bit, n: ref.at[pl.ds(pl.multiple_of(bit * n, 16), n)]
    hops = [
        [
            remote(cut(g, (1 - c) * half, half), bufs[0].at[m], send.at[m], recv.at[m], partner("dp", 1))
            for m, g in enumerate((own, other))
        ]
    ]
    adds = [
        [
            (bufs[0].at[m], (bufs[0].at[m], 0), (kept[m], 0) if kept else (g.at[:, columns], c * half), half)
            for m, g in enumerate((own, other))
        ]
    ]
    keep = []
    if kept:
        keep = [
            pltpu.make_async_copy(cut(g, c * half, half), kept[m], send.at[15 + m])
            for m, g in enumerate((own, other))
        ]
    n, at, two = half, c * half, True
    spans, bits = [(at, n)], [1]
    for i, axis in enumerate(order):
        buf, before = bufs[i + 1], bufs[i]
        if axis == "y":
            two = False
            hops.append([remote(before.at[1], buf.at[0], send.at[2 + 2 * i], recv.at[2 + 2 * i], partner("head", 1))])
            adds.append([(buf.at[0], (buf.at[0], 0), (before.at[0], 0), n)])
        else:
            n = n // 2
            bit = ORDER_BITS[axis]
            b = dp_bit(bit)
            at = at + b * n
            spans.append((at, n))
            bits.append(bit)
            sems = [2 + 2 * i + m for m in range(2 if two else 1)]
            hops.append(
                [
                    remote(part(before.at[m], 1 - b, n), buf.at[m], send.at[k], recv.at[k], partner("dp", bit))
                    for m, k in enumerate(sems)
                ]
            )
            adds.append([(buf.at[m], (buf.at[m], 0), (before.at[m], b * n), n) for m in range(len(sems))])
    dst, a, b, n = adds[-1][0]
    adds[-1] = [(piece, a, b, n)]
    there = lambda start, n: full.at[pl.ds(pl.multiple_of(start, 16), n), columns]
    back = [remote(piece, there(*spans[-1]), send.at[10], recv.at[10], partner("dp", bits[-1]))]
    for i in range(1, 4):
        ref = there(*spans[-1 - i])
        back.append(remote(ref, ref, send.at[10 + i], recv.at[10 + i], partner("dp", bits[-1 - i])))
    local = pltpu.make_async_copy(piece, there(*spans[-1]), send.at[14])

    def first():
        for copy in hops[0] + keep:
            copy.start()

    def reduce(i):
        def phase():
            for copy in keep if i == 0 else ():
                copy.wait()
            for copy in hops[i]:
                copy.wait_recv()
            for dst, a, b, n in adds[i]:
                add_rows((dst, 0, n), a, b, tile)
            if i < 4:
                for copy in hops[i + 1]:
                    copy.start()
            else:
                local.start()
                back[0].start()

        return phase

    def gather(i):
        def phase():
            if i == 1:
                local.wait()
            back[i - 1].wait_recv()
            back[i].start()

        return phase

    def finish():
        back[3].wait_recv()
        for copy in sum(hops, []) + back:
            copy.wait_send()

    return [first, *(reduce(i) for i in range(5)), *(gather(i) for i in range(1, 4)), finish]


def stream_scratch(rows, columns, order, keep):
    n, two = rows // 2, 2
    shapes = [(2, n, columns)]
    for axis in order:
        if axis == "y":
            two = 1
        else:
            n = n // 2
        shapes.append((two, n, columns))
    shapes.append((n, columns))
    if keep:
        shapes += [(rows // 2, columns)] * 2
    return [pltpu.VMEM(s, BF16) for s in shapes] + [pltpu.SemaphoreType.DMA((STREAM_SEMS,))] * 2


def sum_phases(own, other, bufs, send, recv):
    to = [partner("head", 1)] + [partner("dp", b) for b in (1, 2, 4, 8)]
    hops = [
        remote(other if i == 0 else own.at[i - 1], bufs.at[i], send.at[i], recv.at[i], to[i])
        for i in range(5)
    ]

    def phase(i):
        def run():
            if i:
                hops[i - 1].wait_recv()
                if i > 1:
                    own[i - 1] = own[i - 2] + bufs[i - 1]
                else:
                    own[0] = own[5] + bufs[0]
            if i < 5:
                hops[i].start()
            else:
                for copy in hops:
                    copy.wait_send()

        return run

    return [phase(i) for i in range(6)]


def attend_back(q, k, vt, do, p, ds, at, dq, dk, dv, pairs, qb):
    def pair(j, _):
        lanes = pl.ds(pl.multiple_of(j * 128, 128), 128)
        q2 = split_pair(q[:, lanes])
        do2 = split_pair(do[:, lanes])
        dp2 = dot_nn(do2, vt[lanes, :])
        parts = []
        for g in range(2):
            ps = p[2 * j + g].astype(F32)
            ts = ps * dp2[g * qb : (g + 1) * qb]
            inner = jnp.sum(ts, axis=1, keepdims=True)
            parts.append((ts - ps * inner).astype(BF16))
            ds[2 * j + g, pl.ds(at, qb), :] = parts[g]
        d0 = dot_nn(parts[0], k[:, lanes])
        d1 = dot_nn(parts[1], k[:, lanes])
        lane = lax.broadcasted_iota(I32, d0.shape, 1)
        dq[pl.ds(at, qb), lanes] = jnp.where(lane < 64, d0, d1).astype(BF16) * jnp.array(0.125, BF16)
        dk[lanes, :] += dot_tn(q2, jnp.concatenate(parts, axis=0))
        p2 = jnp.concatenate([p[2 * j], p[2 * j + 1]], axis=0)
        dv[lanes, :] += dot_tn(do2, p2)
        return 0

    lax.fori_loop(0, pairs, pair, 0)


def count_rows(code, ds, at, outs, bits, nq):
    heads = ds.shape[0]

    def rows(r, _):
        rs = pl.ds(pl.multiple_of(at + r * 16, 16), 16)
        dfull = [ds[h, rs, :].astype(F32) for h in range(heads)]
        for half in range(2):
            d8 = [d[half * 8 : half * 8 + 8] for d in dfull]
            packed = code[pl.ds(pl.multiple_of(r * 16 + half * 8, 8), 8), :]
            low = 0
            for t in range(3):
                signs = [(((packed << (31 - low - i)) >> 31) | 1).astype(F32) for i in range(bits[t])]
                low += bits[t]
                rhs = jnp.concatenate(
                    [jnp.concatenate([d, d * signs[0]], axis=0).astype(BF16) for d in d8], axis=0
                )
                first = jnp.concatenate([jnp.ones_like(signs[1]), signs[1]], axis=0).astype(BF16)
                tiles = [first]
                for i in range(2, bits[t]):
                    s2 = jnp.concatenate([signs[i], signs[i]], axis=0).astype(BF16)
                    tiles = tiles + [x * s2 for x in tiles]
                outs[t][...] += dot_nt(jnp.concatenate(tiles, axis=0), rhs)
        return 0

    lax.fori_loop(0, nq // 16, rows, 0)


def table_sums(acc, bits, first, heads):
    n = 2**bits
    high = lax.Precision.HIGHEST
    iota = lambda shape, d: lax.broadcasted_iota(I32, shape, d)
    row, col = iota(acc.shape, 0), iota(acc.shape, 1)
    kept = jnp.where((row & 7) == (col & 7), acc, 0.0)
    shape = (n, acc.shape[0])
    odd = (iota(shape, 1) >> 3) & (iota(shape, 0) >> 1)
    odd = odd ^ (odd >> 4)
    odd = odd ^ (odd >> 2)
    odd = odd ^ (odd >> 1)
    left = (1 - 2 * (odd & 1)).astype(F32)
    shape = (n, acc.shape[1])
    odd = iota(shape, 0) & (iota(shape, 1) >> 3) & 1
    mixed = jnp.dot(left, kept, precision=high, preferred_element_type=F32)
    mixed = mixed * (1 - 2 * odd).astype(F32) * (1.0 / n)
    shape = (8, acc.shape[1])
    head = iota(shape, 0)
    pick = ((iota(shape, 1) >> 4) == head + first) & (head < heads)
    return lax.dot_general(
        pick.astype(F32), mixed, (((1,), (1,)), ((), ())), precision=high, preferred_element_type=F32
    )


def back_kernel(*refs, pairs, qb, hb, steps, bits, fast, chunks, plan):
    refs = list(refs)
    take = lambda n: [refs.pop(0) for _ in range(n)]
    sides = [take(5), take(5)]
    code, xt, *weights = take(4)
    down_all, up_all, out_own, out_other, pre_own, pre_other = take(6)
    hidden = up_all.shape[2]
    down_own, down_other = down_all.at[0:hidden], down_all.at[hidden : 2 * hidden]
    up_own, up_other = up_all.at[0], up_all.at[1]
    full_down, full_up, full_out, full_project = take(4) if fast else [None] * 4
    token_out, sum_out = take(2)
    if fast:
        token_far = None
    else:
        token_far, sum_far = take(2)
        project = take(2)
    ds, dk, dv, dq, dkt, dvt = take(6)
    accs = take(3)
    if fast:
        project = take(2)
        token_far, token_near = take(2)
        sums, sum_other, sum_bufs = take(3)
        token_send, sum_send, sum_recv = take(3)
    step = pl.program_id(0)
    width = 2 * pairs * 64
    nq = qb * steps
    model = xt.shape[0]
    h = lax.axis_index("head")
    near = pl.ds(pl.multiple_of(h * nq, nq), nq)
    far = pl.ds(pl.multiple_of((1 - h) * nq, nq), nq)
    last = 2 * steps + 2 + (steps * qb) // hb

    if fast:
        phases = []
        sources = []
        down_chunks, up_chunks = chunks[:2]
        for own, other, full, pieces in (
            (down_own, down_other, full_down, down_chunks),
            (up_own, up_other, full_up, up_chunks),
        ):
            cols = own.shape[1] // pieces
            for i in range(pieces):
                sources.append((own, other, full, slice(i * cols, (i + 1) * cols), True))
        sources.append((out_own, out_other, full_out, slice(0, width), False))
        for start, stop in chunks[2]:
            sources.append((project[0], project[1], full_project, slice(start, stop), False))
        assert all(slot <= steps for slot, stream, phase in plan[0] if stream < down_chunks and phase < 2)
        cols = down_own.shape[1] // down_chunks
        per = 3 * width // cols
        spare = [project[i // per].at[:, i % per * cols : (i % per + 1) * cols] for i in range(2 * down_chunks)]
        for n, (own, other, full, columns, keep) in enumerate(sources):
            bufs = take(5)
            (piece,) = take(1)
            kept = None
            if keep:
                kept = spare[2 * n : 2 * n + 2] if n < down_chunks else take(2)
            send, recv = take(2)
            phases.append(
                stream_phases(own, other, kept, piece, full, columns, bufs, send, recv, plan[1][n])
            )
        token_hop = remote(token_far, token_near, token_send.at[0], token_send.at[1], partner("head", 1))

        def token_end():
            token_hop.wait_recv()
            token_out[...] = token_out[...] + token_near[...].astype(F32)
            token_hop.wait_send()

        phases.append([token_hop.start, token_end])
        phases.append(sum_phases(sums, sum_other, sum_bufs, sum_send, sum_recv))

        @pl.when(step == 0)
        def _():
            greet([partner("head", 1)] + [partner("dp", b) for b in (1, 2, 4, 8)])

        for now in sorted(set(p[0] for p in plan[0])):
            if now < last:

                @pl.when(step == now)
                def _():
                    for slot, stream, phase in plan[0]:
                        if slot == now:
                            phases[stream][phase]()

    @pl.when(step == 0)
    def _():
        for o in accs:
            o[...] = jnp.zeros_like(o)

    for s in range(2):
        q, k, vt, do, p = sides[s]
        first = s * (steps + 1)

        @pl.when((step >= first) & (step < first + steps))
        def _():
            block = step - first

            @pl.when(block == 0)
            def _():
                dk[...] = jnp.zeros_like(dk)
                dv[...] = jnp.zeros_like(dv)

            at = pl.multiple_of(block * qb, qb)
            side_ds = ds.at[s * 2 * pairs : (s + 1) * 2 * pairs]
            attend_back(q, k, vt, do, p, side_ds, at, dq, dk, dv, pairs, qb)

        @pl.when(step == first + steps)
        def _():
            dkt[...] = (dk[...] * 2.0**-SCALE_BITS).astype(BF16)
            dvt[...] = dv[...].astype(BF16)
            w = weights[s]
            wq, wk, wv = (w[i * model : (i + 1) * model, :] for i in range(3))
            project[s][:, :width] = dot_nn(xt[:, near], dq[...]).astype(BF16)
            project[s][:, width : 2 * width] = dot_nt(xt[...], dkt[...]).astype(BF16)
            project[s][:, 2 * width :] = dot_nt(xt[...], dvt[...]).astype(BF16)
            mine = dot_nt(wq, dq[...]) + dot_nn(wk, dkt[:, near]) + dot_nn(wv, dvt[:, near])
            theirs = dot_nn(wk, dkt[:, far]) + dot_nn(wv, dvt[:, far])
            if s:
                token_out[...] += mine
                token_far[...] = (token_far[...].astype(F32) + theirs).astype(BF16)
            else:
                token_out[...] = mine
                token_far[...] = theirs.astype(BF16)
            bias = sum_other if fast and s else sums.at[5] if fast else sum_far if s else sum_out
            ones = jnp.ones((8, nq), BF16)
            bias[8:16, :] = dot_nn(ones, dq[...])
            ones = jnp.ones((8, xt.shape[1]), BF16)
            bias[16:24, :] = dot_nt(ones, dvt[...])

    @pl.when(step >= 2 * steps + 2)
    def _():
        count_rows(code, ds, (step - 2 * steps - 2) * hb, accs, bits, hb)

    @pl.when(step == last - 1)
    def _():
        if fast:
            outs = (sums.at[5], sum_other)
        else:
            outs = (sum_out, sum_far)
        heads = 2 * pairs
        for s, o in enumerate(outs):
            o[0:8, :] = jnp.zeros((8, width), F32)
            for t, (acc, b) in enumerate(zip(accs, bits)):
                o[0:8, t * 128 : t * 128 + 2**b] = table_sums(acc[...], b, s * heads, heads)
            o[24:, :] = (pre_other if s else pre_own)[...]
        if fast:
            for slot, stream, phase in plan[0]:
                if slot >= last:
                    phases[stream][phase]()
            sum_out[...] = sums[4]


def attend_backward(sides, code, xt, weights, bits, grads, pre, collective_id, fast, plan, chunks, qb=128, hb=64):
    nq, width = sides[0][0].shape
    keys = sides[0][1].shape[0]
    model = xt.shape[0]
    pairs = width // 128
    heads = 2 * pairs
    steps = nq // qb
    ratio = qb // hb
    full = lambda shape: pl.BlockSpec(shape, lambda i: (0,) * len(shape), pipeline_mode=pl.Buffered(1))
    anywhere = pl.BlockSpec(memory_space=pl.ANY)
    in_specs, operands = [], []
    for s in range(2):
        clip = lambda i, s=s: jnp.clip(i - s * (steps + 1), 0, steps - 1)
        row = pl.BlockSpec((qb, width), lambda i, clip=clip: (clip(i), 0))
        big = pl.BlockSpec((heads, qb, keys), lambda i, clip=clip: (0, clip(i), 0))
        in_specs += [row, full((keys, width)), full((width, keys)), row, big]
        operands += list(sides[s])
    in_specs.append(
        pl.BlockSpec((hb, keys), lambda i: (jnp.clip(i - 2 * steps - 2, 0, steps * ratio - 1), 0))
    )
    in_specs += [full(a.shape) for a in (xt, *weights)]
    in_specs += [anywhere] * 2 + [full(a.shape) for a in (*grads[2:], *pre)]
    operands += [code, xt, *weights, *grads, *pre]
    sum_shape = (24 + pre[0].shape[0], width)
    project_shape = (model, 3 * width)
    shapes, out_specs = [], []
    if fast:
        hidden = grads[1].shape[2]
        shapes += [((hidden, model), BF16), ((model, hidden), BF16), ((model, width), BF16), (project_shape, BF16)]
        out_specs += [anywhere] * 4
    shapes += [((model, nq), F32), (sum_shape, F32)]
    if not fast:
        shapes += [((model, nq), BF16), (sum_shape, F32)] + [(project_shape, BF16)] * 2
    out_specs += [full(s) for s, _ in shapes[len(out_specs) :]]
    scratch = [
        pltpu.VMEM((2 * heads, nq, keys), BF16),
        pltpu.VMEM((width, keys), F32),
        pltpu.VMEM((width, keys), F32),
        pltpu.VMEM((nq, width), BF16),
        pltpu.VMEM((width, keys), BF16),
        pltpu.VMEM((width, keys), BF16),
    ] + [pltpu.VMEM((2 ** (b - 1) * 8, 2 * heads * 16), F32) for b in bits]
    params = dict(vmem_limit_bytes=BACK_VM)
    if fast:
        scratch += [pltpu.VMEM(project_shape, BF16)] * 2
        scratch += [pltpu.VMEM((model, nq), BF16)] * 2
        scratch += [pltpu.VMEM((6, *sum_shape), F32), pltpu.VMEM(sum_shape, F32)]
        scratch += [pltpu.VMEM((5, *sum_shape), F32)]
        scratch += [pltpu.SemaphoreType.DMA((2,)), pltpu.SemaphoreType.DMA((5,)), pltpu.SemaphoreType.DMA((5,))]
        n = 0
        for rows, columns, pieces in ((hidden, model, chunks[0]), (model, hidden, chunks[1])):
            for _ in range(pieces):
                scratch += stream_scratch(rows, columns // pieces, plan[1][n], n >= chunks[0])
                n += 1
        scratch += stream_scratch(model, width, plan[1][n], False)
        for start, stop in chunks[2]:
            n += 1
            scratch += stream_scratch(model, stop - start, plan[1][n], False)
        params.update(collective_id=collective_id, has_side_effects=True)
    return pl.pallas_call(
        functools.partial(
            back_kernel, pairs=pairs, qb=qb, hb=hb, steps=steps, bits=bits, fast=fast, chunks=chunks, plan=plan
        ),
        out_shape=tuple(jax.ShapeDtypeStruct(s, t) for s, t in shapes),
        grid=(2 * steps + 2 + steps * ratio,),
        in_specs=in_specs,
        out_specs=tuple(out_specs),
        scratch_shapes=scratch,
        compiler_params=pltpu.CompilerParams(**params),
        cost_estimate=pl.CostEstimate(
            flops=16 * nq * keys * width, bytes_accessed=300 * 2**20, transcendentals=0
        ),
    )(*operands)


norm_epsilon = 1e-05


def mm(a, b):
    return jnp.dot(a, b, preferred_element_type=F32)


def normalize(value):
    center = value - jnp.mean(value, axis=-1, keepdims=True)
    spread = jnp.mean(center * center, axis=-1, keepdims=True)
    root = lax.rsqrt(spread + norm_epsilon)
    return center * root, root


def normalize_back(grad, normed, root):
    return root * (
        grad
        - jnp.mean(grad, axis=-1, keepdims=True)
        - normed * jnp.mean(grad * normed, axis=-1, keepdims=True)
    )


def gelu_parts(u):
    t = 1.0 / (1.0 + (0.3275911 * 0.7071067811865476) * jnp.abs(u))
    e = jnp.exp(-0.5 * u * u)
    poly = t * (
        0.254829592 + t * (-0.284496736 + t * (1.421413741 + t * (-1.453152027 + t * 1.061405429)))
    )
    tail = 0.5 * e * poly
    below = jnp.where(u >= 0, 1.0 - tail, tail)
    return u * below, below + u * (e * 0.3989422804014327)


def swap_dp(x, bit):
    n = lax.axis_size("dp")
    return lax.ppermute(x, "dp", [(i, i ^ bit) for i in range(n)])


def swap_head(x):
    return lax.ppermute(x, "head", [(0, 1), (1, 0)])


def dp_bits():
    n, bit, out = lax.axis_size("dp"), 1, []
    while bit < n:
        out.append(bit)
        bit *= 2
    return out


def bit_of(bit):
    return (lax.axis_index("dp") // bit) % 2


def in_order(first, mine, theirs):
    low = jnp.where(first == 0, mine, theirs)
    high = jnp.where(first == 0, theirs, mine)
    return jnp.concatenate([low, high], axis=0)


def rows_of(x, index, rows):
    return lax.dynamic_slice_in_dim(x, index * rows, rows, 0)


def halve(g, bit):
    rows = g.shape[0] // 2
    b = bit_of(bit)
    got = swap_dp(rows_of(g, 1 - b, rows), bit)
    return (rows_of(g, b, rows).astype(F32) + got.astype(F32)).astype(BF16)


def reduce_grad(own, other, head_first):
    bits = dp_bits()
    own, other = halve(own, 1), halve(other, 1)
    if not head_first:
        own, other = halve(own, 2), halve(other, 2)
    g = (own.astype(F32) + swap_head(other).astype(F32)).astype(BF16)
    for bit in bits[1 if head_first else 2 :]:
        g = halve(g, bit)
    for bit in reversed(bits):
        g = in_order(bit_of(bit), g, swap_dp(g, bit))
    return g.astype(F32)


BACK_CHUNKS = (2, 2, ((0, 640), (640, 1152)))
BACK_PLAN = (
    ((0, 0, 0), (0, 1, 0), (0, 2, 0), (0, 3, 0), (0, 4, 0), (2, 0, 1), (3, 1, 1), (4, 2, 1), (5, 3, 1), (6, 0, 2), (6, 4, 1), (7, 1, 2), (8, 2, 2), (9, 0, 3), (10, 6, 0), (10, 7, 0), (10, 5, 0), (10, 0, 4), (10, 3, 2), (10, 1, 3), (10, 2, 3), (11, 0, 5), (11, 6, 1), (11, 4, 2), (12, 0, 6), (12, 5, 1), (12, 1, 4), (12, 3, 3), (12, 2, 4), (13, 0, 7), (13, 1, 5), (14, 7, 1), (14, 6, 2), (14, 2, 5), (15, 1, 6), (15, 4, 3), (15, 3, 4), (15, 0, 8), (15, 5, 2), (16, 0, 9), (16, 6, 3), (16, 2, 6), (16, 1, 7), (16, 3, 5), (17, 6, 4), (17, 5, 3), (17, 4, 4), (17, 3, 6), (18, 8, 0), (18, 6, 5), (18, 5, 4), (18, 2, 7), (18, 1, 8), (18, 8, 1), (18, 3, 7), (18, 6, 6), (18, 1, 9), (18, 8, 2), (18, 5, 5), (18, 4, 5), (18, 2, 8), (18, 3, 8), (18, 5, 6), (18, 8, 3), (18, 6, 7), (18, 4, 6), (18, 2, 9), (18, 8, 4), (18, 5, 7), (18, 3, 9), (18, 4, 7), (18, 8, 5), (18, 6, 8), (18, 5, 8), (18, 6, 9), (18, 4, 8), (18, 5, 9), (18, 4, 9)),
    ('x0y1', '0yx1', 'y0x1', 'x0y1', 'xy01', '0xy1', 'x0y1'),
)


def row_sums(x):
    return jnp.sum(x, axis=0, keepdims=True)


def ffn_kernel(
    x, cot, ctx_a, ctx_b, ow_a, ow_b, params, small_a, small_b, uw_a, uw_b, dw_a, dw_b,
    out, first, do_a, do_b, go_a, go_b, pre_a, pre_b, gd_all, gu_all,
    uw, dw, act, slope, gd, gu, total, bias, bias_sum, sem_in, sem_out,
    *, heads, chunk,
):
    width = ctx_a.shape[1]
    model = x.shape[1]
    hidden = uw_a.shape[1]
    per = hidden // chunk
    for s, (u, d) in enumerate(((uw_a, dw_a), (uw_b, dw_b))):
        for i in range(per):
            n = s * per + i
            cols = slice(i * chunk, (i + 1) * chunk)
            pltpu.make_async_copy(u.at[:, cols], uw.at[n], sem_in.at[n]).start()
            pltpu.make_async_copy(d.at[cols, :], dw.at[n], sem_in.at[2 * per + n]).start()
            small = (small_a, small_b)[s]
            for j in range(chunk // width):
                at = heads + 2 + i * (chunk // width) + j
                bias[n * 8 : n * 8 + 1, j * width : (j + 1) * width] = small[at : at + 1, :]
    gain1, shift1, gain2, shift2, output_shift, down_shift = (params[i : i + 1, :] for i in range(6))

    def put(i, vector):
        for o in (pre_a, pre_b):
            for n in range(model // width):
                o[i * (model // width) + n : i * (model // width) + n + 1, :] = vector[
                    :, n * width : (n + 1) * width
                ]

    attend = dot_nn(ctx_a[...], ow_a[...]) + dot_nn(ctx_b[...], ow_b[...]) + output_shift
    n1, root1 = normalize(x[...].astype(F32) + attend)
    normed = n1 * gain1 + shift1
    low = normed.astype(BF16)
    total[...] = normed + down_shift

    def forward(n, _):
        pltpu.make_async_copy(uw.at[n], uw.at[n], sem_in.at[n]).wait()
        row = bias[pl.ds(pl.multiple_of(n * 8, 8), 8), :][0:1]
        a, slope_n = gelu_parts(dot_nn(low, uw[n]) + row)
        a = a.astype(BF16)
        act[n] = a
        slope[n] = slope_n.astype(BF16)
        pltpu.make_async_copy(dw.at[n], dw.at[n], sem_in.at[2 * per + n]).wait()
        total[...] += dot_nn(a, dw[n])
        return 0

    lax.fori_loop(0, 2 * per, forward, 0)
    n2, root2 = normalize(total[...])
    out[...] = n2 * gain2 + shift2
    g = cot[...].astype(F32)
    put(2, row_sums(g * n2))
    put(3, row_sums(g))
    back = normalize_back(g * gain2, n2, root2)
    back_feed = back.astype(BF16)
    put(5, row_sums(back_feed.astype(F32)))
    total[...] = back

    def stores(n):
        rows = pl.ds(pl.multiple_of(n * chunk, chunk), chunk)
        cols = pl.ds(pl.multiple_of(lax.rem(n, per) * chunk, chunk), chunk)
        return (
            pltpu.make_async_copy(gd.at[n], gd_all.at[rows], sem_out.at[n]),
            pltpu.make_async_copy(gu.at[n], gu_all.at[lax.div(n, per), :, cols], sem_out.at[2 * per + n]),
        )

    def backward(n, _):
        gd[n] = dot_tn(act[n], back_feed).astype(BF16)
        stores(n)[0].start()
        back_up = (dot_nt(back_feed, dw[n]) * slope[n].astype(F32)).astype(BF16)
        bias_sum[pl.ds(pl.multiple_of(n * 8, 8), 8), :] = jnp.broadcast_to(
            row_sums(back_up.astype(F32)), (8, chunk)
        )
        gu[n] = dot_tn(low, back_up).astype(BF16)
        stores(n)[1].start()
        total[...] += dot_nt(back_up, uw[n])
        return 0

    lax.fori_loop(0, 2 * per, backward, 0)
    for n in range(2 * per):
        for j in range(chunk // width):
            at = 6 * (model // width) + (n % per) * (chunk // width) + j
            (pre_a, pre_b)[n // per][at : at + 1, :] = bias_sum[n * 8 : n * 8 + 1, j * width : (j + 1) * width]
    back = total[...]
    put(0, row_sums(back * n1))
    put(1, row_sums(back))
    back = normalize_back(back * gain1, n1, root1)
    first[...] = back
    back_attend = back.astype(BF16)
    put(4, row_sums(back_attend.astype(F32)))
    for ctx, ow, do, go in ((ctx_a, ow_a, do_a, go_a), (ctx_b, ow_b, do_b, go_b)):
        do[...] = dot_nt(back_attend, ow[...]).astype(BF16)
        go[...] = dot_tn(back_attend, ctx[...]).astype(BF16)
    for n in range(2 * per):
        for copy in stores(n):
            copy.wait()


def feed_forward(x, cot, contexts, output_weights, params, smalls, up_weights, down_weights, heads, chunk=768):
    nq, model = x.shape
    width = contexts[0].shape[1]
    hidden = up_weights[0].shape[1]
    n = 2 * hidden // chunk
    here = pl.BlockSpec(memory_space=pltpu.VMEM)
    anywhere = pl.BlockSpec(memory_space=pl.ANY)
    pre_rows = 6 * (model // width) + hidden // width
    shape = jax.ShapeDtypeStruct
    return pl.pallas_call(
        functools.partial(ffn_kernel, heads=heads, chunk=chunk),
        out_shape=(
            shape((nq, model), F32),
            shape((nq, model), F32),
            shape((nq, width), BF16),
            shape((nq, width), BF16),
            shape((model, width), BF16),
            shape((model, width), BF16),
            shape((pre_rows, width), F32),
            shape((pre_rows, width), F32),
            shape((2 * hidden, model), BF16),
            shape((2, model, hidden), BF16),
        ),
        in_specs=[here] * 9 + [anywhere] * 4,
        out_specs=(here,) * 8 + (anywhere,) * 2,
        scratch_shapes=[
            pltpu.VMEM((n, model, chunk), BF16),
            pltpu.VMEM((n, chunk, model), BF16),
            pltpu.VMEM((n, nq, chunk), BF16),
            pltpu.VMEM((n, nq, chunk), BF16),
            pltpu.VMEM((n, chunk, model), BF16),
            pltpu.VMEM((n, model, chunk), BF16),
            pltpu.VMEM((nq, model), F32),
            pltpu.VMEM((n * 8, chunk), F32),
            pltpu.VMEM((n * 8, chunk), F32),
            pltpu.SemaphoreType.DMA((2 * n,)),
            pltpu.SemaphoreType.DMA((2 * n,)),
        ],
        compiler_params=pltpu.CompilerParams(vmem_limit_bytes=VM),
        cost_estimate=pl.CostEstimate(
            flops=12 * nq * model * 2 * hidden, bytes_accessed=100 * 2**20, transcendentals=nq * 4 * hidden
        ),
    )(x, cot, *contexts, *output_weights, params, *smalls, *up_weights, *down_weights)


def finish_kernel(index, *refs, count, heads, scale):
    refs = list(refs)
    take = lambda n: [refs.pop(0) for _ in range(n)]
    down, up, out, project = take(4)
    down_piece, up_piece, out_piece, project_piece = take(4)
    tokens_t, first, sums, params, small = take(5)
    project_w, out_w, up_w, down_w = take(4)
    project_a, query_a, value_a, out_a, out_shift_a, gain1_a, shift1_a = take(7)
    up_a, up_bias_a, down_a, down_shift_a, gain2_a, shift2_a, *table_a = take(9)
    tokens_o, project_o, query_o, value_o, out_o, out_shift_o, gain1_o, shift1_o = take(8)
    up_o, up_bias_o, down_o, down_shift_o, gain2_o, shift2_o, *table_o = take(9)
    project_r, query_r, value_r, out_r, out_shift_r, gain1_r, shift1_r = take(7)
    up_r, up_bias_r, down_r, down_shift_r, gain2_r, shift2_r, *table_r = take(9)
    thirds = project.shape[1] // 3
    wide = lambda ref: ref[...].astype(F32)
    renew = lambda average, weight, grad: 0.5 * average + 0.5 * (weight - grad * scale)

    down_o[...] = wide(down)
    up_o[...] = wide(up)
    out_o[...] = jnp.transpose(wide(out))
    for i in range(3):
        project_o[i] = project[:, i * thirds : (i + 1) * thirds].astype(F32)
    tokens_o[...] = first[...] + jnp.transpose(tokens_t[...])

    @pl.when(pl.program_id(0) == 0)
    def _():
        up_r[...] = renew(up_a[...], wide(up_w), wide(up_piece))
        down_r[...] = renew(down_a[...], wide(down_w), wide(down_piece))
        out_r[...] = renew(out_a[...], jnp.transpose(wide(out_w)), wide(out_piece))
        for i in range(3):
            project_r[i] = renew(project_a[i], project_w[i].astype(F32), project_piece[:, i * thirds : (i + 1) * thirds].astype(F32))
        width = sums.shape[1]

        def vector(ref, at, n):
            return jnp.concatenate([ref[at + i : at + i + 1, :] for i in range(n)], axis=1)

        def flat(o, r, a, weight, grad):
            n = a.shape[0]
            o[...] = grad.reshape(n)
            r[...] = renew(a[...], weight.reshape(n), grad.reshape(n))

        flat(query_o, query_r, query_a, small[heads : heads + 1, :], sums[8:9, :])
        flat(value_o, value_r, value_a, small[heads + 1 : heads + 2, :], sums[16:17, :])
        two = params.shape[1] // width
        commons = (
            (gain1_o, gain1_r, gain1_a),
            (shift1_o, shift1_r, shift1_a),
            (gain2_o, gain2_r, gain2_a),
            (shift2_o, shift2_r, shift2_a),
            (out_shift_o, out_shift_r, out_shift_a),
            (down_shift_o, down_shift_r, down_shift_a),
        )
        for i, (o, r, a) in enumerate(commons):
            flat(o, r, a, params[i : i + 1, :], vector(sums, 24 + two * i, two))
        many = up_bias_a.shape[0] // width
        flat(
            up_bias_o, up_bias_r, up_bias_a, vector(small, heads + 2, many), vector(sums, 24 + 6 * two, many)
        )
        for t, (o, r, a) in enumerate(zip(table_o, table_r, table_a)):
            n = a.shape[1]
            grad = sums[0:heads, t * 128 : t * 128 + n]
            o[...] = grad
            r[...] = renew(a[...], small[0:heads, t * 128 : t * 128 + n], grad)


def finish(index, totals, tokens_t, first, sums, params, small, weights, averages, count, tokens_count, heads):
    swap = lambda a: a.transpose(1, 0, 2) if a.ndim == 3 else a.T
    turned = (0, 3, 13, 14, 15)
    averages = [swap(a) if i in turned else a for i, a in enumerate(averages)]
    down, up, out, project = totals
    model = first.shape[1]
    nq = first.shape[0]
    width = project.shape[1] // 3
    steps = model // 128
    full = lambda a: pl.BlockSpec(a.shape, lambda i, d: (0,) * len(a.shape))
    rows = lambda a: pl.BlockSpec((a.shape[0] // steps, a.shape[1]), lambda i, d: (i, 0))
    piece = lambda a: pl.BlockSpec(
        (a.shape[0] // count, *a.shape[1:]), lambda i, d: (d[0],) + (0,) * (len(a.shape) - 1)
    )
    columns = lambda n: pl.BlockSpec((n, 128), lambda i, d: (0, i))
    shape = lambda s: jax.ShapeDtypeStruct(s, F32)
    project_w, out_w, up_w, down_w = weights
    in_specs = [rows(a) for a in totals] + [piece(a) for a in totals]
    in_specs += [rows(tokens_t), columns(nq), full(sums), full(params), full(small)]
    project_spec = pl.BlockSpec((3, model // count, width), lambda i, d: (0, d[0], 0))
    in_specs += [project_spec, full(out_w), piece(up_w), piece(down_w)] + [full(a) for a in averages]
    grads = [
        shape((3, model, width)), shape((width,)), shape((width,)), shape((width, model)), shape((model,)),
        shape((model,)), shape((model,)), shape(up.shape), shape((up.shape[1],)), shape(down.shape),
        shape((model,)), shape((model,)), shape((model,)), *(shape(a.shape) for a in averages[13:]),
    ]
    specs = [full(g) for g in grads]
    specs[0] = pl.BlockSpec((3, 128, width), lambda i, d: (0, i, 0))
    specs[3] = columns(width)
    specs[7] = rows(up)
    specs[9] = rows(down)
    tokens, *results = pl.pallas_call(
        functools.partial(finish_kernel, count=count, heads=heads, scale=1.0 / tokens_count),
        out_shape=(shape((nq, model)), *grads, *(shape(a.shape) for a in averages)),
        grid_spec=pltpu.PrefetchScalarGridSpec(
            num_scalar_prefetch=1,
            grid=(steps,),
            in_specs=in_specs,
            out_specs=(columns(nq), *specs, *(full(a) for a in averages)),
        ),
        compiler_params=pltpu.CompilerParams(vmem_limit_bytes=VM),
        cost_estimate=pl.CostEstimate(flops=2**24, bytes_accessed=40 * 2**20, transcendentals=0),
    )(index, *totals, *totals, tokens_t, first, sums, params, small, *weights, *averages)
    grads, renewed = results[:16], results[16:]
    grads = [swap(a) if i in turned and i != 3 else a for i, a in enumerate(grads)]
    return tokens, *grads, *(swap(a) if i in turned else a for i, a in enumerate(renewed))


def local(
    tokens,
    cotangent,
    form_number,
    sequence_bucket,
    horizontal_bucket,
    vertical_bucket,
    project_weight,
    query_bias,
    value_bias,
    output_weight,
    output_bias,
    first_gain,
    first_shift,
    up_weight,
    up_bias,
    down_weight,
    down_bias,
    second_gain,
    second_shift,
    sequence_table,
    horizontal_table,
    vertical_table,
    project_weight_average,
    query_bias_average,
    value_bias_average,
    output_weight_average,
    output_bias_average,
    first_gain_average,
    first_shift_average,
    up_weight_average,
    up_bias_average,
    down_weight_average,
    down_bias_average,
    second_gain_average,
    second_shift_average,
    sequence_table_average,
    horizontal_table_average,
    vertical_table_average,
):
    total_rows, model_width = tokens.shape
    local_width = project_weight.shape[2]
    local_heads = sequence_table.shape[1]
    hidden = up_weight.shape[1]
    share_rows = total_rows // lax.axis_size("head")
    head_index = lax.axis_index("head")
    share_start = head_index * share_rows
    block_rows = 128
    buckets = (sequence_bucket, horizontal_bucket, vertical_bucket)
    tables = (sequence_table, horizontal_table, vertical_table)
    bits = tuple((t.shape[0] - 1).bit_length() for t in tables)
    project_stack = project_weight.transpose(1, 0, 2)
    flat_project = project_stack.reshape(3 * model_width, local_width)

    params = jnp.concatenate(
        [first_gain, first_shift, second_gain, second_shift, output_bias, down_bias]
    ).reshape(6, model_width).astype(F32)
    lanes = [jnp.pad(t.T, ((0, 0), (0, local_width // 3 - t.shape[0]))) for t in tables]
    small = jnp.concatenate(
        [
            jnp.concatenate(lanes, axis=1),
            jnp.concatenate([query_bias, value_bias, up_bias]).reshape(-1, local_width),
        ],
        axis=0,
    ).astype(F32)
    small = jnp.pad(small, ((0, 16 - small.shape[0]), (0, 0)))
    smalls, project_weights = [small], [flat_project]
    output_weights, up_weights, down_weights = [output_weight], [up_weight], [down_weight]

    form_row = form_number.reshape(total_rows)
    form_own = lax.dynamic_slice_in_dim(form_row, share_start, share_rows, 0)
    code = encode(
        [rows_of(b, head_index, share_rows) for b in buckets], form_own[:, None] == form_row[None, :]
    )
    own_tokens = rows_of(tokens, head_index, share_rows)

    scaled, keys, values_t, probs, contexts = [], [], [], [], []
    for s in range(2):
        wq, wk, wv = (project_weights[s][i * model_width : (i + 1) * model_width] for i in range(3))
        bq = smalls[s][local_heads : local_heads + 1]
        bv = smalls[s][local_heads + 1 : local_heads + 2]
        q = ((mm(own_tokens, wq) + bq) * 0.125).astype(BF16)
        q = q * jnp.array(2.0**SCALE_BITS, BF16)
        k = mm(tokens, wk).astype(BF16)
        kt = dot_general_t(wk, tokens).astype(BF16)
        v = (mm(tokens, wv) + bv).astype(BF16)
        vt = (dot_general_t(wv, tokens) + bv.reshape(-1, 1)).astype(BF16)
        if s == 0:
            fetch = (
                ("small", (0, -1, -1), small),
                ("all", (0, 3, 7), flat_project),
                ("all", (0, 4, 7), output_weight),
                ("first", (0, -1, -1), up_weight),
            )
        else:
            fetch = (("rest", (-1, 0, 4), up_part), ("all", (0, 4, 8), down_weight))
        p, context, *fetched = attend_fwd(code, smalls[s], q, kt, v, fetch, s, qb=block_rows)
        if s == 0:
            smalls.append(fetched[0])
            project_weights.append(fetched[1])
            output_weights.append(fetched[2])
            up_part = fetched[3]
        else:
            up_weights.append(fetched[0])
            down_weights.append(fetched[1])
        scaled.append(q)
        keys.append(k)
        values_t.append(vt)
        probs.append(p)
        contexts.append(context)
    (
        layer_output, back_first, back_own, back_other, out_own, out_other, pre_own, pre_other, *grads
    ) = feed_forward(
        own_tokens, cotangent, contexts, output_weights, params, smalls, up_weights, down_weights, local_heads
    )

    sides = [
        (scaled[s], keys[s], values_t[s], (back_own, back_other)[s], probs[s]) for s in range(2)
    ]
    pre = (pre_own, pre_other)
    fast = lax.axis_size("dp") == 16
    results = attend_backward(
        sides,
        code,
        tokens.T,
        project_weights,
        bits,
        (*grads, out_own, out_other),
        pre,
        2,
        fast,
        BACK_PLAN,
        BACK_CHUNKS,
        qb=block_rows,
    )
    token_count = total_rows * lax.axis_size("dp")
    group_count = lax.axis_size("dp")
    group_index = lax.axis_index("dp")
    if fast:
        width = model_width // group_count
        output_piece = lax.dynamic_slice_in_dim(output_weight, group_index * width, width, 1)
        averages = (
            project_weight_average, query_bias_average, value_bias_average, output_weight_average,
            output_bias_average, first_gain_average, first_shift_average, up_weight_average, up_bias_average,
            down_weight_average, down_bias_average, second_gain_average, second_shift_average,
            sequence_table_average, horizontal_table_average, vertical_table_average,
        )
        return layer_output, *finish(
            jnp.full((1,), group_index, I32),
            results[:4],
            results[4],
            back_first,
            results[5],
            params,
            small,
            (project_stack, output_piece, up_weight, down_weight),
            averages,
            group_count,
            token_count,
            local_heads,
        )
    tokens_gradient, sums, far, sums_other = results[:4]
    tokens_gradient = tokens_gradient + swap_head(far).astype(F32)
    sums = sums + swap_head(sums_other)
    for bit in dp_bits():
        sums = sums + swap_dp(sums, bit)
    down_total, up_total = reduce_grad(grads[0][:hidden], grads[0][hidden:], True), reduce_grad(*grads[1], False)
    output_total = reduce_grad(out_own, out_other, True)
    project_total = reduce_grad(results[4], results[5], False)
    tokens_gradient = back_first + tokens_gradient.T
    project_total = project_total.reshape(model_width, 3, local_width)
    output_total = output_total.T
    query_bias_total, value_bias_total = sums[8], sums[16]
    tail = sums[24:].reshape(-1)
    (
        first_gain_total,
        first_shift_total,
        second_gain_total,
        second_shift_total,
        output_bias_total,
        down_bias_total,
    ) = (tail[i * model_width : (i + 1) * model_width] for i in range(6))
    up_bias_total = tail[6 * model_width :]
    sequence_total, horizontal_total, vertical_total = (
        sums[:local_heads, i * 128 : i * 128 + t.shape[0]].T for i, t in enumerate(tables)
    )
    up_weight_total, down_weight_total, output_weight_total = up_total, down_total, output_total

    def renew(average, weight, gradient):
        return 0.5 * average + 0.5 * (weight.astype(jnp.float32) - gradient / token_count)

    def part_of(array, along):
        width = array.shape[along] // group_count
        return lax.dynamic_slice_in_dim(array, group_index * width, width, along)

    return (
        layer_output,
        tokens_gradient,
        project_total,
        query_bias_total,
        value_bias_total,
        output_weight_total,
        output_bias_total,
        first_gain_total,
        first_shift_total,
        up_weight_total,
        up_bias_total,
        down_weight_total,
        down_bias_total,
        second_gain_total,
        second_shift_total,
        sequence_total,
        horizontal_total,
        vertical_total,
        renew(project_weight_average, part_of(project_weight, 0), part_of(project_total, 0)),
        renew(query_bias_average, query_bias, query_bias_total),
        renew(value_bias_average, value_bias, value_bias_total),
        renew(output_weight_average, part_of(output_weight, 1), part_of(output_weight_total, 1)),
        renew(output_bias_average, output_bias, output_bias_total),
        renew(first_gain_average, first_gain, first_gain_total),
        renew(first_shift_average, first_shift, first_shift_total),
        renew(up_weight_average, part_of(up_weight, 0), part_of(up_weight_total, 0)),
        renew(up_bias_average, up_bias, up_bias_total),
        renew(down_weight_average, part_of(down_weight, 0), part_of(down_weight_total, 0)),
        renew(down_bias_average, down_bias, down_bias_total),
        renew(second_gain_average, second_gain, second_gain_total),
        renew(second_shift_average, second_shift, second_shift_total),
        renew(sequence_table_average, sequence_table, sequence_total),
        renew(horizontal_table_average, horizontal_table, horizontal_total),
        renew(vertical_table_average, vertical_table, vertical_total),
    )


def solution(mesh):
    in_specs = (
        P("dp", None),
        P(("dp", "head"), None),
        P("dp", None),
        P("dp", None),
        P("dp", None),
        P("dp", None),
        P(None, None, "head"),
        P("head"),
        P("head"),
        P("head", None),
        P(),
        P(),
        P(),
        P(None, "head"),
        P("head"),
        P("head", None),
        P(),
        P(),
        P(),
        P(None, "head"),
        P(None, "head"),
        P(None, "head"),
        P("dp", None, "head"),
        P("head"),
        P("head"),
        P("head", "dp"),
        P(),
        P(),
        P(),
        P("dp", "head"),
        P("head"),
        P(("head", "dp"), None),
        P(),
        P(),
        P(),
        P(None, "head"),
        P(None, "head"),
        P(None, "head"),
    )
    out_specs = (
        P(("dp", "head"), None),
        P(("dp", "head"), None),
        P(None, None, "head"),
        P("head"),
        P("head"),
        P("head", None),
        P(),
        P(),
        P(),
        P(None, "head"),
        P("head"),
        P("head", None),
        P(),
        P(),
        P(),
        P(None, "head"),
        P(None, "head"),
        P(None, "head"),
        P("dp", None, "head"),
        P("head"),
        P("head"),
        P("head", "dp"),
        P(),
        P(),
        P(),
        P("dp", "head"),
        P("head"),
        P(("head", "dp"), None),
        P(),
        P(),
        P(),
        P(None, "head"),
        P(None, "head"),
        P(None, "head"),
    )
    return jax.shard_map(local, mesh=mesh, in_specs=in_specs, out_specs=out_specs, check_vma=False)
```

```python
import functools
import jax
import jax.numpy as jnp
from jax import lax
from jax.experimental import pallas as pl
from jax.sharding import PartitionSpec as P
from jax.experimental.pallas import tpu as pltpu

F32, BF16, I32 = jnp.float32, jnp.bfloat16, jnp.int32
SCALE_BITS = 27
STEP = 2.0**11
VM = 56 * 2**20
BACK_VM = 60 * 2**20
SAME = 2**17


def encode(buckets, same):
    seq, hor, ver = buckets
    return seq + 32 * hor + 2048 * ver + jnp.where(same, SAME, 0)


def buckets_of(code):
    return code & 31, (code >> 5) & 63, (code >> 11) & 63


def dot_nt(a, b):
    return lax.dot_general(a, b, (((1,), (1,)), ((), ())), preferred_element_type=F32)


def dot_tn(a, b):
    return lax.dot_general(a, b, (((0,), (0,)), ((), ())), preferred_element_type=F32)


def dot_general_t(w, x):
    return lax.dot_general(w, x, (((0,), (1,)), ((), ())), preferred_element_type=F32)


def dot_tt(a, b):
    return lax.dot_general(a, b, (((0,), (1,)), ((), ())), preferred_element_type=F32)


def dot_nn(a, b):
    return lax.dot_general(a, b, (((1,), (0,)), ((), ())), preferred_element_type=F32)


def split_pair(x):
    lane = lax.broadcasted_iota(I32, x.shape, 1)
    zero = jnp.zeros_like(x)
    return jnp.concatenate([jnp.where(lane < 64, x, zero), jnp.where(lane < 64, zero, x)], axis=0)


def partner(axis, bit):
    i = lax.axis_index(axis)
    low = lax.rem(lax.div(i, bit), 2)
    return {axis: i + bit * (1 - 2 * low)}


def dp_bit(bit):
    return lax.rem(lax.div(lax.axis_index("dp"), bit), 2)


def announce(partners):
    barrier = pltpu.get_barrier_semaphore()
    for p in partners:
        pl.semaphore_signal(barrier, inc=1, device_id=p, device_id_type=pl.DeviceIdType.MESH)


def greet(partners):
    announce(partners)
    pl.semaphore_wait(pltpu.get_barrier_semaphore(), len(partners))


def remote(src, dst, send, recv, to):
    return pltpu.make_async_remote_copy(
        src_ref=src,
        dst_ref=dst,
        send_sem=send,
        recv_sem=recv,
        device_id=to,
        device_id_type=pl.DeviceIdType.MESH,
    )


def fetch_copies(mode, source, out, send, recv):
    if mode == "small":
        return [remote(source, out, send.at[0], recv.at[0], partner("head", 1)), None, None], []
    rows = source.shape[0] if mode == "rest" else source.shape[0] // 4
    quarter = 2 * dp_bit(1) + dp_bit(2)
    one = pl.ds(pl.multiple_of(quarter * rows, rows), rows)
    two = pl.ds(pl.multiple_of(dp_bit(1) * (2 * rows), 2 * rows), 2 * rows)
    hops, local = [None, None, None], []
    if mode == "first":
        hops[0] = remote(source.at[one], out, send.at[0], recv.at[0], partner("head", 1))
    else:
        if mode == "all":
            hops[0] = remote(source.at[one], out.at[one], send.at[0], recv.at[0], partner("head", 1))
            quarter_ref = out.at[one]
        else:
            quarter_ref = source
            local.append(pltpu.make_async_copy(source, out.at[one], send.at[0]))
        hops[1] = remote(quarter_ref, out.at[one], send.at[1], recv.at[1], partner("dp", 2))
        hops[2] = remote(out.at[two], out.at[two], send.at[2], recv.at[2], partner("dp", 1))
    return hops, local


def fetched_shape(mode, w):
    rows = {"all": 1, "small": 1, "first": 0.25, "rest": 4}[mode] * w.shape[0]
    return jax.ShapeDtypeStruct((int(rows), w.shape[1]), w.dtype)


def fwd_kernel(*refs, pairs, qb, modes, points, steps):
    n = len(modes)
    code, tab, q, kt, v = refs[:5]
    sources = refs[5 : 5 + n]
    p_out, c_out = refs[5 + n : 7 + n]
    outs = refs[7 + n : 7 + 2 * n]
    b_ref, t_ref, send, recv = refs[7 + 2 * n :]
    keys = v.shape[0]
    chunk = 128
    step = pl.program_id(0)
    hops, local = [], []
    for i in range(n):
        h, l = fetch_copies(modes[i], sources[i], outs[i], send.at[i], recv.at[i])
        hops.append(h)
        local += l

    def point(now):
        for i in range(n):
            for hop in range(3):
                if points[i][hop] == now:
                    if hop and hops[i][hop - 1] is not None:
                        hops[i][hop - 1].wait_recv()
                    hops[i][hop].start()

    @pl.when(step == 0)
    def _():
        greet([partner("head", 1), partner("dp", 2), partner("dp", 1)])
        for copy in local:
            copy.start()
        for j in range(pairs):
            for t in range(3):
                ls = slice(t * chunk, (t + 1) * chunk)
                fixed = [jnp.round(tab[2 * j + g : 2 * j + g + 1, ls] * STEP).astype(I32) for g in range(2)]
                t_ref[8 * (3 * j + t) : 8 * (3 * j + t) + 8, :] = jnp.broadcast_to(
                    fixed[0] * 65536 + fixed[1], (8, chunk)
                )
        point(0)

    for now in sorted(set(sum(points, ()))):
        if 0 < now < 2 * steps and now % 2 == 0:

            @pl.when(step == now // 2)
            def _():
                if local and now == min(p[2] for p, m in zip(points, modes) if m == "rest"):
                    for copy in local:
                        copy.wait()
                point(now)

    tbs = [t_ref[8 * i : 8 * i + 8, :] for i in range(3 * pairs)]

    def gather(r, _):
        rs = pl.ds(pl.multiple_of(r * 8, 8), 8)
        for c in range(keys // chunk):
            ls = slice(c * chunk, (c + 1) * chunk)
            sums = [None] * pairs
            for t, idx in enumerate(buckets_of(code[rs, ls])):
                for j in range(pairs):
                    g = jnp.take_along_axis(tbs[3 * j + t], idx, axis=1, mode="promise_in_bounds")
                    sums[j] = g if t == 0 else sums[j] + g
            for j in range(pairs):
                b_ref[j, rs, ls] = sums[j]
        return 0

    lax.fori_loop(0, qb // 8, gather, 0)
    for now in sorted(set(sum(points, ()))):
        if 0 < now < 2 * steps and now % 2 == 1:

            @pl.when(step == now // 2)
            def _():
                point(now)

    same = code[...] >= SAME
    def pair(j, _):
        lanes = pl.ds(pl.multiple_of(j * 128, 128), 128)
        q2 = split_pair(q[:, lanes])
        s2 = dot_nn(q2, kt[lanes, :])
        bias = b_ref[j]
        for g in range(2):
            x = s2[g * qb : (g + 1) * qb] + (bias << 16 if g else bias).astype(F32)
            x = jnp.where(same, x, -1e30)
            top = jnp.max(x, axis=1, keepdims=True)
            e = jnp.exp2((x - top) * (1.4426950408889634 * 2.0**-SCALE_BITS))
            inv = 1.0 / jnp.sum(e, axis=1, keepdims=True)
            p_out[2 * j + g] = (e * inv).astype(BF16)
        c0 = dot_nn(p_out[2 * j], v[:, lanes])
        c1 = dot_nn(p_out[2 * j + 1], v[:, lanes])
        lane = lax.broadcasted_iota(I32, c0.shape, 1)
        c_out[:, lanes] = jnp.where(lane < 64, c0, c1).astype(BF16)
        return 0

    lax.fori_loop(0, pairs, pair, 0)

    @pl.when(step == steps - 1)
    def _():
        for now in range(2 * steps, max(sum(points, ())) + 1):
            point(now)
        for i in range(n):
            last = [copy for copy in hops[i] if copy is not None][-1]
            last.wait_recv()
        for i in range(n):
            for copy in hops[i]:
                if copy is not None:
                    copy.wait_send()


def attend_fwd(code, tab, q, kt, v, fetch, collective_id, qb=128):
    nq, width = q.shape
    keys = v.shape[0]
    pairs = width // 128
    modes = tuple(f[0] for f in fetch)
    points = tuple(f[1] for f in fetch)
    sources = [f[2] for f in fetch]
    n = len(fetch)
    steps = nq // qb
    full = lambda a: pl.BlockSpec(a.shape, lambda i: (0,) * a.ndim)
    anywhere = pl.BlockSpec(memory_space=pl.ANY)
    return pl.pallas_call(
        functools.partial(fwd_kernel, pairs=pairs, qb=qb, modes=modes, points=points, steps=steps),
        out_shape=(
            jax.ShapeDtypeStruct((2 * pairs, nq, keys), BF16),
            jax.ShapeDtypeStruct((nq, width), BF16),
        )
        + tuple(fetched_shape(m, w) for m, w in zip(modes, sources)),
        grid=(steps,),
        in_specs=[
            pl.BlockSpec((qb, keys), lambda i: (i, 0)),
            full(tab),
            pl.BlockSpec((qb, width), lambda i: (i, 0)),
            full(kt),
            full(v),
        ]
        + [full(w) if m == "rest" else anywhere for m, w in zip(modes, sources)],
        out_specs=(
            pl.BlockSpec((2 * pairs, qb, keys), lambda i: (0, i, 0)),
            pl.BlockSpec((qb, width), lambda i: (i, 0)),
        )
        + (anywhere,) * n,
        scratch_shapes=[
            pltpu.VMEM((pairs, qb, keys), I32),
            pltpu.VMEM((pairs * 24, 128), I32),
            pltpu.SemaphoreType.DMA((n, 3)),
            pltpu.SemaphoreType.DMA((n, 3)),
        ],
        compiler_params=pltpu.CompilerParams(
            vmem_limit_bytes=VM, collective_id=collective_id, has_side_effects=True
        ),
        cost_estimate=pl.CostEstimate(
            flops=4 * nq * keys * width, bytes_accessed=90 * 2**20, transcendentals=nq * keys * 2 * pairs
        ),
    )(code, tab, q, kt, v, *sources)


def add_rows(dst, a, b, tile):
    rows = dst[2]

    def body(i, _):
        at = lambda x: pl.ds(pl.multiple_of(x[1] + i * tile, 16), tile)
        dst[0][at(dst), :] = a[0][at(a), :] + b[0][at(b), :]
        return 0

    lax.fori_loop(0, rows // tile, body, 0)


STREAM_SEMS = 17
ORDER_BITS = {"x": 2, "0": 4, "1": 8}


def stream_phases(own, other, kept, piece, full, columns, bufs, send, recv, order, part_of=None):
    rest = part_of == "rest"
    half = (full if rest else own).shape[0] // 2
    tile = half // 8
    c = dp_bit(1)
    cut = lambda ref, start, n: ref.at[pl.ds(pl.multiple_of(start, 16), n), columns]
    part = lambda ref, bit, n: ref.at[pl.ds(pl.multiple_of(bit * n, 16), n)]
    hops, adds = [[]], [[]]
    if not rest:
        for m, g in enumerate((own, other)):
            hops[0].append(
                remote(cut(g, (1 - c) * half, half), bufs[0].at[m], send.at[m], recv.at[m], partner("dp", 1))
            )
            mine = (kept[m], 0) if kept else (g.at[:, columns], c * half)
            adds[0].append((bufs[0].at[m], (bufs[0].at[m], 0), mine, half))
    keep = []
    if kept:
        keep = [
            pltpu.make_async_copy(cut(g, c * half, half), kept[m], send.at[15 + m])
            for m, g in enumerate((own, other))
        ]
    n, at, two = half, c * half, True
    spans, bits = [(at, n)], [1]
    for i, axis in enumerate(order[:1] if part_of == "head" else order):
        buf, before = bufs[i + 1], bufs[i]
        if rest and i == 0:
            two = axis != "y"
            if two:
                n = n // 2
                at = at + dp_bit(ORDER_BITS[axis]) * n
                spans.append((at, n))
                bits.append(ORDER_BITS[axis])
            hops.append([])
            adds.append([])
        elif axis == "y":
            two = False
            hops.append([remote(before.at[1], buf.at[0], send.at[2 + 2 * i], recv.at[2 + 2 * i], partner("head", 1))])
            adds.append([(buf.at[0], (buf.at[0], 0), (before.at[0], 0), n)])
        else:
            n = n // 2
            bit = ORDER_BITS[axis]
            b = dp_bit(bit)
            at = at + b * n
            spans.append((at, n))
            bits.append(bit)
            sems = [2 + 2 * i + m for m in range(2 if two else 1)]
            hops.append(
                [
                    remote(part(before.at[m], 1 - b, n), buf.at[m], send.at[k], recv.at[k], partner("dp", bit))
                    for m, k in enumerate(sems)
                ]
            )
            adds.append([(buf.at[m], (buf.at[m], 0), (before.at[m], b * n), n) for m in range(len(sems))])

    def head():
        for copy in hops[1]:
            copy.wait_recv()
        for dst, a, b, n in adds[1]:
            add_rows((dst, 0, n), a, b, tile)
        for copy in hops[0] + hops[1]:
            copy.wait_send()

    def first():
        for copy in hops[0] + keep:
            copy.start()

    def reduce(i):
        def phase():
            for copy in keep if i == 0 else ():
                copy.wait()
            for copy in hops[i]:
                copy.wait_recv()
            for dst, a, b, n in adds[i]:
                add_rows((dst, 0, n), a, b, tile)
            if i < 4:
                for copy in hops[i + 1]:
                    copy.start()
            else:
                local.start()
                back[0].start()

        return phase

    if part_of == "head":
        return [first, reduce(0), head]
    dst, a, b, n = adds[-1][0]
    adds[-1] = [(piece, a, b, n)]
    there = lambda start, n: full.at[pl.ds(pl.multiple_of(start, 16), n), columns]
    back = [remote(piece, there(*spans[-1]), send.at[10], recv.at[10], partner("dp", bits[-1]))]
    for i in range(1, 4):
        ref = there(*spans[-1 - i])
        back.append(remote(ref, ref, send.at[10 + i], recv.at[10 + i], partner("dp", bits[-1 - i])))
    local = pltpu.make_async_copy(piece, there(*spans[-1]), send.at[14])

    def gather(i):
        def phase():
            if i == 1:
                local.wait()
            back[i - 1].wait_recv()
            back[i].start()

        return phase

    def finish():
        back[3].wait_recv()
        for copy in sum(hops, []) + back:
            copy.wait_send()

    return [first, *(reduce(i) for i in range(5)), *(gather(i) for i in range(1, 4)), finish]


def stream_scratch(rows, columns, order, keep, rest=False):
    n, two = rows // 2, 2
    shapes = [(2, n, columns)]
    for axis in order:
        if axis == "y":
            two = 1
        else:
            n = n // 2
        shapes.append((two, n, columns))
    shapes.append((n, columns))
    if rest:
        shapes = shapes[2:]
    if keep:
        shapes += [(rows // 2, columns)] * 2
    return [pltpu.VMEM(s, BF16) for s in shapes] + [pltpu.SemaphoreType.DMA((STREAM_SEMS,))] * 2


def sum_phases(own, other, bufs, send, recv):
    to = [partner("head", 1)] + [partner("dp", b) for b in (1, 2, 4, 8)]
    hops = [
        remote(other if i == 0 else own.at[i - 1], bufs.at[i], send.at[i], recv.at[i], to[i])
        for i in range(5)
    ]

    def phase(i):
        def run():
            if i:
                hops[i - 1].wait_recv()
                if i > 1:
                    own[i - 1] = own[i - 2] + bufs[i - 1]
                else:
                    own[0] = own[5] + bufs[0]
            if i < 5:
                hops[i].start()
            else:
                for copy in hops:
                    copy.wait_send()

        return run

    return [phase(i) for i in range(6)]


def attend_back(q, kt, v, do, p, ds, at, dq, dk, dv, pairs, qb):
    def pair(j, _):
        lanes = pl.ds(pl.multiple_of(j * 128, 128), 128)
        q2 = split_pair(q[:, lanes])
        do2 = split_pair(do[:, lanes])
        dp2 = dot_nt(do2, v[:, lanes])
        parts = []
        for g in range(2):
            ps = p[2 * j + g].astype(F32)
            ts = ps * dp2[g * qb : (g + 1) * qb]
            inner = jnp.sum(ts, axis=1, keepdims=True)
            parts.append((ts - ps * inner).astype(BF16))
            ds[2 * j + g, pl.ds(at, qb), :] = parts[g]
        d0 = dot_nt(parts[0], kt[lanes, :])
        d1 = dot_nt(parts[1], kt[lanes, :])
        lane = lax.broadcasted_iota(I32, d0.shape, 1)
        dq[pl.ds(at, qb), lanes] = jnp.where(lane < 64, d0, d1).astype(BF16) * jnp.array(0.125, BF16)
        dk[lanes, :] += dot_tn(q2, jnp.concatenate(parts, axis=0))
        p2 = jnp.concatenate([p[2 * j], p[2 * j + 1]], axis=0)
        dv[lanes, :] += dot_tn(do2, p2)
        return 0

    lax.fori_loop(0, pairs, pair, 0)


def count_rows(code, ds, at, outs, bits, nq):
    heads = ds.shape[0]

    def rows(r, _):
        rs = pl.ds(pl.multiple_of(at + r * 16, 16), 16)
        dfull = [ds[h, rs, :].astype(F32) for h in range(heads)]
        for half in range(2):
            d8 = [d[half * 8 : half * 8 + 8] for d in dfull]
            packed = code[pl.ds(pl.multiple_of(r * 16 + half * 8, 8), 8), :]
            low = 0
            for t in range(3):
                signs = [(((packed << (31 - low - i)) >> 31) | 1).astype(F32) for i in range(bits[t])]
                low += bits[t]
                rhs = jnp.concatenate(
                    [jnp.concatenate([d, d * signs[0]], axis=0).astype(BF16) for d in d8], axis=0
                )
                first = jnp.concatenate([jnp.ones_like(signs[1]), signs[1]], axis=0).astype(BF16)
                tiles = [first]
                for i in range(2, bits[t]):
                    s2 = jnp.concatenate([signs[i], signs[i]], axis=0).astype(BF16)
                    tiles = tiles + [x * s2 for x in tiles]
                outs[t][...] += dot_nt(jnp.concatenate(tiles, axis=0), rhs)
        return 0

    lax.fori_loop(0, nq // 16, rows, 0)


def table_sums(acc, bits, first, heads):
    n = 2**bits
    high = lax.Precision.HIGHEST
    iota = lambda shape, d: lax.broadcasted_iota(I32, shape, d)
    row, col = iota(acc.shape, 0), iota(acc.shape, 1)
    kept = jnp.where((row & 7) == (col & 7), acc, 0.0)
    shape = (n, acc.shape[0])
    odd = (iota(shape, 1) >> 3) & (iota(shape, 0) >> 1)
    odd = odd ^ (odd >> 4)
    odd = odd ^ (odd >> 2)
    odd = odd ^ (odd >> 1)
    left = (1 - 2 * (odd & 1)).astype(F32)
    shape = (n, acc.shape[1])
    odd = iota(shape, 0) & (iota(shape, 1) >> 3) & 1
    mixed = jnp.dot(left, kept, precision=high, preferred_element_type=F32)
    mixed = mixed * (1 - 2 * odd).astype(F32) * (1.0 / n)
    shape = (8, acc.shape[1])
    head = iota(shape, 0)
    pick = ((iota(shape, 1) >> 4) == head + first) & (head < heads)
    return lax.dot_general(
        pick.astype(F32), mixed, (((1,), (1,)), ((), ())), precision=high, preferred_element_type=F32
    )


def back_kernel(*refs, pairs, qb, hb, steps, bits, fast, chunks, plan):
    refs = list(refs)
    take = lambda n: [refs.pop(0) for _ in range(n)]
    sides = [take(5), take(5)]
    code, xt, *weights = take(4)
    states = take(chunks[0]) if fast else []
    up_all, out_own, out_other, pre_own, pre_other = take(5)
    hidden = up_all.shape[2]
    up_own, up_other = up_all.at[0], up_all.at[1]
    full_down, full_up, full_out, full_project = take(4) if fast else [None] * 4
    token_out, sum_out = take(2)
    if fast:
        token_far = None
    else:
        token_far, sum_far = take(2)
        project = take(2)
    ds, dk, dv, dq, dkt, dvt = take(6)
    accs = take(3)
    if fast:
        project = take(2)
        token_far, token_near = take(2)
        sums, sum_other, sum_bufs = take(3)
        token_send, sum_send, sum_recv = take(3)
    step = pl.program_id(0)
    width = 2 * pairs * 64
    nq = qb * steps
    model = xt.shape[0]
    h = lax.axis_index("head")
    near = pl.ds(pl.multiple_of(h * nq, nq), nq)
    far = pl.ds(pl.multiple_of((1 - h) * nq, nq), nq)
    last = 2 * steps + 2 + (steps * qb) // hb

    if fast:
        phases = []
        sources = []
        down_chunks, up_chunks = chunks[:2]
        cols = model // down_chunks
        for i in range(down_chunks):
            sources.append((None, None, full_down, slice(i * cols, (i + 1) * cols)))
        cols = hidden // up_chunks
        for i in range(up_chunks):
            sources.append((up_own, up_other, full_up, slice(i * cols, (i + 1) * cols)))
        sources.append((out_own, out_other, full_out, slice(0, width)))
        for start, stop in chunks[2]:
            sources.append((project[0], project[1], full_project, slice(start, stop)))
        for n, (own, other, full, columns) in enumerate(sources):
            rest = n < down_chunks
            bufs = [None, states[n], *take(3)] if rest else take(5)
            (piece,) = take(1)
            kept = take(2) if down_chunks <= n < down_chunks + up_chunks else None
            send, recv = take(2)
            made = stream_phases(
                own, other, kept, piece, full, columns, bufs, send, recv, plan[1][n], "rest" if rest else None
            )
            phases.append(made)
        token_hop = remote(token_far, token_near, token_send.at[0], token_send.at[1], partner("head", 1))

        def token_end():
            token_hop.wait_recv()
            token_out[...] = token_out[...] + token_near[...].astype(F32)
            token_hop.wait_send()

        phases.append([token_hop.start, token_end])
        phases.append(sum_phases(sums, sum_other, sum_bufs, sum_send, sum_recv))

        @pl.when(step == 0)
        def _():
            greet([partner("head", 1)] + [partner("dp", b) for b in (1, 2, 4, 8)])

        for now in sorted(set(p[0] for p in plan[0])):
            if now < last:

                @pl.when(step == now)
                def _():
                    for slot, stream, phase in plan[0]:
                        if slot == now:
                            phases[stream][phase]()

    @pl.when(step == 0)
    def _():
        for o in accs:
            o[...] = jnp.zeros_like(o)

    for s in range(2):
        q, kt, v, do, p = sides[s]
        first = s * (steps + 1)

        @pl.when((step >= first) & (step < first + steps))
        def _():
            block = step - first

            @pl.when(block == 0)
            def _():
                dk[...] = jnp.zeros_like(dk)
                dv[...] = jnp.zeros_like(dv)

            at = pl.multiple_of(block * qb, qb)
            side_ds = ds.at[s * 2 * pairs : (s + 1) * 2 * pairs]
            attend_back(q, kt, v, do, p, side_ds, at, dq, dk, dv, pairs, qb)

        @pl.when(step == first + steps)
        def _():
            dkt[...] = (dk[...] * 2.0**-SCALE_BITS).astype(BF16)
            dvt[...] = dv[...].astype(BF16)
            w = weights[s]
            wq, wk, wv = (w[i * model : (i + 1) * model, :] for i in range(3))
            project[s][:, :width] = dot_nn(xt[:, near], dq[...]).astype(BF16)
            project[s][:, width : 2 * width] = dot_nt(xt[...], dkt[...]).astype(BF16)
            project[s][:, 2 * width :] = dot_nt(xt[...], dvt[...]).astype(BF16)
            mine = dot_nt(wq, dq[...]) + dot_nn(wk, dkt[:, near]) + dot_nn(wv, dvt[:, near])
            theirs = dot_nn(wk, dkt[:, far]) + dot_nn(wv, dvt[:, far])
            if s:
                token_out[...] += mine
                token_far[...] = (token_far[...].astype(F32) + theirs).astype(BF16)
            else:
                token_out[...] = mine
                token_far[...] = theirs.astype(BF16)
            bias = sum_other if fast and s else sums.at[5] if fast else sum_far if s else sum_out
            ones = jnp.ones((8, nq), BF16)
            bias[8:16, :] = dot_nn(ones, dq[...])
            ones = jnp.ones((8, xt.shape[1]), BF16)
            bias[16:24, :] = dot_nt(ones, dvt[...])

    @pl.when(step >= 2 * steps + 2)
    def _():
        count_rows(code, ds, (step - 2 * steps - 2) * hb, accs, bits, hb)

    @pl.when(step == last - 1)
    def _():
        if fast:
            outs = (sums.at[5], sum_other)
        else:
            outs = (sum_out, sum_far)
        heads = 2 * pairs
        for s, o in enumerate(outs):
            o[0:8, :] = jnp.zeros((8, width), F32)
            for t, (acc, b) in enumerate(zip(accs, bits)):
                o[0:8, t * 128 : t * 128 + 2**b] = table_sums(acc[...], b, s * heads, heads)
            o[24:, :] = (pre_other if s else pre_own)[...]
        if fast:
            for slot, stream, phase in plan[0]:
                if slot >= last:
                    phases[stream][phase]()
            sum_out[...] = sums[4]


def attend_backward(sides, code, xt, weights, bits, grads, pre, collective_id, fast, plan, chunks, qb=128, hb=64):
    nq, width = sides[0][0].shape
    keys = sides[0][1].shape[1]
    model = xt.shape[0]
    pairs = width // 128
    heads = 2 * pairs
    steps = nq // qb
    ratio = qb // hb
    full = lambda shape: pl.BlockSpec(shape, lambda i: (0,) * len(shape), pipeline_mode=pl.Buffered(1))
    anywhere = pl.BlockSpec(memory_space=pl.ANY)
    in_specs, operands = [], []
    for s in range(2):
        clip = lambda i, s=s: jnp.clip(i - s * (steps + 1), 0, steps - 1)
        row = pl.BlockSpec((qb, width), lambda i, clip=clip: (clip(i), 0))
        big = pl.BlockSpec((heads, qb, keys), lambda i, clip=clip: (0, clip(i), 0))
        in_specs += [row, full((width, keys)), full((keys, width)), row, big]
        operands += list(sides[s])
    in_specs.append(
        pl.BlockSpec((hb, keys), lambda i: (jnp.clip(i - 2 * steps - 2, 0, steps * ratio - 1), 0))
    )
    in_specs += [full(a.shape) for a in (xt, *weights)]
    in_specs += [full(a.shape) for a in grads[:-3]] + [anywhere] + [full(a.shape) for a in (*grads[-2:], *pre)]
    operands += [code, xt, *weights, *grads, *pre]
    sum_shape = (24 + pre[0].shape[0], width)
    project_shape = (model, 3 * width)
    shapes, out_specs = [], []
    if fast:
        hidden = grads[-3].shape[2]
        shapes += [((hidden, model), BF16), ((model, hidden), BF16), ((model, width), BF16), (project_shape, BF16)]
        out_specs += [anywhere] * 4
    shapes += [((model, nq), F32), (sum_shape, F32)]
    if not fast:
        shapes += [((model, nq), BF16), (sum_shape, F32)] + [(project_shape, BF16)] * 2
    out_specs += [full(s) for s, _ in shapes[len(out_specs) :]]
    scratch = [
        pltpu.VMEM((2 * heads, nq, keys), BF16),
        pltpu.VMEM((width, keys), F32),
        pltpu.VMEM((width, keys), F32),
        pltpu.VMEM((nq, width), BF16),
        pltpu.VMEM((width, keys), BF16),
        pltpu.VMEM((width, keys), BF16),
    ] + [pltpu.VMEM((2 ** (b - 1) * 8, 2 * heads * 16), F32) for b in bits]
    params = dict(vmem_limit_bytes=BACK_VM)
    if fast:
        scratch += [pltpu.VMEM(project_shape, BF16)] * 2
        scratch += [pltpu.VMEM((model, nq), BF16)] * 2
        scratch += [pltpu.VMEM((6, *sum_shape), F32), pltpu.VMEM(sum_shape, F32)]
        scratch += [pltpu.VMEM((5, *sum_shape), F32)]
        scratch += [pltpu.SemaphoreType.DMA((2,)), pltpu.SemaphoreType.DMA((5,)), pltpu.SemaphoreType.DMA((5,))]
        n = 0
        for rows, columns, pieces in ((hidden, model, chunks[0]), (model, hidden, chunks[1])):
            for _ in range(pieces):
                scratch += stream_scratch(rows, columns // pieces, plan[1][n], n >= chunks[0], n < chunks[0])
                n += 1
        scratch += stream_scratch(model, width, plan[1][n], False)
        for start, stop in chunks[2]:
            n += 1
            scratch += stream_scratch(model, stop - start, plan[1][n], False)
        params.update(collective_id=collective_id, has_side_effects=True)
    return pl.pallas_call(
        functools.partial(
            back_kernel, pairs=pairs, qb=qb, hb=hb, steps=steps, bits=bits, fast=fast, chunks=chunks, plan=plan
        ),
        out_shape=tuple(jax.ShapeDtypeStruct(s, t) for s, t in shapes),
        grid=(2 * steps + 2 + steps * ratio,),
        in_specs=in_specs,
        out_specs=tuple(out_specs),
        scratch_shapes=scratch,
        compiler_params=pltpu.CompilerParams(**params),
        cost_estimate=pl.CostEstimate(
            flops=16 * nq * keys * width, bytes_accessed=300 * 2**20, transcendentals=0
        ),
    )(*operands)


norm_epsilon = 1e-05


def mm(a, b):
    return jnp.dot(a, b, preferred_element_type=F32)


def normalize(value):
    center = value - jnp.mean(value, axis=-1, keepdims=True)
    spread = jnp.mean(center * center, axis=-1, keepdims=True)
    root = lax.rsqrt(spread + norm_epsilon)
    return center * root, root


def normalize_back(grad, normed, root):
    return root * (
        grad
        - jnp.mean(grad, axis=-1, keepdims=True)
        - normed * jnp.mean(grad * normed, axis=-1, keepdims=True)
    )


def gelu_parts(u):
    t = 1.0 / (1.0 + (0.3275911 * 0.7071067811865476) * jnp.abs(u))
    e = jnp.exp(-0.5 * u * u)
    poly = t * (
        0.254829592 + t * (-0.284496736 + t * (1.421413741 + t * (-1.453152027 + t * 1.061405429)))
    )
    tail = 0.5 * e * poly
    below = jnp.where(u >= 0, 1.0 - tail, tail)
    return u * below, below + u * (e * 0.3989422804014327)


def swap_dp(x, bit):
    n = lax.axis_size("dp")
    return lax.ppermute(x, "dp", [(i, i ^ bit) for i in range(n)])


def swap_head(x):
    return lax.ppermute(x, "head", [(0, 1), (1, 0)])


def dp_bits():
    n, bit, out = lax.axis_size("dp"), 1, []
    while bit < n:
        out.append(bit)
        bit *= 2
    return out


def bit_of(bit):
    return (lax.axis_index("dp") // bit) % 2


def in_order(first, mine, theirs):
    low = jnp.where(first == 0, mine, theirs)
    high = jnp.where(first == 0, theirs, mine)
    return jnp.concatenate([low, high], axis=0)


def rows_of(x, index, rows):
    return lax.dynamic_slice_in_dim(x, index * rows, rows, 0)


def halve(g, bit):
    rows = g.shape[0] // 2
    b = bit_of(bit)
    got = swap_dp(rows_of(g, 1 - b, rows), bit)
    return (rows_of(g, b, rows).astype(F32) + got.astype(F32)).astype(BF16)


def reduce_grad(own, other, head_first):
    bits = dp_bits()
    own, other = halve(own, 1), halve(other, 1)
    if not head_first:
        own, other = halve(own, 2), halve(other, 2)
    g = (own.astype(F32) + swap_head(other).astype(F32)).astype(BF16)
    for bit in bits[1 if head_first else 2 :]:
        g = halve(g, bit)
    for bit in reversed(bits):
        g = in_order(bit_of(bit), g, swap_dp(g, bit))
    return g.astype(F32)


BACK_CHUNKS = (3, 2, ((0, 384), (384, 768), (768, 1152)))
BACK_PLAN = (
    ((0, 5, 0), (0, 2, 2), (0, 3, 0), (0, 4, 0), (0, 1, 2), (0, 0, 2), (1, 5, 1), (2, 2, 3), (2, 3, 1), (2, 1, 3), (3, 4, 1), (3, 1, 4), (3, 0, 3), (4, 5, 2), (4, 2, 4), (4, 1, 5), (4, 0, 4), (5, 2, 5), (5, 1, 6), (6, 3, 2), (6, 0, 5), (7, 5, 3), (7, 2, 6), (7, 4, 2), (7, 1, 7), (7, 0, 6), (8, 5, 4), (8, 2, 7), (9, 5, 5), (9, 3, 3), (9, 0, 7), (10, 8, 0), (10, 7, 0), (10, 6, 0), (10, 9, 0), (10, 5, 6), (10, 4, 3), (10, 2, 8), (10, 3, 4), (10, 1, 8), (11, 5, 7), (11, 8, 1), (11, 7, 1), (11, 0, 8), (12, 5, 8), (12, 4, 4), (12, 6, 1), (12, 2, 9), (12, 3, 5), (12, 1, 9), (12, 0, 9), (13, 5, 9), (13, 7, 2), (13, 8, 2), (14, 4, 5), (14, 9, 1), (14, 3, 6), (14, 8, 3), (14, 7, 3), (15, 6, 2), (15, 8, 4), (15, 7, 4), (15, 4, 6), (15, 3, 7), (16, 8, 5), (16, 7, 5), (16, 6, 3), (17, 4, 7), (17, 8, 6), (17, 3, 8), (17, 7, 6), (17, 6, 4), (18, 10, 0), (18, 8, 7), (18, 3, 9), (18, 6, 5), (18, 4, 8), (18, 10, 1), (18, 6, 6), (18, 7, 7), (18, 4, 9), (18, 10, 2), (18, 6, 7), (18, 8, 8), (18, 10, 3), (18, 8, 9), (18, 7, 8), (18, 10, 4), (18, 6, 8), (18, 7, 9), (18, 6, 9), (18, 10, 5)),
    ('yx01', 'xy01', '0xy1', 'xy01', 'yx01', 'yx01', 'xy01', '0yx1', 'x0y1'),
)


def row_sums(x):
    return jnp.sum(x, axis=0, keepdims=True)


def ffn_kernel(*refs, heads, chunk, orders):
    refs = list(refs)
    take = lambda n: [refs.pop(0) for _ in range(n)]
    x, cot, ctx_a, ctx_b, ow_a, ow_b, params, small_a, small_b, uw_a, uw_b, dw_a, dw_b = take(13)
    out, first, do_a, do_b, go_a, go_b, pre_a, pre_b = take(8)
    states = take(len(orders))
    (gd_all,) = take(1) if not orders else (None,)
    gu_all, uw, dw, act, slope, gd, gu, total, bias, bias_sum, sem_in, sem_out = take(12)
    width = ctx_a.shape[1]
    model = x.shape[1]
    hidden = uw_a.shape[1]
    per = hidden // chunk
    streams = []
    for i, order in enumerate(orders):
        cols = model // len(orders)
        buf, send, recv = take(3)
        own, other = gd.at[0:hidden], gd.at[hidden : 2 * hidden]
        columns = slice(i * cols, (i + 1) * cols)
        streams.append(
            stream_phases(own, other, None, None, None, columns, [buf, states[i]], send, recv, order, "head")
        )
    for s, (u, d) in enumerate(((uw_a, dw_a), (uw_b, dw_b))):
        for i in range(per):
            n = s * per + i
            cols = slice(i * chunk, (i + 1) * chunk)
            pltpu.make_async_copy(u.at[:, cols], uw.at[n], sem_in.at[n]).start()
            pltpu.make_async_copy(d.at[cols, :], dw.at[n], sem_in.at[2 * per + n]).start()
            small = (small_a, small_b)[s]
            for j in range(chunk // width):
                at = heads + 2 + i * (chunk // width) + j
                bias[n * 8 : n * 8 + 1, j * width : (j + 1) * width] = small[at : at + 1, :]
    if orders:
        near = {"y": ("head", 1), "x": ("dp", 2), "0": ("dp", 4)}
        partners = [partner("dp", 1)] + [partner(*near[axis]) for axis in sorted({order[0] for order in orders})]
        announce(partners)
    gain1, shift1, gain2, shift2, output_shift, down_shift = (params[i : i + 1, :] for i in range(6))

    def put(i, vector):
        for o in (pre_a, pre_b):
            for n in range(model // width):
                o[i * (model // width) + n : i * (model // width) + n + 1, :] = vector[
                    :, n * width : (n + 1) * width
                ]

    attend = dot_nn(ctx_a[...], ow_a[...]) + dot_nn(ctx_b[...], ow_b[...]) + output_shift
    n1, root1 = normalize(x[...].astype(F32) + attend)
    normed = n1 * gain1 + shift1
    low = normed.astype(BF16)
    total[...] = normed + down_shift

    def forward(n, _):
        pltpu.make_async_copy(uw.at[n], uw.at[n], sem_in.at[n]).wait()
        row = bias[pl.ds(pl.multiple_of(n * 8, 8), 8), :][0:1]
        a, slope_n = gelu_parts(dot_nn(low, uw[n]) + row)
        a = a.astype(BF16)
        act[n] = a
        slope[n] = slope_n.astype(BF16)
        pltpu.make_async_copy(dw.at[n], dw.at[n], sem_in.at[2 * per + n]).wait()
        total[...] += dot_nn(a, dw[n])
        return 0

    lax.fori_loop(0, 2 * per, forward, 0)
    n2, root2 = normalize(total[...])
    out[...] = n2 * gain2 + shift2
    g = cot[...].astype(F32)
    put(2, row_sums(g * n2))
    put(3, row_sums(g))
    back = normalize_back(g * gain2, n2, root2)
    back_feed = back.astype(BF16)
    put(5, row_sums(back_feed.astype(F32)))
    total[...] = back

    def stores(n):
        rows = pl.ds(pl.multiple_of(n * chunk, chunk), chunk)
        cols = pl.ds(pl.multiple_of(lax.rem(n, per) * chunk, chunk), chunk)
        copies = [pltpu.make_async_copy(gu.at[n], gu_all.at[lax.div(n, per), :, cols], sem_out.at[n])]
        if not orders:
            copies.append(pltpu.make_async_copy(gd.at[rows], gd_all.at[rows], sem_out.at[2 * per + n]))
        return copies

    def backward_down(n, _):
        gd[pl.ds(pl.multiple_of(n * chunk, chunk), chunk), :] = dot_tn(act[n], back_feed).astype(BF16)
        return 0

    def backward_up(n, _):
        back_up = (dot_nt(back_feed, dw[n]) * slope[n].astype(F32)).astype(BF16)
        bias_sum[pl.ds(pl.multiple_of(n * 8, 8), 8), :] = jnp.broadcast_to(
            row_sums(back_up.astype(F32)), (8, chunk)
        )
        gu[n] = dot_tn(low, back_up).astype(BF16)
        for copy in stores(n):
            copy.start()
        total[...] += dot_nt(back_up, uw[n])
        return 0

    def hop(i):
        for phases in streams:
            phases[i]()

    if orders:
        assert per == 2
        lax.fori_loop(0, 2, lambda i, z: backward_down(2 * i + 1 - dp_bit(1), z), 0)
        pl.semaphore_wait(pltpu.get_barrier_semaphore(), len(partners))
        hop(0)
        lax.fori_loop(0, 2, lambda i, z: backward_down(2 * i + dp_bit(1), z), 0)
    else:
        lax.fori_loop(0, 2 * per, backward_down, 0)
    hop(1)
    lax.fori_loop(0, 2 * per, backward_up, 0)
    for n in range(2 * per):
        for j in range(chunk // width):
            at = 6 * (model // width) + (n % per) * (chunk // width) + j
            (pre_a, pre_b)[n // per][at : at + 1, :] = bias_sum[n * 8 : n * 8 + 1, j * width : (j + 1) * width]
    back = total[...]
    put(0, row_sums(back * n1))
    put(1, row_sums(back))
    back = normalize_back(back * gain1, n1, root1)
    first[...] = back
    back_attend = back.astype(BF16)
    put(4, row_sums(back_attend.astype(F32)))
    for ctx, ow, do, go in ((ctx_a, ow_a, do_a, go_a), (ctx_b, ow_b, do_b, go_b)):
        do[...] = dot_nt(back_attend, ow[...]).astype(BF16)
        go[...] = dot_tn(back_attend, ctx[...]).astype(BF16)
    for n in range(2 * per):
        for copy in stores(n):
            copy.wait()
    hop(2)


def feed_forward(x, cot, contexts, output_weights, params, smalls, up_weights, down_weights, heads, orders,
                 collective_id, chunk=768):
    nq, model = x.shape
    width = contexts[0].shape[1]
    hidden = up_weights[0].shape[1]
    n = 2 * hidden // chunk
    here = pl.BlockSpec(memory_space=pltpu.VMEM)
    anywhere = pl.BlockSpec(memory_space=pl.ANY)
    pre_rows = 6 * (model // width) + hidden // width
    shape = jax.ShapeDtypeStruct
    state_shapes, hop_scratch, compiler = [], [], dict(vmem_limit_bytes=VM)
    for order in orders:
        cols = model // len(orders)
        state_shapes.append((1, hidden // 2, cols) if order[0] == "y" else (2, hidden // 4, cols))
        hop_scratch.append(pltpu.VMEM((2, hidden // 2, cols), BF16))
        hop_scratch += [pltpu.SemaphoreType.DMA((STREAM_SEMS,))] * 2
    if orders:
        compiler.update(collective_id=collective_id, has_side_effects=True)
    return pl.pallas_call(
        functools.partial(ffn_kernel, heads=heads, chunk=chunk, orders=orders),
        out_shape=(
            shape((nq, model), F32),
            shape((nq, model), F32),
            shape((nq, width), BF16),
            shape((nq, width), BF16),
            shape((model, width), BF16),
            shape((model, width), BF16),
            shape((pre_rows, width), F32),
            shape((pre_rows, width), F32),
            *(shape(s, BF16) for s in state_shapes),
            *((shape((2 * hidden, model), BF16),) if not orders else ()),
            shape((2, model, hidden), BF16),
        ),
        in_specs=[here] * 9 + [anywhere] * 4,
        out_specs=(here,) * (8 + len(orders)) + (anywhere,) * (1 if orders else 2),
        scratch_shapes=[
            pltpu.VMEM((n, model, chunk), BF16),
            pltpu.VMEM((n, chunk, model), BF16),
            pltpu.VMEM((n, nq, chunk), BF16),
            pltpu.VMEM((n, nq, chunk), BF16),
            pltpu.VMEM((2 * hidden, model), BF16),
            pltpu.VMEM((n, model, chunk), BF16),
            pltpu.VMEM((nq, model), F32),
            pltpu.VMEM((n * 8, chunk), F32),
            pltpu.VMEM((n * 8, chunk), F32),
            pltpu.SemaphoreType.DMA((2 * n,)),
            pltpu.SemaphoreType.DMA((2 * n,)),
            *hop_scratch,
        ],
        compiler_params=pltpu.CompilerParams(**compiler),
        cost_estimate=pl.CostEstimate(
            flops=12 * nq * model * 2 * hidden, bytes_accessed=100 * 2**20, transcendentals=nq * 4 * hidden
        ),
    )(x, cot, *contexts, *output_weights, params, *smalls, *up_weights, *down_weights)


def finish_kernel(index, *refs, count, heads, scale):
    refs = list(refs)
    take = lambda n: [refs.pop(0) for _ in range(n)]
    down, up, out, project = take(4)
    down_piece, up_piece, out_piece, project_piece = take(4)
    tokens_t, first, sums, params, small = take(5)
    project_w, out_w, up_w, down_w = take(4)
    project_a, query_a, value_a, out_a, out_shift_a, gain1_a, shift1_a = take(7)
    up_a, up_bias_a, down_a, down_shift_a, gain2_a, shift2_a, *table_a = take(9)
    tokens_o, project_o, query_o, value_o, out_o, out_shift_o, gain1_o, shift1_o = take(8)
    up_o, up_bias_o, down_o, down_shift_o, gain2_o, shift2_o, *table_o = take(9)
    project_r, query_r, value_r, out_r, out_shift_r, gain1_r, shift1_r = take(7)
    up_r, up_bias_r, down_r, down_shift_r, gain2_r, shift2_r, *table_r = take(9)
    thirds = project.shape[1] // 3
    wide = lambda ref: ref[...].astype(F32)
    renew = lambda average, weight, grad: 0.5 * average + 0.5 * (weight - grad * scale)

    down_o[...] = wide(down)
    up_o[...] = wide(up)
    out_o[...] = jnp.transpose(wide(out))
    for i in range(3):
        project_o[i] = project[:, i * thirds : (i + 1) * thirds].astype(F32)
    tokens_o[...] = first[...] + jnp.transpose(tokens_t[...])

    @pl.when(pl.program_id(0) == 0)
    def _():
        up_r[...] = renew(up_a[...], wide(up_w), wide(up_piece))
        down_r[...] = renew(down_a[...], wide(down_w), wide(down_piece))
        out_r[...] = renew(out_a[...], jnp.transpose(wide(out_w)), wide(out_piece))
        for i in range(3):
            project_r[i] = renew(project_a[i], project_w[i].astype(F32), project_piece[:, i * thirds : (i + 1) * thirds].astype(F32))
        width = sums.shape[1]

        def vector(ref, at, n):
            return jnp.concatenate([ref[at + i : at + i + 1, :] for i in range(n)], axis=1)

        def flat(o, r, a, weight, grad):
            n = a.shape[0]
            o[...] = grad.reshape(n)
            r[...] = renew(a[...], weight.reshape(n), grad.reshape(n))

        flat(query_o, query_r, query_a, small[heads : heads + 1, :], sums[8:9, :])
        flat(value_o, value_r, value_a, small[heads + 1 : heads + 2, :], sums[16:17, :])
        two = params.shape[1] // width
        commons = (
            (gain1_o, gain1_r, gain1_a),
            (shift1_o, shift1_r, shift1_a),
            (gain2_o, gain2_r, gain2_a),
            (shift2_o, shift2_r, shift2_a),
            (out_shift_o, out_shift_r, out_shift_a),
            (down_shift_o, down_shift_r, down_shift_a),
        )
        for i, (o, r, a) in enumerate(commons):
            flat(o, r, a, params[i : i + 1, :], vector(sums, 24 + two * i, two))
        many = up_bias_a.shape[0] // width
        flat(
            up_bias_o, up_bias_r, up_bias_a, vector(small, heads + 2, many), vector(sums, 24 + 6 * two, many)
        )
        for t, (o, r, a) in enumerate(zip(table_o, table_r, table_a)):
            n = a.shape[1]
            grad = sums[0:heads, t * 128 : t * 128 + n]
            o[...] = grad
            r[...] = renew(a[...], small[0:heads, t * 128 : t * 128 + n], grad)


def finish(index, totals, tokens_t, first, sums, params, small, weights, averages, count, tokens_count, heads):
    swap = lambda a: a.transpose(1, 0, 2) if a.ndim == 3 else a.T
    turned = (0, 3, 13, 14, 15)
    averages = [swap(a) if i in turned else a for i, a in enumerate(averages)]
    down, up, out, project = totals
    model = first.shape[1]
    nq = first.shape[0]
    width = project.shape[1] // 3
    steps = model // 128
    full = lambda a: pl.BlockSpec(a.shape, lambda i, d: (0,) * len(a.shape))
    rows = lambda a: pl.BlockSpec((a.shape[0] // steps, a.shape[1]), lambda i, d: (i, 0))
    piece = lambda a: pl.BlockSpec(
        (a.shape[0] // count, *a.shape[1:]), lambda i, d: (d[0],) + (0,) * (len(a.shape) - 1)
    )
    columns = lambda n: pl.BlockSpec((n, 128), lambda i, d: (0, i))
    shape = lambda s: jax.ShapeDtypeStruct(s, F32)
    project_w, out_w, up_w, down_w = weights
    in_specs = [rows(a) for a in totals] + [piece(a) for a in totals]
    in_specs += [rows(tokens_t), columns(nq), full(sums), full(params), full(small)]
    project_spec = pl.BlockSpec((3, model // count, width), lambda i, d: (0, d[0], 0))
    in_specs += [project_spec, full(out_w), piece(up_w), piece(down_w)] + [full(a) for a in averages]
    grads = [
        shape((3, model, width)), shape((width,)), shape((width,)), shape((width, model)), shape((model,)),
        shape((model,)), shape((model,)), shape(up.shape), shape((up.shape[1],)), shape(down.shape),
        shape((model,)), shape((model,)), shape((model,)), *(shape(a.shape) for a in averages[13:]),
    ]
    specs = [full(g) for g in grads]
    specs[0] = pl.BlockSpec((3, 128, width), lambda i, d: (0, i, 0))
    specs[3] = columns(width)
    specs[7] = rows(up)
    specs[9] = rows(down)
    tokens, *results = pl.pallas_call(
        functools.partial(finish_kernel, count=count, heads=heads, scale=1.0 / tokens_count),
        out_shape=(shape((nq, model)), *grads, *(shape(a.shape) for a in averages)),
        grid_spec=pltpu.PrefetchScalarGridSpec(
            num_scalar_prefetch=1,
            grid=(steps,),
            in_specs=in_specs,
            out_specs=(columns(nq), *specs, *(full(a) for a in averages)),
        ),
        compiler_params=pltpu.CompilerParams(vmem_limit_bytes=VM),
        cost_estimate=pl.CostEstimate(flops=2**24, bytes_accessed=40 * 2**20, transcendentals=0),
    )(index, *totals, *totals, tokens_t, first, sums, params, small, *weights, *averages)
    grads, renewed = results[:16], results[16:]
    grads = [swap(a) if i in turned and i != 3 else a for i, a in enumerate(grads)]
    return tokens, *grads, *(swap(a) if i in turned else a for i, a in enumerate(renewed))


def local(
    tokens,
    cotangent,
    form_number,
    sequence_bucket,
    horizontal_bucket,
    vertical_bucket,
    project_weight,
    query_bias,
    value_bias,
    output_weight,
    output_bias,
    first_gain,
    first_shift,
    up_weight,
    up_bias,
    down_weight,
    down_bias,
    second_gain,
    second_shift,
    sequence_table,
    horizontal_table,
    vertical_table,
    project_weight_average,
    query_bias_average,
    value_bias_average,
    output_weight_average,
    output_bias_average,
    first_gain_average,
    first_shift_average,
    up_weight_average,
    up_bias_average,
    down_weight_average,
    down_bias_average,
    second_gain_average,
    second_shift_average,
    sequence_table_average,
    horizontal_table_average,
    vertical_table_average,
):
    total_rows, model_width = tokens.shape
    local_width = project_weight.shape[2]
    local_heads = sequence_table.shape[1]
    hidden = up_weight.shape[1]
    share_rows = total_rows // lax.axis_size("head")
    head_index = lax.axis_index("head")
    share_start = head_index * share_rows
    block_rows = 128
    buckets = (sequence_bucket, horizontal_bucket, vertical_bucket)
    tables = (sequence_table, horizontal_table, vertical_table)
    bits = tuple((t.shape[0] - 1).bit_length() for t in tables)
    project_stack = project_weight.transpose(1, 0, 2)
    flat_project = project_stack.reshape(3 * model_width, local_width)

    params = jnp.concatenate(
        [first_gain, first_shift, second_gain, second_shift, output_bias, down_bias]
    ).reshape(6, model_width).astype(F32)
    lanes = [jnp.pad(t.T, ((0, 0), (0, local_width // 3 - t.shape[0]))) for t in tables]
    small = jnp.concatenate(
        [
            jnp.concatenate(lanes, axis=1),
            jnp.concatenate([query_bias, value_bias, up_bias]).reshape(-1, local_width),
        ],
        axis=0,
    ).astype(F32)
    small = jnp.pad(small, ((0, 16 - small.shape[0]), (0, 0)))
    smalls, project_weights = [small], [flat_project]
    output_weights, up_weights, down_weights = [output_weight], [up_weight], [down_weight]

    form_row = form_number.reshape(total_rows)
    form_own = lax.dynamic_slice_in_dim(form_row, share_start, share_rows, 0)
    code = encode(
        [rows_of(b, head_index, share_rows) for b in buckets], form_own[:, None] == form_row[None, :]
    )
    own_tokens = rows_of(tokens, head_index, share_rows)

    scaled, keys_t, values, probs, contexts = [], [], [], [], []
    for s in range(2):
        wq, wk, wv = (project_weights[s][i * model_width : (i + 1) * model_width] for i in range(3))
        bq = smalls[s][local_heads : local_heads + 1]
        bv = smalls[s][local_heads + 1 : local_heads + 2]
        q = ((mm(own_tokens, wq) + bq) * 0.125).astype(BF16)
        q = q * jnp.array(2.0**SCALE_BITS, BF16)
        kt = dot_general_t(wk, tokens).astype(BF16)
        v = (mm(tokens, wv) + bv).astype(BF16)
        if s == 0:
            fetch = (
                ("small", (0, -1, -1), small),
                ("all", (0, 3, 7), flat_project),
                ("all", (0, 4, 7), output_weight),
                ("first", (0, -1, -1), up_weight),
            )
        else:
            fetch = (("rest", (-1, 0, 4), up_part), ("all", (0, 4, 8), down_weight))
        p, context, *fetched = attend_fwd(code, smalls[s], q, kt, v, fetch, s, qb=block_rows)
        if s == 0:
            smalls.append(fetched[0])
            project_weights.append(fetched[1])
            output_weights.append(fetched[2])
            up_part = fetched[3]
        else:
            up_weights.append(fetched[0])
            down_weights.append(fetched[1])
        scaled.append(q)
        keys_t.append(kt)
        values.append(v)
        probs.append(p)
        contexts.append(context)
    fast = lax.axis_size("dp") == 16
    (
        layer_output, back_first, back_own, back_other, out_own, out_other, pre_own, pre_other, *grads
    ) = feed_forward(
        own_tokens, cotangent, contexts, output_weights, params, smalls, up_weights, down_weights, local_heads,
        BACK_PLAN[1][: BACK_CHUNKS[0]] if fast else (), 3,
    )

    sides = [
        (scaled[s], keys_t[s], values[s], (back_own, back_other)[s], probs[s]) for s in range(2)
    ]
    pre = (pre_own, pre_other)
    results = attend_backward(
        sides,
        code,
        tokens.T,
        project_weights,
        bits,
        (*(grads if fast else grads[1:]), out_own, out_other),
        pre,
        2,
        fast,
        BACK_PLAN,
        BACK_CHUNKS,
        qb=block_rows,
    )
    token_count = total_rows * lax.axis_size("dp")
    group_count = lax.axis_size("dp")
    group_index = lax.axis_index("dp")
    if fast:
        width = model_width // group_count
        output_piece = lax.dynamic_slice_in_dim(output_weight, group_index * width, width, 1)
        averages = (
            project_weight_average, query_bias_average, value_bias_average, output_weight_average,
            output_bias_average, first_gain_average, first_shift_average, up_weight_average, up_bias_average,
            down_weight_average, down_bias_average, second_gain_average, second_shift_average,
            sequence_table_average, horizontal_table_average, vertical_table_average,
        )
        return layer_output, *finish(
            jnp.full((1,), group_index, I32),
            results[:4],
            results[4],
            back_first,
            results[5],
            params,
            small,
            (project_stack, output_piece, up_weight, down_weight),
            averages,
            group_count,
            token_count,
            local_heads,
        )
    tokens_gradient, sums, far, sums_other = results[:4]
    tokens_gradient = tokens_gradient + swap_head(far).astype(F32)
    sums = sums + swap_head(sums_other)
    for bit in dp_bits():
        sums = sums + swap_dp(sums, bit)
    down_total, up_total = reduce_grad(grads[0][:hidden], grads[0][hidden:], True), reduce_grad(*grads[1], False)
    output_total = reduce_grad(out_own, out_other, True)
    project_total = reduce_grad(results[4], results[5], False)
    tokens_gradient = back_first + tokens_gradient.T
    project_total = project_total.reshape(model_width, 3, local_width)
    output_total = output_total.T
    query_bias_total, value_bias_total = sums[8], sums[16]
    tail = sums[24:].reshape(-1)
    (
        first_gain_total,
        first_shift_total,
        second_gain_total,
        second_shift_total,
        output_bias_total,
        down_bias_total,
    ) = (tail[i * model_width : (i + 1) * model_width] for i in range(6))
    up_bias_total = tail[6 * model_width :]
    sequence_total, horizontal_total, vertical_total = (
        sums[:local_heads, i * 128 : i * 128 + t.shape[0]].T for i, t in enumerate(tables)
    )
    up_weight_total, down_weight_total, output_weight_total = up_total, down_total, output_total

    def renew(average, weight, gradient):
        return 0.5 * average + 0.5 * (weight.astype(jnp.float32) - gradient / token_count)

    def part_of(array, along):
        width = array.shape[along] // group_count
        return lax.dynamic_slice_in_dim(array, group_index * width, width, along)

    return (
        layer_output,
        tokens_gradient,
        project_total,
        query_bias_total,
        value_bias_total,
        output_weight_total,
        output_bias_total,
        first_gain_total,
        first_shift_total,
        up_weight_total,
        up_bias_total,
        down_weight_total,
        down_bias_total,
        second_gain_total,
        second_shift_total,
        sequence_total,
        horizontal_total,
        vertical_total,
        renew(project_weight_average, part_of(project_weight, 0), part_of(project_total, 0)),
        renew(query_bias_average, query_bias, query_bias_total),
        renew(value_bias_average, value_bias, value_bias_total),
        renew(output_weight_average, part_of(output_weight, 1), part_of(output_weight_total, 1)),
        renew(output_bias_average, output_bias, output_bias_total),
        renew(first_gain_average, first_gain, first_gain_total),
        renew(first_shift_average, first_shift, first_shift_total),
        renew(up_weight_average, part_of(up_weight, 0), part_of(up_weight_total, 0)),
        renew(up_bias_average, up_bias, up_bias_total),
        renew(down_weight_average, part_of(down_weight, 0), part_of(down_weight_total, 0)),
        renew(down_bias_average, down_bias, down_bias_total),
        renew(second_gain_average, second_gain, second_gain_total),
        renew(second_shift_average, second_shift, second_shift_total),
        renew(sequence_table_average, sequence_table, sequence_total),
        renew(horizontal_table_average, horizontal_table, horizontal_total),
        renew(vertical_table_average, vertical_table, vertical_total),
    )


def solution(mesh):
    in_specs = (
        P("dp", None),
        P(("dp", "head"), None),
        P("dp", None),
        P("dp", None),
        P("dp", None),
        P("dp", None),
        P(None, None, "head"),
        P("head"),
        P("head"),
        P("head", None),
        P(),
        P(),
        P(),
        P(None, "head"),
        P("head"),
        P("head", None),
        P(),
        P(),
        P(),
        P(None, "head"),
        P(None, "head"),
        P(None, "head"),
        P("dp", None, "head"),
        P("head"),
        P("head"),
        P("head", "dp"),
        P(),
        P(),
        P(),
        P("dp", "head"),
        P("head"),
        P(("head", "dp"), None),
        P(),
        P(),
        P(),
        P(None, "head"),
        P(None, "head"),
        P(None, "head"),
    )
    out_specs = (
        P(("dp", "head"), None),
        P(("dp", "head"), None),
        P(None, None, "head"),
        P("head"),
        P("head"),
        P("head", None),
        P(),
        P(),
        P(),
        P(None, "head"),
        P("head"),
        P("head", None),
        P(),
        P(),
        P(),
        P(None, "head"),
        P(None, "head"),
        P(None, "head"),
        P("dp", None, "head"),
        P("head"),
        P("head"),
        P("head", "dp"),
        P(),
        P(),
        P(),
        P("dp", "head"),
        P("head"),
        P(("head", "dp"), None),
        P(),
        P(),
        P(),
        P(None, "head"),
        P(None, "head"),
        P(None, "head"),
    )
    return jax.shard_map(local, mesh=mesh, in_specs=in_specs, out_specs=out_specs, check_vma=False)
```

```python
import functools
import jax
import jax.numpy as jnp
from jax import lax
from jax.experimental import pallas as pl
from jax.sharding import PartitionSpec as P
from jax.experimental.pallas import tpu as pltpu

F32, BF16, I32 = jnp.float32, jnp.bfloat16, jnp.int32
SCALE_BITS = 27
STEP = 2.0**11
VM = 56 * 2**20
BACK_VM = 60 * 2**20
SAME = 2**17


def encode(buckets, same):
    seq, hor, ver = buckets
    return seq + 32 * hor + 2048 * ver + jnp.where(same, SAME, 0)


def buckets_of(code):
    return code & 31, (code >> 5) & 63, (code >> 11) & 63


def dot_nt(a, b):
    return lax.dot_general(a, b, (((1,), (1,)), ((), ())), preferred_element_type=F32)


def dot_tn(a, b):
    return lax.dot_general(a, b, (((0,), (0,)), ((), ())), preferred_element_type=F32)


def dot_general_t(w, x):
    return lax.dot_general(w, x, (((0,), (1,)), ((), ())), preferred_element_type=F32)


def dot_tt(a, b):
    return lax.dot_general(a, b, (((0,), (1,)), ((), ())), preferred_element_type=F32)


def dot_nn(a, b):
    return lax.dot_general(a, b, (((1,), (0,)), ((), ())), preferred_element_type=F32)


def split_pair(x):
    lane = lax.broadcasted_iota(I32, x.shape, 1)
    zero = jnp.zeros_like(x)
    return jnp.concatenate([jnp.where(lane < 64, x, zero), jnp.where(lane < 64, zero, x)], axis=0)


def partner(axis, bit):
    i = lax.axis_index(axis)
    low = lax.rem(lax.div(i, bit), 2)
    return {axis: i + bit * (1 - 2 * low)}


def dp_bit(bit):
    return lax.rem(lax.div(lax.axis_index("dp"), bit), 2)


def announce(partners):
    barrier = pltpu.get_barrier_semaphore()
    for p in partners:
        pl.semaphore_signal(barrier, inc=1, device_id=p, device_id_type=pl.DeviceIdType.MESH)


def greet(partners):
    announce(partners)
    pl.semaphore_wait(pltpu.get_barrier_semaphore(), len(partners))


def remote(src, dst, send, recv, to):
    return pltpu.make_async_remote_copy(
        src_ref=src,
        dst_ref=dst,
        send_sem=send,
        recv_sem=recv,
        device_id=to,
        device_id_type=pl.DeviceIdType.MESH,
    )


def fetch_copies(mode, source, out, send, recv):
    if mode == "small":
        return [remote(source, out, send.at[0], recv.at[0], partner("head", 1)), None, None], []
    rows = source.shape[0] if mode == "rest" else source.shape[0] // 4
    quarter = 2 * dp_bit(1) + dp_bit(2)
    one = pl.ds(pl.multiple_of(quarter * rows, rows), rows)
    two = pl.ds(pl.multiple_of(dp_bit(1) * (2 * rows), 2 * rows), 2 * rows)
    hops, local = [None, None, None], []
    if mode == "first":
        hops[0] = remote(source.at[one], out, send.at[0], recv.at[0], partner("head", 1))
    else:
        if mode == "all":
            hops[0] = remote(source.at[one], out.at[one], send.at[0], recv.at[0], partner("head", 1))
            quarter_ref = out.at[one]
        else:
            quarter_ref = source
            local.append(pltpu.make_async_copy(source, out.at[one], send.at[0]))
        hops[1] = remote(quarter_ref, out.at[one], send.at[1], recv.at[1], partner("dp", 2))
        hops[2] = remote(out.at[two], out.at[two], send.at[2], recv.at[2], partner("dp", 1))
    return hops, local


def fetched_shape(mode, w):
    rows = {"all": 1, "small": 1, "first": 0.25, "rest": 4}[mode] * w.shape[0]
    return jax.ShapeDtypeStruct((int(rows), w.shape[1]), w.dtype)


def fwd_kernel(*refs, pairs, qb, modes, points, steps):
    n = len(modes)
    code, tab, q, kt, v = refs[:5]
    sources = refs[5 : 5 + n]
    p_out, c_out = refs[5 + n : 7 + n]
    outs = refs[7 + n : 7 + 2 * n]
    b_ref, t_ref, send, recv = refs[7 + 2 * n :]
    keys = v.shape[0]
    chunk = 128
    step = pl.program_id(0)
    hops, local = [], []
    for i in range(n):
        h, l = fetch_copies(modes[i], sources[i], outs[i], send.at[i], recv.at[i])
        hops.append(h)
        local += l

    def point(now):
        for i in range(n):
            for hop in range(3):
                if points[i][hop] == now:
                    if hop and hops[i][hop - 1] is not None:
                        hops[i][hop - 1].wait_recv()
                    hops[i][hop].start()

    @pl.when(step == 0)
    def _():
        greet([partner("head", 1), partner("dp", 2), partner("dp", 1)])
        for copy in local:
            copy.start()
        for j in range(pairs):
            for t in range(3):
                ls = slice(t * chunk, (t + 1) * chunk)
                fixed = [jnp.round(tab[2 * j + g : 2 * j + g + 1, ls] * STEP).astype(I32) for g in range(2)]
                t_ref[8 * (3 * j + t) : 8 * (3 * j + t) + 8, :] = jnp.broadcast_to(
                    fixed[0] * 65536 + fixed[1], (8, chunk)
                )
        point(0)

    for now in sorted(set(sum(points, ()))):
        if 0 < now < 2 * steps and now % 2 == 0:

            @pl.when(step == now // 2)
            def _():
                if local and now == min(p[2] for p, m in zip(points, modes) if m == "rest"):
                    for copy in local:
                        copy.wait()
                point(now)

    tbs = [t_ref[8 * i : 8 * i + 8, :] for i in range(3 * pairs)]

    def gather(r, _):
        rs = pl.ds(pl.multiple_of(r * 8, 8), 8)
        for c in range(keys // chunk):
            ls = slice(c * chunk, (c + 1) * chunk)
            sums = [None] * pairs
            for t, idx in enumerate(buckets_of(code[rs, ls])):
                for j in range(pairs):
                    g = jnp.take_along_axis(tbs[3 * j + t], idx, axis=1, mode="promise_in_bounds")
                    sums[j] = g if t == 0 else sums[j] + g
            for j in range(pairs):
                b_ref[j, rs, ls] = sums[j]
        return 0

    lax.fori_loop(0, qb // 8, gather, 0)
    for now in sorted(set(sum(points, ()))):
        if 0 < now < 2 * steps and now % 2 == 1:

            @pl.when(step == now // 2)
            def _():
                point(now)

    same = code[...] >= SAME
    def pair(j, _):
        lanes = pl.ds(pl.multiple_of(j * 128, 128), 128)
        q2 = split_pair(q[:, lanes])
        s2 = dot_nn(q2, kt[lanes, :])
        bias = b_ref[j]
        for g in range(2):
            x = s2[g * qb : (g + 1) * qb] + (bias << 16 if g else bias).astype(F32)
            x = jnp.where(same, x, -1e30)
            top = jnp.max(x, axis=1, keepdims=True)
            e = jnp.exp2((x - top) * (1.4426950408889634 * 2.0**-SCALE_BITS))
            inv = 1.0 / jnp.sum(e, axis=1, keepdims=True)
            p_out[2 * j + g] = (e * inv).astype(BF16)
        c0 = dot_nn(p_out[2 * j], v[:, lanes])
        c1 = dot_nn(p_out[2 * j + 1], v[:, lanes])
        lane = lax.broadcasted_iota(I32, c0.shape, 1)
        c_out[:, lanes] = jnp.where(lane < 64, c0, c1).astype(BF16)
        return 0

    lax.fori_loop(0, pairs, pair, 0)

    @pl.when(step == steps - 1)
    def _():
        for now in range(2 * steps, max(sum(points, ())) + 1):
            point(now)
        for i in range(n):
            last = [copy for copy in hops[i] if copy is not None][-1]
            last.wait_recv()
        for i in range(n):
            for copy in hops[i]:
                if copy is not None:
                    copy.wait_send()


def attend_fwd(code, tab, q, kt, v, fetch, collective_id, qb=128):
    nq, width = q.shape
    keys = v.shape[0]
    pairs = width // 128
    modes = tuple(f[0] for f in fetch)
    points = tuple(f[1] for f in fetch)
    sources = [f[2] for f in fetch]
    n = len(fetch)
    steps = nq // qb
    full = lambda a: pl.BlockSpec(a.shape, lambda i: (0,) * a.ndim)
    anywhere = pl.BlockSpec(memory_space=pl.ANY)
    return pl.pallas_call(
        functools.partial(fwd_kernel, pairs=pairs, qb=qb, modes=modes, points=points, steps=steps),
        out_shape=(
            jax.ShapeDtypeStruct((2 * pairs, nq, keys), BF16),
            jax.ShapeDtypeStruct((nq, width), BF16),
        )
        + tuple(fetched_shape(m, w) for m, w in zip(modes, sources)),
        grid=(steps,),
        in_specs=[
            pl.BlockSpec((qb, keys), lambda i: (i, 0)),
            full(tab),
            pl.BlockSpec((qb, width), lambda i: (i, 0)),
            full(kt),
            full(v),
        ]
        + [full(w) if m == "rest" else anywhere for m, w in zip(modes, sources)],
        out_specs=(
            pl.BlockSpec((2 * pairs, qb, keys), lambda i: (0, i, 0)),
            pl.BlockSpec((qb, width), lambda i: (i, 0)),
        )
        + (anywhere,) * n,
        scratch_shapes=[
            pltpu.VMEM((pairs, qb, keys), I32),
            pltpu.VMEM((pairs * 24, 128), I32),
            pltpu.SemaphoreType.DMA((n, 3)),
            pltpu.SemaphoreType.DMA((n, 3)),
        ],
        compiler_params=pltpu.CompilerParams(
            vmem_limit_bytes=VM, collective_id=collective_id, has_side_effects=True
        ),
        cost_estimate=pl.CostEstimate(
            flops=4 * nq * keys * width, bytes_accessed=90 * 2**20, transcendentals=nq * keys * 2 * pairs
        ),
    )(code, tab, q, kt, v, *sources)


def add_rows(dst, a, b, tile):
    rows = dst[2]

    def body(i, _):
        at = lambda x: pl.ds(pl.multiple_of(x[1] + i * tile, 16), tile)
        dst[0][at(dst), :] = a[0][at(a), :] + b[0][at(b), :]
        return 0

    lax.fori_loop(0, rows // tile, body, 0)


STREAM_SEMS = 17
ORDER_BITS = {"x": 2, "0": 4, "1": 8}


def stream_phases(own, other, kept, piece, full, columns, bufs, send, recv, order, part_of=None):
    rest = part_of == "rest"
    half = (full if rest else own).shape[0] // 2
    tile = half // 8
    c = dp_bit(1)
    cut = lambda ref, start, n: ref.at[pl.ds(pl.multiple_of(start, 16), n), columns]
    part = lambda ref, bit, n: ref.at[pl.ds(pl.multiple_of(bit * n, 16), n)]
    hops, adds = [[]], [[]]
    if not rest:
        for m, g in enumerate((own, other)):
            hops[0].append(
                remote(cut(g, (1 - c) * half, half), bufs[0].at[m], send.at[m], recv.at[m], partner("dp", 1))
            )
            mine = (kept[m], 0) if kept else (g.at[:, columns], c * half)
            adds[0].append((bufs[0].at[m], (bufs[0].at[m], 0), mine, half))
    keep = []
    if kept:
        keep = [
            pltpu.make_async_copy(cut(g, c * half, half), kept[m], send.at[15 + m])
            for m, g in enumerate((own, other))
        ]
    n, at, two = half, c * half, True
    spans, bits = [(at, n)], [1]
    for i, axis in enumerate(order[:1] if part_of == "head" else order):
        buf, before = bufs[i + 1], bufs[i]
        if rest and i == 0:
            two = axis != "y"
            if two:
                n = n // 2
                at = at + dp_bit(ORDER_BITS[axis]) * n
                spans.append((at, n))
                bits.append(ORDER_BITS[axis])
            hops.append([])
            adds.append([])
        elif axis == "y":
            two = False
            hops.append([remote(before.at[1], buf.at[0], send.at[2 + 2 * i], recv.at[2 + 2 * i], partner("head", 1))])
            adds.append([(buf.at[0], (buf.at[0], 0), (before.at[0], 0), n)])
        else:
            n = n // 2
            bit = ORDER_BITS[axis]
            b = dp_bit(bit)
            at = at + b * n
            spans.append((at, n))
            bits.append(bit)
            sems = [2 + 2 * i + m for m in range(2 if two else 1)]
            hops.append(
                [
                    remote(part(before.at[m], 1 - b, n), buf.at[m], send.at[k], recv.at[k], partner("dp", bit))
                    for m, k in enumerate(sems)
                ]
            )
            adds.append([(buf.at[m], (buf.at[m], 0), (before.at[m], b * n), n) for m in range(len(sems))])

    def head():
        for copy in hops[1]:
            copy.wait_recv()
        for dst, a, b, n in adds[1]:
            add_rows((dst, 0, n), a, b, tile)
        for copy in hops[0] + hops[1]:
            copy.wait_send()

    def first():
        for copy in hops[0] + keep:
            copy.start()

    def reduce(i):
        def phase():
            for copy in keep if i == 0 else ():
                copy.wait()
            for copy in hops[i]:
                copy.wait_recv()
            for dst, a, b, n in adds[i]:
                add_rows((dst, 0, n), a, b, tile)
            if i < 4:
                for copy in hops[i + 1]:
                    copy.start()
            else:
                local.start()
                back[0].start()

        return phase

    if part_of == "head":
        return [first, reduce(0), head]
    dst, a, b, n = adds[-1][0]
    adds[-1] = [(piece, a, b, n)]
    there = lambda start, n: full.at[pl.ds(pl.multiple_of(start, 16), n), columns]
    back = [remote(piece, there(*spans[-1]), send.at[10], recv.at[10], partner("dp", bits[-1]))]
    for i in range(1, 4):
        ref = there(*spans[-1 - i])
        back.append(remote(ref, ref, send.at[10 + i], recv.at[10 + i], partner("dp", bits[-1 - i])))
    local = pltpu.make_async_copy(piece, there(*spans[-1]), send.at[14])

    def gather(i):
        def phase():
            if i == 1:
                local.wait()
            back[i - 1].wait_recv()
            back[i].start()

        return phase

    def finish():
        back[3].wait_recv()
        for copy in sum(hops, []) + back:
            copy.wait_send()

    return [first, *(reduce(i) for i in range(5)), *(gather(i) for i in range(1, 4)), finish]


def stream_scratch(rows, columns, order, keep, rest=False):
    n, two = rows // 2, 2
    shapes = [(2, n, columns)]
    for axis in order:
        if axis == "y":
            two = 1
        else:
            n = n // 2
        shapes.append((two, n, columns))
    shapes.append((n, columns))
    if rest:
        shapes = shapes[2:]
    if keep:
        shapes += [(rows // 2, columns)] * 2
    return [pltpu.VMEM(s, BF16) for s in shapes] + [pltpu.SemaphoreType.DMA((STREAM_SEMS,))] * 2


def sum_phases(own, other, bufs, send, recv):
    to = [partner("head", 1)] + [partner("dp", b) for b in (1, 2, 4, 8)]
    hops = [
        remote(other if i == 0 else own.at[i - 1], bufs.at[i], send.at[i], recv.at[i], to[i])
        for i in range(5)
    ]

    def phase(i):
        def run():
            if i:
                hops[i - 1].wait_recv()
                if i > 1:
                    own[i - 1] = own[i - 2] + bufs[i - 1]
                else:
                    own[0] = own[5] + bufs[0]
            if i < 5:
                hops[i].start()
            else:
                for copy in hops:
                    copy.wait_send()

        return run

    return [phase(i) for i in range(6)]


def attend_back(q, kt, v, do, p, ds, at, dq, dk, dv, pairs, qb):
    def pair(j, _):
        lanes = pl.ds(pl.multiple_of(j * 128, 128), 128)
        q2 = split_pair(q[:, lanes])
        do2 = split_pair(do[:, lanes])
        dp2 = dot_nt(do2, v[:, lanes])
        parts = []
        for g in range(2):
            ps = p[2 * j + g].astype(F32)
            ts = ps * dp2[g * qb : (g + 1) * qb]
            inner = jnp.sum(ts, axis=1, keepdims=True)
            parts.append((ts - ps * inner).astype(BF16))
            ds[2 * j + g, pl.ds(at, qb), :] = parts[g]
        d0 = dot_nt(parts[0], kt[lanes, :])
        d1 = dot_nt(parts[1], kt[lanes, :])
        lane = lax.broadcasted_iota(I32, d0.shape, 1)
        dq[pl.ds(at, qb), lanes] = jnp.where(lane < 64, d0, d1).astype(BF16) * jnp.array(0.125, BF16)
        dk[lanes, :] += dot_tn(q2, jnp.concatenate(parts, axis=0))
        p2 = jnp.concatenate([p[2 * j], p[2 * j + 1]], axis=0)
        dv[lanes, :] += dot_tn(do2, p2)
        return 0

    lax.fori_loop(0, pairs, pair, 0)


def count_rows(code, ds, at, outs, bits, nq):
    heads = ds.shape[0]

    def rows(r, _):
        rs = pl.ds(pl.multiple_of(at + r * 16, 16), 16)
        dfull = [ds[h, rs, :].astype(F32) for h in range(heads)]
        for half in range(2):
            d8 = [d[half * 8 : half * 8 + 8] for d in dfull]
            packed = code[pl.ds(pl.multiple_of(r * 16 + half * 8, 8), 8), :]
            low = 0
            for t in range(3):
                signs = [(((packed << (31 - low - i)) >> 31) | 1).astype(F32) for i in range(bits[t])]
                low += bits[t]
                rhs = jnp.concatenate(
                    [jnp.concatenate([d, d * signs[0]], axis=0).astype(BF16) for d in d8], axis=0
                )
                first = jnp.concatenate([jnp.ones_like(signs[1]), signs[1]], axis=0).astype(BF16)
                tiles = [first]
                for i in range(2, bits[t]):
                    s2 = jnp.concatenate([signs[i], signs[i]], axis=0).astype(BF16)
                    tiles = tiles + [x * s2 for x in tiles]
                outs[t][...] += dot_nt(jnp.concatenate(tiles, axis=0), rhs)
        return 0

    lax.fori_loop(0, nq // 16, rows, 0)


def table_sums(acc, bits, first, heads):
    n = 2**bits
    high = lax.Precision.HIGHEST
    iota = lambda shape, d: lax.broadcasted_iota(I32, shape, d)
    row, col = iota(acc.shape, 0), iota(acc.shape, 1)
    kept = jnp.where((row & 7) == (col & 7), acc, 0.0)
    shape = (n, acc.shape[0])
    odd = (iota(shape, 1) >> 3) & (iota(shape, 0) >> 1)
    odd = odd ^ (odd >> 4)
    odd = odd ^ (odd >> 2)
    odd = odd ^ (odd >> 1)
    left = (1 - 2 * (odd & 1)).astype(F32)
    shape = (n, acc.shape[1])
    odd = iota(shape, 0) & (iota(shape, 1) >> 3) & 1
    mixed = jnp.dot(left, kept, precision=high, preferred_element_type=F32)
    mixed = mixed * (1 - 2 * odd).astype(F32) * (1.0 / n)
    shape = (8, acc.shape[1])
    head = iota(shape, 0)
    pick = ((iota(shape, 1) >> 4) == head + first) & (head < heads)
    return lax.dot_general(
        pick.astype(F32), mixed, (((1,), (1,)), ((), ())), precision=high, preferred_element_type=F32
    )


def back_kernel(*refs, pairs, qb, hb, steps, bits, fast, chunks, plan):
    refs = list(refs)
    take = lambda n: [refs.pop(0) for _ in range(n)]
    sides = [take(5), take(5)]
    code, xt, *weights = take(4)
    states = take(chunks[0]) if fast else []
    up_all, out_own, out_other, pre_own, pre_other = take(5)
    hidden = up_all.shape[2]
    up_own, up_other = up_all.at[0], up_all.at[1]
    full_down, full_up, full_out, full_project = take(4) if fast else [None] * 4
    token_out, sum_out = take(2)
    if fast:
        token_far = None
    else:
        token_far, sum_far = take(2)
        project = take(2)
    ds, dk, dv, dq, dkt, dvt = take(6)
    accs = take(3)
    if fast:
        project = take(2)
        token_far, token_near = take(2)
        sums, sum_other, sum_bufs = take(3)
        token_send, sum_send, sum_recv = take(3)
    step = pl.program_id(0)
    width = 2 * pairs * 64
    nq = qb * steps
    model = xt.shape[0]
    h = lax.axis_index("head")
    near = pl.ds(pl.multiple_of(h * nq, nq), nq)
    far = pl.ds(pl.multiple_of((1 - h) * nq, nq), nq)
    last = 2 * steps + 2 + (steps * qb) // hb

    if fast:
        phases = []
        sources = []
        down_chunks, up_chunks = chunks[:2]
        cols = model // down_chunks
        for i in range(down_chunks):
            sources.append((None, None, full_down, slice(i * cols, (i + 1) * cols)))
        cols = hidden // up_chunks
        for i in range(up_chunks):
            sources.append((up_own, up_other, full_up, slice(i * cols, (i + 1) * cols)))
        sources.append((out_own, out_other, full_out, slice(0, width)))
        for start, stop in chunks[2]:
            sources.append((project[0], project[1], full_project, slice(start, stop)))
        for n, (own, other, full, columns) in enumerate(sources):
            rest = n < down_chunks
            bufs = [None, states[n], *take(3)] if rest else take(5)
            (piece,) = take(1)
            kept = take(2) if down_chunks <= n < down_chunks + up_chunks else None
            send, recv = take(2)
            made = stream_phases(
                own, other, kept, piece, full, columns, bufs, send, recv, plan[1][n], "rest" if rest else None
            )
            phases.append(made)
        token_hop = remote(token_far, token_near, token_send.at[0], token_send.at[1], partner("head", 1))

        def token_end():
            token_hop.wait_recv()
            token_out[...] = token_out[...] + token_near[...].astype(F32)
            token_hop.wait_send()

        phases.append([token_hop.start, token_end])
        phases.append(sum_phases(sums, sum_other, sum_bufs, sum_send, sum_recv))

        @pl.when(step == 0)
        def _():
            greet([partner("head", 1)] + [partner("dp", b) for b in (1, 2, 4, 8)])

        for now in sorted(set(p[0] for p in plan[0])):
            if now < last:

                @pl.when(step == now)
                def _():
                    for slot, stream, phase in plan[0]:
                        if slot == now:
                            phases[stream][phase]()

    @pl.when(step == 0)
    def _():
        for o in accs:
            o[...] = jnp.zeros_like(o)

    for s in range(2):
        q, kt, v, do, p = sides[s]
        first = s * (steps + 1)

        @pl.when((step >= first) & (step < first + steps))
        def _():
            block = step - first

            @pl.when(block == 0)
            def _():
                dk[...] = jnp.zeros_like(dk)
                dv[...] = jnp.zeros_like(dv)

            at = pl.multiple_of(block * qb, qb)
            side_ds = ds.at[s * 2 * pairs : (s + 1) * 2 * pairs]
            attend_back(q, kt, v, do, p, side_ds, at, dq, dk, dv, pairs, qb)

        @pl.when(step == first + steps)
        def _():
            dkt[...] = (dk[...] * 2.0**-SCALE_BITS).astype(BF16)
            dvt[...] = dv[...].astype(BF16)
            w = weights[s]
            wq, wk, wv = (w[i * model : (i + 1) * model, :] for i in range(3))
            project[s][:, :width] = dot_nn(xt[:, near], dq[...]).astype(BF16)
            project[s][:, width : 2 * width] = dot_nt(xt[...], dkt[...]).astype(BF16)
            project[s][:, 2 * width :] = dot_nt(xt[...], dvt[...]).astype(BF16)
            mine = dot_nt(wq, dq[...]) + dot_nn(wk, dkt[:, near]) + dot_nn(wv, dvt[:, near])
            theirs = dot_nn(wk, dkt[:, far]) + dot_nn(wv, dvt[:, far])
            if s:
                token_out[...] += mine
                token_far[...] = (token_far[...].astype(F32) + theirs).astype(BF16)
            else:
                token_out[...] = mine
                token_far[...] = theirs.astype(BF16)
            bias = sum_other if fast and s else sums.at[5] if fast else sum_far if s else sum_out
            ones = jnp.ones((8, nq), BF16)
            bias[8:16, :] = dot_nn(ones, dq[...])
            ones = jnp.ones((8, xt.shape[1]), BF16)
            bias[16:24, :] = dot_nt(ones, dvt[...])

    @pl.when(step >= 2 * steps + 2)
    def _():
        count_rows(code, ds, (step - 2 * steps - 2) * hb, accs, bits, hb)

    @pl.when(step == last - 1)
    def _():
        if fast:
            outs = (sums.at[5], sum_other)
        else:
            outs = (sum_out, sum_far)
        heads = 2 * pairs
        for s, o in enumerate(outs):
            o[0:8, :] = jnp.zeros((8, width), F32)
            for t, (acc, b) in enumerate(zip(accs, bits)):
                o[0:8, t * 128 : t * 128 + 2**b] = table_sums(acc[...], b, s * heads, heads)
            o[24:, :] = (pre_other if s else pre_own)[...]
        if fast:
            for slot, stream, phase in plan[0]:
                if slot >= last:
                    phases[stream][phase]()
            sum_out[...] = sums[4]


def attend_backward(sides, code, xt, weights, bits, grads, pre, collective_id, fast, plan, chunks, qb=128, hb=64):
    nq, width = sides[0][0].shape
    keys = sides[0][1].shape[1]
    model = xt.shape[0]
    pairs = width // 128
    heads = 2 * pairs
    steps = nq // qb
    ratio = qb // hb
    full = lambda shape: pl.BlockSpec(shape, lambda i: (0,) * len(shape), pipeline_mode=pl.Buffered(1))
    anywhere = pl.BlockSpec(memory_space=pl.ANY)
    in_specs, operands = [], []
    for s in range(2):
        clip = lambda i, s=s: jnp.clip(i - s * (steps + 1), 0, steps - 1)
        row = pl.BlockSpec((qb, width), lambda i, clip=clip: (clip(i), 0))
        big = pl.BlockSpec((heads, qb, keys), lambda i, clip=clip: (0, clip(i), 0))
        in_specs += [row, full((width, keys)), full((keys, width)), row, big]
        operands += list(sides[s])
    in_specs.append(
        pl.BlockSpec((hb, keys), lambda i: (jnp.clip(i - 2 * steps - 2, 0, steps * ratio - 1), 0))
    )
    in_specs += [full(a.shape) for a in (xt, *weights)]
    in_specs += [full(a.shape) for a in grads[:-3]] + [anywhere] + [full(a.shape) for a in (*grads[-2:], *pre)]
    operands += [code, xt, *weights, *grads, *pre]
    sum_shape = (24 + pre[0].shape[0], width)
    project_shape = (model, 3 * width)
    shapes, out_specs = [], []
    if fast:
        hidden = grads[-3].shape[2]
        shapes += [((hidden, model), BF16), ((model, hidden), BF16), ((model, width), BF16), (project_shape, BF16)]
        out_specs += [anywhere] * 4
    shapes += [((model, nq), F32), (sum_shape, F32)]
    if not fast:
        shapes += [((model, nq), BF16), (sum_shape, F32)] + [(project_shape, BF16)] * 2
    out_specs += [full(s) for s, _ in shapes[len(out_specs) :]]
    scratch = [
        pltpu.VMEM((2 * heads, nq, keys), BF16),
        pltpu.VMEM((width, keys), F32),
        pltpu.VMEM((width, keys), F32),
        pltpu.VMEM((nq, width), BF16),
        pltpu.VMEM((width, keys), BF16),
        pltpu.VMEM((width, keys), BF16),
    ] + [pltpu.VMEM((2 ** (b - 1) * 8, 2 * heads * 16), F32) for b in bits]
    params = dict(vmem_limit_bytes=BACK_VM)
    if fast:
        scratch += [pltpu.VMEM(project_shape, BF16)] * 2
        scratch += [pltpu.VMEM((model, nq), BF16)] * 2
        scratch += [pltpu.VMEM((6, *sum_shape), F32), pltpu.VMEM(sum_shape, F32)]
        scratch += [pltpu.VMEM((5, *sum_shape), F32)]
        scratch += [pltpu.SemaphoreType.DMA((2,)), pltpu.SemaphoreType.DMA((5,)), pltpu.SemaphoreType.DMA((5,))]
        n = 0
        for rows, columns, pieces in ((hidden, model, chunks[0]), (model, hidden, chunks[1])):
            for _ in range(pieces):
                scratch += stream_scratch(rows, columns // pieces, plan[1][n], n >= chunks[0], n < chunks[0])
                n += 1
        scratch += stream_scratch(model, width, plan[1][n], False)
        for start, stop in chunks[2]:
            n += 1
            scratch += stream_scratch(model, stop - start, plan[1][n], False)
        params.update(collective_id=collective_id, has_side_effects=True)
    return pl.pallas_call(
        functools.partial(
            back_kernel, pairs=pairs, qb=qb, hb=hb, steps=steps, bits=bits, fast=fast, chunks=chunks, plan=plan
        ),
        out_shape=tuple(jax.ShapeDtypeStruct(s, t) for s, t in shapes),
        grid=(2 * steps + 2 + steps * ratio,),
        in_specs=in_specs,
        out_specs=tuple(out_specs),
        scratch_shapes=scratch,
        compiler_params=pltpu.CompilerParams(**params),
        cost_estimate=pl.CostEstimate(
            flops=16 * nq * keys * width, bytes_accessed=300 * 2**20, transcendentals=0
        ),
    )(*operands)


norm_epsilon = 1e-05


def mm(a, b):
    return jnp.dot(a, b, preferred_element_type=F32)


def normalize(value):
    center = value - jnp.mean(value, axis=-1, keepdims=True)
    spread = jnp.mean(center * center, axis=-1, keepdims=True)
    root = lax.rsqrt(spread + norm_epsilon)
    return center * root, root


def normalize_back(grad, normed, root):
    return root * (
        grad
        - jnp.mean(grad, axis=-1, keepdims=True)
        - normed * jnp.mean(grad * normed, axis=-1, keepdims=True)
    )


def gelu_parts(u):
    t = 1.0 / (1.0 + (0.3275911 * 0.7071067811865476) * jnp.abs(u))
    e = jnp.exp2((-0.5 * 1.4426950408889634) * (u * u))
    poly = t * (
        0.254829592 + t * (-0.284496736 + t * (1.421413741 + t * (-1.453152027 + t * 1.061405429)))
    )
    tail = 0.5 * e * poly
    below = jnp.where(u >= 0, 1.0 - tail, tail)
    return u * below, below + u * (e * 0.3989422804014327)


def swap_dp(x, bit):
    n = lax.axis_size("dp")
    return lax.ppermute(x, "dp", [(i, i ^ bit) for i in range(n)])


def swap_head(x):
    return lax.ppermute(x, "head", [(0, 1), (1, 0)])


def dp_bits():
    n, bit, out = lax.axis_size("dp"), 1, []
    while bit < n:
        out.append(bit)
        bit *= 2
    return out


def bit_of(bit):
    return (lax.axis_index("dp") // bit) % 2


def in_order(first, mine, theirs):
    low = jnp.where(first == 0, mine, theirs)
    high = jnp.where(first == 0, theirs, mine)
    return jnp.concatenate([low, high], axis=0)


def rows_of(x, index, rows):
    return lax.dynamic_slice_in_dim(x, index * rows, rows, 0)


def halve(g, bit):
    rows = g.shape[0] // 2
    b = bit_of(bit)
    got = swap_dp(rows_of(g, 1 - b, rows), bit)
    return (rows_of(g, b, rows).astype(F32) + got.astype(F32)).astype(BF16)


def reduce_grad(own, other, head_first):
    bits = dp_bits()
    own, other = halve(own, 1), halve(other, 1)
    if not head_first:
        own, other = halve(own, 2), halve(other, 2)
    g = (own.astype(F32) + swap_head(other).astype(F32)).astype(BF16)
    for bit in bits[1 if head_first else 2 :]:
        g = halve(g, bit)
    for bit in reversed(bits):
        g = in_order(bit_of(bit), g, swap_dp(g, bit))
    return g.astype(F32)


BACK_CHUNKS = (3, 2, ((0, 384), (384, 768), (768, 1152)))
BACK_PLAN = (
    ((0, 5, 0), (0, 2, 2), (0, 3, 0), (0, 4, 0), (0, 1, 2), (0, 0, 2), (1, 5, 1), (2, 2, 3), (2, 3, 1), (2, 1, 3), (3, 4, 1), (3, 1, 4), (3, 0, 3), (4, 5, 2), (4, 2, 4), (4, 1, 5), (4, 0, 4), (5, 2, 5), (5, 1, 6), (6, 3, 2), (6, 0, 5), (7, 5, 3), (7, 2, 6), (7, 4, 2), (7, 1, 7), (7, 0, 6), (8, 5, 4), (8, 2, 7), (9, 5, 5), (9, 3, 3), (9, 0, 7), (10, 8, 0), (10, 7, 0), (10, 6, 0), (10, 9, 0), (10, 5, 6), (10, 4, 3), (10, 2, 8), (10, 3, 4), (10, 1, 8), (11, 5, 7), (11, 8, 1), (11, 7, 1), (11, 0, 8), (12, 5, 8), (12, 4, 4), (12, 6, 1), (12, 2, 9), (12, 3, 5), (12, 1, 9), (12, 0, 9), (13, 5, 9), (13, 7, 2), (13, 8, 2), (14, 4, 5), (14, 9, 1), (14, 3, 6), (14, 8, 3), (14, 7, 3), (15, 6, 2), (15, 8, 4), (15, 7, 4), (15, 4, 6), (15, 3, 7), (16, 8, 5), (16, 7, 5), (16, 6, 3), (17, 4, 7), (17, 8, 6), (17, 3, 8), (17, 7, 6), (17, 6, 4), (18, 10, 0), (18, 8, 7), (18, 3, 9), (18, 6, 5), (18, 4, 8), (18, 10, 1), (18, 6, 6), (18, 7, 7), (18, 4, 9), (18, 10, 2), (18, 6, 7), (18, 8, 8), (18, 10, 3), (18, 8, 9), (18, 7, 8), (18, 10, 4), (18, 6, 8), (18, 7, 9), (18, 6, 9), (18, 10, 5)),
    ('yx01', 'xy01', '0xy1', 'xy01', 'yx01', 'yx01', 'xy01', '0yx1', 'x0y1'),
)


def row_sums(x):
    return jnp.sum(x, axis=0, keepdims=True)


def ffn_kernel(*refs, heads, chunk, orders):
    refs = list(refs)
    take = lambda n: [refs.pop(0) for _ in range(n)]
    x, cot, ctx_a, ctx_b, ow_a, ow_b, params, small_a, small_b, uw_a, uw_b, dw_a, dw_b = take(13)
    out, first, do_a, do_b, go_a, go_b, pre_a, pre_b = take(8)
    states = take(len(orders))
    (gd_all,) = take(1) if not orders else (None,)
    gu_all, uw, dw, act, slope, gd, gu, total, bias, bias_sum, sem_in, sem_out = take(12)
    width = ctx_a.shape[1]
    model = x.shape[1]
    hidden = uw_a.shape[1]
    per = hidden // chunk
    streams = []
    for i, order in enumerate(orders):
        cols = model // len(orders)
        buf, send, recv = take(3)
        own, other = gd.at[0:hidden], gd.at[hidden : 2 * hidden]
        columns = slice(i * cols, (i + 1) * cols)
        streams.append(
            stream_phases(own, other, None, None, None, columns, [buf, states[i]], send, recv, order, "head")
        )
    for s, (u, d) in enumerate(((uw_a, dw_a), (uw_b, dw_b))):
        for i in range(per):
            n = s * per + i
            cols = slice(i * chunk, (i + 1) * chunk)
            pltpu.make_async_copy(u.at[:, cols], uw.at[n], sem_in.at[n]).start()
            pltpu.make_async_copy(d.at[cols, :], dw.at[n], sem_in.at[2 * per + n]).start()
            small = (small_a, small_b)[s]
            for j in range(chunk // width):
                at = heads + 2 + i * (chunk // width) + j
                bias[n * 8 : n * 8 + 1, j * width : (j + 1) * width] = small[at : at + 1, :]
    if orders:
        near = {"y": ("head", 1), "x": ("dp", 2), "0": ("dp", 4)}
        partners = [partner("dp", 1)] + [partner(*near[axis]) for axis in sorted({order[0] for order in orders})]
        announce(partners)
    gain1, shift1, gain2, shift2, output_shift, down_shift = (params[i : i + 1, :] for i in range(6))

    def put(i, vector):
        for o in (pre_a, pre_b):
            for n in range(model // width):
                o[i * (model // width) + n : i * (model // width) + n + 1, :] = vector[
                    :, n * width : (n + 1) * width
                ]

    attend = dot_nn(ctx_a[...], ow_a[...]) + dot_nn(ctx_b[...], ow_b[...]) + output_shift
    n1, root1 = normalize(x[...].astype(F32) + attend)
    normed = n1 * gain1 + shift1
    low = normed.astype(BF16)
    total[...] = normed + down_shift

    def forward(i, _):
        both = (2 * i, 2 * i + 1)
        for n in both:
            pltpu.make_async_copy(uw.at[n], uw.at[n], sem_in.at[n]).wait()
            pltpu.make_async_copy(dw.at[n], dw.at[n], sem_in.at[2 * per + n]).wait()
        ups = [dot_nn(low, uw[n]) + bias[pl.ds(pl.multiple_of(n * 8, 8), 8), :][0:1] for n in both]
        parts = []
        for n, u in zip(both, ups):
            a, slope_n = gelu_parts(u)
            a = a.astype(BF16)
            act[n] = a
            slope[n] = slope_n.astype(BF16)
            parts.append(dot_nn(a, dw[n]))
        total[...] += parts[0] + parts[1]
        return 0

    lax.fori_loop(0, per, forward, 0)
    n2, root2 = normalize(total[...])
    out[...] = n2 * gain2 + shift2
    g = cot[...].astype(F32)
    put(2, row_sums(g * n2))
    put(3, row_sums(g))
    back = normalize_back(g * gain2, n2, root2)
    back_feed = back.astype(BF16)
    put(5, row_sums(back_feed.astype(F32)))
    total[...] = back

    def stores(n):
        rows = pl.ds(pl.multiple_of(n * chunk, chunk), chunk)
        cols = pl.ds(pl.multiple_of(lax.rem(n, per) * chunk, chunk), chunk)
        copies = [pltpu.make_async_copy(gu.at[n], gu_all.at[lax.div(n, per), :, cols], sem_out.at[n])]
        if not orders:
            copies.append(pltpu.make_async_copy(gd.at[rows], gd_all.at[rows], sem_out.at[2 * per + n]))
        return copies

    def backward_down(n, _):
        gd[pl.ds(pl.multiple_of(n * chunk, chunk), chunk), :] = dot_tn(act[n], back_feed).astype(BF16)
        return 0

    def backward_up(n, _):
        back_up = (dot_nt(back_feed, dw[n]) * slope[n].astype(F32)).astype(BF16)
        bias_sum[pl.ds(pl.multiple_of(n * 8, 8), 8), :] = jnp.broadcast_to(
            row_sums(back_up.astype(F32)), (8, chunk)
        )
        gu[n] = dot_tn(low, back_up).astype(BF16)
        for copy in stores(n):
            copy.start()
        total[...] += dot_nt(back_up, uw[n])
        return 0

    def hop(i):
        for phases in streams:
            phases[i]()

    if orders:
        assert per == 2
        lax.fori_loop(0, 2, lambda i, z: backward_down(2 * i + 1 - dp_bit(1), z), 0)
        pl.semaphore_wait(pltpu.get_barrier_semaphore(), len(partners))
        hop(0)
        lax.fori_loop(0, 2, lambda i, z: backward_down(2 * i + dp_bit(1), z), 0)
    else:
        lax.fori_loop(0, 2 * per, backward_down, 0)
    hop(1)
    lax.fori_loop(0, 2 * per, backward_up, 0)
    for n in range(2 * per):
        for j in range(chunk // width):
            at = 6 * (model // width) + (n % per) * (chunk // width) + j
            (pre_a, pre_b)[n // per][at : at + 1, :] = bias_sum[n * 8 : n * 8 + 1, j * width : (j + 1) * width]
    back = total[...]
    put(0, row_sums(back * n1))
    put(1, row_sums(back))
    back = normalize_back(back * gain1, n1, root1)
    first[...] = back
    back_attend = back.astype(BF16)
    put(4, row_sums(back_attend.astype(F32)))
    for ctx, ow, do, go in ((ctx_a, ow_a, do_a, go_a), (ctx_b, ow_b, do_b, go_b)):
        do[...] = dot_nt(back_attend, ow[...]).astype(BF16)
        go[...] = dot_tn(back_attend, ctx[...]).astype(BF16)
    for n in range(2 * per):
        for copy in stores(n):
            copy.wait()
    hop(2)


def feed_forward(x, cot, contexts, output_weights, params, smalls, up_weights, down_weights, heads, orders,
                 collective_id, chunk=768):
    nq, model = x.shape
    width = contexts[0].shape[1]
    hidden = up_weights[0].shape[1]
    n = 2 * hidden // chunk
    here = pl.BlockSpec(memory_space=pltpu.VMEM)
    anywhere = pl.BlockSpec(memory_space=pl.ANY)
    pre_rows = 6 * (model // width) + hidden // width
    shape = jax.ShapeDtypeStruct
    state_shapes, hop_scratch, compiler = [], [], dict(vmem_limit_bytes=VM)
    for order in orders:
        cols = model // len(orders)
        state_shapes.append((1, hidden // 2, cols) if order[0] == "y" else (2, hidden // 4, cols))
        hop_scratch.append(pltpu.VMEM((2, hidden // 2, cols), BF16))
        hop_scratch += [pltpu.SemaphoreType.DMA((STREAM_SEMS,))] * 2
    if orders:
        compiler.update(collective_id=collective_id, has_side_effects=True)
    return pl.pallas_call(
        functools.partial(ffn_kernel, heads=heads, chunk=chunk, orders=orders),
        out_shape=(
            shape((nq, model), F32),
            shape((nq, model), F32),
            shape((nq, width), BF16),
            shape((nq, width), BF16),
            shape((model, width), BF16),
            shape((model, width), BF16),
            shape((pre_rows, width), F32),
            shape((pre_rows, width), F32),
            *(shape(s, BF16) for s in state_shapes),
            *((shape((2 * hidden, model), BF16),) if not orders else ()),
            shape((2, model, hidden), BF16),
        ),
        in_specs=[here] * 9 + [anywhere] * 4,
        out_specs=(here,) * (8 + len(orders)) + (anywhere,) * (1 if orders else 2),
        scratch_shapes=[
            pltpu.VMEM((n, model, chunk), BF16),
            pltpu.VMEM((n, chunk, model), BF16),
            pltpu.VMEM((n, nq, chunk), BF16),
            pltpu.VMEM((n, nq, chunk), BF16),
            pltpu.VMEM((2 * hidden, model), BF16),
            pltpu.VMEM((n, model, chunk), BF16),
            pltpu.VMEM((nq, model), F32),
            pltpu.VMEM((n * 8, chunk), F32),
            pltpu.VMEM((n * 8, chunk), F32),
            pltpu.SemaphoreType.DMA((2 * n,)),
            pltpu.SemaphoreType.DMA((2 * n,)),
            *hop_scratch,
        ],
        compiler_params=pltpu.CompilerParams(**compiler),
        cost_estimate=pl.CostEstimate(
            flops=12 * nq * model * 2 * hidden, bytes_accessed=100 * 2**20, transcendentals=nq * 4 * hidden
        ),
    )(x, cot, *contexts, *output_weights, params, *smalls, *up_weights, *down_weights)


def finish_kernel(index, *refs, count, heads, scale):
    refs = list(refs)
    take = lambda n: [refs.pop(0) for _ in range(n)]
    down, up, out, project = take(4)
    down_piece, up_piece, out_piece, project_piece = take(4)
    tokens_t, first, sums, params, small = take(5)
    project_w, out_w, up_w, down_w = take(4)
    project_a, query_a, value_a, out_a, out_shift_a, gain1_a, shift1_a = take(7)
    up_a, up_bias_a, down_a, down_shift_a, gain2_a, shift2_a, *table_a = take(9)
    tokens_o, project_o, query_o, value_o, out_o, out_shift_o, gain1_o, shift1_o = take(8)
    up_o, up_bias_o, down_o, down_shift_o, gain2_o, shift2_o, *table_o = take(9)
    project_r, query_r, value_r, out_r, out_shift_r, gain1_r, shift1_r = take(7)
    up_r, up_bias_r, down_r, down_shift_r, gain2_r, shift2_r, *table_r = take(9)
    thirds = project.shape[1] // 3
    wide = lambda ref: ref[...].astype(F32)
    renew = lambda average, weight, grad: 0.5 * average + 0.5 * (weight - grad * scale)

    down_o[...] = wide(down)
    up_o[...] = wide(up)
    out_o[...] = jnp.transpose(wide(out))
    for i in range(3):
        project_o[i] = project[:, i * thirds : (i + 1) * thirds].astype(F32)
    tokens_o[...] = first[...] + jnp.transpose(tokens_t[...])

    @pl.when(pl.program_id(0) == 0)
    def _():
        up_r[...] = renew(up_a[...], wide(up_w), wide(up_piece))
        down_r[...] = renew(down_a[...], wide(down_w), wide(down_piece))
        out_r[...] = renew(out_a[...], jnp.transpose(wide(out_w)), wide(out_piece))
        for i in range(3):
            project_r[i] = renew(project_a[i], project_w[i].astype(F32), project_piece[:, i * thirds : (i + 1) * thirds].astype(F32))
        width = sums.shape[1]

        def vector(ref, at, n):
            return jnp.concatenate([ref[at + i : at + i + 1, :] for i in range(n)], axis=1)

        def flat(o, r, a, weight, grad):
            n = a.shape[0]
            o[...] = grad.reshape(n)
            r[...] = renew(a[...], weight.reshape(n), grad.reshape(n))

        flat(query_o, query_r, query_a, small[heads : heads + 1, :], sums[8:9, :])
        flat(value_o, value_r, value_a, small[heads + 1 : heads + 2, :], sums[16:17, :])
        two = params.shape[1] // width
        commons = (
            (gain1_o, gain1_r, gain1_a),
            (shift1_o, shift1_r, shift1_a),
            (gain2_o, gain2_r, gain2_a),
            (shift2_o, shift2_r, shift2_a),
            (out_shift_o, out_shift_r, out_shift_a),
            (down_shift_o, down_shift_r, down_shift_a),
        )
        for i, (o, r, a) in enumerate(commons):
            flat(o, r, a, params[i : i + 1, :], vector(sums, 24 + two * i, two))
        many = up_bias_a.shape[0] // width
        flat(
            up_bias_o, up_bias_r, up_bias_a, vector(small, heads + 2, many), vector(sums, 24 + 6 * two, many)
        )
        for t, (o, r, a) in enumerate(zip(table_o, table_r, table_a)):
            n = a.shape[1]
            grad = sums[0:heads, t * 128 : t * 128 + n]
            o[...] = grad
            r[...] = renew(a[...], small[0:heads, t * 128 : t * 128 + n], grad)


def finish(index, totals, tokens_t, first, sums, params, small, weights, averages, count, tokens_count, heads):
    swap = lambda a: a.transpose(1, 0, 2) if a.ndim == 3 else a.T
    turned = (0, 3, 13, 14, 15)
    averages = [swap(a) if i in turned else a for i, a in enumerate(averages)]
    down, up, out, project = totals
    model = first.shape[1]
    nq = first.shape[0]
    width = project.shape[1] // 3
    steps = model // 128
    full = lambda a: pl.BlockSpec(a.shape, lambda i, d: (0,) * len(a.shape))
    rows = lambda a: pl.BlockSpec((a.shape[0] // steps, a.shape[1]), lambda i, d: (i, 0))
    piece = lambda a: pl.BlockSpec(
        (a.shape[0] // count, *a.shape[1:]), lambda i, d: (d[0],) + (0,) * (len(a.shape) - 1)
    )
    columns = lambda n: pl.BlockSpec((n, 128), lambda i, d: (0, i))
    shape = lambda s: jax.ShapeDtypeStruct(s, F32)
    project_w, out_w, up_w, down_w = weights
    in_specs = [rows(a) for a in totals] + [piece(a) for a in totals]
    in_specs += [rows(tokens_t), columns(nq), full(sums), full(params), full(small)]
    project_spec = pl.BlockSpec((3, model // count, width), lambda i, d: (0, d[0], 0))
    in_specs += [project_spec, full(out_w), piece(up_w), piece(down_w)] + [full(a) for a in averages]
    grads = [
        shape((3, model, width)), shape((width,)), shape((width,)), shape((width, model)), shape((model,)),
        shape((model,)), shape((model,)), shape(up.shape), shape((up.shape[1],)), shape(down.shape),
        shape((model,)), shape((model,)), shape((model,)), *(shape(a.shape) for a in averages[13:]),
    ]
    specs = [full(g) for g in grads]
    specs[0] = pl.BlockSpec((3, 128, width), lambda i, d: (0, i, 0))
    specs[3] = columns(width)
    specs[7] = rows(up)
    specs[9] = rows(down)
    tokens, *results = pl.pallas_call(
        functools.partial(finish_kernel, count=count, heads=heads, scale=1.0 / tokens_count),
        out_shape=(shape((nq, model)), *grads, *(shape(a.shape) for a in averages)),
        grid_spec=pltpu.PrefetchScalarGridSpec(
            num_scalar_prefetch=1,
            grid=(steps,),
            in_specs=in_specs,
            out_specs=(columns(nq), *specs, *(full(a) for a in averages)),
        ),
        compiler_params=pltpu.CompilerParams(vmem_limit_bytes=VM),
        cost_estimate=pl.CostEstimate(flops=2**24, bytes_accessed=40 * 2**20, transcendentals=0),
    )(index, *totals, *totals, tokens_t, first, sums, params, small, *weights, *averages)
    grads, renewed = results[:16], results[16:]
    grads = [swap(a) if i in turned and i != 3 else a for i, a in enumerate(grads)]
    return tokens, *grads, *(swap(a) if i in turned else a for i, a in enumerate(renewed))


def local(
    tokens,
    cotangent,
    form_number,
    sequence_bucket,
    horizontal_bucket,
    vertical_bucket,
    project_weight,
    query_bias,
    value_bias,
    output_weight,
    output_bias,
    first_gain,
    first_shift,
    up_weight,
    up_bias,
    down_weight,
    down_bias,
    second_gain,
    second_shift,
    sequence_table,
    horizontal_table,
    vertical_table,
    project_weight_average,
    query_bias_average,
    value_bias_average,
    output_weight_average,
    output_bias_average,
    first_gain_average,
    first_shift_average,
    up_weight_average,
    up_bias_average,
    down_weight_average,
    down_bias_average,
    second_gain_average,
    second_shift_average,
    sequence_table_average,
    horizontal_table_average,
    vertical_table_average,
):
    total_rows, model_width = tokens.shape
    local_width = project_weight.shape[2]
    local_heads = sequence_table.shape[1]
    hidden = up_weight.shape[1]
    share_rows = total_rows // lax.axis_size("head")
    head_index = lax.axis_index("head")
    share_start = head_index * share_rows
    block_rows = 128
    buckets = (sequence_bucket, horizontal_bucket, vertical_bucket)
    tables = (sequence_table, horizontal_table, vertical_table)
    bits = tuple((t.shape[0] - 1).bit_length() for t in tables)
    project_stack = project_weight.transpose(1, 0, 2)
    flat_project = project_stack.reshape(3 * model_width, local_width)

    params = jnp.concatenate(
        [first_gain, first_shift, second_gain, second_shift, output_bias, down_bias]
    ).reshape(6, model_width).astype(F32)
    lanes = [jnp.pad(t.T, ((0, 0), (0, local_width // 3 - t.shape[0]))) for t in tables]
    small = jnp.concatenate(
        [
            jnp.concatenate(lanes, axis=1),
            jnp.concatenate([query_bias, value_bias, up_bias]).reshape(-1, local_width),
        ],
        axis=0,
    ).astype(F32)
    small = jnp.pad(small, ((0, 16 - small.shape[0]), (0, 0)))
    smalls, project_weights = [small], [flat_project]
    output_weights, up_weights, down_weights = [output_weight], [up_weight], [down_weight]

    form_row = form_number.reshape(total_rows)
    form_own = lax.dynamic_slice_in_dim(form_row, share_start, share_rows, 0)
    code = encode(
        [rows_of(b, head_index, share_rows) for b in buckets], form_own[:, None] == form_row[None, :]
    )
    own_tokens = rows_of(tokens, head_index, share_rows)

    scaled, keys_t, values, probs, contexts = [], [], [], [], []
    for s in range(2):
        wq, wk, wv = (project_weights[s][i * model_width : (i + 1) * model_width] for i in range(3))
        bq = smalls[s][local_heads : local_heads + 1]
        bv = smalls[s][local_heads + 1 : local_heads + 2]
        q = ((mm(own_tokens, wq) + bq) * 0.125).astype(BF16)
        q = q * jnp.array(2.0**SCALE_BITS, BF16)
        kt = dot_general_t(wk, tokens).astype(BF16)
        v = (mm(tokens, wv) + bv).astype(BF16)
        if s == 0:
            fetch = (
                ("small", (0, -1, -1), small),
                ("all", (0, 3, 7), flat_project),
                ("all", (0, 4, 7), output_weight),
                ("first", (0, -1, -1), up_weight),
            )
        else:
            fetch = (("rest", (-1, 0, 4), up_part), ("all", (0, 4, 7), down_weight))
        p, context, *fetched = attend_fwd(code, smalls[s], q, kt, v, fetch, s, qb=block_rows)
        if s == 0:
            smalls.append(fetched[0])
            project_weights.append(fetched[1])
            output_weights.append(fetched[2])
            up_part = fetched[3]
        else:
            up_weights.append(fetched[0])
            down_weights.append(fetched[1])
        scaled.append(q)
        keys_t.append(kt)
        values.append(v)
        probs.append(p)
        contexts.append(context)
    fast = lax.axis_size("dp") == 16
    (
        layer_output, back_first, back_own, back_other, out_own, out_other, pre_own, pre_other, *grads
    ) = feed_forward(
        own_tokens, cotangent, contexts, output_weights, params, smalls, up_weights, down_weights, local_heads,
        BACK_PLAN[1][: BACK_CHUNKS[0]] if fast else (), 3,
    )

    sides = [
        (scaled[s], keys_t[s], values[s], (back_own, back_other)[s], probs[s]) for s in range(2)
    ]
    pre = (pre_own, pre_other)
    results = attend_backward(
        sides,
        code,
        tokens.T,
        project_weights,
        bits,
        (*(grads if fast else grads[1:]), out_own, out_other),
        pre,
        2,
        fast,
        BACK_PLAN,
        BACK_CHUNKS,
        qb=block_rows,
    )
    token_count = total_rows * lax.axis_size("dp")
    group_count = lax.axis_size("dp")
    group_index = lax.axis_index("dp")
    if fast:
        width = model_width // group_count
        output_piece = lax.dynamic_slice_in_dim(output_weight, group_index * width, width, 1)
        averages = (
            project_weight_average, query_bias_average, value_bias_average, output_weight_average,
            output_bias_average, first_gain_average, first_shift_average, up_weight_average, up_bias_average,
            down_weight_average, down_bias_average, second_gain_average, second_shift_average,
            sequence_table_average, horizontal_table_average, vertical_table_average,
        )
        return layer_output, *finish(
            jnp.full((1,), group_index, I32),
            results[:4],
            results[4],
            back_first,
            results[5],
            params,
            small,
            (project_stack, output_piece, up_weight, down_weight),
            averages,
            group_count,
            token_count,
            local_heads,
        )
    tokens_gradient, sums, far, sums_other = results[:4]
    tokens_gradient = tokens_gradient + swap_head(far).astype(F32)
    sums = sums + swap_head(sums_other)
    for bit in dp_bits():
        sums = sums + swap_dp(sums, bit)
    down_total, up_total = reduce_grad(grads[0][:hidden], grads[0][hidden:], True), reduce_grad(*grads[1], False)
    output_total = reduce_grad(out_own, out_other, True)
    project_total = reduce_grad(results[4], results[5], False)
    tokens_gradient = back_first + tokens_gradient.T
    project_total = project_total.reshape(model_width, 3, local_width)
    output_total = output_total.T
    query_bias_total, value_bias_total = sums[8], sums[16]
    tail = sums[24:].reshape(-1)
    (
        first_gain_total,
        first_shift_total,
        second_gain_total,
        second_shift_total,
        output_bias_total,
        down_bias_total,
    ) = (tail[i * model_width : (i + 1) * model_width] for i in range(6))
    up_bias_total = tail[6 * model_width :]
    sequence_total, horizontal_total, vertical_total = (
        sums[:local_heads, i * 128 : i * 128 + t.shape[0]].T for i, t in enumerate(tables)
    )
    up_weight_total, down_weight_total, output_weight_total = up_total, down_total, output_total

    def renew(average, weight, gradient):
        return 0.5 * average + 0.5 * (weight.astype(jnp.float32) - gradient / token_count)

    def part_of(array, along):
        width = array.shape[along] // group_count
        return lax.dynamic_slice_in_dim(array, group_index * width, width, along)

    return (
        layer_output,
        tokens_gradient,
        project_total,
        query_bias_total,
        value_bias_total,
        output_weight_total,
        output_bias_total,
        first_gain_total,
        first_shift_total,
        up_weight_total,
        up_bias_total,
        down_weight_total,
        down_bias_total,
        second_gain_total,
        second_shift_total,
        sequence_total,
        horizontal_total,
        vertical_total,
        renew(project_weight_average, part_of(project_weight, 0), part_of(project_total, 0)),
        renew(query_bias_average, query_bias, query_bias_total),
        renew(value_bias_average, value_bias, value_bias_total),
        renew(output_weight_average, part_of(output_weight, 1), part_of(output_weight_total, 1)),
        renew(output_bias_average, output_bias, output_bias_total),
        renew(first_gain_average, first_gain, first_gain_total),
        renew(first_shift_average, first_shift, first_shift_total),
        renew(up_weight_average, part_of(up_weight, 0), part_of(up_weight_total, 0)),
        renew(up_bias_average, up_bias, up_bias_total),
        renew(down_weight_average, part_of(down_weight, 0), part_of(down_weight_total, 0)),
        renew(down_bias_average, down_bias, down_bias_total),
        renew(second_gain_average, second_gain, second_gain_total),
        renew(second_shift_average, second_shift, second_shift_total),
        renew(sequence_table_average, sequence_table, sequence_total),
        renew(horizontal_table_average, horizontal_table, horizontal_total),
        renew(vertical_table_average, vertical_table, vertical_total),
    )


def solution(mesh):
    in_specs = (
        P("dp", None),
        P(("dp", "head"), None),
        P("dp", None),
        P("dp", None),
        P("dp", None),
        P("dp", None),
        P(None, None, "head"),
        P("head"),
        P("head"),
        P("head", None),
        P(),
        P(),
        P(),
        P(None, "head"),
        P("head"),
        P("head", None),
        P(),
        P(),
        P(),
        P(None, "head"),
        P(None, "head"),
        P(None, "head"),
        P("dp", None, "head"),
        P("head"),
        P("head"),
        P("head", "dp"),
        P(),
        P(),
        P(),
        P("dp", "head"),
        P("head"),
        P(("head", "dp"), None),
        P(),
        P(),
        P(),
        P(None, "head"),
        P(None, "head"),
        P(None, "head"),
    )
    out_specs = (
        P(("dp", "head"), None),
        P(("dp", "head"), None),
        P(None, None, "head"),
        P("head"),
        P("head"),
        P("head", None),
        P(),
        P(),
        P(),
        P(None, "head"),
        P("head"),
        P("head", None),
        P(),
        P(),
        P(),
        P(None, "head"),
        P(None, "head"),
        P(None, "head"),
        P("dp", None, "head"),
        P("head"),
        P("head"),
        P("head", "dp"),
        P(),
        P(),
        P(),
        P("dp", "head"),
        P("head"),
        P(("head", "dp"), None),
        P(),
        P(),
        P(),
        P(None, "head"),
        P(None, "head"),
        P(None, "head"),
    )
    return jax.shard_map(local, mesh=mesh, in_specs=in_specs, out_specs=out_specs, check_vma=False)
```

```python
import functools
import jax
import jax.numpy as jnp
from jax import lax
from jax.experimental import pallas as pl
from jax.sharding import PartitionSpec as P
from jax.experimental.pallas import tpu as pltpu

F32, BF16, I32 = jnp.float32, jnp.bfloat16, jnp.int32
SCALE_BITS = 27
STEP = 2.0**11
VM = 56 * 2**20
BACK_VM = 60 * 2**20
SAME = 2**17


def encode(buckets, same):
    seq, hor, ver = buckets
    return seq + 32 * hor + 2048 * ver + jnp.where(same, SAME, 0)


def buckets_of(code):
    return code & 31, (code >> 5) & 63, (code >> 11) & 63


def dot_nt(a, b):
    return lax.dot_general(a, b, (((1,), (1,)), ((), ())), preferred_element_type=F32)


def dot_tn(a, b):
    return lax.dot_general(a, b, (((0,), (0,)), ((), ())), preferred_element_type=F32)


def dot_general_t(w, x):
    return lax.dot_general(w, x, (((0,), (1,)), ((), ())), preferred_element_type=F32)


def dot_tt(a, b):
    return lax.dot_general(a, b, (((0,), (1,)), ((), ())), preferred_element_type=F32)


def dot_nn(a, b):
    return lax.dot_general(a, b, (((1,), (0,)), ((), ())), preferred_element_type=F32)


def split_pair(x):
    lane = lax.broadcasted_iota(I32, x.shape, 1)
    zero = jnp.zeros_like(x)
    return jnp.concatenate([jnp.where(lane < 64, x, zero), jnp.where(lane < 64, zero, x)], axis=0)


def partner(axis, bit):
    i = lax.axis_index(axis)
    low = lax.rem(lax.div(i, bit), 2)
    return {axis: i + bit * (1 - 2 * low)}


def dp_bit(bit):
    return lax.rem(lax.div(lax.axis_index("dp"), bit), 2)


def announce(partners):
    barrier = pltpu.get_barrier_semaphore()
    for p in partners:
        pl.semaphore_signal(barrier, inc=1, device_id=p, device_id_type=pl.DeviceIdType.MESH)


def greet(partners):
    announce(partners)
    pl.semaphore_wait(pltpu.get_barrier_semaphore(), len(partners))


def remote(src, dst, send, recv, to):
    return pltpu.make_async_remote_copy(
        src_ref=src,
        dst_ref=dst,
        send_sem=send,
        recv_sem=recv,
        device_id=to,
        device_id_type=pl.DeviceIdType.MESH,
    )


def fetch_copies(mode, source, out, send, recv):
    if mode == "small":
        return [remote(source, out, send.at[0], recv.at[0], partner("head", 1)), None, None], []
    rows = source.shape[0] if mode == "rest" else source.shape[0] // 4
    quarter = 2 * dp_bit(1) + dp_bit(2)
    one = pl.ds(pl.multiple_of(quarter * rows, rows), rows)
    two = pl.ds(pl.multiple_of(dp_bit(1) * (2 * rows), 2 * rows), 2 * rows)
    hops, local = [None, None, None], []
    if mode == "first":
        hops[0] = remote(source.at[one], out, send.at[0], recv.at[0], partner("head", 1))
    else:
        if mode == "all":
            hops[0] = remote(source.at[one], out.at[one], send.at[0], recv.at[0], partner("head", 1))
            quarter_ref = out.at[one]
        else:
            quarter_ref = source
            local.append(pltpu.make_async_copy(source, out.at[one], send.at[0]))
        hops[1] = remote(quarter_ref, out.at[one], send.at[1], recv.at[1], partner("dp", 2))
        hops[2] = remote(out.at[two], out.at[two], send.at[2], recv.at[2], partner("dp", 1))
    return hops, local


def fetched_shape(mode, w):
    rows = {"all": 1, "small": 1, "first": 0.25, "rest": 4}[mode] * w.shape[0]
    return jax.ShapeDtypeStruct((int(rows), w.shape[1]), w.dtype)


def fwd_kernel(*refs, pairs, qb, modes, points, steps):
    n = len(modes)
    code, tab, q, kt, v = refs[:5]
    sources = refs[5 : 5 + n]
    p_out, c_out = refs[5 + n : 7 + n]
    outs = refs[7 + n : 7 + 2 * n]
    b_ref, t_ref, send, recv = refs[7 + 2 * n :]
    keys = v.shape[0]
    chunk = 128
    step = pl.program_id(0)
    hops, local = [], []
    for i in range(n):
        h, l = fetch_copies(modes[i], sources[i], outs[i], send.at[i], recv.at[i])
        hops.append(h)
        local += l

    def point(now):
        for i in range(n):
            for hop in range(3):
                if points[i][hop] == now:
                    if hop and hops[i][hop - 1] is not None:
                        hops[i][hop - 1].wait_recv()
                    hops[i][hop].start()

    @pl.when(step == 0)
    def _():
        greet([partner("head", 1), partner("dp", 2), partner("dp", 1)])
        for copy in local:
            copy.start()
        for j in range(pairs):
            for t in range(3):
                ls = slice(t * chunk, (t + 1) * chunk)
                fixed = [jnp.round(tab[2 * j + g : 2 * j + g + 1, ls] * STEP).astype(I32) for g in range(2)]
                t_ref[8 * (3 * j + t) : 8 * (3 * j + t) + 8, :] = jnp.broadcast_to(
                    fixed[0] * 65536 + fixed[1], (8, chunk)
                )
        point(0)

    for now in sorted(set(sum(points, ()))):
        if 0 < now < 2 * steps and now % 2 == 0:

            @pl.when(step == now // 2)
            def _():
                if local and now == min(p[2] for p, m in zip(points, modes) if m == "rest"):
                    for copy in local:
                        copy.wait()
                point(now)

    tbs = [t_ref[8 * i : 8 * i + 8, :] for i in range(3 * pairs)]

    def gather(r, _):
        rs = pl.ds(pl.multiple_of(r * 8, 8), 8)
        for c in range(keys // chunk):
            ls = slice(c * chunk, (c + 1) * chunk)
            sums = [None] * pairs
            for t, idx in enumerate(buckets_of(code[rs, ls])):
                for j in range(pairs):
                    g = jnp.take_along_axis(tbs[3 * j + t], idx, axis=1, mode="promise_in_bounds")
                    sums[j] = g if t == 0 else sums[j] + g
            for j in range(pairs):
                b_ref[j, rs, ls] = sums[j]
        return 0

    lax.fori_loop(0, qb // 8, gather, 0)
    for now in sorted(set(sum(points, ()))):
        if 0 < now < 2 * steps and now % 2 == 1:

            @pl.when(step == now // 2)
            def _():
                point(now)

    same = code[...] >= SAME
    def pair(j, _):
        lanes = pl.ds(pl.multiple_of(j * 128, 128), 128)
        q2 = split_pair(q[:, lanes])
        s2 = dot_nn(q2, kt[lanes, :])
        bias = b_ref[j]
        for g in range(2):
            x = s2[g * qb : (g + 1) * qb] + (bias << 16 if g else bias).astype(F32)
            x = jnp.where(same, x, -1e30)
            top = jnp.max(x, axis=1, keepdims=True)
            e = jnp.exp2((x - top) * (1.4426950408889634 * 2.0**-SCALE_BITS))
            inv = 1.0 / jnp.sum(e, axis=1, keepdims=True)
            p_out[2 * j + g] = (e * inv).astype(BF16)
        c0 = dot_nn(p_out[2 * j], v[:, lanes])
        c1 = dot_nn(p_out[2 * j + 1], v[:, lanes])
        lane = lax.broadcasted_iota(I32, c0.shape, 1)
        c_out[:, lanes] = jnp.where(lane < 64, c0, c1).astype(BF16)
        return 0

    lax.fori_loop(0, pairs, pair, 0)

    @pl.when(step == steps - 1)
    def _():
        for now in range(2 * steps, max(sum(points, ())) + 1):
            point(now)
        for i in range(n):
            last = [copy for copy in hops[i] if copy is not None][-1]
            last.wait_recv()
        for i in range(n):
            for copy in hops[i]:
                if copy is not None:
                    copy.wait_send()


def attend_fwd(code, tab, q, kt, v, fetch, collective_id, qb=128):
    nq, width = q.shape
    keys = v.shape[0]
    pairs = width // 128
    modes = tuple(f[0] for f in fetch)
    points = tuple(f[1] for f in fetch)
    sources = [f[2] for f in fetch]
    n = len(fetch)
    steps = nq // qb
    full = lambda a: pl.BlockSpec(a.shape, lambda i: (0,) * a.ndim)
    anywhere = pl.BlockSpec(memory_space=pl.ANY)
    return pl.pallas_call(
        functools.partial(fwd_kernel, pairs=pairs, qb=qb, modes=modes, points=points, steps=steps),
        out_shape=(
            jax.ShapeDtypeStruct((2 * pairs, nq, keys), BF16),
            jax.ShapeDtypeStruct((nq, width), BF16),
        )
        + tuple(fetched_shape(m, w) for m, w in zip(modes, sources)),
        grid=(steps,),
        in_specs=[
            pl.BlockSpec((qb, keys), lambda i: (i, 0)),
            full(tab),
            pl.BlockSpec((qb, width), lambda i: (i, 0)),
            full(kt),
            full(v),
        ]
        + [full(w) if m == "rest" else anywhere for m, w in zip(modes, sources)],
        out_specs=(
            pl.BlockSpec((2 * pairs, qb, keys), lambda i: (0, i, 0)),
            pl.BlockSpec((qb, width), lambda i: (i, 0)),
        )
        + (anywhere,) * n,
        scratch_shapes=[
            pltpu.VMEM((pairs, qb, keys), I32),
            pltpu.VMEM((pairs * 24, 128), I32),
            pltpu.SemaphoreType.DMA((n, 3)),
            pltpu.SemaphoreType.DMA((n, 3)),
        ],
        compiler_params=pltpu.CompilerParams(
            vmem_limit_bytes=VM, collective_id=collective_id, has_side_effects=True
        ),
        cost_estimate=pl.CostEstimate(
            flops=4 * nq * keys * width, bytes_accessed=90 * 2**20, transcendentals=nq * keys * 2 * pairs
        ),
    )(code, tab, q, kt, v, *sources)


def add_rows(dst, a, b, tile):
    rows = dst[2]

    def body(i, _):
        at = lambda x: pl.ds(pl.multiple_of(x[1] + i * tile, 16), tile)
        dst[0][at(dst), :] = a[0][at(a), :] + b[0][at(b), :]
        return 0

    lax.fori_loop(0, rows // tile, body, 0)


STREAM_SEMS = 17
ORDER_BITS = {"x": 2, "0": 4, "1": 8}


def stream_phases(own, other, kept, piece, full, columns, bufs, send, recv, order, part_of=None):
    rest = part_of == "rest"
    half = (full if rest else own).shape[0] // 2
    tile = half // 8
    c = dp_bit(1)
    cut = lambda ref, start, n: ref.at[pl.ds(pl.multiple_of(start, 16), n), columns]
    part = lambda ref, bit, n: ref.at[pl.ds(pl.multiple_of(bit * n, 16), n)]
    hops, adds = [[]], [[]]
    if not rest:
        for m, g in enumerate((own, other)):
            hops[0].append(
                remote(cut(g, (1 - c) * half, half), bufs[0].at[m], send.at[m], recv.at[m], partner("dp", 1))
            )
            mine = (kept[m], 0) if kept else (g.at[:, columns], c * half)
            adds[0].append((bufs[0].at[m], (bufs[0].at[m], 0), mine, half))
    keep = []
    if kept:
        keep = [
            pltpu.make_async_copy(cut(g, c * half, half), kept[m], send.at[15 + m])
            for m, g in enumerate((own, other))
        ]
    n, at, two = half, c * half, True
    spans, bits = [(at, n)], [1]
    for i, axis in enumerate(order[:1] if part_of == "head" else order):
        buf, before = bufs[i + 1], bufs[i]
        if rest and i == 0:
            two = axis != "y"
            if two:
                n = n // 2
                at = at + dp_bit(ORDER_BITS[axis]) * n
                spans.append((at, n))
                bits.append(ORDER_BITS[axis])
            hops.append([])
            adds.append([])
        elif axis == "y":
            two = False
            hops.append([remote(before.at[1], buf.at[0], send.at[2 + 2 * i], recv.at[2 + 2 * i], partner("head", 1))])
            adds.append([(buf.at[0], (buf.at[0], 0), (before.at[0], 0), n)])
        else:
            n = n // 2
            bit = ORDER_BITS[axis]
            b = dp_bit(bit)
            at = at + b * n
            spans.append((at, n))
            bits.append(bit)
            sems = [2 + 2 * i + m for m in range(2 if two else 1)]
            hops.append(
                [
                    remote(part(before.at[m], 1 - b, n), buf.at[m], send.at[k], recv.at[k], partner("dp", bit))
                    for m, k in enumerate(sems)
                ]
            )
            adds.append([(buf.at[m], (buf.at[m], 0), (before.at[m], b * n), n) for m in range(len(sems))])

    def head():
        for copy in hops[1]:
            copy.wait_recv()
        for dst, a, b, n in adds[1]:
            add_rows((dst, 0, n), a, b, tile)
        for copy in hops[0] + hops[1]:
            copy.wait_send()

    def first():
        for copy in hops[0] + keep:
            copy.start()

    def reduce(i):
        def phase():
            for copy in keep if i == 0 else ():
                copy.wait()
            for copy in hops[i]:
                copy.wait_recv()
            for dst, a, b, n in adds[i]:
                add_rows((dst, 0, n), a, b, tile)
            if i < 4:
                for copy in hops[i + 1]:
                    copy.start()
            else:
                local.start()
                back[0].start()

        return phase

    if part_of == "head":
        return [first, reduce(0), head]
    dst, a, b, n = adds[-1][0]
    adds[-1] = [(piece, a, b, n)]
    there = lambda start, n: full.at[pl.ds(pl.multiple_of(start, 16), n), columns]
    back = [remote(piece, there(*spans[-1]), send.at[10], recv.at[10], partner("dp", bits[-1]))]
    for i in range(1, 4):
        ref = there(*spans[-1 - i])
        back.append(remote(ref, ref, send.at[10 + i], recv.at[10 + i], partner("dp", bits[-1 - i])))
    local = pltpu.make_async_copy(piece, there(*spans[-1]), send.at[14])

    def gather(i):
        def phase():
            if i == 1:
                local.wait()
            back[i - 1].wait_recv()
            back[i].start()

        return phase

    def finish():
        back[3].wait_recv()
        for copy in sum(hops, []) + back:
            copy.wait_send()

    return [first, *(reduce(i) for i in range(5)), *(gather(i) for i in range(1, 4)), finish]


def stream_scratch(rows, columns, order, keep, rest=False):
    n, two = rows // 2, 2
    shapes = [(2, n, columns)]
    for axis in order:
        if axis == "y":
            two = 1
        else:
            n = n // 2
        shapes.append((two, n, columns))
    shapes.append((n, columns))
    if rest:
        shapes = shapes[2:]
    if keep:
        shapes += [(rows // 2, columns)] * 2
    return [pltpu.VMEM(s, BF16) for s in shapes] + [pltpu.SemaphoreType.DMA((STREAM_SEMS,))] * 2


def sum_phases(own, other, bufs, send, recv):
    to = [partner("head", 1)] + [partner("dp", b) for b in (1, 2, 4, 8)]
    hops = [
        remote(other if i == 0 else own.at[i - 1], bufs.at[i], send.at[i], recv.at[i], to[i])
        for i in range(5)
    ]

    def phase(i):
        def run():
            if i:
                hops[i - 1].wait_recv()
                if i > 1:
                    own[i - 1] = own[i - 2] + bufs[i - 1]
                else:
                    own[0] = own[5] + bufs[0]
            if i < 5:
                hops[i].start()
            else:
                for copy in hops:
                    copy.wait_send()

        return run

    return [phase(i) for i in range(6)]


def attend_back(q, kt, v, do, p, ds, at, dq, dk, dv, pairs, qb):
    def pair(j, _):
        lanes = pl.ds(pl.multiple_of(j * 128, 128), 128)
        q2 = split_pair(q[:, lanes])
        do2 = split_pair(do[:, lanes])
        dp2 = dot_nt(do2, v[:, lanes])
        parts = []
        for g in range(2):
            ps = p[2 * j + g].astype(F32)
            ts = ps * dp2[g * qb : (g + 1) * qb]
            inner = jnp.sum(ts, axis=1, keepdims=True)
            parts.append((ts - ps * inner).astype(BF16))
            ds[2 * j + g, pl.ds(at, qb), :] = parts[g]
        d0 = dot_nt(parts[0], kt[lanes, :])
        d1 = dot_nt(parts[1], kt[lanes, :])
        lane = lax.broadcasted_iota(I32, d0.shape, 1)
        dq[pl.ds(at, qb), lanes] = jnp.where(lane < 64, d0, d1).astype(BF16) * jnp.array(0.125, BF16)
        dk[lanes, :] += dot_tn(q2, jnp.concatenate(parts, axis=0))
        p2 = jnp.concatenate([p[2 * j], p[2 * j + 1]], axis=0)
        dv[lanes, :] += dot_tn(do2, p2)
        return 0

    lax.fori_loop(0, pairs, pair, 0)


def count_rows(code, ds, at, outs, bits, nq):
    heads = ds.shape[0]

    def rows(r, _):
        rs = pl.ds(pl.multiple_of(at + r * 16, 16), 16)
        dfull = [ds[h, rs, :].astype(F32) for h in range(heads)]
        for half in range(2):
            d8 = [d[half * 8 : half * 8 + 8] for d in dfull]
            packed = code[pl.ds(pl.multiple_of(r * 16 + half * 8, 8), 8), :]
            low = 0
            for t in range(3):
                signs = [(((packed << (31 - low - i)) >> 31) | 1).astype(F32) for i in range(bits[t])]
                low += bits[t]
                rhs = jnp.concatenate(
                    [jnp.concatenate([d, d * signs[0]], axis=0).astype(BF16) for d in d8], axis=0
                )
                first = jnp.concatenate([jnp.ones_like(signs[1]), signs[1]], axis=0).astype(BF16)
                tiles = [first]
                for i in range(2, bits[t]):
                    s2 = jnp.concatenate([signs[i], signs[i]], axis=0).astype(BF16)
                    tiles = tiles + [x * s2 for x in tiles]
                outs[t][...] += dot_nt(jnp.concatenate(tiles, axis=0), rhs)
        return 0

    lax.fori_loop(0, nq // 16, rows, 0)


def table_sums(acc, bits, first, heads):
    n = 2**bits
    high = lax.Precision.HIGHEST
    iota = lambda shape, d: lax.broadcasted_iota(I32, shape, d)
    row, col = iota(acc.shape, 0), iota(acc.shape, 1)
    kept = jnp.where((row & 7) == (col & 7), acc, 0.0)
    shape = (n, acc.shape[0])
    odd = (iota(shape, 1) >> 3) & (iota(shape, 0) >> 1)
    odd = odd ^ (odd >> 4)
    odd = odd ^ (odd >> 2)
    odd = odd ^ (odd >> 1)
    left = (1 - 2 * (odd & 1)).astype(F32)
    shape = (n, acc.shape[1])
    odd = iota(shape, 0) & (iota(shape, 1) >> 3) & 1
    mixed = jnp.dot(left, kept, precision=high, preferred_element_type=F32)
    mixed = mixed * (1 - 2 * odd).astype(F32) * (1.0 / n)
    shape = (8, acc.shape[1])
    head = iota(shape, 0)
    pick = ((iota(shape, 1) >> 4) == head + first) & (head < heads)
    return lax.dot_general(
        pick.astype(F32), mixed, (((1,), (1,)), ((), ())), precision=high, preferred_element_type=F32
    )


def back_kernel(*refs, pairs, qb, hb, steps, bits, fast, chunks, plan):
    refs = list(refs)
    take = lambda n: [refs.pop(0) for _ in range(n)]
    sides = [take(5), take(5)]
    code, xt, *weights = take(4)
    states = take(chunks[0]) if fast else []
    up_all, out_own, out_other, pre_own, pre_other = take(5)
    hidden = up_all.shape[2]
    up_own, up_other = up_all.at[0], up_all.at[1]
    full_down, full_up, full_out, full_project = take(4) if fast else [None] * 4
    token_out, sum_out = take(2)
    if fast:
        token_far = None
    else:
        token_far, sum_far = take(2)
        project = take(2)
    ds, dk, dv, dq, dkt, dvt = take(6)
    accs = take(3)
    if fast:
        project = take(2)
        token_far, token_near = take(2)
        sums, sum_other, sum_bufs = take(3)
        token_send, sum_send, sum_recv = take(3)
    step = pl.program_id(0)
    width = 2 * pairs * 64
    nq = qb * steps
    model = xt.shape[0]
    h = lax.axis_index("head")
    near = pl.ds(pl.multiple_of(h * nq, nq), nq)
    far = pl.ds(pl.multiple_of((1 - h) * nq, nq), nq)
    last = 2 * steps + 2 + (steps * qb) // hb

    if fast:
        phases = []
        sources = []
        down_chunks, up_chunks = chunks[:2]
        cols = model // down_chunks
        for i in range(down_chunks):
            sources.append((None, None, full_down, slice(i * cols, (i + 1) * cols)))
        cols = hidden // up_chunks
        for i in range(up_chunks):
            sources.append((up_own, up_other, full_up, slice(i * cols, (i + 1) * cols)))
        sources.append((out_own, out_other, full_out, slice(0, width)))
        for start, stop in chunks[2]:
            sources.append((project[0], project[1], full_project, slice(start, stop)))
        for n, (own, other, full, columns) in enumerate(sources):
            rest = n < down_chunks
            bufs = [None, states[n], *take(3)] if rest else take(5)
            (piece,) = take(1)
            kept = take(2) if down_chunks <= n < down_chunks + up_chunks else None
            send, recv = take(2)
            made = stream_phases(
                own, other, kept, piece, full, columns, bufs, send, recv, plan[1][n], "rest" if rest else None
            )
            phases.append(made)
        token_hop = remote(token_far, token_near, token_send.at[0], token_send.at[1], partner("head", 1))

        def token_end():
            token_hop.wait_recv()
            token_out[...] = token_out[...] + token_near[...].astype(F32)
            token_hop.wait_send()

        phases.append([token_hop.start, token_end])
        phases.append(sum_phases(sums, sum_other, sum_bufs, sum_send, sum_recv))

        @pl.when(step == 0)
        def _():
            greet([partner("head", 1)] + [partner("dp", b) for b in (1, 2, 4, 8)])

        for now in sorted(set(p[0] for p in plan[0])):
            if now < last:

                @pl.when(step == now)
                def _():
                    for slot, stream, phase in plan[0]:
                        if slot == now:
                            phases[stream][phase]()

    @pl.when(step == 0)
    def _():
        for o in accs:
            o[...] = jnp.zeros_like(o)

    for s in range(2):
        q, kt, v, do, p = sides[s]
        first = s * (steps + 1)

        @pl.when((step >= first) & (step < first + steps))
        def _():
            block = step - first

            @pl.when(block == 0)
            def _():
                dk[...] = jnp.zeros_like(dk)
                dv[...] = jnp.zeros_like(dv)

            at = pl.multiple_of(block * qb, qb)
            side_ds = ds.at[s * 2 * pairs : (s + 1) * 2 * pairs]
            attend_back(q, kt, v, do, p, side_ds, at, dq, dk, dv, pairs, qb)

        @pl.when(step == first + steps)
        def _():
            dkt[...] = (dk[...] * 2.0**-SCALE_BITS).astype(BF16)
            dvt[...] = dv[...].astype(BF16)
            w = weights[s]
            wq, wk, wv = (w[i * model : (i + 1) * model, :] for i in range(3))
            project[s][:, :width] = dot_nn(xt[:, near], dq[...]).astype(BF16)
            project[s][:, width : 2 * width] = dot_nt(xt[...], dkt[...]).astype(BF16)
            project[s][:, 2 * width :] = dot_nt(xt[...], dvt[...]).astype(BF16)
            mine = dot_nt(wq, dq[...]) + dot_nn(wk, dkt[:, near]) + dot_nn(wv, dvt[:, near])
            theirs = dot_nn(wk, dkt[:, far]) + dot_nn(wv, dvt[:, far])
            if s:
                token_out[...] += mine
                token_far[...] = (token_far[...].astype(F32) + theirs).astype(BF16)
            else:
                token_out[...] = mine
                token_far[...] = theirs.astype(BF16)
            bias = sum_other if fast and s else sums.at[5] if fast else sum_far if s else sum_out
            ones = jnp.ones((8, nq), BF16)
            bias[8:16, :] = dot_nn(ones, dq[...])
            ones = jnp.ones((8, xt.shape[1]), BF16)
            bias[16:24, :] = dot_nt(ones, dvt[...])

    @pl.when(step >= 2 * steps + 2)
    def _():
        count_rows(code, ds, (step - 2 * steps - 2) * hb, accs, bits, hb)

    @pl.when(step == last - 1)
    def _():
        if fast:
            outs = (sums.at[5], sum_other)
        else:
            outs = (sum_out, sum_far)
        heads = 2 * pairs
        for s, o in enumerate(outs):
            o[0:8, :] = jnp.zeros((8, width), F32)
            for t, (acc, b) in enumerate(zip(accs, bits)):
                o[0:8, t * 128 : t * 128 + 2**b] = table_sums(acc[...], b, s * heads, heads)
            o[24:, :] = (pre_other if s else pre_own)[...]
        if fast:
            for slot, stream, phase in plan[0]:
                if slot >= last:
                    phases[stream][phase]()
            sum_out[...] = sums[4]


def attend_backward(sides, code, xt, weights, bits, grads, pre, collective_id, fast, plan, chunks, qb=128, hb=64):
    nq, width = sides[0][0].shape
    keys = sides[0][1].shape[1]
    model = xt.shape[0]
    pairs = width // 128
    heads = 2 * pairs
    steps = nq // qb
    ratio = qb // hb
    full = lambda shape: pl.BlockSpec(shape, lambda i: (0,) * len(shape), pipeline_mode=pl.Buffered(1))
    anywhere = pl.BlockSpec(memory_space=pl.ANY)
    in_specs, operands = [], []
    for s in range(2):
        clip = lambda i, s=s: jnp.clip(i - s * (steps + 1), 0, steps - 1)
        row = pl.BlockSpec((qb, width), lambda i, clip=clip: (clip(i), 0))
        big = pl.BlockSpec((heads, qb, keys), lambda i, clip=clip: (0, clip(i), 0))
        in_specs += [row, full((width, keys)), full((keys, width)), row, big]
        operands += list(sides[s])
    in_specs.append(
        pl.BlockSpec((hb, keys), lambda i: (jnp.clip(i - 2 * steps - 2, 0, steps * ratio - 1), 0))
    )
    in_specs += [full(a.shape) for a in (xt, *weights)]
    in_specs += [full(a.shape) for a in grads[:-3]] + [anywhere] + [full(a.shape) for a in (*grads[-2:], *pre)]
    operands += [code, xt, *weights, *grads, *pre]
    sum_shape = (24 + pre[0].shape[0], width)
    project_shape = (model, 3 * width)
    shapes, out_specs = [], []
    if fast:
        hidden = grads[-3].shape[2]
        shapes += [((hidden, model), BF16), ((model, hidden), BF16), ((model, width), BF16), (project_shape, BF16)]
        out_specs += [anywhere] * 4
    shapes += [((model, nq), F32), (sum_shape, F32)]
    if not fast:
        shapes += [((model, nq), BF16), (sum_shape, F32)] + [(project_shape, BF16)] * 2
    out_specs += [full(s) for s, _ in shapes[len(out_specs) :]]
    scratch = [
        pltpu.VMEM((2 * heads, nq, keys), BF16),
        pltpu.VMEM((width, keys), F32),
        pltpu.VMEM((width, keys), F32),
        pltpu.VMEM((nq, width), BF16),
        pltpu.VMEM((width, keys), BF16),
        pltpu.VMEM((width, keys), BF16),
    ] + [pltpu.VMEM((2 ** (b - 1) * 8, 2 * heads * 16), F32) for b in bits]
    params = dict(vmem_limit_bytes=BACK_VM)
    if fast:
        scratch += [pltpu.VMEM(project_shape, BF16)] * 2
        scratch += [pltpu.VMEM((model, nq), BF16)] * 2
        scratch += [pltpu.VMEM((6, *sum_shape), F32), pltpu.VMEM(sum_shape, F32)]
        scratch += [pltpu.VMEM((5, *sum_shape), F32)]
        scratch += [pltpu.SemaphoreType.DMA((2,)), pltpu.SemaphoreType.DMA((5,)), pltpu.SemaphoreType.DMA((5,))]
        n = 0
        for rows, columns, pieces in ((hidden, model, chunks[0]), (model, hidden, chunks[1])):
            for _ in range(pieces):
                scratch += stream_scratch(rows, columns // pieces, plan[1][n], n >= chunks[0], n < chunks[0])
                n += 1
        scratch += stream_scratch(model, width, plan[1][n], False)
        for start, stop in chunks[2]:
            n += 1
            scratch += stream_scratch(model, stop - start, plan[1][n], False)
        params.update(collective_id=collective_id, has_side_effects=True)
    return pl.pallas_call(
        functools.partial(
            back_kernel, pairs=pairs, qb=qb, hb=hb, steps=steps, bits=bits, fast=fast, chunks=chunks, plan=plan
        ),
        out_shape=tuple(jax.ShapeDtypeStruct(s, t) for s, t in shapes),
        grid=(2 * steps + 2 + steps * ratio,),
        in_specs=in_specs,
        out_specs=tuple(out_specs),
        scratch_shapes=scratch,
        compiler_params=pltpu.CompilerParams(**params),
        cost_estimate=pl.CostEstimate(
            flops=16 * nq * keys * width, bytes_accessed=300 * 2**20, transcendentals=0
        ),
    )(*operands)


norm_epsilon = 1e-05


def mm(a, b):
    return jnp.dot(a, b, preferred_element_type=F32)


def normalize(value):
    center = value - jnp.mean(value, axis=-1, keepdims=True)
    spread = jnp.mean(center * center, axis=-1, keepdims=True)
    root = lax.rsqrt(spread + norm_epsilon)
    return center * root, root


def normalize_back(grad, normed, root):
    return root * (
        grad
        - jnp.mean(grad, axis=-1, keepdims=True)
        - normed * jnp.mean(grad * normed, axis=-1, keepdims=True)
    )


def gelu_parts(u):
    t = 1.0 / (1.0 + (0.3275911 * 0.7071067811865476) * jnp.abs(u))
    e = jnp.exp2((-0.5 * 1.4426950408889634) * (u * u))
    poly = t * (
        0.254829592 + t * (-0.284496736 + t * (1.421413741 + t * (-1.453152027 + t * 1.061405429)))
    )
    tail = 0.5 * e * poly
    below = jnp.where(u >= 0, 1.0 - tail, tail)
    return u * below, below + u * (e * 0.3989422804014327)


def swap_dp(x, bit):
    n = lax.axis_size("dp")
    return lax.ppermute(x, "dp", [(i, i ^ bit) for i in range(n)])


def swap_head(x):
    return lax.ppermute(x, "head", [(0, 1), (1, 0)])


def dp_bits():
    n, bit, out = lax.axis_size("dp"), 1, []
    while bit < n:
        out.append(bit)
        bit *= 2
    return out


def bit_of(bit):
    return (lax.axis_index("dp") // bit) % 2


def in_order(first, mine, theirs):
    low = jnp.where(first == 0, mine, theirs)
    high = jnp.where(first == 0, theirs, mine)
    return jnp.concatenate([low, high], axis=0)


def rows_of(x, index, rows):
    return lax.dynamic_slice_in_dim(x, index * rows, rows, 0)


def halve(g, bit):
    rows = g.shape[0] // 2
    b = bit_of(bit)
    got = swap_dp(rows_of(g, 1 - b, rows), bit)
    return (rows_of(g, b, rows).astype(F32) + got.astype(F32)).astype(BF16)


def reduce_grad(own, other, head_first):
    bits = dp_bits()
    own, other = halve(own, 1), halve(other, 1)
    if not head_first:
        own, other = halve(own, 2), halve(other, 2)
    g = (own.astype(F32) + swap_head(other).astype(F32)).astype(BF16)
    for bit in bits[1 if head_first else 2 :]:
        g = halve(g, bit)
    for bit in reversed(bits):
        g = in_order(bit_of(bit), g, swap_dp(g, bit))
    return g.astype(F32)


BACK_CHUNKS = (3, 2, ((0, 384), (384, 768), (768, 1152)))
BACK_PLAN = (
    ((0, 5, 0), (0, 2, 2), (0, 3, 0), (0, 4, 0), (0, 1, 2), (0, 0, 2), (1, 5, 1), (2, 2, 3), (2, 3, 1), (2, 1, 3), (3, 4, 1), (3, 1, 4), (3, 0, 3), (4, 5, 2), (4, 2, 4), (4, 1, 5), (4, 0, 4), (5, 2, 5), (5, 1, 6), (6, 3, 2), (6, 0, 5), (7, 5, 3), (7, 2, 6), (7, 4, 2), (7, 1, 7), (7, 0, 6), (8, 5, 4), (8, 2, 7), (9, 5, 5), (9, 3, 3), (9, 0, 7), (10, 8, 0), (10, 7, 0), (10, 6, 0), (10, 9, 0), (10, 5, 6), (10, 4, 3), (10, 2, 8), (10, 3, 4), (10, 1, 8), (11, 5, 7), (11, 8, 1), (11, 7, 1), (11, 0, 8), (12, 5, 8), (12, 4, 4), (12, 6, 1), (12, 2, 9), (12, 3, 5), (12, 1, 9), (12, 0, 9), (13, 5, 9), (13, 7, 2), (13, 8, 2), (14, 4, 5), (14, 9, 1), (14, 3, 6), (14, 8, 3), (14, 7, 3), (15, 6, 2), (15, 8, 4), (15, 7, 4), (15, 4, 6), (15, 3, 7), (16, 8, 5), (16, 7, 5), (16, 6, 3), (17, 4, 7), (17, 8, 6), (17, 3, 8), (17, 7, 6), (17, 6, 4), (18, 10, 0), (18, 8, 7), (18, 3, 9), (18, 6, 5), (18, 4, 8), (18, 10, 1), (18, 6, 6), (18, 7, 7), (18, 4, 9), (18, 10, 2), (18, 6, 7), (18, 8, 8), (18, 10, 3), (18, 8, 9), (18, 7, 8), (18, 10, 4), (18, 6, 8), (18, 7, 9), (18, 6, 9), (18, 10, 5)),
    ('yx01', 'xy01', '0xy1', 'xy01', 'yx01', 'yx01', 'xy01', '0yx1', 'x0y1'),
)


def row_sums(x):
    return jnp.sum(x, axis=0, keepdims=True)


def ffn_kernel(*refs, heads, chunk, orders):
    refs = list(refs)
    take = lambda n: [refs.pop(0) for _ in range(n)]
    x, cot, ctx_a, ctx_b, ow_a, ow_b, params, small_a, small_b, uw_a, uw_b, dw_a, dw_b = take(13)
    out, first, do_a, do_b, go_a, go_b, pre_a, pre_b = take(8)
    states = take(len(orders))
    (gd_all,) = take(1) if not orders else (None,)
    gu_all, uw, dw, act, slope, gd, gu, total, bias, bias_sum, sem_in, sem_out = take(12)
    width = ctx_a.shape[1]
    model = x.shape[1]
    hidden = uw_a.shape[1]
    per = hidden // chunk
    streams = []
    for i, order in enumerate(orders):
        cols = model // len(orders)
        buf, send, recv = take(3)
        own, other = gd.at[0:hidden], gd.at[hidden : 2 * hidden]
        columns = slice(i * cols, (i + 1) * cols)
        streams.append(
            stream_phases(own, other, None, None, None, columns, [buf, states[i]], send, recv, order, "head")
        )
    for s, (u, d) in enumerate(((uw_a, dw_a), (uw_b, dw_b))):
        for i in range(per):
            n = s * per + i
            cols = slice(i * chunk, (i + 1) * chunk)
            pltpu.make_async_copy(u.at[:, cols], uw.at[n], sem_in.at[n]).start()
            pltpu.make_async_copy(d.at[cols, :], dw.at[n], sem_in.at[2 * per + n]).start()
            small = (small_a, small_b)[s]
            for j in range(chunk // width):
                at = heads + 2 + i * (chunk // width) + j
                bias[n * 8 : n * 8 + 1, j * width : (j + 1) * width] = small[at : at + 1, :]
    if orders:
        near = {"y": ("head", 1), "x": ("dp", 2), "0": ("dp", 4)}
        partners = [partner("dp", 1)] + [partner(*near[axis]) for axis in sorted({order[0] for order in orders})]
        announce(partners)
    gain1, shift1, gain2, shift2, output_shift, down_shift = (params[i : i + 1, :] for i in range(6))

    def put(i, vector):
        for o in (pre_a, pre_b):
            for n in range(model // width):
                o[i * (model // width) + n : i * (model // width) + n + 1, :] = vector[
                    :, n * width : (n + 1) * width
                ]

    attend = dot_nn(ctx_a[...], ow_a[...]) + dot_nn(ctx_b[...], ow_b[...]) + output_shift
    n1, root1 = normalize(x[...].astype(F32) + attend)
    normed = n1 * gain1 + shift1
    low = normed.astype(BF16)
    total[...] = normed + down_shift

    def forward(i, _):
        both = (2 * i, 2 * i + 1)
        for n in both:
            pltpu.make_async_copy(uw.at[n], uw.at[n], sem_in.at[n]).wait()
            pltpu.make_async_copy(dw.at[n], dw.at[n], sem_in.at[2 * per + n]).wait()
        ups = [dot_nn(low, uw[n]) + bias[pl.ds(pl.multiple_of(n * 8, 8), 8), :][0:1] for n in both]
        parts = []
        for n, u in zip(both, ups):
            a, slope_n = gelu_parts(u)
            a = a.astype(BF16)
            act[n] = a
            slope[n] = slope_n.astype(BF16)
            parts.append(dot_nn(a, dw[n]))
        total[...] += parts[0] + parts[1]
        return 0

    lax.fori_loop(0, per, forward, 0)
    n2, root2 = normalize(total[...])
    out[...] = n2 * gain2 + shift2
    g = cot[...].astype(F32)
    put(2, row_sums(g * n2))
    put(3, row_sums(g))
    back = normalize_back(g * gain2, n2, root2)
    back_feed = back.astype(BF16)
    put(5, row_sums(back_feed.astype(F32)))
    total[...] = back

    def stores(n):
        rows = pl.ds(pl.multiple_of(n * chunk, chunk), chunk)
        cols = pl.ds(pl.multiple_of(lax.rem(n, per) * chunk, chunk), chunk)
        copies = [pltpu.make_async_copy(gu.at[n], gu_all.at[lax.div(n, per), :, cols], sem_out.at[n])]
        if not orders:
            copies.append(pltpu.make_async_copy(gd.at[rows], gd_all.at[rows], sem_out.at[2 * per + n]))
        return copies

    def backward_down(n, _):
        gd[pl.ds(pl.multiple_of(n * chunk, chunk), chunk), :] = dot_tn(act[n], back_feed).astype(BF16)
        return 0

    def backward_up(n, _):
        back_up = (dot_nt(back_feed, dw[n]) * slope[n].astype(F32)).astype(BF16)
        bias_sum[pl.ds(pl.multiple_of(n * 8, 8), 8), :] = jnp.broadcast_to(
            row_sums(back_up.astype(F32)), (8, chunk)
        )
        gu[n] = dot_tn(low, back_up).astype(BF16)
        for copy in stores(n):
            copy.start()
        total[...] += dot_nt(back_up, uw[n])
        return 0

    def hop(i):
        for phases in streams:
            phases[i]()

    if orders:
        assert per == 2
        lax.fori_loop(0, 2, lambda i, z: backward_down(2 * i + 1 - dp_bit(1), z), 0)
        pl.semaphore_wait(pltpu.get_barrier_semaphore(), len(partners))
        hop(0)
        lax.fori_loop(0, 2, lambda i, z: backward_down(2 * i + dp_bit(1), z), 0)
    else:
        lax.fori_loop(0, 2 * per, backward_down, 0)
    hop(1)
    lax.fori_loop(0, 2 * per, backward_up, 0)
    for n in range(2 * per):
        for j in range(chunk // width):
            at = 6 * (model // width) + (n % per) * (chunk // width) + j
            (pre_a, pre_b)[n // per][at : at + 1, :] = bias_sum[n * 8 : n * 8 + 1, j * width : (j + 1) * width]
    back = total[...]
    put(0, row_sums(back * n1))
    put(1, row_sums(back))
    back = normalize_back(back * gain1, n1, root1)
    first[...] = back
    back_attend = back.astype(BF16)
    put(4, row_sums(back_attend.astype(F32)))
    for ctx, ow, do, go in ((ctx_a, ow_a, do_a, go_a), (ctx_b, ow_b, do_b, go_b)):
        do[...] = dot_nt(back_attend, ow[...]).astype(BF16)
        go[...] = dot_tn(back_attend, ctx[...]).astype(BF16)
    for n in range(2 * per):
        for copy in stores(n):
            copy.wait()
    hop(2)


def feed_forward(x, cot, contexts, output_weights, params, smalls, up_weights, down_weights, heads, orders,
                 collective_id, chunk=768):
    nq, model = x.shape
    width = contexts[0].shape[1]
    hidden = up_weights[0].shape[1]
    n = 2 * hidden // chunk
    here = pl.BlockSpec(memory_space=pltpu.VMEM)
    anywhere = pl.BlockSpec(memory_space=pl.ANY)
    pre_rows = 6 * (model // width) + hidden // width
    shape = jax.ShapeDtypeStruct
    state_shapes, hop_scratch, compiler = [], [], dict(vmem_limit_bytes=VM)
    for order in orders:
        cols = model // len(orders)
        state_shapes.append((1, hidden // 2, cols) if order[0] == "y" else (2, hidden // 4, cols))
        hop_scratch.append(pltpu.VMEM((2, hidden // 2, cols), BF16))
        hop_scratch += [pltpu.SemaphoreType.DMA((STREAM_SEMS,))] * 2
    if orders:
        compiler.update(collective_id=collective_id, has_side_effects=True)
    return pl.pallas_call(
        functools.partial(ffn_kernel, heads=heads, chunk=chunk, orders=orders),
        out_shape=(
            shape((nq, model), F32),
            shape((nq, model), F32),
            shape((nq, width), BF16),
            shape((nq, width), BF16),
            shape((model, width), BF16),
            shape((model, width), BF16),
            shape((pre_rows, width), F32),
            shape((pre_rows, width), F32),
            *(shape(s, BF16) for s in state_shapes),
            *((shape((2 * hidden, model), BF16),) if not orders else ()),
            shape((2, model, hidden), BF16),
        ),
        in_specs=[here] * 9 + [anywhere] * 4,
        out_specs=(here,) * (8 + len(orders)) + (anywhere,) * (1 if orders else 2),
        scratch_shapes=[
            pltpu.VMEM((n, model, chunk), BF16),
            pltpu.VMEM((n, chunk, model), BF16),
            pltpu.VMEM((n, nq, chunk), BF16),
            pltpu.VMEM((n, nq, chunk), BF16),
            pltpu.VMEM((2 * hidden, model), BF16),
            pltpu.VMEM((n, model, chunk), BF16),
            pltpu.VMEM((nq, model), F32),
            pltpu.VMEM((n * 8, chunk), F32),
            pltpu.VMEM((n * 8, chunk), F32),
            pltpu.SemaphoreType.DMA((2 * n,)),
            pltpu.SemaphoreType.DMA((2 * n,)),
            *hop_scratch,
        ],
        compiler_params=pltpu.CompilerParams(**compiler),
        cost_estimate=pl.CostEstimate(
            flops=12 * nq * model * 2 * hidden, bytes_accessed=100 * 2**20, transcendentals=nq * 4 * hidden
        ),
    )(x, cot, *contexts, *output_weights, params, *smalls, *up_weights, *down_weights)


def finish_kernel(index, *refs, count, heads, scale):
    refs = list(refs)
    take = lambda n: [refs.pop(0) for _ in range(n)]
    down, up, out, project = take(4)
    down_piece, up_piece, out_piece, project_piece = take(4)
    tokens_t, first, sums, params, small = take(5)
    project_w, out_w, up_w, down_w = take(4)
    project_a, query_a, value_a, out_a, out_shift_a, gain1_a, shift1_a = take(7)
    up_a, up_bias_a, down_a, down_shift_a, gain2_a, shift2_a, *table_a = take(9)
    tokens_o, project_o, query_o, value_o, out_o, out_shift_o, gain1_o, shift1_o = take(8)
    up_o, up_bias_o, down_o, down_shift_o, gain2_o, shift2_o, *table_o = take(9)
    project_r, query_r, value_r, out_r, out_shift_r, gain1_r, shift1_r = take(7)
    up_r, up_bias_r, down_r, down_shift_r, gain2_r, shift2_r, *table_r = take(9)
    thirds = project.shape[1] // 3
    wide = lambda ref: ref[...].astype(F32)
    renew = lambda average, weight, grad: 0.5 * average + 0.5 * (weight - grad * scale)

    down_o[...] = wide(down)
    up_o[...] = wide(up)
    out_o[...] = jnp.transpose(wide(out))
    for i in range(3):
        project_o[i] = project[:, i * thirds : (i + 1) * thirds].astype(F32)
    tokens_o[...] = first[...] + jnp.transpose(tokens_t[...])

    @pl.when(pl.program_id(0) == 0)
    def _():
        up_r[...] = renew(up_a[...], wide(up_w), wide(up_piece))
        down_r[...] = renew(down_a[...], wide(down_w), wide(down_piece))
        out_r[...] = renew(out_a[...], jnp.transpose(wide(out_w)), wide(out_piece))
        for i in range(3):
            project_r[i] = renew(project_a[i], project_w[i].astype(F32), project_piece[:, i * thirds : (i + 1) * thirds].astype(F32))
        width = sums.shape[1]

        def vector(ref, at, n):
            return jnp.concatenate([ref[at + i : at + i + 1, :] for i in range(n)], axis=1)

        def flat(o, r, a, weight, grad):
            n = a.shape[0]
            o[...] = grad.reshape(n)
            r[...] = renew(a[...], weight.reshape(n), grad.reshape(n))

        flat(query_o, query_r, query_a, small[heads : heads + 1, :], sums[8:9, :])
        flat(value_o, value_r, value_a, small[heads + 1 : heads + 2, :], sums[16:17, :])
        two = params.shape[1] // width
        commons = (
            (gain1_o, gain1_r, gain1_a),
            (shift1_o, shift1_r, shift1_a),
            (gain2_o, gain2_r, gain2_a),
            (shift2_o, shift2_r, shift2_a),
            (out_shift_o, out_shift_r, out_shift_a),
            (down_shift_o, down_shift_r, down_shift_a),
        )
        for i, (o, r, a) in enumerate(commons):
            flat(o, r, a, params[i : i + 1, :], vector(sums, 24 + two * i, two))
        many = up_bias_a.shape[0] // width
        flat(
            up_bias_o, up_bias_r, up_bias_a, vector(small, heads + 2, many), vector(sums, 24 + 6 * two, many)
        )
        for t, (o, r, a) in enumerate(zip(table_o, table_r, table_a)):
            n = a.shape[1]
            grad = sums[0:heads, t * 128 : t * 128 + n]
            o[...] = grad
            r[...] = renew(a[...], small[0:heads, t * 128 : t * 128 + n], grad)


def finish(index, totals, tokens_t, first, sums, params, small, weights, averages, count, tokens_count, heads):
    swap = lambda a: a.transpose(1, 0, 2) if a.ndim == 3 else a.T
    turned = (0, 3, 13, 14, 15)
    averages = [swap(a) if i in turned else a for i, a in enumerate(averages)]
    down, up, out, project = totals
    model = first.shape[1]
    nq = first.shape[0]
    width = project.shape[1] // 3
    steps = model // 128
    full = lambda a: pl.BlockSpec(a.shape, lambda i, d: (0,) * len(a.shape))
    rows = lambda a: pl.BlockSpec((a.shape[0] // steps, a.shape[1]), lambda i, d: (i, 0))
    piece = lambda a: pl.BlockSpec(
        (a.shape[0] // count, *a.shape[1:]), lambda i, d: (d[0],) + (0,) * (len(a.shape) - 1)
    )
    columns = lambda n: pl.BlockSpec((n, 128), lambda i, d: (0, i))
    shape = lambda s: jax.ShapeDtypeStruct(s, F32)
    project_w, out_w, up_w, down_w = weights
    in_specs = [rows(a) for a in totals] + [piece(a) for a in totals]
    in_specs += [rows(tokens_t), columns(nq), full(sums), full(params), full(small)]
    project_spec = pl.BlockSpec((3, model // count, width), lambda i, d: (0, d[0], 0))
    in_specs += [project_spec, full(out_w), piece(up_w), piece(down_w)] + [full(a) for a in averages]
    grads = [
        shape((3, model, width)), shape((width,)), shape((width,)), shape((width, model)), shape((model,)),
        shape((model,)), shape((model,)), shape(up.shape), shape((up.shape[1],)), shape(down.shape),
        shape((model,)), shape((model,)), shape((model,)), *(shape(a.shape) for a in averages[13:]),
    ]
    specs = [full(g) for g in grads]
    specs[0] = pl.BlockSpec((3, 128, width), lambda i, d: (0, i, 0))
    specs[3] = columns(width)
    specs[7] = rows(up)
    specs[9] = rows(down)
    tokens, *results = pl.pallas_call(
        functools.partial(finish_kernel, count=count, heads=heads, scale=1.0 / tokens_count),
        out_shape=(shape((nq, model)), *grads, *(shape(a.shape) for a in averages)),
        grid_spec=pltpu.PrefetchScalarGridSpec(
            num_scalar_prefetch=1,
            grid=(steps,),
            in_specs=in_specs,
            out_specs=(columns(nq), *specs, *(full(a) for a in averages)),
        ),
        compiler_params=pltpu.CompilerParams(vmem_limit_bytes=VM),
        cost_estimate=pl.CostEstimate(flops=2**24, bytes_accessed=40 * 2**20, transcendentals=0),
    )(index, *totals, *totals, tokens_t, first, sums, params, small, *weights, *averages)
    grads, renewed = results[:16], results[16:]
    grads = [swap(a) if i in turned and i != 3 else a for i, a in enumerate(grads)]
    return tokens, *grads, *(swap(a) if i in turned else a for i, a in enumerate(renewed))


def local(
    tokens,
    cotangent,
    form_number,
    sequence_bucket,
    horizontal_bucket,
    vertical_bucket,
    project_weight,
    query_bias,
    value_bias,
    output_weight,
    output_bias,
    first_gain,
    first_shift,
    up_weight,
    up_bias,
    down_weight,
    down_bias,
    second_gain,
    second_shift,
    sequence_table,
    horizontal_table,
    vertical_table,
    project_weight_average,
    query_bias_average,
    value_bias_average,
    output_weight_average,
    output_bias_average,
    first_gain_average,
    first_shift_average,
    up_weight_average,
    up_bias_average,
    down_weight_average,
    down_bias_average,
    second_gain_average,
    second_shift_average,
    sequence_table_average,
    horizontal_table_average,
    vertical_table_average,
):
    total_rows, model_width = tokens.shape
    local_width = project_weight.shape[2]
    local_heads = sequence_table.shape[1]
    hidden = up_weight.shape[1]
    share_rows = total_rows // lax.axis_size("head")
    head_index = lax.axis_index("head")
    share_start = head_index * share_rows
    block_rows = 128
    buckets = (sequence_bucket, horizontal_bucket, vertical_bucket)
    tables = (sequence_table, horizontal_table, vertical_table)
    bits = tuple((t.shape[0] - 1).bit_length() for t in tables)
    project_stack = project_weight.transpose(1, 0, 2)
    flat_project = project_stack.reshape(3 * model_width, local_width)

    params = jnp.concatenate(
        [first_gain, first_shift, second_gain, second_shift, output_bias, down_bias]
    ).reshape(6, model_width).astype(F32)
    lanes = [jnp.pad(t.T, ((0, 0), (0, local_width // 3 - t.shape[0]))) for t in tables]
    small = jnp.concatenate(
        [
            jnp.concatenate(lanes, axis=1),
            jnp.concatenate([query_bias, value_bias, up_bias]).reshape(-1, local_width),
        ],
        axis=0,
    ).astype(F32)
    small = jnp.pad(small, ((0, 16 - small.shape[0]), (0, 0)))
    smalls, project_weights = [small], [flat_project]
    output_weights, up_weights, down_weights = [output_weight], [up_weight], [down_weight]

    form_row = form_number.reshape(total_rows)
    form_own = lax.dynamic_slice_in_dim(form_row, share_start, share_rows, 0)
    code = encode(
        [rows_of(b, head_index, share_rows) for b in buckets], form_own[:, None] == form_row[None, :]
    )
    own_tokens = rows_of(tokens, head_index, share_rows)

    scaled, keys_t, values, probs, contexts = [], [], [], [], []
    for s in range(2):
        wq, wk, wv = (project_weights[s][i * model_width : (i + 1) * model_width] for i in range(3))
        bq = smalls[s][local_heads : local_heads + 1]
        bv = smalls[s][local_heads + 1 : local_heads + 2]
        q = ((mm(own_tokens, wq) + bq) * 0.125).astype(BF16)
        q = q * jnp.array(2.0**SCALE_BITS, BF16)
        kt = dot_general_t(wk, tokens).astype(BF16)
        v = (mm(tokens, wv) + bv).astype(BF16)
        if s == 0:
            fetch = (
                ("small", (0, -1, -1), small),
                ("all", (0, 3, 7), flat_project),
                ("all", (0, 4, 7), output_weight),
                ("first", (0, -1, -1), up_weight),
            )
        else:
            fetch = (("rest", (-1, 0, 4), up_part), ("all", (0, 3, 7), down_weight))
        p, context, *fetched = attend_fwd(code, smalls[s], q, kt, v, fetch, s, qb=block_rows)
        if s == 0:
            smalls.append(fetched[0])
            project_weights.append(fetched[1])
            output_weights.append(fetched[2])
            up_part = fetched[3]
        else:
            up_weights.append(fetched[0])
            down_weights.append(fetched[1])
        scaled.append(q)
        keys_t.append(kt)
        values.append(v)
        probs.append(p)
        contexts.append(context)
    fast = lax.axis_size("dp") == 16
    (
        layer_output, back_first, back_own, back_other, out_own, out_other, pre_own, pre_other, *grads
    ) = feed_forward(
        own_tokens, cotangent, contexts, output_weights, params, smalls, up_weights, down_weights, local_heads,
        BACK_PLAN[1][: BACK_CHUNKS[0]] if fast else (), 3,
    )

    sides = [
        (scaled[s], keys_t[s], values[s], (back_own, back_other)[s], probs[s]) for s in range(2)
    ]
    pre = (pre_own, pre_other)
    results = attend_backward(
        sides,
        code,
        tokens.T,
        project_weights,
        bits,
        (*(grads if fast else grads[1:]), out_own, out_other),
        pre,
        2,
        fast,
        BACK_PLAN,
        BACK_CHUNKS,
        qb=block_rows,
    )
    token_count = total_rows * lax.axis_size("dp")
    group_count = lax.axis_size("dp")
    group_index = lax.axis_index("dp")
    if fast:
        width = model_width // group_count
        output_piece = lax.dynamic_slice_in_dim(output_weight, group_index * width, width, 1)
        averages = (
            project_weight_average, query_bias_average, value_bias_average, output_weight_average,
            output_bias_average, first_gain_average, first_shift_average, up_weight_average, up_bias_average,
            down_weight_average, down_bias_average, second_gain_average, second_shift_average,
            sequence_table_average, horizontal_table_average, vertical_table_average,
        )
        return layer_output, *finish(
            jnp.full((1,), group_index, I32),
            results[:4],
            results[4],
            back_first,
            results[5],
            params,
            small,
            (project_stack, output_piece, up_weight, down_weight),
            averages,
            group_count,
            token_count,
            local_heads,
        )
    tokens_gradient, sums, far, sums_other = results[:4]
    tokens_gradient = tokens_gradient + swap_head(far).astype(F32)
    sums = sums + swap_head(sums_other)
    for bit in dp_bits():
        sums = sums + swap_dp(sums, bit)
    down_total, up_total = reduce_grad(grads[0][:hidden], grads[0][hidden:], True), reduce_grad(*grads[1], False)
    output_total = reduce_grad(out_own, out_other, True)
    project_total = reduce_grad(results[4], results[5], False)
    tokens_gradient = back_first + tokens_gradient.T
    project_total = project_total.reshape(model_width, 3, local_width)
    output_total = output_total.T
    query_bias_total, value_bias_total = sums[8], sums[16]
    tail = sums[24:].reshape(-1)
    (
        first_gain_total,
        first_shift_total,
        second_gain_total,
        second_shift_total,
        output_bias_total,
        down_bias_total,
    ) = (tail[i * model_width : (i + 1) * model_width] for i in range(6))
    up_bias_total = tail[6 * model_width :]
    sequence_total, horizontal_total, vertical_total = (
        sums[:local_heads, i * 128 : i * 128 + t.shape[0]].T for i, t in enumerate(tables)
    )
    up_weight_total, down_weight_total, output_weight_total = up_total, down_total, output_total

    def renew(average, weight, gradient):
        return 0.5 * average + 0.5 * (weight.astype(jnp.float32) - gradient / token_count)

    def part_of(array, along):
        width = array.shape[along] // group_count
        return lax.dynamic_slice_in_dim(array, group_index * width, width, along)

    return (
        layer_output,
        tokens_gradient,
        project_total,
        query_bias_total,
        value_bias_total,
        output_weight_total,
        output_bias_total,
        first_gain_total,
        first_shift_total,
        up_weight_total,
        up_bias_total,
        down_weight_total,
        down_bias_total,
        second_gain_total,
        second_shift_total,
        sequence_total,
        horizontal_total,
        vertical_total,
        renew(project_weight_average, part_of(project_weight, 0), part_of(project_total, 0)),
        renew(query_bias_average, query_bias, query_bias_total),
        renew(value_bias_average, value_bias, value_bias_total),
        renew(output_weight_average, part_of(output_weight, 1), part_of(output_weight_total, 1)),
        renew(output_bias_average, output_bias, output_bias_total),
        renew(first_gain_average, first_gain, first_gain_total),
        renew(first_shift_average, first_shift, first_shift_total),
        renew(up_weight_average, part_of(up_weight, 0), part_of(up_weight_total, 0)),
        renew(up_bias_average, up_bias, up_bias_total),
        renew(down_weight_average, part_of(down_weight, 0), part_of(down_weight_total, 0)),
        renew(down_bias_average, down_bias, down_bias_total),
        renew(second_gain_average, second_gain, second_gain_total),
        renew(second_shift_average, second_shift, second_shift_total),
        renew(sequence_table_average, sequence_table, sequence_total),
        renew(horizontal_table_average, horizontal_table, horizontal_total),
        renew(vertical_table_average, vertical_table, vertical_total),
    )


def solution(mesh):
    in_specs = (
        P("dp", None),
        P(("dp", "head"), None),
        P("dp", None),
        P("dp", None),
        P("dp", None),
        P("dp", None),
        P(None, None, "head"),
        P("head"),
        P("head"),
        P("head", None),
        P(),
        P(),
        P(),
        P(None, "head"),
        P("head"),
        P("head", None),
        P(),
        P(),
        P(),
        P(None, "head"),
        P(None, "head"),
        P(None, "head"),
        P("dp", None, "head"),
        P("head"),
        P("head"),
        P("head", "dp"),
        P(),
        P(),
        P(),
        P("dp", "head"),
        P("head"),
        P(("head", "dp"), None),
        P(),
        P(),
        P(),
        P(None, "head"),
        P(None, "head"),
        P(None, "head"),
    )
    out_specs = (
        P(("dp", "head"), None),
        P(("dp", "head"), None),
        P(None, None, "head"),
        P("head"),
        P("head"),
        P("head", None),
        P(),
        P(),
        P(),
        P(None, "head"),
        P("head"),
        P("head", None),
        P(),
        P(),
        P(),
        P(None, "head"),
        P(None, "head"),
        P(None, "head"),
        P("dp", None, "head"),
        P("head"),
        P("head"),
        P("head", "dp"),
        P(),
        P(),
        P(),
        P("dp", "head"),
        P("head"),
        P(("head", "dp"), None),
        P(),
        P(),
        P(),
        P(None, "head"),
        P(None, "head"),
        P(None, "head"),
    )
    return jax.shard_map(local, mesh=mesh, in_specs=in_specs, out_specs=out_specs, check_vma=False)
```
